32 devices in a mesh: shard: 8 (over z, core), ctx: 2 (over x), tp: 2 (over y).
Axes of the slice: x: 2, y: 2, z: 4, core: 2. Of those that a mesh axis runs over, the one named last changes fastest.
Arguments:
- tokens: bfloat16 [16, 2048, 1024], P('shard', 'ctx'), may hold values from -6 to 6
- cotangent: bfloat16 [16, 2048, 1024], P('shard', 'ctx'), may hold values from -6 to 6
- adapter_pick: int32 [16], P('shard'), may hold values from 0 to 7
- positions: int32 [3, 16, 2048], P(None, 'shard', 'ctx'), may hold values from 0 to 15
- first_gain: float32 [1024], replicated, may hold values from 0.1 to 1.9
- first_shift: float32 [1024], replicated, may hold values from -3 to 3
- joined_weight: bfloat16 [1024, 3, 1024], P('shard', None, 'tp'), may hold values from -0.1875 to 0.1875
- joined_bias: float32 [3, 1024], P(None, 'tp'), may hold values from -3 to 3
- output_weight: bfloat16 [1024, 1024], P('tp', 'shard'), may hold values from -0.75 to 0.75
- mixing_exit_offset: float32 [1024], replicated, may hold values from -3 to 3
- second_gain: float32 [1024], replicated, may hold values from 0.1 to 1.9
- second_shift: float32 [1024], replicated, may hold values from -3 to 3
- expand_weight: bfloat16 [1024, 4096], P('shard', 'tp'), may hold values from -0.1875 to 0.1875
- widening_offset: float32 [4096], P('tp'), may hold values from -3 to 3
- reduce_weight: bfloat16 [4096, 1024], P('tp', 'shard'), may hold values from -0.09375 to 0.09375
- shrinking_offset: float32 [1024], replicated, may hold values from -3 to 3
- joined_down: bfloat16 [8, 1024, 16], replicated, may hold values from -0.1875 to 0.1875
- joined_up: bfloat16 [8, 16, 3, 1024], P(None, None, None, 'tp'), may hold values from -1.5 to 1.5
- output_down: bfloat16 [8, 1024, 16], P(None, 'tp'), may hold values from -0.75 to 0.75
- output_up: bfloat16 [8, 16, 1024], replicated, may hold values from -1.5 to 1.5
- expand_down: bfloat16 [8, 1024, 16], replicated, may hold values from -0.1875 to 0.1875
- expand_up: bfloat16 [8, 16, 4096], P(None, None, 'tp'), may hold values from -1.5 to 1.5
- reduce_down: bfloat16 [8, 4096, 16], P(None, 'tp'), may hold values from -0.09375 to 0.09375
- reduce_up: bfloat16 [8, 16, 1024], replicated, may hold values from -1.5 to 1.5
Outputs:
- output: bfloat16 [16, 2048, 1024], P('shard', 'ctx')
- tokens_grad: bfloat16 [16, 2048, 1024], P('shard', ('ctx', 'tp'))
- joined_down_grad: float32 [8, 1024, 16], replicated
- joined_up_grad: float32 [8, 16, 3, 1024], P(None, None, None, 'tp')
- output_down_grad: float32 [8, 1024, 16], P(None, 'tp')
- output_up_grad: float32 [8, 16, 1024], replicated
- expand_down_grad: float32 [8, 1024, 16], replicated
- expand_up_grad: float32 [8, 16, 4096], P(None, None, 'tp')
- reduce_down_grad: float32 [8, 4096, 16], P(None, 'tp')
- reduce_up_grad: float32 [8, 16, 1024], replicated
The draws below stay inside these ranges and needn't reach their ends.
Inputs may be any that keep to these rules, and one draw needn't show every extreme that they name: `positions`: integer places on a grid of 16 frames by 16 by 16 patches.
All inputs are finite; a program needn't handle non-finite values.
Results may differ from the reference program's by a relative error of at most 0.022.
The reference program's roundings to bfloat16 on the way count: a program that leaves them out, or rounds other values in their place, can miss the bound.
Values may be sent and summed in bfloat16 or wider, within the bound.
A program may use at most 448 MiB of HBM per device.

```python
import math
import jax
import jax.numpy as jnp
from jax import lax

EMBED_WIDTH = 1024
HEADS = 16
HEAD_DIM = 64
FF = 4096
ADAPT_DIM = 16
ADAPTERS = 8
CLIP_LEN = 2048
CLIPS = 16


def place_ends(values, key, least, largest):
    place = [jax.random.randint(jax.random.fold_in(key, axis), (), 0, length) for axis, length in enumerate(values.shape)]
    longest = values.shape.index(max(values.shape))
    beside = place[:longest] + [(place[longest] + 1) % values.shape[longest]] + place[longest + 1:]
    return values.at[tuple(place)].set(least).at[tuple(beside)].set(largest)


def level_of(key, shape, pieces, least, top_value):
    loudness, own = 1.0, jax.random.fold_in(key, 6)
    for axis_at, shards_of in pieces:
        draws = jnp.exp(jax.random.uniform(jax.random.fold_in(own, axis_at), (shards_of,), jnp.float32, least / len(pieces), top_value / len(pieces)))
        loudness = loudness * jnp.repeat(draws, shape[axis_at] // shards_of).reshape([-1 if axis == axis_at else 1 for axis in range(len(shape))])
    return loudness


def scatter_about(own_key, dims, width, most, shards=(), kind=jnp.bfloat16):
    factor_of = level_of(own_key, dims, shards, -0.22, 0.18) if shards else 1.0
    values = jax.random.normal(own_key, dims, jnp.float32) * width * factor_of
    return jnp.minimum(jnp.maximum(values, -most), most).astype(kind)


def setup_inputs(seed: int = 0) -> dict:
    key_of = jax.random.split(jax.random.key(seed), 25)
    tokens = scatter_about(key_of[0], (CLIPS, CLIP_LEN, EMBED_WIDTH), 1.0, 6.0, ((0, 8), (1, 2)))
    cotangent = scatter_about(key_of[1], (CLIPS, CLIP_LEN, EMBED_WIDTH), 1.0, 6.0, ((0, 8), (1, 2)))
    adapter_pick = place_ends(jax.random.randint(key_of[2], (CLIPS,), 0, ADAPTERS), jax.random.fold_in(key_of[2], 1), 0, ADAPTERS - 1).astype(jnp.int32)
    positions = place_ends(jax.random.randint(key_of[3], (3, CLIPS, CLIP_LEN), 0, 16), jax.random.fold_in(key_of[3], 1), 0, 15).astype(jnp.int32)
    first_gain = jnp.clip(1.0 + 0.18 * jax.random.normal(key_of[4], (EMBED_WIDTH,), jnp.float32), 0.1, 1.9)
    first_shift = scatter_about(key_of[5], (EMBED_WIDTH,), 0.5, 3.0, (), jnp.float32)
    joined_weight = scatter_about(key_of[6], (EMBED_WIDTH, 3, EMBED_WIDTH), EMBED_WIDTH ** -0.5, 0.1875, ((0, 8), (2, 2)))
    joined_bias = scatter_about(key_of[7], (3, EMBED_WIDTH), 0.5, 3.0, ((1, 2),), jnp.float32)
    output_weight = scatter_about(key_of[8], (EMBED_WIDTH, EMBED_WIDTH), (EMBED_WIDTH // 16) ** -0.5, 0.75, ((0, 2), (1, 8)))
    mixing_exit_offset = scatter_about(key_of[9], (EMBED_WIDTH,), 0.5, 3.0, (), jnp.float32)
    second_gain = jnp.clip(1.0 + 0.18 * jax.random.normal(key_of[10], (EMBED_WIDTH,), jnp.float32), 0.1, 1.9)
    second_shift = scatter_about(key_of[11], (EMBED_WIDTH,), 0.5, 3.0, (), jnp.float32)
    expand_weight = scatter_about(key_of[12], (EMBED_WIDTH, FF), EMBED_WIDTH ** -0.5, 0.1875, ((0, 8), (1, 2)))
    widening_offset = scatter_about(key_of[13], (FF,), 0.5, 3.0, ((0, 2),), jnp.float32)
    reduce_weight = scatter_about(key_of[14], (FF, EMBED_WIDTH), FF ** -0.5, 0.09375, ((0, 2), (1, 8)))
    shrinking_offset = scatter_about(key_of[15], (EMBED_WIDTH,), 0.5, 3.0, (), jnp.float32)
    joined_down = scatter_about(key_of[16], (ADAPTERS, EMBED_WIDTH, ADAPT_DIM), EMBED_WIDTH ** -0.5, 0.1875)
    joined_up = scatter_about(key_of[17], (ADAPTERS, ADAPT_DIM, 3, EMBED_WIDTH), ADAPT_DIM ** -0.5, 1.5, ((3, 2),))
    output_down = scatter_about(key_of[18], (ADAPTERS, EMBED_WIDTH, ADAPT_DIM), (EMBED_WIDTH // 16) ** -0.5, 0.75, ((1, 2),))
    output_up = scatter_about(key_of[19], (ADAPTERS, ADAPT_DIM, EMBED_WIDTH), ADAPT_DIM ** -0.5, 1.5)
    expand_down = scatter_about(key_of[20], (ADAPTERS, EMBED_WIDTH, ADAPT_DIM), EMBED_WIDTH ** -0.5, 0.1875)
    expand_up = scatter_about(key_of[21], (ADAPTERS, ADAPT_DIM, FF), ADAPT_DIM ** -0.5, 1.5, ((2, 2),))
    reduce_down = scatter_about(key_of[22], (ADAPTERS, FF, ADAPT_DIM), FF ** -0.5, 0.09375, ((1, 2),))
    reduce_up = scatter_about(key_of[23], (ADAPTERS, ADAPT_DIM, EMBED_WIDTH), ADAPT_DIM ** -0.5, 1.5)
    return {"tokens": tokens, "cotangent": cotangent, "adapter_pick": adapter_pick, "positions": positions, "first_gain": first_gain, "first_shift": first_shift, "joined_weight": joined_weight, "joined_bias": joined_bias, "output_weight": output_weight, "mixing_exit_offset": mixing_exit_offset, "second_gain": second_gain, "second_shift": second_shift, "expand_weight": expand_weight, "widening_offset": widening_offset, "reduce_weight": reduce_weight, "shrinking_offset": shrinking_offset, "joined_down": joined_down, "joined_up": joined_up, "output_down": output_down, "output_up": output_up, "expand_down": expand_down, "expand_up": expand_up, "reduce_down": reduce_down, "reduce_up": reduce_up}


@jax.custom_vjp
def narrow_coordinates(v):
    return lax.optimization_barrier(v.astype(jnp.bfloat16)).astype(jnp.float32)

@jax.custom_vjp
def slim_update_pullback(v):
    return v

def low_keep(v):
    return (narrow_coordinates(v), None)

def low_pass(kept, grad):
    return (grad,)

def back_keep(v):
    return (v, None)

def back_low(kept, grad):
    return (narrow_coordinates(grad),)
narrow_coordinates.defvjp(low_keep, low_pass)
slim_update_pullback.defvjp(back_keep, back_low)
eps_norm = 1e-06
score_scale = 0.125
highest = lax.Precision.HIGHEST

def linear_composition(left, right):
    return jnp.dot(left, right, precision=highest, preferred_element_type=jnp.float32)

def normalize(values, gain, shift):
    centred = values - lax.optimization_barrier(jnp.mean(values, -1, keepdims=True))
    inverse = lax.rsqrt(lax.optimization_barrier(jnp.mean(centred * centred, -1, keepdims=True)) + eps_norm)
    return centred * inverse * gain + shift

def rope_tables(places):
    band = jnp.arange(10, dtype=jnp.float32)
    rates = jnp.exp(band * (-math.log(10000.0) / 10.0))
    angle = places.astype(jnp.float32)[..., None] * rates
    cos_parts = []
    sin_parts = []
    for band_index in range(3):
        cosine = jnp.cos(angle[band_index])
        sine = jnp.sin(angle[band_index])
        cos_parts = cos_parts + [cosine, cosine]
        sin_parts = sin_parts + [-sine, sine]
    rest_shape = angle.shape[1:-1] + (4,)
    cos_parts.append(jnp.ones(rest_shape, jnp.float32))
    sin_parts.append(jnp.zeros(rest_shape, jnp.float32))
    return (jnp.concatenate(cos_parts, -1), jnp.concatenate(sin_parts, -1))

def swap_pairs(values):
    leading = values.shape[:-1]
    turned = values[..., :60].reshape(leading + (3, 2, 10))[..., ::-1, :].reshape(leading + (60,))
    return jnp.concatenate([turned, values[..., 60:]], -1)

def rotate(values, cosine, sine):
    return values * cosine[..., None, :] + swap_pairs(values) * sine[..., None, :]

def attend(query, key, value):
    block = min(512, CLIP_LEN)

    def one_block(query_block):
        scores = slim_update_pullback(jnp.einsum('qhd,khd->hqk', query_block, key, precision=highest) * score_scale)
        expd = jnp.exp(scores - lax.optimization_barrier(jnp.max(scores, -1, keepdims=True)))
        probs = expd / lax.optimization_barrier(jnp.sum(expd, -1, keepdims=True))
        return jnp.einsum('hqk,khd->qhd', narrow_coordinates(probs), value, precision=highest)
    blocks = query.reshape((CLIP_LEN // block, block) + query.shape[1:])
    result = lax.map(jax.checkpoint(one_block), blocks)
    return result.reshape(query.shape)

def reference(tokens, cotangent, adapter_pick, positions, first_gain, first_shift, joined_weight, joined_bias, output_weight, mixing_exit_offset, second_gain, second_shift, expand_weight, widening_offset, reduce_weight, shrinking_offset, joined_down, joined_up, output_down, output_up, expand_down, expand_up, reduce_down, reduce_up):
    combined_projection_dense = joined_weight.astype(jnp.float32).reshape(EMBED_WIDTH, 3 * EMBED_WIDTH)
    combined_offset = joined_bias.reshape(3 * EMBED_WIDTH)
    exit_projection_dense = output_weight.astype(jnp.float32)
    widening_combined_coefficients = expand_weight.astype(jnp.float32)
    shrinking_dense = reduce_weight.astype(jnp.float32)
    places_all = jnp.transpose(positions, (1, 0, 2))

    def encoder_block_pass(block_arguments, combined_narrow_factor, combined_broad_factor, exit_narrow_factor, exit_broad_factor, widening_narrow_factor, widening_broad_factor, shrinking_narrow_factor, shrinking_broad_factor):

        def step(carry, items):
            tokens_clip, places_clip, pick_video_segment_module = items
            initial_standardized = narrow_coordinates(normalize(tokens_clip, first_gain, first_shift))
            initial_slim_derivative = narrow_coordinates(slim_update_pullback(linear_composition(initial_standardized, combined_narrow_factor[pick_video_segment_module])))
            mapped_vectors = linear_composition(initial_standardized, combined_projection_dense) + combined_offset + linear_composition(initial_slim_derivative, combined_broad_factor[pick_video_segment_module].reshape(ADAPT_DIM, 3 * EMBED_WIDTH))
            mapped_vectors = slim_update_pullback(mapped_vectors).reshape(CLIP_LEN, 3, HEADS, HEAD_DIM)
            cosine, sine = rope_tables(places_clip)
            query = narrow_coordinates(rotate(mapped_vectors[:, 0], cosine, sine))
            key = narrow_coordinates(rotate(mapped_vectors[:, 1], cosine, sine))
            value = narrow_coordinates(mapped_vectors[:, 2])
            mixing_outcome = narrow_coordinates(slim_update_pullback(attend(query, key, value).reshape(CLIP_LEN, EMBED_WIDTH)))
            middle_slim_derivative = narrow_coordinates(slim_update_pullback(linear_composition(mixing_outcome, exit_narrow_factor[pick_video_segment_module])))
            side_path = slim_update_pullback(linear_composition(mixing_outcome, exit_projection_dense) + mixing_exit_offset + linear_composition(middle_slim_derivative, exit_broad_factor[pick_video_segment_module]))
            first_hidden = tokens_clip + side_path
            latter_standardized = narrow_coordinates(normalize(first_hidden, second_gain, second_shift))
            penultimate_slim_derivative = narrow_coordinates(slim_update_pullback(linear_composition(latter_standardized, widening_narrow_factor[pick_video_segment_module])))
            skip_stream_vectors = slim_update_pullback(linear_composition(latter_standardized, widening_combined_coefficients) + widening_offset + linear_composition(penultimate_slim_derivative, widening_broad_factor[pick_video_segment_module]))
            gaussian_error_unit = narrow_coordinates(jax.nn.gelu(skip_stream_vectors, approximate=False))
            closing_slim_derivative = narrow_coordinates(slim_update_pullback(linear_composition(gaussian_error_unit, shrinking_narrow_factor[pick_video_segment_module])))
            perceptron_path = slim_update_pullback(linear_composition(gaussian_error_unit, shrinking_dense) + shrinking_offset + linear_composition(closing_slim_derivative, shrinking_broad_factor[pick_video_segment_module]))
            return (carry, first_hidden + perceptron_path)
        start = jnp.zeros((), jnp.float32)
        _, results = lax.scan(step, start, (block_arguments, places_all, adapter_pick))
        return results
    factors = (joined_down, joined_up, output_down, output_up, expand_down, expand_up, reduce_down, reduce_up)
    factors = tuple((item.astype(jnp.float32) for item in factors))
    outputs, pullback = jax.vjp(encoder_block_pass, tokens.astype(jnp.float32), *factors)
    grads = pullback(cotangent.astype(jnp.float32))
    return (outputs.astype(jnp.bfloat16), grads[0].astype(jnp.bfloat16), grads[1], grads[2], grads[3], grads[4], grads[5], grads[6], grads[7], grads[8])
```

```python
import functools
import math

import jax
import jax.numpy as jnp
from jax import lax
from jax.experimental import pallas as pl
from jax.experimental.pallas import tpu as pltpu
from jax.sharding import PartitionSpec as P

eps_norm = 1e-06
score_scale = 0.125


def rope_tables(places):
    band = jnp.arange(10, dtype=jnp.float32)
    rates = jnp.exp(band * (-math.log(10000.0) / 10.0))
    angle = places.astype(jnp.float32)[..., None] * rates
    cos_parts = []
    sin_parts = []
    for band_index in range(3):
        cosine = jnp.cos(angle[band_index])
        sine = jnp.sin(angle[band_index])
        cos_parts = cos_parts + [cosine, cosine]
        sin_parts = sin_parts + [-sine, sine]
    rest_shape = angle.shape[1:-1] + (4,)
    cos_parts.append(jnp.ones(rest_shape, jnp.float32))
    sin_parts.append(jnp.zeros(rest_shape, jnp.float32))
    return (jnp.concatenate(cos_parts, -1), jnp.concatenate(sin_parts, -1))


def swap_pairs(values):
    leading = values.shape[:-1]
    turned = values[..., :60].reshape(leading + (3, 2, 10))[..., ::-1, :].reshape(leading + (60,))
    return jnp.concatenate([turned, values[..., 60:]], -1)


def rotate(values, cosine, sine):
    return values * cosine[..., None, :] + swap_pairs(values) * sine[..., None, :]


def rotate_back(grads, cosine, sine):
    return grads * cosine[..., None, :] + swap_pairs(grads * sine[..., None, :])


def norm_forward(values, gain, shift):
    centred = values - jnp.mean(values, -1, keepdims=True)
    inverse = lax.rsqrt(jnp.mean(centred * centred, -1, keepdims=True) + eps_norm)
    scaled = centred * inverse
    return (scaled * gain + shift, scaled, inverse)


def norm_back(grads, scaled, inverse, gain):
    weighted = grads * gain
    return inverse * (
        weighted
        - jnp.mean(weighted, -1, keepdims=True)
        - scaled * jnp.mean(weighted * scaled, -1, keepdims=True)
    )


def select_factor(choose, table):
    return jnp.einsum("ca,a...->c...", choose, table, preferred_element_type=jnp.float32).astype(
        jnp.bfloat16
    )


def gelu_exact(values):
    return jax.nn.gelu(values, approximate=False)


def matrix_product(form, left, right):
    return jnp.einsum(form, left, right, preferred_element_type=jnp.float32)


def general_shards(
    tokens,
    cotangent,
    adapter_pick,
    positions,
    first_gain,
    first_shift,
    joined_weight,
    joined_bias,
    output_weight,
    mixing_exit_offset,
    second_gain,
    second_shift,
    expand_weight,
    widening_offset,
    reduce_weight,
    shrinking_offset,
    joined_down,
    joined_up,
    output_down,
    output_up,
    expand_down,
    expand_up,
    reduce_down,
    reduce_up,
):
    whole_joined, whole_output, whole_expand, whole_reduce = (
        lax.all_gather(joined_weight, "shard", axis=0, tiled=True),
        lax.all_gather(output_weight, "shard", axis=1, tiled=True),
        lax.all_gather(expand_weight, "shard", axis=0, tiled=True),
        lax.all_gather(reduce_weight, "shard", axis=1, tiled=True),
    )
    clip_count, local_len, width = tokens.shape
    local_width = whole_joined.shape[2]
    head_count = local_width // 64
    choose = (
        adapter_pick[:, None] == jnp.arange(joined_down.shape[0], dtype=jnp.int32)[None, :]
    ).astype(jnp.bfloat16)
    select_joined_down = select_factor(choose, joined_down)
    select_joined_up = select_factor(choose, joined_up)
    select_output_down = select_factor(choose, output_down)
    select_output_up = select_factor(choose, output_up)
    select_expand_down = select_factor(choose, expand_down)
    select_expand_up = select_factor(choose, expand_up)
    select_reduce_down = select_factor(choose, reduce_down)
    select_reduce_up = select_factor(choose, reduce_up)
    cosine, sine = rope_tables(positions)
    block_arguments = tokens.astype(jnp.float32)
    norm_one, scaled_one, inverse_one = norm_forward(block_arguments, first_gain, first_shift)
    initial_standardized = norm_one.astype(jnp.bfloat16)
    initial_slim_derivative = matrix_product(
        "zgh,zhe->zge", initial_standardized, select_joined_down
    ).astype(jnp.bfloat16)
    mapped_vectors = (
        matrix_product("cld,dje->clje", initial_standardized, whole_joined)
        + joined_bias
        + matrix_product("uip,upqg->uiqg", initial_slim_derivative, select_joined_up)
    )
    head_shape = (clip_count, local_len, head_count, 64)
    query = rotate(mapped_vectors[:, :, 0].reshape(head_shape), cosine, sine).astype(jnp.bfloat16)
    keys = rotate(mapped_vectors[:, :, 1].reshape(head_shape), cosine, sine).astype(jnp.bfloat16)
    values = mapped_vectors[:, :, 2].reshape(head_shape).astype(jnp.bfloat16)
    stats_shape = (clip_count, head_count, local_len)
    run_max = jnp.full(stats_shape, -1e30, jnp.float32)
    key_part = lax.all_gather(keys, "ctx", axis=1, tiled=True)
    value_part = lax.all_gather(values, "ctx", axis=1, tiled=True)
    scores = matrix_product("cqhd,ckhd->chqk", query, key_part) * score_scale
    new_max = jnp.maximum(run_max, jnp.max(scores, -1))
    weights = jnp.exp(scores - new_max[..., None])
    run_total = jnp.sum(weights, -1)
    update = matrix_product("chqk,ckhd->cqhd", weights.astype(jnp.bfloat16), value_part)
    accum = update
    run_max, run_total, accum = (new_max, run_total, accum)
    log_total = run_max + jnp.log(run_total)
    attended_full = accum / jnp.transpose(run_total, (0, 2, 1))[..., None]
    mixing_outcome = attended_full.reshape(clip_count, local_len, local_width).astype(jnp.bfloat16)
    out_part = matrix_product("cle,ed->cld", mixing_outcome, whole_output)
    rank_partial = matrix_product("fig,fgt->fit", mixing_outcome, select_output_down)
    output_total, rank_sum = (
        lax.psum(out_part.astype(jnp.bfloat16), "tp").astype(jnp.float32),
        lax.psum(rank_partial.astype(jnp.bfloat16), "tp").astype(jnp.float32),
    )
    middle_slim_derivative = rank_sum.astype(jnp.bfloat16)
    first_hidden = (
        block_arguments
        + output_total
        + mixing_exit_offset
        + matrix_product("wnk,wke->wne", middle_slim_derivative, select_output_up)
    )
    norm_two, scaled_two, inverse_two = norm_forward(first_hidden, second_gain, second_shift)
    latter_standardized = norm_two.astype(jnp.bfloat16)
    penultimate_slim_derivative = matrix_product(
        "zgh,zhe->zge", latter_standardized, select_expand_down
    ).astype(jnp.bfloat16)
    skip_stream_vectors = (
        matrix_product("cld,df->clf", latter_standardized, whole_expand)
        + widening_offset
        + matrix_product("uqz,uze->uqe", penultimate_slim_derivative, select_expand_up)
    )
    activity, gelu_pull = jax.vjp(gelu_exact, skip_stream_vectors)
    gaussian_error_unit = activity.astype(jnp.bfloat16)
    mlp_part = matrix_product("clf,fd->cld", gaussian_error_unit, whole_reduce)
    fourth_rank_partial = matrix_product("xpv,xvy->xpy", gaussian_error_unit, select_reduce_down)
    feedforward_sum, rank_four_sum = (
        lax.psum(mlp_part.astype(jnp.bfloat16), "tp").astype(jnp.float32),
        lax.psum(fourth_rank_partial.astype(jnp.bfloat16), "tp").astype(jnp.float32),
    )
    closing_slim_derivative = rank_four_sum.astype(jnp.bfloat16)
    output = (
        first_hidden
        + feedforward_sum
        + shrinking_offset
        + matrix_product("wnk,wke->wne", closing_slim_derivative, select_reduce_up)
    ).astype(jnp.bfloat16)
    back_joined, back_output, back_expand, back_reduce = (
        lax.all_gather(joined_weight, "shard", axis=0, tiled=True),
        lax.all_gather(output_weight, "shard", axis=1, tiled=True),
        lax.all_gather(expand_weight, "shard", axis=0, tiled=True),
        lax.all_gather(reduce_weight, "shard", axis=1, tiled=True),
    )
    reduce_up_term = matrix_product("vkn,vkm->vnm", closing_slim_derivative, cotangent)
    gradient_fourth = matrix_product("abj,awj->abw", cotangent, select_reduce_up).astype(
        jnp.bfloat16
    )
    reduce_down_term = matrix_product("mpg,mpu->mgu", gaussian_error_unit, gradient_fourth)
    grad_active = matrix_product("cld,fd->clf", cotangent, back_reduce) + matrix_product(
        "gez,guz->geu", gradient_fourth, select_reduce_down
    )
    residual_gradient = gelu_pull(grad_active)[0].astype(jnp.bfloat16)
    expand_up_term = matrix_product("jge,jgn->jen", penultimate_slim_derivative, residual_gradient)
    grad_norm_part = matrix_product("clf,df->cld", residual_gradient, back_expand)
    third_gradient_part = matrix_product("aik,adk->aid", residual_gradient, select_expand_up)
    norm_gradient_sum, grad_three_sum = (
        lax.psum(grad_norm_part.astype(jnp.bfloat16), "tp").astype(jnp.float32),
        lax.psum(third_gradient_part.astype(jnp.bfloat16), "tp").astype(jnp.float32),
    )
    gradient_third = grad_three_sum.astype(jnp.bfloat16)
    expand_down_term = matrix_product("kgt,kgh->kth", latter_standardized, gradient_third)
    second_norm_gradient = norm_gradient_sum + matrix_product(
        "jqt,jit->jqi", gradient_third, select_expand_down
    )
    grad_hidden = cotangent.astype(jnp.float32) + norm_back(
        second_norm_gradient, scaled_two, inverse_two, second_gain
    )
    branch_gradient = grad_hidden.astype(jnp.bfloat16)
    output_up_term = matrix_product("vkn,vkm->vnm", middle_slim_derivative, branch_gradient)
    gradient_second = matrix_product("abj,awj->abw", branch_gradient, select_output_up).astype(
        jnp.bfloat16
    )
    output_down_term = matrix_product("nua,nui->nai", mixing_outcome, gradient_second)
    grad_attended = (
        (
            matrix_product("cld,ed->cle", branch_gradient, back_output)
            + matrix_product("gsq,ghq->gsh", gradient_second, select_output_down)
        )
        .astype(jnp.bfloat16)
        .reshape(head_shape)
    )
    key_whole, value_whole = (
        lax.all_gather(keys, "ctx", axis=1, tiled=True),
        lax.all_gather(values, "ctx", axis=1, tiled=True),
    )
    flat_shape = (clip_count, local_len, local_width)

    def clip_back(items):
        query_clip, key_clip, value_clip, grad_clip, total_clip = items
        scores = matrix_product("qhd,khd->hqk", query_clip, key_clip) * score_scale
        probs = jnp.exp(scores - total_clip[..., None])
        grad_probs = matrix_product("qhd,khd->hqk", grad_clip, value_clip)
        middle = jnp.sum(probs * grad_probs, -1, keepdims=True)
        grad_scores = (probs * (grad_probs - middle)).astype(jnp.bfloat16)
        grad_query = matrix_product("hqk,khd->qhd", grad_scores, key_clip) * score_scale
        grad_key = matrix_product("hqk,qhd->khd", grad_scores, query_clip) * score_scale
        grad_value = matrix_product("hqk,qhd->khd", probs.astype(jnp.bfloat16), grad_clip)
        return (grad_query, grad_key, grad_value)

    grad_query, key_terms, value_terms = lax.map(
        clip_back, (query, key_whole, value_whole, grad_attended, log_total)
    )
    full_len = key_whole.shape[1]
    key_sum, value_sum = (
        lax.psum_scatter(
            key_terms.reshape(clip_count, full_len, local_width).astype(jnp.bfloat16),
            "ctx",
            scatter_dimension=1,
            tiled=True,
        ).astype(jnp.float32),
        lax.psum_scatter(
            value_terms.reshape(clip_count, full_len, local_width).astype(jnp.bfloat16),
            "ctx",
            scatter_dimension=1,
            tiled=True,
        ).astype(jnp.float32),
    )
    query_key_value_gradient = jnp.stack(
        [
            rotate_back(grad_query, cosine, sine).reshape(flat_shape),
            rotate_back(key_sum.reshape(head_shape), cosine, sine).reshape(flat_shape),
            value_sum,
        ],
        axis=2,
    ).astype(jnp.bfloat16)
    joined_up_term = matrix_product(
        "pvh,pvfo->phfo", initial_slim_derivative, query_key_value_gradient
    )
    first_gradient_part = matrix_product(
        "kxsd,ktsd->kxt", query_key_value_gradient, select_joined_up
    )
    grad_norm_one_part = matrix_product("clje,dje->cld", query_key_value_gradient, back_joined)
    gradient_first = lax.psum(first_gradient_part.astype(jnp.bfloat16), "tp")
    grad_norm_share = lax.psum_scatter(
        grad_norm_one_part.astype(jnp.bfloat16), "tp", scatter_dimension=1, tiled=True
    ).astype(jnp.float32)
    joined_down_term = matrix_product("kgt,kgh->kth", initial_standardized, gradient_first)
    half_len = grad_norm_share.shape[1]
    begin = lax.axis_index("tp") * half_len

    def shared_rows(array):
        return lax.dynamic_slice_in_dim(array, begin, half_len, 1)

    grad_norm_one = grad_norm_share + matrix_product(
        "jqt,jit->jqi", shared_rows(gradient_first), select_joined_down
    )
    tokens_grad = (
        shared_rows(grad_hidden)
        + norm_back(grad_norm_one, shared_rows(scaled_one), shared_rows(inverse_one), first_gain)
    ).astype(jnp.bfloat16)
    choose_full = choose.astype(jnp.float32)

    def by_adapter(term):
        return jnp.einsum(
            "ca,c...->a...",
            choose_full,
            term,
            precision=lax.Precision.HIGHEST,
            preferred_element_type=jnp.float32,
        )

    summed = lax.psum(
        (
            by_adapter(joined_down_term),
            by_adapter(joined_up_term),
            by_adapter(output_down_term),
            by_adapter(output_up_term),
            by_adapter(expand_down_term),
            by_adapter(expand_up_term),
            by_adapter(reduce_down_term),
            by_adapter(reduce_up_term),
        ),
        ("shard", "ctx"),
    )
    return (
        output,
        tokens_grad,
        summed[0],
        summed[1],
        summed[2],
        summed[3],
        summed[4],
        summed[5],
        summed[6],
        summed[7],
    )


B16 = jnp.bfloat16
F32 = jnp.float32
VMEM_LIMIT = 60 * 2**20
exp_scale = score_scale * math.log2(math.e)


def dot(left, right, left_dim=1, right_dim=0):
    return lax.dot_general(
        left, right, (((left_dim,), (right_dim,)), ((), ())), preferred_element_type=F32
    )


def params():
    return pltpu.CompilerParams(vmem_limit_bytes=VMEM_LIMIT)


def low_lanes():
    return lax.broadcasted_iota(jnp.int32, (1, 128), 1) < 64


def partner(values):
    lane = lax.broadcasted_iota(jnp.int32, (1, 128), 1) % 64 % 20
    return jnp.where(lane < 10, pltpu.roll(values, 118, 1), pltpu.roll(values, 10, 1))


def row_norm(values):
    centred = values - jnp.mean(values, -1, keepdims=True)
    inverse = lax.rsqrt(jnp.mean(centred * centred, -1, keepdims=True) + eps_norm)
    return centred * inverse, inverse


def back_norm(weighted, scaled, inverse):
    return inverse * (
        weighted
        - jnp.mean(weighted, -1, keepdims=True)
        - scaled * jnp.mean(weighted * scaled, -1, keepdims=True)
    )


def project_body(
    side, x_ref, gain_ref, shift_ref, w_own, w_other, bias_ref, down_ref, up_ref, cos_ref, sin_ref,
    own_q, own_k, own_v, other_q, other_k, other_v, xn_ref, u_ref,
):
    scaled, _ = row_norm(x_ref[...].astype(F32))
    xn = (scaled * gain_ref[...] + shift_ref[...]).astype(B16)
    xn_ref[...] = xn
    u = dot(xn, down_ref[...], 1, 1).astype(B16)
    u_ref[...] = u
    core = side[0]
    for w_ref, half, outs in (
        (w_own, core, (own_q, own_k, own_v)),
        (w_other, 1 - core, (other_q, other_k, other_v)),
    ):
        for part in range(3):
            w = w_ref[:, 0, part].reshape(-1, w_ref.shape[-1])
            value = dot(xn, w) + bias_ref[half, part] + dot(u, up_ref[half, part])
            if part == 2:
                outs[2][...] = value.astype(B16)
                continue
            for at in range(0, value.shape[1], 128):
                piece = value[:, at : at + 128]
                outs[part][:, at : at + 128] = (
                    piece * cos_ref[...] + partner(piece) * sin_ref[...]
                ).astype(B16)


def project(side, x, gain, shift, weight, bias, down, up, cosine, sine):
    rows, width = x.shape
    shards_, _, _, depth, half = weight.shape
    block = 256
    row = lambda columns: pl.BlockSpec((block, columns), lambda i, s: (i, 0))
    whole = lambda shape: pl.BlockSpec(shape, lambda i, s: (0,) * len(shape))
    w_spec = lambda pick: pl.BlockSpec(
        (shards_, 1, 3, depth, half), lambda i, s: (0, pick(s[0]), 0, 0, 0)
    )
    part = jax.ShapeDtypeStruct((rows, half), B16)
    return pl.pallas_call(
        project_body,
        grid_spec=pltpu.PrefetchScalarGridSpec(
            num_scalar_prefetch=1,
            grid=(rows // block,),
            in_specs=[
                row(width), whole((1, width)), whole((1, width)),
                w_spec(lambda s: s), w_spec(lambda s: 1 - s),
                whole(bias.shape), whole(down.shape), whole(up.shape), row(128), row(128),
            ],
            out_specs=[row(half)] * 6 + [row(width), row(down.shape[0])],
        ),
        out_shape=[part] * 6
        + [
            jax.ShapeDtypeStruct((rows, width), B16),
            jax.ShapeDtypeStruct((rows, down.shape[0]), B16),
        ],
        compiler_params=params(),
        cost_estimate=pl.CostEstimate(
            flops=2 * rows * width * 6 * half, bytes_accessed=16 * 2**20, transcendentals=0
        ),
    )(side, x, gain, shift, weight, weight, bias, down, up, cosine, sine)


def attend_body(q_ref, k_ref, v_ref, o_ref, inv_ref, e_ref, vm_ref):
    rows_all, length = q_ref.shape[0], k_ref.shape[0]
    low = low_lanes()

    @pl.when(pl.program_id(1) == 0)
    def _():
        vm_ref[0] = jnp.where(low, v_ref[...], 1).astype(B16)
        vm_ref[1] = jnp.where(low, 1, v_ref[...]).astype(B16)

    step = min(256, rows_all)
    for at in range(0, rows_all, step):
        rows = pl.ds(at, step)
        q = q_ref[rows, :]
        sums = []
        for head in range(2):
            mine = low if head == 0 else ~low
            scores = dot(jnp.where(mine, q, 0).astype(B16), k_ref[...], 1, 1)
            top = jnp.max(scores, 1, keepdims=True)
            weights = jnp.exp2((scores - top) * exp_scale).astype(B16)
            e_ref[head, rows, :] = weights
            sums.append(dot(weights, vm_ref[head]))
        total = pltpu.roll(jnp.where(low, sums[1], sums[0]), 64, 1)
        inverse = 1.0 / total
        o_ref[rows, :] = (jnp.where(low, sums[0], sums[1]) * inverse).astype(B16)
        inv_ref[rows, :] = inverse


def attend(query, key, value):
    length, width = query.shape
    block = min(1024, length)
    rows = pl.BlockSpec((block, 128), lambda p, i: (i, p))
    full = pl.BlockSpec((length, 128), lambda p, i: (0, p))
    return pl.pallas_call(
        attend_body,
        grid=(width // 128, length // block),
        in_specs=[rows, full, full],
        out_specs=[rows, rows, pl.BlockSpec((2, block, length), lambda p, i: (p, i, 0))],
        out_shape=[
            jax.ShapeDtypeStruct((length, width), B16),
            jax.ShapeDtypeStruct((length, width), F32),
            jax.ShapeDtypeStruct((width // 64, length, length), B16),
        ],
        scratch_shapes=[pltpu.VMEM((2, length, 128), B16)],
        compiler_params=params(),
        cost_estimate=pl.CostEstimate(
            flops=16 * length * length * width,
            bytes_accessed=width // 64 * length * length * 2,
            transcendentals=width // 64 * length * length,
        ),
    )(query, key, value)


def attend_back_body(
    q_ref, k_ref, v_ref, o_ref, inv_ref, g_ref, e_ref, cos_ref, sin_ref, cos_all, sin_all,
    gq_ref, gk_ref, gv_ref, key_sum, value_sum, vm_ref,
):
    rows_all, length = q_ref.shape[0], k_ref.shape[0]
    low = low_lanes()
    at_step = pl.program_id(1)

    @pl.when(at_step == 0)
    def _():
        key_sum[...] = jnp.zeros_like(key_sum)
        value_sum[...] = jnp.zeros_like(value_sum)
        vm_ref[0] = jnp.where(low, v_ref[...], -1).astype(B16)
        vm_ref[1] = jnp.where(low, -1, v_ref[...]).astype(B16)

    step = min(256, rows_all)
    for at in range(0, rows_all, step):
        rows = pl.ds(at, step)
        grad = g_ref[rows, :].astype(F32) * inv_ref[rows, :]
        grad_low = grad.astype(B16)
        product = pltpu.roll(grad * o_ref[rows, :].astype(F32), 64, 1).astype(B16)
        q_turned = q_ref[rows, :].T
        g_turned = grad_low.T
        parts = []
        for head in range(2):
            mine = low if head == 0 else ~low
            weights = e_ref[head, rows, :]
            grad_probs = dot(jnp.where(mine, grad_low, product), vm_ref[head], 1, 1)
            grad_scores = (weights.astype(F32) * grad_probs).astype(B16)
            parts.append(dot(grad_scores, k_ref[...]))
            span = pl.ds(head * 64, 64)
            key_sum[span, :] += dot(q_turned[head * 64 : head * 64 + 64], grad_scores)
            value_sum[span, :] += dot(g_turned[head * 64 : head * 64 + 64], weights)
        gq = jnp.where(low, parts[0], parts[1]) * score_scale
        gq_ref[rows, :] = (gq * cos_ref[rows, :] + partner(gq * sin_ref[rows, :])).astype(B16)

    @pl.when(at_step == pl.num_programs(1) - 1)
    def _():
        gk = key_sum[...].T * score_scale
        gk_ref[...] = (gk * cos_all[...] + partner(gk * sin_all[...])).astype(B16)
        gv_ref[...] = value_sum[...].T.astype(B16)


def attend_back(query, key, value, attended, inverse, grad, weights, cosine, sine):
    length, width = query.shape
    block = min(512, length)
    rows = pl.BlockSpec((block, 128), lambda p, i: (i, p))
    full = pl.BlockSpec((length, 128), lambda p, i: (0, p))
    table = pl.BlockSpec((block, 128), lambda p, i: (i, 0))
    table_all = pl.BlockSpec((length, 128), lambda p, i: (0, 0))
    return pl.pallas_call(
        attend_back_body,
        grid=(width // 128, length // block),
        in_specs=[
            rows, full, full, rows, rows, rows,
            pl.BlockSpec((2, block, length), lambda p, i: (p, i, 0)),
            table, table, table_all, table_all,
        ],
        out_specs=[rows, full, full],
        out_shape=[jax.ShapeDtypeStruct((length, width), B16)] * 3,
        scratch_shapes=[
            pltpu.VMEM((128, length), F32),
            pltpu.VMEM((128, length), F32),
            pltpu.VMEM((2, length, 128), B16),
        ],
        compiler_params=params(),
        cost_estimate=pl.CostEstimate(
            flops=20 * length * length * width,
            bytes_accessed=width // 64 * length * length * 2,
            transcendentals=0,
        ),
    )(query, key, value, attended, inverse, grad, weights, cosine, sine, cosine, sine)


def gauss_parts(z):
    t = 1.0 / (1.0 + (0.3275911 * math.sqrt(0.5)) * jnp.abs(z))
    poly = t * (0.254829592 + t * (-0.284496736 + t * (1.421413741 + t * (-1.453152027 + t * 1.061405429))))
    bell = jnp.exp2((z * z) * (-0.5 * math.log2(math.e)))
    upper = 0.5 * poly * bell
    cdf = jnp.where(z >= 0, 1.0 - upper, upper)
    return cdf, bell * (1.0 / math.sqrt(2.0 * math.pi))


def middle_body(
    side, x_ref, cot_ref, own_ref, other_ref, wo_ref, e_ref, r_ref,
    out_off, gain_ref, shift_ref, wide_off, shrink_off,
    od_ref, ou_ref, ed_ref, ru_ref, eu_ref, rd_ref,
    output_ref, gh_ref, gown_ref, gother_ref,
    t_od, t_ou, t_ed, t_ru, t_eu, t_rd,
    hidden, xn_ref, total, back, u2_ref, u3_ref, u4_sum, g4_ref, g3_sum,
):
    f = pl.program_id(0)
    last = pl.num_programs(0) - 1
    core = side[0]
    rows_all = x_ref.shape[0]
    step = 256

    def wo_half(half):
        w = wo_ref[:, half]
        return jnp.concatenate([w[i] for i in range(w.shape[0])], axis=1)

    @pl.when(f == 0)
    def _():
        w_own, w_other = wo_half(core), wo_half(1 - core)
        for at in range(0, rows_all, step):
            rows = pl.ds(at, step)
            own, other = own_ref[rows, :], other_ref[rows, :]
            u2 = (dot(own, od_ref[core], 1, 1) + dot(other, od_ref[1 - core], 1, 1)).astype(B16)
            u2_ref[rows, :] = u2
            h = (
                x_ref[rows, :].astype(F32) + dot(own, w_own) + dot(other, w_other)
                + out_off[...] + dot(u2, ou_ref[...])
            )
            hidden[rows, :] = h
            scaled, _ = row_norm(h)
            xn = (scaled * gain_ref[...] + shift_ref[...]).astype(B16)
            xn_ref[rows, :] = xn
            u3_ref[rows, :] = dot(xn, ed_ref[...], 1, 1).astype(B16)
            g4_ref[rows, :] = dot(cot_ref[rows, :], ru_ref[...], 1, 1).astype(B16)
            total[rows, :] = h + shrink_off[...]
            back[rows, :] = jnp.zeros_like(h)
            u4_sum[rows, :] = jnp.zeros((step, u4_sum.shape[1]), F32)
            g3_sum[rows, :] = jnp.zeros((step, g3_sum.shape[1]), F32)

    w_e = e_ref[:, 0].reshape(-1, e_ref.shape[-1])
    w_r = jnp.concatenate([r_ref[i, 0] for i in range(r_ref.shape[0])], axis=1)
    eu, rd = eu_ref[0], rd_ref[0]
    sum_eu, sum_rd = 0.0, 0.0
    for at in range(0, rows_all, step):
        rows = pl.ds(at, step)
        u3, g4 = u3_ref[rows, :], g4_ref[rows, :]
        z = dot(xn_ref[rows, :], w_e) + wide_off[...] + dot(u3, eu)
        gact = dot(cot_ref[rows, :], w_r, 1, 1) + dot(g4, rd)
        cdf, density = gauss_parts(z)
        act = (z * cdf).astype(B16)
        gz = (gact * (cdf + z * density)).astype(B16)
        total[rows, :] += dot(act, w_r)
        u4_sum[rows, :] += dot(act, rd, 1, 1)
        back[rows, :] += dot(gz, w_e, 1, 1)
        g3_sum[rows, :] += dot(gz, eu, 1, 1)
        sum_rd += dot(g4, act, 0, 0)
        sum_eu += dot(u3, gz, 0, 0)
    t_rd[0] = sum_rd
    t_eu[0] = sum_eu

    @pl.when(f == last)
    def _():
        w_own, w_other = wo_half(core), wo_half(1 - core)
        s_ru, s_ed, s_ou, s_own, s_other = 0.0, 0.0, 0.0, 0.0, 0.0
        for at in range(0, rows_all, step):
            rows = pl.ds(at, step)
            cot = cot_ref[rows, :]
            u4 = u4_sum[rows, :].astype(B16)
            output_ref[rows, :] = (total[rows, :] + dot(u4, ru_ref[...])).astype(B16)
            s_ru += dot(u4, cot, 0, 0)
            g3 = g3_sum[rows, :].astype(B16)
            s_ed += dot(g3, xn_ref[rows, :], 0, 0)
            gx = back[rows, :] + dot(g3, ed_ref[...])
            scaled, inverse = row_norm(hidden[rows, :])
            gh = cot.astype(F32) + back_norm(gx * gain_ref[...], scaled, inverse)
            gh_ref[rows, :] = gh
            gb = gh.astype(B16)
            s_ou += dot(u2_ref[rows, :], gb, 0, 0)
            g2 = dot(gb, ou_ref[...], 1, 1).astype(B16)
            s_own += dot(g2, own_ref[rows, :], 0, 0)
            s_other += dot(g2, other_ref[rows, :], 0, 0)
            gown_ref[rows, :] = (dot(gb, w_own, 1, 1) + dot(g2, od_ref[core])).astype(B16)
            gother_ref[rows, :] = (dot(gb, w_other, 1, 1) + dot(g2, od_ref[1 - core])).astype(B16)
        t_ru[...] = s_ru
        t_ed[...] = s_ed
        t_ou[...] = s_ou
        t_od[core] = s_own
        t_od[1 - core] = s_other


def middle(
    side, x, cot, own, other, w_o, w_e, w_r, out_off, gain, shift, wide_off, shrink_off,
    od, ou, ed, ru, eu, rd,
):
    rows, width = x.shape
    half = own.shape[1]
    shards_, _, depth, hidden_half = w_e.shape
    rank = ou.shape[0]
    block = 512
    per = hidden_half // block
    steps = 2 * per
    one = lambda shape: pl.BlockSpec(
        shape, lambda f, s: (0,) * len(shape), pipeline_mode=pl.Buffered(1)
    )
    small = pl.BlockSpec((1, rank, block), lambda f, s: (f // per, 0, f % per))
    full_t = jax.ShapeDtypeStruct((rank, width), F32)
    split_t = jax.ShapeDtypeStruct((2, rank, hidden_half), F32)
    return pl.pallas_call(
        middle_body,
        grid_spec=pltpu.PrefetchScalarGridSpec(
            num_scalar_prefetch=1,
            grid=(steps,),
            in_specs=[
                one((rows, width)), one((rows, width)), one((rows, half)), one((rows, half)),
                one(w_o.shape),
                pl.BlockSpec((shards_, 1, depth, block), lambda f, s: (0, f // per, 0, f % per)),
                pl.BlockSpec((shards_, 1, block, w_r.shape[3]), lambda f, s: (0, f // per, f % per, 0)),
                one((1, width)), one((1, width)), one((1, width)),
                pl.BlockSpec((1, block), lambda f, s: (0, f)),
                one((1, width)),
                one(od.shape), one(ou.shape), one(ed.shape), one(ru.shape), small, small,
            ],
            out_specs=[
                one((rows, width)), one((rows, width)), one((rows, half)), one((rows, half)),
                one((2, rank, half)), one((rank, width)), one((rank, width)), one((rank, width)),
                small, small,
            ],
            scratch_shapes=[
                pltpu.VMEM((rows, width), F32), pltpu.VMEM((rows, width), B16),
                pltpu.VMEM((rows, width), F32), pltpu.VMEM((rows, width), F32),
                pltpu.VMEM((rows, rank), B16), pltpu.VMEM((rows, rank), B16),
                pltpu.VMEM((rows, rank), F32), pltpu.VMEM((rows, rank), B16),
                pltpu.VMEM((rows, rank), F32),
            ],
        ),
        out_shape=[
            jax.ShapeDtypeStruct((rows, width), B16),
            jax.ShapeDtypeStruct((rows, width), F32),
            jax.ShapeDtypeStruct((rows, half), B16),
            jax.ShapeDtypeStruct((rows, half), B16),
            jax.ShapeDtypeStruct((2, rank, half), F32),
            full_t, full_t, full_t, split_t, split_t,
        ],
        compiler_params=params(),
        cost_estimate=pl.CostEstimate(
            flops=2 * rows * width * (16 * hidden_half // 2 + 4 * half),
            bytes_accessed=40 * 2**20,
            transcendentals=rows * hidden_half * 2,
        ),
    )(
        side, x, cot, own, other, w_o, w_e, w_r, out_off, gain, shift, wide_off, shrink_off,
        od, ou, ed, ru, eu, rd,
    )


def unproject_body(
    side, x_ref, gh_ref, xn_ref, u_ref, gain_ref, w_own, w_other, down_ref, up_ref,
    own_q, own_k, own_v, other_q, other_k, other_v,
    grad_ref, t_fd, t_fu,
):
    core = side[0]
    first = pl.program_id(0) == 0

    @pl.when(first)
    def _():
        t_fd[...] = jnp.zeros_like(t_fd)
        t_fu[...] = jnp.zeros_like(t_fu)

    u = u_ref[...]
    g1, gx = 0.0, 0.0
    for w_ref, half, grads in (
        (w_own, core, (own_q, own_k, own_v)),
        (w_other, 1 - core, (other_q, other_k, other_v)),
    ):
        for part in range(3):
            grad = grads[part][...]
            w = w_ref[:, 0, part].reshape(-1, w_ref.shape[-1])
            gx += dot(grad, w, 1, 1)
            g1 += dot(grad, up_ref[half, part], 1, 1)
            t_fu[half, part] += dot(u, grad, 0, 0)
    g1 = g1.astype(B16)
    t_fd[...] += dot(g1, xn_ref[...], 0, 0)
    gx += dot(g1, down_ref[...])
    scaled, inverse = row_norm(x_ref[...].astype(F32))
    grad_ref[...] = (gh_ref[...] + back_norm(gx * gain_ref[...], scaled, inverse)).astype(B16)


def unproject(side, x, gh, xn, u, gain, weight, down, up, own, other):
    rows, width = x.shape
    shards_, _, _, depth, half = weight.shape
    rank = down.shape[0]
    block = 256
    row = lambda columns: pl.BlockSpec((block, columns), lambda i, s: (i, 0))
    whole = lambda shape: pl.BlockSpec(shape, lambda i, s: (0,) * len(shape))
    w_spec = lambda pick: pl.BlockSpec(
        (shards_, 1, 3, depth, half), lambda i, s: (0, pick(s[0]), 0, 0, 0)
    )
    return pl.pallas_call(
        unproject_body,
        grid_spec=pltpu.PrefetchScalarGridSpec(
            num_scalar_prefetch=1,
            grid=(rows // block,),
            in_specs=[
                row(width), row(width), row(width), row(rank), whole((1, width)),
                w_spec(lambda s: s), w_spec(lambda s: 1 - s), whole(down.shape), whole(up.shape),
            ]
            + [row(half)] * 6,
            out_specs=[row(width), whole((rank, width)), whole(up.shape)],
        ),
        out_shape=[
            jax.ShapeDtypeStruct((rows, width), B16),
            jax.ShapeDtypeStruct((rank, width), F32),
            jax.ShapeDtypeStruct(up.shape, F32),
        ],
        compiler_params=params(),
        cost_estimate=pl.CostEstimate(
            flops=2 * rows * width * 6 * half, bytes_accessed=20 * 2**20, transcendentals=0
        ),
    )(side, x, gh, xn, u, gain, weight, weight, down, up, *own, *other)


def clip_shards(
    planes,
    tokens,
    cotangent,
    adapter_pick,
    positions,
    first_gain,
    first_shift,
    joined_weight,
    joined_bias,
    output_weight,
    mixing_exit_offset,
    second_gain,
    second_shift,
    expand_weight,
    widening_offset,
    reduce_weight,
    shrinking_offset,
    joined_down,
    joined_up,
    output_down,
    output_up,
    expand_down,
    expand_up,
    reduce_down,
    reduce_up,
):
    core = lax.axis_index("shard") % 2
    ctx = lax.axis_index("ctx")
    tp = lax.axis_index("tp")
    side = jnp.reshape(core, (1,)).astype(jnp.int32)
    cores = [(i, i ^ 1) for i in range(2 * planes)]
    pair = [(0, 1), (1, 0)]
    place = lambda z, c, x: (2 * z + c) * 2 + x
    turns = [
        (place(z, c, x), place(z, x, c)) for z in range(planes) for c in range(2) for x in range(2)
    ]
    turns_flip = [(2 * a + y, 2 * b + 1 - y) for a, b in turns for y in range(2)]

    def turn(array):
        return lax.ppermute(array, ("shard", "ctx"), turns)

    def to_core(array):
        return lax.ppermute(array, "shard", cores)

    def to_tp(array):
        return lax.ppermute(array, "tp", pair)

    def to_ctx(array):
        return lax.ppermute(array, "ctx", pair)

    def by_tp(mine, others):
        return jnp.where(tp == 0, jnp.stack([mine, others]), jnp.stack([others, mine]))

    mine_of = lambda array, axis=0: lax.dynamic_index_in_dim(array, tp, axis, keepdims=False)

    def gather(weight):
        whole = lax.all_gather(weight, ("shard", "tp"), axis=0, tiled=False)
        return whole.reshape((2 * planes, 2) + weight.shape)

    x = turn(mine_of(tokens))
    w_j = gather(jnp.transpose(joined_weight, (1, 0, 2)))
    places = turn(mine_of(positions, 1))
    cot = turn(mine_of(cotangent))
    w_o = gather(output_weight)
    w_e = gather(expand_weight)
    w_r = gather(reduce_weight)

    away = to_core(adapter_pick)
    picks = jnp.where(core == ctx, adapter_pick, away)
    pick = lax.dynamic_index_in_dim(picks, tp, 0, keepdims=False)
    pick_next = lax.dynamic_index_in_dim(picks, 1 - tp, 0, keepdims=False)

    def row(table, at):
        return lax.dynamic_index_in_dim(table, at, 0, keepdims=False)

    def split_factors(at):
        ju, od, eu, rd = row(joined_up, at), row(output_down, at), row(expand_up, at), row(reduce_down, at)
        return jnp.concatenate([ju.reshape(ju.shape[0], -1), od.T, eu, rd.T], axis=1)

    packed = by_tp(split_factors(pick), to_tp(split_factors(pick_next)))
    half = joined_weight.shape[2]
    hidden_half = expand_weight.shape[1]
    rank = joined_up.shape[1]
    ju = jnp.transpose(packed[:, :, : 3 * half].reshape(2, rank, 3, half), (0, 2, 1, 3))
    od = packed[:, :, 3 * half : 4 * half]
    eu = packed[:, :, 4 * half : 4 * half + hidden_half]
    rd = packed[:, :, 4 * half + hidden_half :]
    jd, ed = row(joined_down, pick).T, row(expand_down, pick).T
    ou, ru = row(output_up, pick), row(reduce_up, pick)
    offsets = jnp.concatenate([joined_bias.reshape(-1), widening_offset])[None]
    offsets = by_tp(offsets, to_tp(offsets))
    bias = offsets[:, :, : 3 * half].reshape(2, 3, 1, half)
    wide_off = offsets[:, 0, 3 * half :].reshape(1, 2 * hidden_half)

    places_all = jnp.concatenate([places, to_core(places)], axis=1).astype(F32)
    lane = jnp.arange(128, dtype=jnp.int32) % 64
    within = lane % 20
    rates = jnp.exp((within % 10).astype(F32) * (-math.log(10000.0) / 10.0))
    spot = jnp.where(
        lane < 20, places_all[0][:, None], jnp.where(lane < 40, places_all[1][:, None], places_all[2][:, None])
    )
    angle = spot * rates
    turned = lane < 60
    cosine = jnp.where(turned, jnp.cos(angle), 1.0)
    sine = jnp.where(turned, jnp.where(within < 10, -jnp.sin(angle), jnp.sin(angle)), 0.0)
    rows = x.shape[0]

    *qkv, xn1, u1 = project(
        side, x, first_gain[None], first_shift[None], w_j, bias, jd, ju, cosine[:rows], sine[:rows]
    )
    query, key, value = (
        jnp.concatenate([mine, to_core(sent)], axis=0) for mine, sent in zip(qkv[:3], qkv[3:])
    )
    attended, inverse, weights = attend(query, key, value)
    own_heads, other_heads = attended[:rows], to_core(attended[rows:])
    out, gh, gown, gother, t_od, t_ou, t_ed, t_ru, t_eu, t_rd = middle(
        side, x, cot, own_heads, other_heads, w_o, w_e, w_r,
        mixing_exit_offset[None], second_gain[None], second_shift[None], wide_off, shrinking_offset[None],
        od, ou, ed, ru, eu, rd,
    )
    out = turn(out)
    output = by_tp(out, to_tp(out))
    grad_att = jnp.concatenate([gown, to_core(gother)], axis=0)
    grads = attend_back(query, key, value, attended, inverse, grad_att, weights, cosine, sine)
    tokens_part, t_fd, t_fu = unproject(
        side, x, gh, xn1, u1, first_gain[None], w_j, jd, ju,
        [g[:rows] for g in grads], [to_core(g[rows:]) for g in grads],
    )
    quarter = rows // 2
    stay = lax.dynamic_slice_in_dim(tokens_part, tp * quarter, quarter, 0)
    leave = lax.dynamic_slice_in_dim(tokens_part, (1 - tp) * quarter, quarter, 0)
    tokens_grad = by_tp(turn(stay), lax.ppermute(leave, ("shard", "ctx", "tp"), turns_flip))

    def spread(split, full):
        low_rank = rank // 2
        split_parts = jnp.concatenate(split, axis=2)
        full_part = jnp.concatenate(full, axis=1)
        wide = jnp.concatenate([split_parts[0], split_parts[1], full_part], axis=1)
        keep = lax.dynamic_slice_in_dim(wide, core * low_rank, low_rank, 0)
        send = lax.dynamic_slice_in_dim(wide, (1 - core) * low_rank, low_rank, 0)
        total = (keep + to_core(send.astype(B16)).astype(F32)).astype(B16)
        width = split_parts.shape[2]
        tag = jnp.full((low_rank, 128), pick.astype(B16))
        rest = jnp.concatenate([total[:, 2 * width :], tag], axis=1)
        keep = jnp.concatenate([lax.dynamic_slice_in_dim(total, tp * width, width, 1), rest], axis=1)
        send = jnp.concatenate([lax.dynamic_slice_in_dim(total, (1 - tp) * width, width, 1), rest], axis=1)
        stack = jnp.stack([keep, to_tp(send)])
        stack = jnp.concatenate([stack, to_ctx(stack)], axis=0)
        stacks = [stack]
        for shift in range(1, planes):
            stacks.append(
                lax.ppermute(stack, "shard", [(i, (i + 2 * shift) % (2 * planes)) for i in range(2 * planes)])
            )
        stack = jnp.concatenate(stacks, axis=0)
        others = to_core(stack)
        stack = jnp.where(
            core == 0,
            jnp.concatenate([stack, others], axis=1),
            jnp.concatenate([others, stack], axis=1),
        )
        chosen = stack[:, 0, -1].astype(F32)
        choose = (chosen[None, :] == jnp.arange(joined_down.shape[0], dtype=F32)[:, None]).astype(B16)
        summed = lax.dot_general(
            choose, stack[:, :, :-128], (((1,), (0,)), ((), ())), preferred_element_type=F32
        )
        pieces = []
        at = 0
        for item in split:
            pieces.append(summed[:, :, at : at + item.shape[2]])
            at += item.shape[2]
        for item in full:
            pieces.append(summed[:, :, at : at + item.shape[1]])
            at += item.shape[1]
        return pieces

    s_od, s_eu, s_rd, s_ou, s_ed, s_ru = spread([t_od, t_eu, t_rd], [t_ou, t_ed, t_ru])
    t_fu = jnp.transpose(t_fu, (0, 2, 1, 3)).reshape(2, rank, 3 * half)
    s_fu, s_fd = spread([t_fu], [t_fd])
    turn_last = lambda array: jnp.swapaxes(array, 1, 2)
    return (
        output,
        tokens_grad,
        turn_last(s_fd),
        s_fu.reshape(s_fu.shape[0], rank, 3, half),
        turn_last(s_od),
        s_ou,
        turn_last(s_ed),
        s_eu,
        turn_last(s_rd),
        s_ru,
    )


def solution(mesh):
    sizes = dict(mesh.shape)
    if sizes["ctx"] == 2 and sizes["tp"] == 2 and sizes["shard"] % 2 == 0:
        body = functools.partial(clip_shards, sizes["shard"] // 2)
    else:
        body = general_shards
    return jax.shard_map(
        body,
        mesh=mesh,
        in_specs=(
            P("shard", "ctx", None),
            P("shard", "ctx", None),
            P("shard"),
            P(None, "shard", "ctx"),
            P(),
            P(),
            P("shard", None, "tp"),
            P(None, "tp"),
            P("tp", "shard"),
            P(),
            P(),
            P(),
            P("shard", "tp"),
            P("tp"),
            P("tp", "shard"),
            P(),
            P(),
            P(None, None, None, "tp"),
            P(None, "tp", None),
            P(),
            P(),
            P(None, None, "tp"),
            P(None, "tp", None),
            P(),
        ),
        out_specs=(
            P("shard", "ctx", None),
            P("shard", ("ctx", "tp"), None),
            P(),
            P(None, None, None, "tp"),
            P(None, "tp", None),
            P(),
            P(),
            P(None, None, "tp"),
            P(None, "tp", None),
            P(),
        ),
        check_vma=False,
    )
```

```python
import functools
import math

import jax
import jax.numpy as jnp
from jax import lax
from jax.experimental import pallas as pl
from jax.experimental.pallas import tpu as pltpu
from jax.sharding import PartitionSpec as P

eps_norm = 1e-06
score_scale = 0.125


def rope_tables(places):
    band = jnp.arange(10, dtype=jnp.float32)
    rates = jnp.exp(band * (-math.log(10000.0) / 10.0))
    angle = places.astype(jnp.float32)[..., None] * rates
    cos_parts = []
    sin_parts = []
    for band_index in range(3):
        cosine = jnp.cos(angle[band_index])
        sine = jnp.sin(angle[band_index])
        cos_parts = cos_parts + [cosine, cosine]
        sin_parts = sin_parts + [-sine, sine]
    rest_shape = angle.shape[1:-1] + (4,)
    cos_parts.append(jnp.ones(rest_shape, jnp.float32))
    sin_parts.append(jnp.zeros(rest_shape, jnp.float32))
    return (jnp.concatenate(cos_parts, -1), jnp.concatenate(sin_parts, -1))


def swap_pairs(values):
    leading = values.shape[:-1]
    turned = values[..., :60].reshape(leading + (3, 2, 10))[..., ::-1, :].reshape(leading + (60,))
    return jnp.concatenate([turned, values[..., 60:]], -1)


def rotate(values, cosine, sine):
    return values * cosine[..., None, :] + swap_pairs(values) * sine[..., None, :]


def rotate_back(grads, cosine, sine):
    return grads * cosine[..., None, :] + swap_pairs(grads * sine[..., None, :])


def norm_forward(values, gain, shift):
    centred = values - jnp.mean(values, -1, keepdims=True)
    inverse = lax.rsqrt(jnp.mean(centred * centred, -1, keepdims=True) + eps_norm)
    scaled = centred * inverse
    return (scaled * gain + shift, scaled, inverse)


def norm_back(grads, scaled, inverse, gain):
    weighted = grads * gain
    return inverse * (
        weighted
        - jnp.mean(weighted, -1, keepdims=True)
        - scaled * jnp.mean(weighted * scaled, -1, keepdims=True)
    )


def select_factor(choose, table):
    return jnp.einsum("ca,a...->c...", choose, table, preferred_element_type=jnp.float32).astype(
        jnp.bfloat16
    )


def gelu_exact(values):
    return jax.nn.gelu(values, approximate=False)


def matrix_product(form, left, right):
    return jnp.einsum(form, left, right, preferred_element_type=jnp.float32)


def general_shards(
    tokens,
    cotangent,
    adapter_pick,
    positions,
    first_gain,
    first_shift,
    joined_weight,
    joined_bias,
    output_weight,
    mixing_exit_offset,
    second_gain,
    second_shift,
    expand_weight,
    widening_offset,
    reduce_weight,
    shrinking_offset,
    joined_down,
    joined_up,
    output_down,
    output_up,
    expand_down,
    expand_up,
    reduce_down,
    reduce_up,
):
    whole_joined, whole_output, whole_expand, whole_reduce = (
        lax.all_gather(joined_weight, "shard", axis=0, tiled=True),
        lax.all_gather(output_weight, "shard", axis=1, tiled=True),
        lax.all_gather(expand_weight, "shard", axis=0, tiled=True),
        lax.all_gather(reduce_weight, "shard", axis=1, tiled=True),
    )
    clip_count, local_len, width = tokens.shape
    local_width = whole_joined.shape[2]
    head_count = local_width // 64
    choose = (
        adapter_pick[:, None] == jnp.arange(joined_down.shape[0], dtype=jnp.int32)[None, :]
    ).astype(jnp.bfloat16)
    select_joined_down = select_factor(choose, joined_down)
    select_joined_up = select_factor(choose, joined_up)
    select_output_down = select_factor(choose, output_down)
    select_output_up = select_factor(choose, output_up)
    select_expand_down = select_factor(choose, expand_down)
    select_expand_up = select_factor(choose, expand_up)
    select_reduce_down = select_factor(choose, reduce_down)
    select_reduce_up = select_factor(choose, reduce_up)
    cosine, sine = rope_tables(positions)
    block_arguments = tokens.astype(jnp.float32)
    norm_one, scaled_one, inverse_one = norm_forward(block_arguments, first_gain, first_shift)
    initial_standardized = norm_one.astype(jnp.bfloat16)
    initial_slim_derivative = matrix_product(
        "zgh,zhe->zge", initial_standardized, select_joined_down
    ).astype(jnp.bfloat16)
    mapped_vectors = (
        matrix_product("cld,dje->clje", initial_standardized, whole_joined)
        + joined_bias
        + matrix_product("uip,upqg->uiqg", initial_slim_derivative, select_joined_up)
    )
    head_shape = (clip_count, local_len, head_count, 64)
    query = rotate(mapped_vectors[:, :, 0].reshape(head_shape), cosine, sine).astype(jnp.bfloat16)
    keys = rotate(mapped_vectors[:, :, 1].reshape(head_shape), cosine, sine).astype(jnp.bfloat16)
    values = mapped_vectors[:, :, 2].reshape(head_shape).astype(jnp.bfloat16)
    stats_shape = (clip_count, head_count, local_len)
    run_max = jnp.full(stats_shape, -1e30, jnp.float32)
    key_part = lax.all_gather(keys, "ctx", axis=1, tiled=True)
    value_part = lax.all_gather(values, "ctx", axis=1, tiled=True)
    scores = matrix_product("cqhd,ckhd->chqk", query, key_part) * score_scale
    new_max = jnp.maximum(run_max, jnp.max(scores, -1))
    weights = jnp.exp(scores - new_max[..., None])
    run_total = jnp.sum(weights, -1)
    update = matrix_product("chqk,ckhd->cqhd", weights.astype(jnp.bfloat16), value_part)
    accum = update
    run_max, run_total, accum = (new_max, run_total, accum)
    log_total = run_max + jnp.log(run_total)
    attended_full = accum / jnp.transpose(run_total, (0, 2, 1))[..., None]
    mixing_outcome = attended_full.reshape(clip_count, local_len, local_width).astype(jnp.bfloat16)
    out_part = matrix_product("cle,ed->cld", mixing_outcome, whole_output)
    rank_partial = matrix_product("fig,fgt->fit", mixing_outcome, select_output_down)
    output_total, rank_sum = (
        lax.psum(out_part.astype(jnp.bfloat16), "tp").astype(jnp.float32),
        lax.psum(rank_partial.astype(jnp.bfloat16), "tp").astype(jnp.float32),
    )
    middle_slim_derivative = rank_sum.astype(jnp.bfloat16)
    first_hidden = (
        block_arguments
        + output_total
        + mixing_exit_offset
        + matrix_product("wnk,wke->wne", middle_slim_derivative, select_output_up)
    )
    norm_two, scaled_two, inverse_two = norm_forward(first_hidden, second_gain, second_shift)
    latter_standardized = norm_two.astype(jnp.bfloat16)
    penultimate_slim_derivative = matrix_product(
        "zgh,zhe->zge", latter_standardized, select_expand_down
    ).astype(jnp.bfloat16)
    skip_stream_vectors = (
        matrix_product("cld,df->clf", latter_standardized, whole_expand)
        + widening_offset
        + matrix_product("uqz,uze->uqe", penultimate_slim_derivative, select_expand_up)
    )
    activity, gelu_pull = jax.vjp(gelu_exact, skip_stream_vectors)
    gaussian_error_unit = activity.astype(jnp.bfloat16)
    mlp_part = matrix_product("clf,fd->cld", gaussian_error_unit, whole_reduce)
    fourth_rank_partial = matrix_product("xpv,xvy->xpy", gaussian_error_unit, select_reduce_down)
    feedforward_sum, rank_four_sum = (
        lax.psum(mlp_part.astype(jnp.bfloat16), "tp").astype(jnp.float32),
        lax.psum(fourth_rank_partial.astype(jnp.bfloat16), "tp").astype(jnp.float32),
    )
    closing_slim_derivative = rank_four_sum.astype(jnp.bfloat16)
    output = (
        first_hidden
        + feedforward_sum
        + shrinking_offset
        + matrix_product("wnk,wke->wne", closing_slim_derivative, select_reduce_up)
    ).astype(jnp.bfloat16)
    back_joined, back_output, back_expand, back_reduce = (
        lax.all_gather(joined_weight, "shard", axis=0, tiled=True),
        lax.all_gather(output_weight, "shard", axis=1, tiled=True),
        lax.all_gather(expand_weight, "shard", axis=0, tiled=True),
        lax.all_gather(reduce_weight, "shard", axis=1, tiled=True),
    )
    reduce_up_term = matrix_product("vkn,vkm->vnm", closing_slim_derivative, cotangent)
    gradient_fourth = matrix_product("abj,awj->abw", cotangent, select_reduce_up).astype(
        jnp.bfloat16
    )
    reduce_down_term = matrix_product("mpg,mpu->mgu", gaussian_error_unit, gradient_fourth)
    grad_active = matrix_product("cld,fd->clf", cotangent, back_reduce) + matrix_product(
        "gez,guz->geu", gradient_fourth, select_reduce_down
    )
    residual_gradient = gelu_pull(grad_active)[0].astype(jnp.bfloat16)
    expand_up_term = matrix_product("jge,jgn->jen", penultimate_slim_derivative, residual_gradient)
    grad_norm_part = matrix_product("clf,df->cld", residual_gradient, back_expand)
    third_gradient_part = matrix_product("aik,adk->aid", residual_gradient, select_expand_up)
    norm_gradient_sum, grad_three_sum = (
        lax.psum(grad_norm_part.astype(jnp.bfloat16), "tp").astype(jnp.float32),
        lax.psum(third_gradient_part.astype(jnp.bfloat16), "tp").astype(jnp.float32),
    )
    gradient_third = grad_three_sum.astype(jnp.bfloat16)
    expand_down_term = matrix_product("kgt,kgh->kth", latter_standardized, gradient_third)
    second_norm_gradient = norm_gradient_sum + matrix_product(
        "jqt,jit->jqi", gradient_third, select_expand_down
    )
    grad_hidden = cotangent.astype(jnp.float32) + norm_back(
        second_norm_gradient, scaled_two, inverse_two, second_gain
    )
    branch_gradient = grad_hidden.astype(jnp.bfloat16)
    output_up_term = matrix_product("vkn,vkm->vnm", middle_slim_derivative, branch_gradient)
    gradient_second = matrix_product("abj,awj->abw", branch_gradient, select_output_up).astype(
        jnp.bfloat16
    )
    output_down_term = matrix_product("nua,nui->nai", mixing_outcome, gradient_second)
    grad_attended = (
        (
            matrix_product("cld,ed->cle", branch_gradient, back_output)
            + matrix_product("gsq,ghq->gsh", gradient_second, select_output_down)
        )
        .astype(jnp.bfloat16)
        .reshape(head_shape)
    )
    key_whole, value_whole = (
        lax.all_gather(keys, "ctx", axis=1, tiled=True),
        lax.all_gather(values, "ctx", axis=1, tiled=True),
    )
    flat_shape = (clip_count, local_len, local_width)

    def clip_back(items):
        query_clip, key_clip, value_clip, grad_clip, total_clip = items
        scores = matrix_product("qhd,khd->hqk", query_clip, key_clip) * score_scale
        probs = jnp.exp(scores - total_clip[..., None])
        grad_probs = matrix_product("qhd,khd->hqk", grad_clip, value_clip)
        middle = jnp.sum(probs * grad_probs, -1, keepdims=True)
        grad_scores = (probs * (grad_probs - middle)).astype(jnp.bfloat16)
        grad_query = matrix_product("hqk,khd->qhd", grad_scores, key_clip) * score_scale
        grad_key = matrix_product("hqk,qhd->khd", grad_scores, query_clip) * score_scale
        grad_value = matrix_product("hqk,qhd->khd", probs.astype(jnp.bfloat16), grad_clip)
        return (grad_query, grad_key, grad_value)

    grad_query, key_terms, value_terms = lax.map(
        clip_back, (query, key_whole, value_whole, grad_attended, log_total)
    )
    full_len = key_whole.shape[1]
    key_sum, value_sum = (
        lax.psum_scatter(
            key_terms.reshape(clip_count, full_len, local_width).astype(jnp.bfloat16),
            "ctx",
            scatter_dimension=1,
            tiled=True,
        ).astype(jnp.float32),
        lax.psum_scatter(
            value_terms.reshape(clip_count, full_len, local_width).astype(jnp.bfloat16),
            "ctx",
            scatter_dimension=1,
            tiled=True,
        ).astype(jnp.float32),
    )
    query_key_value_gradient = jnp.stack(
        [
            rotate_back(grad_query, cosine, sine).reshape(flat_shape),
            rotate_back(key_sum.reshape(head_shape), cosine, sine).reshape(flat_shape),
            value_sum,
        ],
        axis=2,
    ).astype(jnp.bfloat16)
    joined_up_term = matrix_product(
        "pvh,pvfo->phfo", initial_slim_derivative, query_key_value_gradient
    )
    first_gradient_part = matrix_product(
        "kxsd,ktsd->kxt", query_key_value_gradient, select_joined_up
    )
    grad_norm_one_part = matrix_product("clje,dje->cld", query_key_value_gradient, back_joined)
    gradient_first = lax.psum(first_gradient_part.astype(jnp.bfloat16), "tp")
    grad_norm_share = lax.psum_scatter(
        grad_norm_one_part.astype(jnp.bfloat16), "tp", scatter_dimension=1, tiled=True
    ).astype(jnp.float32)
    joined_down_term = matrix_product("kgt,kgh->kth", initial_standardized, gradient_first)
    half_len = grad_norm_share.shape[1]
    begin = lax.axis_index("tp") * half_len

    def shared_rows(array):
        return lax.dynamic_slice_in_dim(array, begin, half_len, 1)

    grad_norm_one = grad_norm_share + matrix_product(
        "jqt,jit->jqi", shared_rows(gradient_first), select_joined_down
    )
    tokens_grad = (
        shared_rows(grad_hidden)
        + norm_back(grad_norm_one, shared_rows(scaled_one), shared_rows(inverse_one), first_gain)
    ).astype(jnp.bfloat16)
    choose_full = choose.astype(jnp.float32)

    def by_adapter(term):
        return jnp.einsum(
            "ca,c...->a...",
            choose_full,
            term,
            precision=lax.Precision.HIGHEST,
            preferred_element_type=jnp.float32,
        )

    summed = lax.psum(
        (
            by_adapter(joined_down_term),
            by_adapter(joined_up_term),
            by_adapter(output_down_term),
            by_adapter(output_up_term),
            by_adapter(expand_down_term),
            by_adapter(expand_up_term),
            by_adapter(reduce_down_term),
            by_adapter(reduce_up_term),
        ),
        ("shard", "ctx"),
    )
    return (
        output,
        tokens_grad,
        summed[0],
        summed[1],
        summed[2],
        summed[3],
        summed[4],
        summed[5],
        summed[6],
        summed[7],
    )


B16 = jnp.bfloat16
F32 = jnp.float32
VMEM_LIMIT = 60 * 2**20
exp_scale = score_scale * math.log2(math.e)


def dot(left, right, left_dim=1, right_dim=0):
    return lax.dot_general(
        left, right, (((left_dim,), (right_dim,)), ((), ())), preferred_element_type=F32
    )


def params():
    return pltpu.CompilerParams(vmem_limit_bytes=VMEM_LIMIT)


def low_lanes():
    return lax.broadcasted_iota(jnp.int32, (1, 128), 1) < 64


def partner(values):
    lane = lax.broadcasted_iota(jnp.int32, (1, 128), 1) % 64 % 20
    return jnp.where(lane < 10, pltpu.roll(values, 118, 1), pltpu.roll(values, 10, 1))


def row_norm(values):
    centred = values - jnp.mean(values, -1, keepdims=True)
    inverse = lax.rsqrt(jnp.mean(centred * centred, -1, keepdims=True) + eps_norm)
    return centred * inverse, inverse


def back_norm(weighted, scaled, inverse):
    return inverse * (
        weighted
        - jnp.mean(weighted, -1, keepdims=True)
        - scaled * jnp.mean(weighted * scaled, -1, keepdims=True)
    )


MESH = pl.DeviceIdType.MESH
HIDDEN_BLOCK = 512
(UP_SENT, DOWN_SENT, Z_CAME, TP_SENT, TP_CAME, OWN_SENT, OWN_CAME, NEXT_SENT, NEXT_CAME) = range(9)


class Place:
    def __init__(self, planes):
        self.planes = planes
        self.shard = lax.axis_index("shard")
        self.z = self.shard // 2
        self.core = self.shard % 2
        self.ctx = lax.axis_index("ctx")
        self.tp = lax.axis_index("tp")
        self.has_up = self.z < planes - 1
        self.has_down = self.z > 0
        self.crosses = self.core != self.ctx
        self.up = {"shard": self.shard + 2}
        self.down = {"shard": self.shard - 2}
        self.next_tp = {"tp": 1 - self.tp}
        self.next_core = {"shard": 2 * self.z + 1 - self.core}
        self.turned = {"shard": 2 * self.z + self.ctx, "ctx": self.core}

    def greet(self, planes_too, turned):
        barrier = pltpu.get_barrier_semaphore()
        count = 2

        def signal(device):
            pl.semaphore_signal(barrier, inc=1, device_id=device, device_id_type=MESH)

        signal(self.next_tp)
        signal(self.next_core)
        if planes_too:
            pl.when(self.has_up)(lambda: signal(self.up))
            pl.when(self.has_down)(lambda: signal(self.down))
            count = count + self.has_up.astype(jnp.int32) + self.has_down.astype(jnp.int32)
        if turned:
            pl.when(self.crosses)(lambda: signal(self.turned))
            count = count + self.crosses.astype(jnp.int32)
        pl.semaphore_wait(barrier, count)


class Flow:
    def __init__(self, at, own, slot, sems):
        self.at, self.own, self.slot, self.sems = at, own, slot, sems

    def copy(self, kind, plane, own=False):
        at = self.at
        half = 1 - at.tp if kind == NEXT_SENT else at.tp
        piece = self.slot(2 * plane + at.core, half)
        device, came = {
            UP_SENT: (at.up, Z_CAME),
            DOWN_SENT: (at.down, Z_CAME),
            TP_SENT: (at.next_tp, TP_CAME),
            OWN_SENT: (at.next_core, OWN_CAME),
            NEXT_SENT: (at.next_core, NEXT_CAME),
        }[kind]
        return pltpu.make_async_remote_copy(
            src_ref=self.own if own else piece,
            dst_ref=piece,
            send_sem=self.sems.at[kind, plane],
            recv_sem=self.sems.at[came, plane],
            device_id=device,
            device_id_type=MESH,
        )

    def came(self, kind, plane):
        sent = {Z_CAME: UP_SENT, TP_CAME: TP_SENT, OWN_CAME: OWN_SENT, NEXT_CAME: NEXT_SENT}[kind]
        at = self.at
        shard = 2 * plane + (at.core if kind in (Z_CAME, TP_CAME) else 1 - at.core)
        half = at.tp if kind in (Z_CAME, OWN_CAME) else 1 - at.tp
        piece = self.slot(shard, half)
        return pltpu.make_async_remote_copy(
            src_ref=piece, dst_ref=piece, send_sem=self.sems.at[sent, plane],
            recv_sem=self.sems.at[kind, plane], device_id=at.next_core, device_id_type=MESH,
        )

    def pieces(self, distance):
        at = self.at
        if distance == 0:
            return [(None, at.z, True, True)]
        return [
            (at.z >= distance, at.z - distance, True, False),
            (at.z < at.planes - distance, at.z + distance, False, True),
        ]

    def each(self, distance, act):
        for there, plane, below, above in self.pieces(distance):
            if there is None:
                act(plane, below, above)
            else:
                pl.when(there)(functools.partial(act, plane, below, above))

    def pass_on(self, distance, z=False, tp=False, core=False, fresh=None, wait=False):
        own = (distance == 0) if fresh is None else fresh

        def act(plane, below, above):
            if wait:
                self.came(Z_CAME, plane).wait_recv()
            if z:
                if below:
                    pl.when(self.at.has_up)(lambda: self.copy(UP_SENT, plane, own).start())
                if above:
                    pl.when(self.at.has_down)(lambda: self.copy(DOWN_SENT, plane, own).start())
            if tp:
                self.copy(TP_SENT, plane, own).start()
            if core:
                self.copy(OWN_SENT, plane, own).start()

        self.each(distance, act)

    def sent(self, distance, z=False, tp=False, core=False):
        def act(plane, below, above):
            if z:
                if below:
                    pl.when(self.at.has_up)(lambda: self.copy(UP_SENT, plane).wait_send())
                if above:
                    pl.when(self.at.has_down)(lambda: self.copy(DOWN_SENT, plane).wait_send())
            if tp:
                self.copy(TP_SENT, plane).wait_send()
            if core:
                self.copy(OWN_SENT, plane).wait_send()

        self.each(distance, act)

    def wait(self, kind, distance):
        self.each(distance, lambda plane, below, above: self.came(kind, plane).wait_recv())

    def pass_next(self, distance, wait=True):
        def act(plane, below, above):
            if wait:
                self.came(TP_CAME, plane).wait_recv()
            self.copy(NEXT_SENT, plane).start()

        self.each(distance, act)

    def sent_next(self, distance):
        self.each(distance, lambda plane, below, above: self.copy(NEXT_SENT, plane).wait_send())


def weight_flows(at, own_o, own_e, own_r, full_o, full_e, full_r, sems, blocks):
    flow_o = Flow(at, own_o, lambda s, h: full_o.at[s, h], sems.at[0])
    flows = []
    for block in range(blocks):
        span = pl.ds(block * HIDDEN_BLOCK, HIDDEN_BLOCK)
        flows.append(
            [
                Flow(at, own_e.at[:, span], lambda s, h, span=span: full_e.at[s, h, :, span], sems.at[1 + 2 * block]),
                Flow(at, own_r.at[span, :], lambda s, h, span=span: full_r.at[s, h, span, :], sems.at[2 + 2 * block]),
            ]
        )
    return flow_o, flows


def turned_copy(at, source, target, sems):
    return pltpu.make_async_remote_copy(
        src_ref=source, dst_ref=target, send_sem=sems.at[0], recv_sem=sems.at[1],
        device_id=at.turned, device_id_type=MESH,
    )


ROWS = 256


def project_body(
    planes, blocks,
    tokens_ref, spots_ref, factors_ref, factors_next, shared_ref, offsets_ref, w_ref, own_o, own_e, own_r,
    gain_ref, shift_ref, rates_ref,
    x_out, factors_out, shared_out, offsets_out, w_out, full_o, full_e, full_r,
    q_out, k_out, v_out, xn_out, u_out, cos_out, sin_out,
    x_vm, w_vm, stage, spots_all, factors_vm, offsets_vm, jd_vm,
    w_sems, flow_sems, x_sems, spot_sems, factor_sems, shared_sems, offset_sems, local_sems, out_sems, move_sems,
):
    at = Place(planes)
    rows_all, width = x_vm.shape
    half = w_ref.shape[2]
    at.greet(True, True)
    chunks = rows_all // ROWS
    flow = Flow(at, w_ref, lambda s, h: w_out.at[s, h], w_sems)
    flow_o, flows = weight_flows(at, own_o, own_e, own_r, full_o, full_e, full_r, flow_sems, blocks)
    ahead = [flow_o] + [f for pair in flows[: blocks - 1] for f in pair]
    holds = at.core == at.ctx

    def local(source, target, index):
        return pltpu.make_async_copy(source, target, local_sems.at[index])

    flow.pass_on(0, z=True, tp=True)

    def x_chunk(i):
        span = pl.ds(i * ROWS, ROWS)
        return turned_copy(at, tokens_ref.at[at.tp, span], x_vm.at[span], x_sems.at[i])

    spot_copy = turned_copy(at, spots_ref, spots_all.at[0], spot_sems.at[0])
    spot_here = local(spots_ref, spots_all.at[0], 0)

    @pl.when(at.crosses)
    def _():
        spot_copy.start()
        for i in range(chunks):
            x_chunk(i).start()

    @pl.when(holds)
    def _():
        spot_here.start()
        for i in range(chunks):
            span = pl.ds(i * ROWS, ROWS)
            local(tokens_ref.at[at.tp, span], x_vm.at[span], 1 + i).start()

    flow.pass_on(0, core=True)

    def remote(source, target, sems, device):
        return pltpu.make_async_remote_copy(
            src_ref=source, dst_ref=target, send_sem=sems.at[0], recv_sem=sems.at[1],
            device_id=device, device_id_type=MESH,
        )

    offset_copy = remote(offsets_ref, offsets_out.at[at.tp], offset_sems, at.next_tp)
    offset_came = remote(offsets_ref, offsets_out.at[1 - at.tp], offset_sems, at.next_tp)
    offset_copy.start()
    local(offsets_ref, offsets_out.at[at.tp], 1 + chunks).start()
    next_copy = remote(factors_next, factors_out.at[at.tp], factor_sems.at[0], at.next_tp)
    next_came = remote(factors_next, factors_out.at[1 - at.tp], factor_sems.at[0], at.next_tp)
    own_factors = remote(factors_ref, factors_out.at[at.tp], factor_sems.at[1], at.next_core)
    shared_copy = remote(shared_ref, shared_out, shared_sems, at.next_core)
    next_factors = remote(factors_out.at[1 - at.tp], factors_out.at[1 - at.tp], factor_sems.at[2], at.next_core)

    @pl.when(holds)
    def _():
        next_copy.start()
        own_factors.start()
        shared_copy.start()
        local(factors_ref, factors_out.at[at.tp], 2 + chunks).start()
        local(shared_ref, shared_out, 3 + chunks).start()

    local(w_ref, w_out.at[at.shard, at.tp], 4 + chunks).start()
    local(own_o, full_o.at[at.shard, at.tp], 5 + chunks).start()
    local(own_e, full_e.at[at.shard, at.tp], 6 + chunks).start()
    local(own_r, full_r.at[at.shard, at.tp], 7 + chunks).start()

    @pl.when(at.crosses)
    def _():
        spot_copy.wait_recv()

    @pl.when(holds)
    def _():
        spot_here.wait()

    spot_next = remote(spots_all.at[0], spots_all.at[1], spot_sems.at[1], at.next_core)
    spot_next.start()

    @pl.when(holds)
    def _():
        next_came.wait_recv()
        next_factors.start()

    lane = lax.broadcasted_iota(jnp.int32, (1, 128), 1) % 64
    turned = lane < 60
    early = lane % 20 < 10

    def tables(part):
        def body(i, carry):
            span = pl.ds(pl.multiple_of(i * ROWS, ROWS), ROWS)
            angle = dot(spots_all[part, :, span], rates_ref[...], 0, 0)
            out = pl.ds(pl.multiple_of(part * rows_all + i * ROWS, ROWS), ROWS)
            cos_out[out, :] = jnp.where(turned, jnp.cos(angle), 1.0)
            sine = jnp.sin(angle)
            sin_out[out, :] = jnp.where(turned, jnp.where(early, -sine, sine), 0.0)
            return carry

        lax.fori_loop(0, chunks, body, 0)

    tables(0)
    flow.pass_on(1, z=True, tp=True, core=True, wait=True)
    spot_next.wait()
    tables(1)

    @pl.when(holds)
    def _():
        local(factors_ref, factors_out.at[at.tp], 2 + chunks).wait()
        local(shared_ref, shared_out, 3 + chunks).wait()
        own_factors.wait_send()
        shared_copy.wait_send()
        next_copy.wait_send()
        next_factors.wait_send()

    @pl.when(at.crosses)
    def _():
        own_factors.wait_recv()
        shared_copy.wait_recv()
        remote(factors_out.at[1 - at.tp], factors_out.at[1 - at.tp], factor_sems.at[2], at.next_core).wait_recv()

    offset_copy.wait_send()
    offset_came.wait_recv()
    local(offsets_ref, offsets_out.at[at.tp], 1 + chunks).wait()
    loads = [
        pltpu.make_async_copy(factors_out, factors_vm, out_sems.at[0]),
        pltpu.make_async_copy(offsets_out, offsets_vm, out_sems.at[1]),
        pltpu.make_async_copy(shared_out.at[:, pl.ds(0, width)], jd_vm, out_sems.at[2]),
    ]
    for load in loads:
        load.start()
    if planes > 2:
        flow.pass_on(2, z=True, tp=True, core=True, wait=True)
    for load in loads:
        load.wait()

    kept = []

    def x_ready(i):
        span = pl.ds(i * ROWS, ROWS)

        @pl.when(at.crosses)
        def _():
            x_chunk(i).wait()

        @pl.when(holds)
        def _():
            local(tokens_ref.at[at.tp, span], x_vm.at[span], 1 + i).wait()

        keep = pltpu.make_async_copy(x_vm.at[span], x_out.at[span], x_sems.at[i, 2])
        keep.start()
        kept.append(keep)
        scaled, _ = row_norm(x_vm[span, :].astype(F32))
        xn = (scaled * gain_ref[...] + shift_ref[...]).astype(B16)
        xn_out[span, :] = xn
        u_out[span, :] = dot(xn, jd_vm[...], 1, 1).astype(B16)

    for i in range(chunks // 2):
        x_ready(i)
    for far in range(3, planes):
        flow.pass_on(far, z=True, tp=True, core=True, wait=True)
    for other in ahead:
        other.pass_on(0, z=True)
    for i in range(chunks // 2, chunks):
        x_ready(i)

    outs = (q_out, k_out, v_out)
    sending = []

    def compute(order, owner):
        for part in range(3):
            load = pltpu.make_async_copy(w_out.at[:, owner, part], w_vm.at[part], out_sems.at[part])
            load.start()
        for part in range(3):
            pltpu.make_async_copy(w_out.at[:, owner, part], w_vm.at[part], out_sems.at[part]).wait()
            w = w_vm[part].reshape(width, half)
            bias = offsets_vm[owner, :, part * half : (part + 1) * half]
            up = factors_vm[owner, :, part * half : (part + 1) * half]

            def body(i, carry):
                span = pl.ds(pl.multiple_of(i * ROWS, ROWS), ROWS)
                value = dot(xn_out[span, :], w) + bias + dot(u_out[span, :], up)
                if part == 2:
                    stage[order, part, span, :] = value.astype(B16)
                else:
                    for col in range(0, half, 128):
                        piece = value[:, col : col + 128]
                        stage[order, part, span, col : col + 128] = (
                            piece * cos_out[span, :] + partner(piece) * sin_out[span, :]
                        ).astype(B16)
                return carry

            lax.fori_loop(0, chunks, body, 0)

            def moves(part=part):
                here = pltpu.make_async_copy(
                    stage.at[order, part], outs[part].at[pl.ds(0, rows_all)], out_sems.at[3 + part]
                )
                there = remote(
                    stage.at[order, part], outs[part].at[pl.ds(rows_all, rows_all)],
                    move_sems.at[part], at.next_core,
                )
                return here, there

            @pl.when(owner == at.core)
            def _():
                moves()[0].start()

            @pl.when(owner != at.core)
            def _():
                moves()[1].start()

            sending.append((owner, moves))

    for far in range(planes):
        flow.wait(OWN_CAME, far)
    local(w_ref, w_out.at[at.shard, at.tp], 4 + chunks).wait()
    for far in range(planes - 1):
        flow.pass_next(far)
    compute(0, at.tp)
    flow.pass_next(planes - 1)
    for far in range(planes):
        flow.wait(NEXT_CAME, far)
    compute(1, 1 - at.tp)

    for keep in kept:
        keep.wait()
    for other in ahead:
        other.wait(Z_CAME, 1)
        other.sent(0, z=True)
    for far in range(planes):
        flow.sent(far, z=True, tp=True, core=True)
        flow.sent_next(far)
    for i in range(3):
        local((own_o, own_e, own_r)[i], (full_o, full_e, full_r)[i].at[at.shard, at.tp], 5 + i + chunks).wait()

    @pl.when(at.crosses)
    def _():
        spot_copy.wait_send()

    for owner, moves in sending:

        @pl.when(owner == at.core)
        def _():
            moves()[0].wait()

        @pl.when(owner != at.core)
        def _():
            moves()[1].wait_send()

    for _, moves in sending[:3]:
        moves()[1].wait_recv()


def project(planes, tokens, spots, factors, factors_next, shared, offsets, weight, own_o, own_e, own_r, gain, shift, rates):
    rows, width = tokens.shape[1:]
    _, depth, half = weight.shape
    rank = factors.shape[0]
    blocks = own_e.shape[1] // HIDDEN_BLOCK
    chunks = rows // ROWS
    shape = jax.ShapeDtypeStruct
    hbm = pl.BlockSpec(memory_space=pl.ANY)
    vmem = pl.BlockSpec(memory_space=pltpu.VMEM)
    dma = pltpu.SemaphoreType.DMA
    return pl.pallas_call(
        functools.partial(project_body, planes, blocks),
        in_specs=[hbm] * 1 + [vmem] * 12,
        out_specs=[hbm] * 11 + [vmem] * 4,
        out_shape=[
            shape((rows, width), B16),
            shape((2,) + factors.shape, B16),
            shape(shared.shape, B16),
            shape((2,) + offsets.shape, F32),
            shape((2 * planes, 2) + weight.shape, B16),
            shape((2 * planes, 2) + own_o.shape, B16),
            shape((2 * planes, 2) + own_e.shape, B16),
            shape((2 * planes, 2) + own_r.shape, B16),
            shape((2 * rows, half), B16),
            shape((2 * rows, half), B16),
            shape((2 * rows, half), B16),
            shape((rows, width), B16),
            shape((rows, rank), B16),
            shape((2 * rows, 128), F32),
            shape((2 * rows, 128), F32),
        ],
        scratch_shapes=[
            pltpu.VMEM((rows, width), B16),
            pltpu.VMEM((3, 2 * planes, depth, half), B16),
            pltpu.VMEM((2, 3, rows, half), B16),
            pltpu.VMEM((2,) + spots.shape, B16),
            pltpu.VMEM((2,) + factors.shape, B16),
            pltpu.VMEM((2,) + offsets.shape, F32),
            pltpu.VMEM((rank, width), B16),
            dma((9, planes)),
            dma((1 + 2 * blocks, 9, planes)),
            dma((chunks, 3)),
            dma((2, 2)),
            dma((3, 2)),
            dma((2,)),
            dma((2,)),
            dma((8 + chunks,)),
            dma((6,)),
            dma((3, 2)),
        ],
        compiler_params=pltpu.CompilerParams(
            vmem_limit_bytes=VMEM_LIMIT, collective_id=0, has_side_effects=True
        ),
        cost_estimate=pl.CostEstimate(
            flops=2 * rows * width * 6 * half, bytes_accessed=100 * 2**20, transcendentals=0
        ),
    )(tokens, spots, factors, factors_next, shared, offsets, weight, own_o, own_e, own_r, gain, shift, rates)


def attend_body(
    planes, blocks,
    q_ref, k_ref, v_ref, cot_ref, own_o, own_e, own_r, in_o, in_e, in_r,
    o_ref, inv_ref, e_ref, o_next, cot_out, full_o, full_e, full_r,
    vm_ref, stage, cot_vm, flow_sems, stage_sems, cot_sems,
):
    at = Place(planes)
    rows_all, length = q_ref.shape[0], k_ref.shape[0]
    low = low_lanes()
    pair, turn = pl.program_id(0), pl.program_id(1)
    turns = length // rows_all
    now = pair * turns + turn
    pairs = stage.shape[0] // (turns // 2)
    count = pairs * turns
    flow_o, flows = weight_flows(at, own_o, own_e, own_r, full_o, full_e, full_r, flow_sems, blocks)
    zero = [flow_o] + flows[0]
    last = planes - 1
    cot_move = turned_copy(at, cot_ref.at[at.tp], cot_out, cot_sems)
    cot_load = pltpu.make_async_copy(cot_ref.at[at.tp], cot_vm, cot_sems.at[2])
    cot_keep = pltpu.make_async_copy(cot_vm, cot_out, cot_sems.at[3])

    def when(step, act):
        pl.when(now == min(step * count // 16, count - 1))(act)

    @pl.when(now == 0)
    def _():
        at.greet(True, True)
        for flow in zero:
            flow.pass_on(1, z=True, tp=True, core=True)
            flow.pass_on(0, tp=True, core=True)
        for flow in flows[1]:
            flow.pass_on(1, z=True, core=True)
        pl.when(at.crosses)(lambda: cot_move.start())
        pl.when(jnp.logical_not(at.crosses))(lambda: cot_load.start())
        for flow in flows[1] + flows[2]:
            flow.pass_on(0, core=True)

    def at_3():
        @pl.when(jnp.logical_not(at.crosses))
        def _():
            cot_load.wait()
            cot_keep.start()

        for flow in zero:
            flow.pass_on(2, z=True, tp=True, core=True, wait=True)

    def at_4():
        for flow in flows[2]:
            flow.pass_on(1, z=True, core=True)

    def at_5():
        for flow in flows[1]:
            flow.pass_on(2, z=True, core=True, wait=True)

    def at_7():
        for flow in zero:
            flow.pass_on(3, tp=True, core=True, wait=True)
        for flow in flows[1]:
            flow.pass_on(0, tp=True)
            flow.pass_on(1, tp=True)
            flow.pass_on(2, tp=True)
        for flow in zero:
            flow.pass_next(0)
            flow.pass_next(1)

    def at_8():
        for flow in flows[2]:
            flow.pass_on(2, z=True, core=True, wait=True)
        for flow in flows[3]:
            flow.pass_on(0, z=True)

    def at_10():
        for flow in flows[1]:
            flow.pass_on(3, tp=True, core=True, wait=True)
        for flow in zero:
            flow.pass_next(2)
            flow.pass_next(3)

    def at_12():
        for flow in flows[2]:
            flow.pass_on(3, core=True, wait=True)

    def at_13():
        for flow in flows[3]:
            flow.pass_on(1, z=True, wait=True)

    def at_15():
        for flow in flows[3]:
            flow.pass_on(2, z=True, wait=True)

    for step, act in ((3, at_3), (4, at_4), (5, at_5), (7, at_7), (8, at_8), (10, at_10), (12, at_12), (13, at_13), (15, at_15)):
        when(step, act)

    @pl.when(turn == 0)
    def _():
        vm_ref[0] = jnp.where(low, v_ref[...], 1).astype(B16)
        vm_ref[1] = jnp.where(low, 1, v_ref[...]).astype(B16)

    step = min(256, rows_all)
    for begin in range(0, rows_all, step):
        rows = pl.ds(begin, step)
        q = q_ref[rows, :]
        sums = []
        for head in range(2):
            mine = low if head == 0 else ~low
            scores = dot(jnp.where(mine, q, 0).astype(B16), k_ref[...], 1, 1)
            top = jnp.max(scores, 1, keepdims=True)
            weights = jnp.exp2((scores - top) * exp_scale).astype(B16)
            e_ref[head, rows, :] = weights
            sums.append(dot(weights, vm_ref[head]))
        total = pltpu.roll(jnp.where(low, sums[1], sums[0]), 64, 1)
        inverse = 1.0 / total
        o_ref[rows, :] = (jnp.where(low, sums[0], sums[1]) * inverse).astype(B16)
        inv_ref[rows, :] = inverse

    def o_move(index):
        per = turns // 2
        rows = pl.ds(pl.multiple_of(index % per * rows_all, rows_all), rows_all)
        columns = pl.ds(pl.multiple_of(index // per * 128, 128), 128)
        return pltpu.make_async_remote_copy(
            src_ref=stage.at[index], dst_ref=o_next.at[rows, columns],
            send_sem=stage_sems.at[0, index], recv_sem=stage_sems.at[1, index],
            device_id=at.next_core, device_id_type=MESH,
        )

    @pl.when(turn >= turns // 2)
    def _():
        index = pair * (turns // 2) + turn - turns // 2
        stage[index] = o_ref[...]
        o_move(index).start()

    @pl.when(now == count - 1)
    def _():
        for flow in flows[3]:
            flow.wait(Z_CAME, 3)
        for flow in zero + flows[1] + flows[2]:
            for far in range(planes):
                flow.wait(OWN_CAME, far)
        for flow in zero:
            for far in range(planes):
                flow.wait(NEXT_CAME, far)
                flow.sent_next(far)
        for flow in flows[1]:
            for far in range(planes):
                flow.wait(TP_CAME, far)
        for flow in zero + flows[1] + flows[2] + flows[3]:
            for far in range(planes):
                moved = flow in flows[3]
                flow.sent(
                    far,
                    z=(far < last) and (moved or far > 0),
                    tp=flow in zero or flow in flows[1],
                    core=not moved,
                )

        @pl.when(at.crosses)
        def _():
            cot_move.wait()

        @pl.when(jnp.logical_not(at.crosses))
        def _():
            cot_keep.wait()

        for index in range(count // 2):
            o_move(index).wait()


def attend(planes, query, key, value, cotangent, own_o, own_e, own_r, full_o, full_e, full_r):
    length, width = query.shape
    block = min(512, length // 2)
    blocks = own_e.shape[1] // HIDDEN_BLOCK
    turns = length // block
    pairs = width // 128
    rows = pl.BlockSpec((block, 128), lambda p, i: (i, p))
    full = pl.BlockSpec((length, 128), lambda p, i: (0, p))
    hbm = pl.BlockSpec(memory_space=pl.ANY)
    shape = jax.ShapeDtypeStruct
    like = lambda array: shape(array.shape, array.dtype)
    dma = pltpu.SemaphoreType.DMA
    return pl.pallas_call(
        functools.partial(attend_body, planes, blocks),
        grid=(pairs, turns),
        in_specs=[rows, full, full] + [hbm] * 7,
        out_specs=[rows, rows, pl.BlockSpec((2, block, length), lambda p, i: (p, i, 0))] + [hbm] * 5,
        out_shape=[
            shape((length, width), B16),
            shape((length, width), F32),
            shape((width // 64, length, length), B16),
            shape((length // 2, width), B16),
            shape(cotangent.shape[1:], B16),
            like(full_o), like(full_e), like(full_r),
        ],
        input_output_aliases={7: 5, 8: 6, 9: 7},
        scratch_shapes=[
            pltpu.VMEM((2, length, 128), B16),
            pltpu.VMEM((pairs * turns // 2, block, 128), B16),
            pltpu.VMEM(cotangent.shape[1:], B16),
            dma((1 + 2 * blocks, 9, planes)),
            dma((2, pairs * turns // 2)),
            dma((4,)),
        ],
        compiler_params=pltpu.CompilerParams(
            vmem_limit_bytes=VMEM_LIMIT, collective_id=1, has_side_effects=True
        ),
        cost_estimate=pl.CostEstimate(
            flops=16 * length * length * width,
            bytes_accessed=width // 64 * length * length * 2,
            transcendentals=width // 64 * length * length,
        ),
    )(query, key, value, cotangent, own_o, own_e, own_r, full_o, full_e, full_r)


def attend_back_body(
    q_ref, k_ref, v_ref, o_ref, inv_ref, g_ref, e_ref, cos_ref, sin_ref, cos_all, sin_all,
    gq_ref, gk_ref, gv_ref, key_sum, value_sum, vm_ref,
):
    rows_all, length = q_ref.shape[0], k_ref.shape[0]
    low = low_lanes()
    at_step = pl.program_id(1)

    @pl.when(at_step == 0)
    def _():
        key_sum[...] = jnp.zeros_like(key_sum)
        value_sum[...] = jnp.zeros_like(value_sum)
        vm_ref[0] = jnp.where(low, v_ref[...], -1).astype(B16)
        vm_ref[1] = jnp.where(low, -1, v_ref[...]).astype(B16)

    step = min(256, rows_all)
    for at in range(0, rows_all, step):
        rows = pl.ds(at, step)
        grad = g_ref[rows, :].astype(F32) * inv_ref[rows, :]
        grad_low = grad.astype(B16)
        product = pltpu.roll(grad * o_ref[rows, :].astype(F32), 64, 1).astype(B16)
        q_turned = q_ref[rows, :].T
        g_turned = grad_low.T
        parts = []
        for head in range(2):
            mine = low if head == 0 else ~low
            weights = e_ref[head, rows, :]
            grad_probs = dot(jnp.where(mine, grad_low, product), vm_ref[head], 1, 1)
            grad_scores = (weights.astype(F32) * grad_probs).astype(B16)
            parts.append(dot(grad_scores, k_ref[...]))
            span = pl.ds(head * 64, 64)
            key_sum[span, :] += dot(q_turned[head * 64 : head * 64 + 64], grad_scores)
            value_sum[span, :] += dot(g_turned[head * 64 : head * 64 + 64], weights)
        gq = jnp.where(low, parts[0], parts[1]) * score_scale
        gq_ref[rows, :] = (gq * cos_ref[rows, :] + partner(gq * sin_ref[rows, :])).astype(B16)

    @pl.when(at_step == pl.num_programs(1) - 1)
    def _():
        gk = key_sum[...].T * score_scale
        gk_ref[...] = (gk * cos_all[...] + partner(gk * sin_all[...])).astype(B16)
        gv_ref[...] = value_sum[...].T.astype(B16)


def attend_back(query, key, value, attended, inverse, grad, weights, cosine, sine):
    length, width = query.shape
    block = min(512, length)
    rows = pl.BlockSpec((block, 128), lambda p, i: (i, p))
    full = pl.BlockSpec((length, 128), lambda p, i: (0, p))
    table = pl.BlockSpec((block, 128), lambda p, i: (i, 0))
    table_all = pl.BlockSpec((length, 128), lambda p, i: (0, 0))
    return pl.pallas_call(
        attend_back_body,
        grid=(width // 128, length // block),
        in_specs=[
            rows, full, full, rows, rows, rows,
            pl.BlockSpec((2, block, length), lambda p, i: (p, i, 0)),
            table, table, table_all, table_all,
        ],
        out_specs=[rows, full, full],
        out_shape=[jax.ShapeDtypeStruct((length, width), B16)] * 3,
        scratch_shapes=[
            pltpu.VMEM((128, length), F32),
            pltpu.VMEM((128, length), F32),
            pltpu.VMEM((2, length, 128), B16),
        ],
        compiler_params=params(),
        cost_estimate=pl.CostEstimate(
            flops=20 * length * length * width,
            bytes_accessed=width // 64 * length * length * 2,
            transcendentals=0,
        ),
    )(query, key, value, attended, inverse, grad, weights, cosine, sine, cosine, sine)


def gauss_parts(z):
    t = 1.0 / (1.0 + (0.3275911 * math.sqrt(0.5)) * jnp.abs(z))
    poly = t * (0.254829592 + t * (-0.284496736 + t * (1.421413741 + t * (-1.453152027 + t * 1.061405429))))
    bell = jnp.exp2((z * z) * (-0.5 * math.log2(math.e)))
    upper = 0.5 * poly * bell
    cdf = jnp.where(z >= 0, 1.0 - upper, upper)
    return cdf, bell * (1.0 / math.sqrt(2.0 * math.pi))


def middle_body(
    planes, blocks,
    x_ref, cot_ref, own_ref, other_ref, wo_ref, factors_ref, shared_ref, offsets_ref,
    out_off, gain_ref, shift_ref, shrink_off, in_e, in_r,
    output_ref, gh_ref, t_od, t_ou, t_ed, t_ru, t_eu, t_rd, gatt_out, full_e, full_r,
    hidden, xn_ref, total, back, u2_ref, u3_ref, u4_sum, g4_ref, g3_sum,
    e_vm, r_vm, gown_vm, gother_vm, load_sems, flow_sems, grad_sems,
):
    at = Place(planes)
    f = pl.program_id(0)
    last = 2 * blocks - 1
    core = at.core
    rows_all, width = x_ref.shape
    half = own_ref.shape[1]
    hidden_half = blocks * HIDDEN_BLOCK
    step = 256
    flows = []
    for block in range(blocks):
        span = pl.ds(block * HIDDEN_BLOCK, HIDDEN_BLOCK)
        flows.append(
            [
                Flow(at, None, lambda s, h, span=span: full_e.at[s, h, :, span], flow_sems.at[2 * block]),
                Flow(at, None, lambda s, h, span=span: full_r.at[s, h, span, :], flow_sems.at[2 * block + 1]),
            ]
        )
    planes_all = range(planes)

    def pass_on(pair, **how):
        for flow in pair:
            for far in planes_all:
                flow.pass_on(far, fresh=False, **how)

    def pass_next(pair, wait):
        for flow in pair:
            for far in planes_all:
                flow.pass_next(far, wait)

    def arrived(pair, kind):
        for flow in pair:
            for far in planes_all:
                flow.wait(kind, far)

    def loads(index, slot):
        tp_half = jnp.where(index < blocks, at.tp, 1 - at.tp)
        span = pl.ds(pl.multiple_of(index % blocks * HIDDEN_BLOCK, HIDDEN_BLOCK), HIDDEN_BLOCK)
        return (
            pltpu.make_async_copy(full_e.at[:, tp_half, :, span], e_vm.at[slot], load_sems.at[0, slot]),
            pltpu.make_async_copy(full_r.at[:, tp_half, span, :], r_vm.at[slot], load_sems.at[1, slot]),
        )

    def wo_half(part):
        w = wo_ref[:, part]
        return jnp.concatenate([w[i] for i in range(w.shape[0])], axis=1)

    jd, ed, ou, ru = (pl.ds(i * width, width) for i in range(4))
    od = pl.ds(3 * half, half)

    @pl.when(f == 0)
    def _():
        for load in loads(0, 0):
            load.start()
        at.greet(False, False)
        pass_on(flows[2], tp=True)
        pass_on(flows[3], core=True)
        pass_next(flows[1], False)
        w_own, w_other = wo_half(core), wo_half(1 - core)
        for begin in range(0, rows_all, step):
            rows = pl.ds(begin, step)
            own, other = own_ref[rows, :], other_ref[rows, :]
            u2 = (
                dot(own, factors_ref[core, :, od], 1, 1) + dot(other, factors_ref[1 - core, :, od], 1, 1)
            ).astype(B16)
            u2_ref[rows, :] = u2
            h = (
                x_ref[rows, :].astype(F32) + dot(own, w_own) + dot(other, w_other)
                + out_off[...] + dot(u2, shared_ref[:, ou])
            )
            hidden[rows, :] = h
            scaled, _ = row_norm(h)
            xn = (scaled * gain_ref[...] + shift_ref[...]).astype(B16)
            xn_ref[rows, :] = xn
            u3_ref[rows, :] = dot(xn, shared_ref[:, ed], 1, 1).astype(B16)
            g4_ref[rows, :] = dot(cot_ref[rows, :], shared_ref[:, ru], 1, 1).astype(B16)
            total[rows, :] = h + shrink_off[...]
            back[rows, :] = jnp.zeros_like(h)
            u4_sum[rows, :] = jnp.zeros((step, u4_sum.shape[1]), F32)
            g3_sum[rows, :] = jnp.zeros((step, g3_sum.shape[1]), F32)

    @pl.when(f == 2)
    def _():
        pass_on(flows[3], tp=True)
        arrived(flows[3], OWN_CAME)

    @pl.when(f == 3)
    def _():
        pass_next(flows[2], True)

    @pl.when(f == 4)
    def _():
        arrived(flows[1], NEXT_CAME)

    @pl.when(f == 5)
    def _():
        pass_next(flows[3], True)
        arrived(flows[2], NEXT_CAME)

    @pl.when(f == 6)
    def _():
        arrived(flows[3], NEXT_CAME)

    slot = f % 2

    @pl.when(f < last)
    def _():
        for load in loads(f + 1, 1 - slot):
            load.start()

    for load in loads(f, slot):
        load.wait()
    tp_half = jnp.where(f < blocks, at.tp, 1 - at.tp)
    begin_block = f % blocks * HIDDEN_BLOCK

    def block_of(first):
        return pl.ds(pl.multiple_of(first + begin_block, 128), HIDDEN_BLOCK)

    w_e = e_vm[slot].reshape(width, HIDDEN_BLOCK)
    w_r = jnp.concatenate([r_vm[slot, i] for i in range(2 * planes)], axis=1)
    eu = factors_ref[tp_half, :, block_of(4 * half)]
    rd = factors_ref[tp_half, :, block_of(4 * half + hidden_half)]
    wide_off = offsets_ref[tp_half, :, block_of(3 * half)]
    sum_eu, sum_rd = 0.0, 0.0
    for begin in range(0, rows_all, step):
        rows = pl.ds(begin, step)
        u3, g4 = u3_ref[rows, :], g4_ref[rows, :]
        z = dot(xn_ref[rows, :], w_e) + wide_off + dot(u3, eu)
        gact = dot(cot_ref[rows, :], w_r, 1, 1) + dot(g4, rd)
        cdf, density = gauss_parts(z)
        act = (z * cdf).astype(B16)
        gz = (gact * (cdf + z * density)).astype(B16)
        total[rows, :] += dot(act, w_r)
        u4_sum[rows, :] += dot(act, rd, 1, 1)
        back[rows, :] += dot(gz, w_e, 1, 1)
        g3_sum[rows, :] += dot(gz, eu, 1, 1)
        sum_rd += dot(g4, act, 0, 0)
        sum_eu += dot(u3, gz, 0, 0)
    t_rd[tp_half, :, block_of(0)] = sum_rd
    t_eu[tp_half, :, block_of(0)] = sum_eu

    @pl.when(f == last)
    def _():
        w_own, w_other = wo_half(core), wo_half(1 - core)
        s_ru, s_ed, s_ou, s_own, s_other = 0.0, 0.0, 0.0, 0.0, 0.0
        moves = []
        for index, begin in enumerate(range(0, rows_all, step)):
            rows = pl.ds(begin, step)
            cot = cot_ref[rows, :]
            u4 = u4_sum[rows, :].astype(B16)
            output_ref[rows, :] = (total[rows, :] + dot(u4, shared_ref[:, ru])).astype(B16)
            s_ru += dot(u4, cot, 0, 0)
            g3 = g3_sum[rows, :].astype(B16)
            s_ed += dot(g3, xn_ref[rows, :], 0, 0)
            gx = back[rows, :] + dot(g3, shared_ref[:, ed])
            scaled, inverse = row_norm(hidden[rows, :])
            gh = cot.astype(F32) + back_norm(gx * gain_ref[...], scaled, inverse)
            gh_ref[rows, :] = gh
            gb = gh.astype(B16)
            s_ou += dot(u2_ref[rows, :], gb, 0, 0)
            g2 = dot(gb, shared_ref[:, ou], 1, 1).astype(B16)
            s_own += dot(g2, own_ref[rows, :], 0, 0)
            s_other += dot(g2, other_ref[rows, :], 0, 0)
            gother_vm[rows, :] = (
                dot(gb, w_other, 1, 1) + dot(g2, factors_ref[1 - core, :, od])
            ).astype(B16)
            there = pltpu.make_async_remote_copy(
                src_ref=gother_vm.at[rows], dst_ref=gatt_out.at[pl.ds(rows_all + begin, step)],
                send_sem=grad_sems.at[0, index], recv_sem=grad_sems.at[1, index],
                device_id=at.next_core, device_id_type=MESH,
            )
            there.start()
            gown_vm[rows, :] = (dot(gb, w_own, 1, 1) + dot(g2, factors_ref[core, :, od])).astype(B16)
            here = pltpu.make_async_copy(gown_vm.at[rows], gatt_out.at[rows], grad_sems.at[2, index])
            here.start()
            moves += [there, here]
        t_ru[...] = s_ru
        t_ed[...] = s_ed
        t_ou[...] = s_ou
        t_od[core] = s_own
        t_od[1 - core] = s_other
        for pair in (flows[2], flows[3]):
            for flow in pair:
                for far in planes_all:
                    flow.sent(far, tp=True, core=pair is flows[3])
                    flow.sent_next(far)
        for flow in flows[1]:
            for far in planes_all:
                flow.sent_next(far)
        for move in moves:
            move.wait()


def middle(
    planes, x, cot, attended, other, w_o, factors, shared, offsets, out_off, gain, shift, shrink_off, w_e, w_r
):
    rows, width = x.shape
    half = attended.shape[1]
    shards_, _, depth, hidden_half = w_e.shape
    rank = factors.shape[1]
    blocks = hidden_half // HIDDEN_BLOCK
    one = lambda shape: pl.BlockSpec(
        shape, lambda f: (0,) * len(shape), pipeline_mode=pl.Buffered(1)
    )
    hbm = pl.BlockSpec(memory_space=pl.ANY)
    shape = jax.ShapeDtypeStruct
    dma = pltpu.SemaphoreType.DMA
    chunks = rows // 256
    return pl.pallas_call(
        functools.partial(middle_body, planes, blocks),
        grid=(2 * blocks,),
        in_specs=[
            one((rows, width)), one((rows, width)), one((rows, half)), one((rows, half)),
            one(w_o.shape), one(factors.shape), one(shared.shape), one(offsets.shape),
            one((1, width)), one((1, width)), one((1, width)), one((1, width)), hbm, hbm,
        ],
        out_specs=[
            one((rows, width)), one((rows, width)),
            one((2, rank, half)), one((rank, width)), one((rank, width)), one((rank, width)),
            one((2, rank, hidden_half)), one((2, rank, hidden_half)), hbm, hbm, hbm,
        ],
        out_shape=[
            shape((rows, width), B16), shape((rows, width), F32),
            shape((2, rank, half), F32), shape((rank, width), F32), shape((rank, width), F32),
            shape((rank, width), F32), shape((2, rank, hidden_half), F32), shape((2, rank, hidden_half), F32),
            shape((2 * rows, half), B16), shape(w_e.shape, B16), shape(w_r.shape, B16),
        ],
        input_output_aliases={12: 9, 13: 10},
        scratch_shapes=[
            pltpu.VMEM((rows, width), F32), pltpu.VMEM((rows, width), B16),
            pltpu.VMEM((rows, width), F32), pltpu.VMEM((rows, width), F32),
            pltpu.VMEM((rows, rank), B16), pltpu.VMEM((rows, rank), B16),
            pltpu.VMEM((rows, rank), F32), pltpu.VMEM((rows, rank), B16),
            pltpu.VMEM((rows, rank), F32),
            pltpu.VMEM((2, shards_, depth, HIDDEN_BLOCK), B16),
            pltpu.VMEM((2, shards_, HIDDEN_BLOCK, w_r.shape[3]), B16),
            pltpu.VMEM((rows, half), B16), pltpu.VMEM((rows, half), B16),
            dma((2, 2)), dma((2 * blocks, 9, planes)), dma((3, chunks)),
        ],
        compiler_params=pltpu.CompilerParams(
            vmem_limit_bytes=VMEM_LIMIT, collective_id=2, has_side_effects=True
        ),
        cost_estimate=pl.CostEstimate(
            flops=2 * rows * width * (16 * hidden_half // 2 + 4 * half),
            bytes_accessed=40 * 2**20,
            transcendentals=rows * hidden_half * 2,
        ),
    )(x, cot, attended, other, w_o, factors, shared, offsets, out_off, gain, shift, shrink_off, w_e, w_r)


def unproject_body(
    side, x_ref, gh_ref, xn_ref, u_ref, gain_ref, w_own, w_other, down_ref, up_ref,
    own_q, own_k, own_v, other_q, other_k, other_v,
    grad_ref, t_fd, t_fu,
):
    core = side[0]
    first = pl.program_id(0) == 0

    @pl.when(first)
    def _():
        t_fd[...] = jnp.zeros_like(t_fd)
        t_fu[...] = jnp.zeros_like(t_fu)

    u = u_ref[...]
    g1, gx = 0.0, 0.0
    for w_ref, half, grads in (
        (w_own, core, (own_q, own_k, own_v)),
        (w_other, 1 - core, (other_q, other_k, other_v)),
    ):
        for part in range(3):
            grad = grads[part][...]
            w = w_ref[:, 0, part].reshape(-1, w_ref.shape[-1])
            gx += dot(grad, w, 1, 1)
            g1 += dot(grad, up_ref[half, part], 1, 1)
            t_fu[half, part] += dot(u, grad, 0, 0)
    g1 = g1.astype(B16)
    t_fd[...] += dot(g1, xn_ref[...], 0, 0)
    gx += dot(g1, down_ref[...])
    scaled, inverse = row_norm(x_ref[...].astype(F32))
    grad_ref[...] = (gh_ref[...] + back_norm(gx * gain_ref[...], scaled, inverse)).astype(B16)


def unproject(side, x, gh, xn, u, gain, weight, down, up, own, other):
    rows, width = x.shape
    shards_, _, _, depth, half = weight.shape
    rank = down.shape[0]
    block = 256
    row = lambda columns: pl.BlockSpec((block, columns), lambda i, s: (i, 0))
    whole = lambda shape: pl.BlockSpec(shape, lambda i, s: (0,) * len(shape))
    w_spec = lambda pick: pl.BlockSpec(
        (shards_, 1, 3, depth, half), lambda i, s: (0, pick(s[0]), 0, 0, 0)
    )
    return pl.pallas_call(
        unproject_body,
        grid_spec=pltpu.PrefetchScalarGridSpec(
            num_scalar_prefetch=1,
            grid=(rows // block,),
            in_specs=[
                row(width), row(width), row(width), row(rank), whole((1, width)),
                w_spec(lambda s: s), w_spec(lambda s: 1 - s), whole(down.shape), whole(up.shape),
            ]
            + [row(half)] * 6,
            out_specs=[row(width), whole((rank, width)), whole(up.shape)],
        ),
        out_shape=[
            jax.ShapeDtypeStruct((rows, width), B16),
            jax.ShapeDtypeStruct((rank, width), F32),
            jax.ShapeDtypeStruct(up.shape, F32),
        ],
        compiler_params=params(),
        cost_estimate=pl.CostEstimate(
            flops=2 * rows * width * 6 * half, bytes_accessed=20 * 2**20, transcendentals=0
        ),
    )(side, x, gh, xn, u, gain, weight, weight, down, up, *own, *other)


def clip_shards(
    planes,
    tokens,
    cotangent,
    adapter_pick,
    positions,
    first_gain,
    first_shift,
    joined_weight,
    joined_bias,
    output_weight,
    mixing_exit_offset,
    second_gain,
    second_shift,
    expand_weight,
    widening_offset,
    reduce_weight,
    shrinking_offset,
    joined_down,
    joined_up,
    output_down,
    output_up,
    expand_down,
    expand_up,
    reduce_down,
    reduce_up,
):
    core = lax.axis_index("shard") % 2
    ctx = lax.axis_index("ctx")
    tp = lax.axis_index("tp")
    side = jnp.reshape(core, (1,)).astype(jnp.int32)
    cores = [(i, i ^ 1) for i in range(2 * planes)]
    pair = [(0, 1), (1, 0)]
    place = lambda z, c, x: (2 * z + c) * 2 + x
    turns = [
        (place(z, c, x), place(z, x, c)) for z in range(planes) for c in range(2) for x in range(2)
    ]
    turns_flip = [(2 * a + y, 2 * b + 1 - y) for a, b in turns for y in range(2)]

    def turn(array):
        return lax.ppermute(array, ("shard", "ctx"), turns)

    def to_core(array):
        return lax.ppermute(array, "shard", cores)

    def to_tp(array):
        return lax.ppermute(array, "tp", pair)

    def to_ctx(array):
        return lax.ppermute(array, "ctx", pair)

    def by_tp(mine, others):
        return jnp.where(tp == 0, jnp.stack([mine, others]), jnp.stack([others, mine]))

    mine_of = lambda array, axis=0: lax.dynamic_index_in_dim(array, tp, axis, keepdims=False)
    half = joined_weight.shape[2]
    hidden_half = expand_weight.shape[1]
    rank = joined_up.shape[1]
    rows = tokens.shape[1]

    pick = lax.dynamic_index_in_dim(adapter_pick, tp, 0, keepdims=False)
    pick_next = lax.dynamic_index_in_dim(adapter_pick, 1 - tp, 0, keepdims=False)

    def row(table, at):
        return lax.dynamic_index_in_dim(table, at, 0, keepdims=False)

    def split_factors(at):
        ju, od, eu, rd = row(joined_up, at), row(output_down, at), row(expand_up, at), row(reduce_down, at)
        return jnp.concatenate([ju.reshape(ju.shape[0], -1), od.T, eu, rd.T], axis=1)

    shared = jnp.concatenate(
        [
            row(joined_down, pick).T, row(expand_down, pick).T, row(output_up, pick), row(reduce_up, pick),
            jnp.full((rank, 128), pick.astype(B16)),
        ],
        axis=1,
    )
    offsets = jnp.concatenate([joined_bias.reshape(-1), widening_offset])[None]

    lane = jnp.arange(128, dtype=jnp.int32) % 64
    rates = jnp.exp((lane % 10).astype(F32) * (-math.log(10000.0) / 10.0))
    rates = jnp.where(lane[None] // 20 == jnp.arange(3)[:, None], rates[None], 0.0)
    high = lax.reduce_precision(rates, 8, 7)
    mid = lax.reduce_precision(rates - high, 8, 7)
    low = lax.reduce_precision(rates - high - mid, 8, 7)
    rates = jnp.concatenate([high, mid, low, jnp.zeros((7, 128), F32)], axis=0).astype(B16)
    spots = mine_of(positions, 1).astype(B16)
    spots = jnp.concatenate([spots, spots, spots, jnp.zeros((7, rows), B16)], axis=0)

    (
        x, factors, shared, offsets, w_j, w_o, w_e, w_r, query, key, value, xn1, u1, cosine, sine,
    ) = project(
        planes, tokens, spots, split_factors(pick), split_factors(pick_next), shared, offsets,
        jnp.transpose(joined_weight, (1, 0, 2)), output_weight, expand_weight, reduce_weight,
        first_gain[None], first_shift[None], rates,
    )
    attended, inverse, weights, other_heads, cot, w_o, w_e, w_r = attend(
        planes, query, key, value, cotangent, output_weight, expand_weight, reduce_weight, w_o, w_e, w_r
    )
    out, gh, t_od, t_ou, t_ed, t_ru, t_eu, t_rd, grad_att, w_e, w_r = middle(
        planes, x, cot, attended, other_heads, w_o, factors, shared, offsets,
        mixing_exit_offset[None], second_gain[None], second_shift[None], shrinking_offset[None], w_e, w_r,
    )
    jd = shared[:, : tokens.shape[2]]
    ju = jnp.transpose(factors[:, :, : 3 * half].reshape(2, rank, 3, half), (0, 2, 1, 3))
    tag = shared[: rank // 2, -128:]
    out = turn(out)
    output = by_tp(out, to_tp(out))
    grads = attend_back(query, key, value, attended, inverse, grad_att, weights, cosine, sine)
    tokens_part, t_fd, t_fu = unproject(
        side, x, gh, xn1, u1, first_gain[None], w_j, jd, ju,
        [g[:rows] for g in grads], [to_core(g[rows:]) for g in grads],
    )
    quarter = rows // 2
    stay = lax.dynamic_slice_in_dim(tokens_part, tp * quarter, quarter, 0)
    leave = lax.dynamic_slice_in_dim(tokens_part, (1 - tp) * quarter, quarter, 0)
    tokens_grad = by_tp(turn(stay), lax.ppermute(leave, ("shard", "ctx", "tp"), turns_flip))

    def spread(split, full):
        low_rank = rank // 2
        split_parts = jnp.concatenate(split, axis=2)
        full_part = jnp.concatenate(full, axis=1)
        wide = jnp.concatenate([split_parts[0], split_parts[1], full_part], axis=1)
        keep = lax.dynamic_slice_in_dim(wide, core * low_rank, low_rank, 0)
        send = lax.dynamic_slice_in_dim(wide, (1 - core) * low_rank, low_rank, 0)
        total = (keep + to_core(send.astype(B16)).astype(F32)).astype(B16)
        width = split_parts.shape[2]
        rest = jnp.concatenate([total[:, 2 * width :], tag], axis=1)
        keep = jnp.concatenate([lax.dynamic_slice_in_dim(total, tp * width, width, 1), rest], axis=1)
        send = jnp.concatenate([lax.dynamic_slice_in_dim(total, (1 - tp) * width, width, 1), rest], axis=1)
        stack = jnp.stack([keep, to_tp(send)])
        stack = jnp.concatenate([stack, to_ctx(stack)], axis=0)
        stacks = [stack]
        for shift in range(1, planes):
            stacks.append(
                lax.ppermute(stack, "shard", [(i, (i + 2 * shift) % (2 * planes)) for i in range(2 * planes)])
            )
        stack = jnp.concatenate(stacks, axis=0)
        others = to_core(stack)
        stack = jnp.where(
            core == 0,
            jnp.concatenate([stack, others], axis=1),
            jnp.concatenate([others, stack], axis=1),
        )
        chosen = stack[:, 0, -1].astype(F32)
        choose = (chosen[None, :] == jnp.arange(joined_down.shape[0], dtype=F32)[:, None]).astype(B16)
        summed = lax.dot_general(
            choose, stack[:, :, :-128], (((1,), (0,)), ((), ())), preferred_element_type=F32
        )
        pieces = []
        at = 0
        for item in split:
            pieces.append(summed[:, :, at : at + item.shape[2]])
            at += item.shape[2]
        for item in full:
            pieces.append(summed[:, :, at : at + item.shape[1]])
            at += item.shape[1]
        return pieces

    s_od, s_eu, s_rd, s_ou, s_ed, s_ru = spread([t_od, t_eu, t_rd], [t_ou, t_ed, t_ru])
    t_fu = jnp.transpose(t_fu, (0, 2, 1, 3)).reshape(2, rank, 3 * half)
    s_fu, s_fd = spread([t_fu], [t_fd])
    turn_last = lambda array: jnp.swapaxes(array, 1, 2)
    return (
        output,
        tokens_grad,
        turn_last(s_fd),
        s_fu.reshape(s_fu.shape[0], rank, 3, half),
        turn_last(s_od),
        s_ou,
        turn_last(s_ed),
        s_eu,
        turn_last(s_rd),
        s_ru,
    )


def solution(mesh):
    sizes = dict(mesh.shape)
    if sizes["ctx"] == 2 and sizes["tp"] == 2 and sizes["shard"] == 8:
        body = functools.partial(clip_shards, sizes["shard"] // 2)
    else:
        body = general_shards
    return jax.shard_map(
        body,
        mesh=mesh,
        in_specs=(
            P("shard", "ctx", None),
            P("shard", "ctx", None),
            P("shard"),
            P(None, "shard", "ctx"),
            P(),
            P(),
            P("shard", None, "tp"),
            P(None, "tp"),
            P("tp", "shard"),
            P(),
            P(),
            P(),
            P("shard", "tp"),
            P("tp"),
            P("tp", "shard"),
            P(),
            P(),
            P(None, None, None, "tp"),
            P(None, "tp", None),
            P(),
            P(),
            P(None, None, "tp"),
            P(None, "tp", None),
            P(),
        ),
        out_specs=(
            P("shard", "ctx", None),
            P("shard", ("ctx", "tp"), None),
            P(),
            P(None, None, None, "tp"),
            P(None, "tp", None),
            P(),
            P(),
            P(None, None, "tp"),
            P(None, "tp", None),
            P(),
        ),
        check_vma=False,
    )
```

```python
import functools
import math

import jax
import jax.numpy as jnp
from jax import lax
from jax.experimental import pallas as pl
from jax.experimental.pallas import tpu as pltpu
from jax.sharding import PartitionSpec as P

eps_norm = 1e-06
score_scale = 0.125


def rope_tables(places):
    band = jnp.arange(10, dtype=jnp.float32)
    rates = jnp.exp(band * (-math.log(10000.0) / 10.0))
    angle = places.astype(jnp.float32)[..., None] * rates
    cos_parts = []
    sin_parts = []
    for band_index in range(3):
        cosine = jnp.cos(angle[band_index])
        sine = jnp.sin(angle[band_index])
        cos_parts = cos_parts + [cosine, cosine]
        sin_parts = sin_parts + [-sine, sine]
    rest_shape = angle.shape[1:-1] + (4,)
    cos_parts.append(jnp.ones(rest_shape, jnp.float32))
    sin_parts.append(jnp.zeros(rest_shape, jnp.float32))
    return (jnp.concatenate(cos_parts, -1), jnp.concatenate(sin_parts, -1))


def swap_pairs(values):
    leading = values.shape[:-1]
    turned = values[..., :60].reshape(leading + (3, 2, 10))[..., ::-1, :].reshape(leading + (60,))
    return jnp.concatenate([turned, values[..., 60:]], -1)


def rotate(values, cosine, sine):
    return values * cosine[..., None, :] + swap_pairs(values) * sine[..., None, :]


def rotate_back(grads, cosine, sine):
    return grads * cosine[..., None, :] + swap_pairs(grads * sine[..., None, :])


def norm_forward(values, gain, shift):
    centred = values - jnp.mean(values, -1, keepdims=True)
    inverse = lax.rsqrt(jnp.mean(centred * centred, -1, keepdims=True) + eps_norm)
    scaled = centred * inverse
    return (scaled * gain + shift, scaled, inverse)


def norm_back(grads, scaled, inverse, gain):
    weighted = grads * gain
    return inverse * (
        weighted
        - jnp.mean(weighted, -1, keepdims=True)
        - scaled * jnp.mean(weighted * scaled, -1, keepdims=True)
    )


def select_factor(choose, table):
    return jnp.einsum("ca,a...->c...", choose, table, preferred_element_type=jnp.float32).astype(
        jnp.bfloat16
    )


def gelu_exact(values):
    return jax.nn.gelu(values, approximate=False)


def matrix_product(form, left, right):
    return jnp.einsum(form, left, right, preferred_element_type=jnp.float32)


def general_shards(
    tokens,
    cotangent,
    adapter_pick,
    positions,
    first_gain,
    first_shift,
    joined_weight,
    joined_bias,
    output_weight,
    mixing_exit_offset,
    second_gain,
    second_shift,
    expand_weight,
    widening_offset,
    reduce_weight,
    shrinking_offset,
    joined_down,
    joined_up,
    output_down,
    output_up,
    expand_down,
    expand_up,
    reduce_down,
    reduce_up,
):
    whole_joined, whole_output, whole_expand, whole_reduce = (
        lax.all_gather(joined_weight, "shard", axis=0, tiled=True),
        lax.all_gather(output_weight, "shard", axis=1, tiled=True),
        lax.all_gather(expand_weight, "shard", axis=0, tiled=True),
        lax.all_gather(reduce_weight, "shard", axis=1, tiled=True),
    )
    clip_count, local_len, width = tokens.shape
    local_width = whole_joined.shape[2]
    head_count = local_width // 64
    choose = (
        adapter_pick[:, None] == jnp.arange(joined_down.shape[0], dtype=jnp.int32)[None, :]
    ).astype(jnp.bfloat16)
    select_joined_down = select_factor(choose, joined_down)
    select_joined_up = select_factor(choose, joined_up)
    select_output_down = select_factor(choose, output_down)
    select_output_up = select_factor(choose, output_up)
    select_expand_down = select_factor(choose, expand_down)
    select_expand_up = select_factor(choose, expand_up)
    select_reduce_down = select_factor(choose, reduce_down)
    select_reduce_up = select_factor(choose, reduce_up)
    cosine, sine = rope_tables(positions)
    block_arguments = tokens.astype(jnp.float32)
    norm_one, scaled_one, inverse_one = norm_forward(block_arguments, first_gain, first_shift)
    initial_standardized = norm_one.astype(jnp.bfloat16)
    initial_slim_derivative = matrix_product(
        "zgh,zhe->zge", initial_standardized, select_joined_down
    ).astype(jnp.bfloat16)
    mapped_vectors = (
        matrix_product("cld,dje->clje", initial_standardized, whole_joined)
        + joined_bias
        + matrix_product("uip,upqg->uiqg", initial_slim_derivative, select_joined_up)
    )
    head_shape = (clip_count, local_len, head_count, 64)
    query = rotate(mapped_vectors[:, :, 0].reshape(head_shape), cosine, sine).astype(jnp.bfloat16)
    keys = rotate(mapped_vectors[:, :, 1].reshape(head_shape), cosine, sine).astype(jnp.bfloat16)
    values = mapped_vectors[:, :, 2].reshape(head_shape).astype(jnp.bfloat16)
    stats_shape = (clip_count, head_count, local_len)
    run_max = jnp.full(stats_shape, -1e30, jnp.float32)
    key_part = lax.all_gather(keys, "ctx", axis=1, tiled=True)
    value_part = lax.all_gather(values, "ctx", axis=1, tiled=True)
    scores = matrix_product("cqhd,ckhd->chqk", query, key_part) * score_scale
    new_max = jnp.maximum(run_max, jnp.max(scores, -1))
    weights = jnp.exp(scores - new_max[..., None])
    run_total = jnp.sum(weights, -1)
    update = matrix_product("chqk,ckhd->cqhd", weights.astype(jnp.bfloat16), value_part)
    accum = update
    run_max, run_total, accum = (new_max, run_total, accum)
    log_total = run_max + jnp.log(run_total)
    attended_full = accum / jnp.transpose(run_total, (0, 2, 1))[..., None]
    mixing_outcome = attended_full.reshape(clip_count, local_len, local_width).astype(jnp.bfloat16)
    out_part = matrix_product("cle,ed->cld", mixing_outcome, whole_output)
    rank_partial = matrix_product("fig,fgt->fit", mixing_outcome, select_output_down)
    output_total, rank_sum = (
        lax.psum(out_part.astype(jnp.bfloat16), "tp").astype(jnp.float32),
        lax.psum(rank_partial.astype(jnp.bfloat16), "tp").astype(jnp.float32),
    )
    middle_slim_derivative = rank_sum.astype(jnp.bfloat16)
    first_hidden = (
        block_arguments
        + output_total
        + mixing_exit_offset
        + matrix_product("wnk,wke->wne", middle_slim_derivative, select_output_up)
    )
    norm_two, scaled_two, inverse_two = norm_forward(first_hidden, second_gain, second_shift)
    latter_standardized = norm_two.astype(jnp.bfloat16)
    penultimate_slim_derivative = matrix_product(
        "zgh,zhe->zge", latter_standardized, select_expand_down
    ).astype(jnp.bfloat16)
    skip_stream_vectors = (
        matrix_product("cld,df->clf", latter_standardized, whole_expand)
        + widening_offset
        + matrix_product("uqz,uze->uqe", penultimate_slim_derivative, select_expand_up)
    )
    activity, gelu_pull = jax.vjp(gelu_exact, skip_stream_vectors)
    gaussian_error_unit = activity.astype(jnp.bfloat16)
    mlp_part = matrix_product("clf,fd->cld", gaussian_error_unit, whole_reduce)
    fourth_rank_partial = matrix_product("xpv,xvy->xpy", gaussian_error_unit, select_reduce_down)
    feedforward_sum, rank_four_sum = (
        lax.psum(mlp_part.astype(jnp.bfloat16), "tp").astype(jnp.float32),
        lax.psum(fourth_rank_partial.astype(jnp.bfloat16), "tp").astype(jnp.float32),
    )
    closing_slim_derivative = rank_four_sum.astype(jnp.bfloat16)
    output = (
        first_hidden
        + feedforward_sum
        + shrinking_offset
        + matrix_product("wnk,wke->wne", closing_slim_derivative, select_reduce_up)
    ).astype(jnp.bfloat16)
    back_joined, back_output, back_expand, back_reduce = (
        lax.all_gather(joined_weight, "shard", axis=0, tiled=True),
        lax.all_gather(output_weight, "shard", axis=1, tiled=True),
        lax.all_gather(expand_weight, "shard", axis=0, tiled=True),
        lax.all_gather(reduce_weight, "shard", axis=1, tiled=True),
    )
    reduce_up_term = matrix_product("vkn,vkm->vnm", closing_slim_derivative, cotangent)
    gradient_fourth = matrix_product("abj,awj->abw", cotangent, select_reduce_up).astype(
        jnp.bfloat16
    )
    reduce_down_term = matrix_product("mpg,mpu->mgu", gaussian_error_unit, gradient_fourth)
    grad_active = matrix_product("cld,fd->clf", cotangent, back_reduce) + matrix_product(
        "gez,guz->geu", gradient_fourth, select_reduce_down
    )
    residual_gradient = gelu_pull(grad_active)[0].astype(jnp.bfloat16)
    expand_up_term = matrix_product("jge,jgn->jen", penultimate_slim_derivative, residual_gradient)
    grad_norm_part = matrix_product("clf,df->cld", residual_gradient, back_expand)
    third_gradient_part = matrix_product("aik,adk->aid", residual_gradient, select_expand_up)
    norm_gradient_sum, grad_three_sum = (
        lax.psum(grad_norm_part.astype(jnp.bfloat16), "tp").astype(jnp.float32),
        lax.psum(third_gradient_part.astype(jnp.bfloat16), "tp").astype(jnp.float32),
    )
    gradient_third = grad_three_sum.astype(jnp.bfloat16)
    expand_down_term = matrix_product("kgt,kgh->kth", latter_standardized, gradient_third)
    second_norm_gradient = norm_gradient_sum + matrix_product(
        "jqt,jit->jqi", gradient_third, select_expand_down
    )
    grad_hidden = cotangent.astype(jnp.float32) + norm_back(
        second_norm_gradient, scaled_two, inverse_two, second_gain
    )
    branch_gradient = grad_hidden.astype(jnp.bfloat16)
    output_up_term = matrix_product("vkn,vkm->vnm", middle_slim_derivative, branch_gradient)
    gradient_second = matrix_product("abj,awj->abw", branch_gradient, select_output_up).astype(
        jnp.bfloat16
    )
    output_down_term = matrix_product("nua,nui->nai", mixing_outcome, gradient_second)
    grad_attended = (
        (
            matrix_product("cld,ed->cle", branch_gradient, back_output)
            + matrix_product("gsq,ghq->gsh", gradient_second, select_output_down)
        )
        .astype(jnp.bfloat16)
        .reshape(head_shape)
    )
    key_whole, value_whole = (
        lax.all_gather(keys, "ctx", axis=1, tiled=True),
        lax.all_gather(values, "ctx", axis=1, tiled=True),
    )
    flat_shape = (clip_count, local_len, local_width)

    def clip_back(items):
        query_clip, key_clip, value_clip, grad_clip, total_clip = items
        scores = matrix_product("qhd,khd->hqk", query_clip, key_clip) * score_scale
        probs = jnp.exp(scores - total_clip[..., None])
        grad_probs = matrix_product("qhd,khd->hqk", grad_clip, value_clip)
        middle = jnp.sum(probs * grad_probs, -1, keepdims=True)
        grad_scores = (probs * (grad_probs - middle)).astype(jnp.bfloat16)
        grad_query = matrix_product("hqk,khd->qhd", grad_scores, key_clip) * score_scale
        grad_key = matrix_product("hqk,qhd->khd", grad_scores, query_clip) * score_scale
        grad_value = matrix_product("hqk,qhd->khd", probs.astype(jnp.bfloat16), grad_clip)
        return (grad_query, grad_key, grad_value)

    grad_query, key_terms, value_terms = lax.map(
        clip_back, (query, key_whole, value_whole, grad_attended, log_total)
    )
    full_len = key_whole.shape[1]
    key_sum, value_sum = (
        lax.psum_scatter(
            key_terms.reshape(clip_count, full_len, local_width).astype(jnp.bfloat16),
            "ctx",
            scatter_dimension=1,
            tiled=True,
        ).astype(jnp.float32),
        lax.psum_scatter(
            value_terms.reshape(clip_count, full_len, local_width).astype(jnp.bfloat16),
            "ctx",
            scatter_dimension=1,
            tiled=True,
        ).astype(jnp.float32),
    )
    query_key_value_gradient = jnp.stack(
        [
            rotate_back(grad_query, cosine, sine).reshape(flat_shape),
            rotate_back(key_sum.reshape(head_shape), cosine, sine).reshape(flat_shape),
            value_sum,
        ],
        axis=2,
    ).astype(jnp.bfloat16)
    joined_up_term = matrix_product(
        "pvh,pvfo->phfo", initial_slim_derivative, query_key_value_gradient
    )
    first_gradient_part = matrix_product(
        "kxsd,ktsd->kxt", query_key_value_gradient, select_joined_up
    )
    grad_norm_one_part = matrix_product("clje,dje->cld", query_key_value_gradient, back_joined)
    gradient_first = lax.psum(first_gradient_part.astype(jnp.bfloat16), "tp")
    grad_norm_share = lax.psum_scatter(
        grad_norm_one_part.astype(jnp.bfloat16), "tp", scatter_dimension=1, tiled=True
    ).astype(jnp.float32)
    joined_down_term = matrix_product("kgt,kgh->kth", initial_standardized, gradient_first)
    half_len = grad_norm_share.shape[1]
    begin = lax.axis_index("tp") * half_len

    def shared_rows(array):
        return lax.dynamic_slice_in_dim(array, begin, half_len, 1)

    grad_norm_one = grad_norm_share + matrix_product(
        "jqt,jit->jqi", shared_rows(gradient_first), select_joined_down
    )
    tokens_grad = (
        shared_rows(grad_hidden)
        + norm_back(grad_norm_one, shared_rows(scaled_one), shared_rows(inverse_one), first_gain)
    ).astype(jnp.bfloat16)
    choose_full = choose.astype(jnp.float32)

    def by_adapter(term):
        return jnp.einsum(
            "ca,c...->a...",
            choose_full,
            term,
            precision=lax.Precision.HIGHEST,
            preferred_element_type=jnp.float32,
        )

    summed = lax.psum(
        (
            by_adapter(joined_down_term),
            by_adapter(joined_up_term),
            by_adapter(output_down_term),
            by_adapter(output_up_term),
            by_adapter(expand_down_term),
            by_adapter(expand_up_term),
            by_adapter(reduce_down_term),
            by_adapter(reduce_up_term),
        ),
        ("shard", "ctx"),
    )
    return (
        output,
        tokens_grad,
        summed[0],
        summed[1],
        summed[2],
        summed[3],
        summed[4],
        summed[5],
        summed[6],
        summed[7],
    )


B16 = jnp.bfloat16
F32 = jnp.float32
VMEM_LIMIT = 60 * 2**20
exp_scale = score_scale * math.log2(math.e)


def dot(left, right, left_dim=1, right_dim=0):
    return lax.dot_general(
        left, right, (((left_dim,), (right_dim,)), ((), ())), preferred_element_type=F32
    )


def params():
    return pltpu.CompilerParams(vmem_limit_bytes=VMEM_LIMIT)


def low_lanes():
    return lax.broadcasted_iota(jnp.int32, (1, 128), 1) < 64


def partner(values):
    lane = lax.broadcasted_iota(jnp.int32, (1, 128), 1) % 64 % 20
    return jnp.where(lane < 10, pltpu.roll(values, 118, 1), pltpu.roll(values, 10, 1))


def row_norm(values):
    centred = values - jnp.mean(values, -1, keepdims=True)
    inverse = lax.rsqrt(jnp.mean(centred * centred, -1, keepdims=True) + eps_norm)
    return centred * inverse, inverse


def back_norm(weighted, scaled, inverse):
    return inverse * (
        weighted
        - jnp.mean(weighted, -1, keepdims=True)
        - scaled * jnp.mean(weighted * scaled, -1, keepdims=True)
    )


MESH = pl.DeviceIdType.MESH
HIDDEN_BLOCK = 512
(UP_SENT, DOWN_SENT, Z_CAME, TP_SENT, TP_CAME, OWN_SENT, OWN_CAME, NEXT_SENT, NEXT_CAME) = range(9)


class Place:
    def __init__(self, planes):
        self.planes = planes
        self.shard = lax.axis_index("shard")
        self.z = self.shard // 2
        self.core = self.shard % 2
        self.ctx = lax.axis_index("ctx")
        self.tp = lax.axis_index("tp")
        self.has_up = self.z < planes - 1
        self.has_down = self.z > 0
        self.crosses = self.core != self.ctx
        self.up = {"shard": self.shard + 2}
        self.down = {"shard": self.shard - 2}
        self.next_tp = {"tp": 1 - self.tp}
        self.next_core = {"shard": 2 * self.z + 1 - self.core}
        self.turned = {"shard": 2 * self.z + self.ctx, "ctx": self.core}

    def greet(self, planes_too, turned, ctx_too=False, flipped=False):
        barrier = pltpu.get_barrier_semaphore()
        count = 2

        def signal(device):
            pl.semaphore_signal(barrier, inc=1, device_id=device, device_id_type=MESH)

        signal(self.next_tp)
        signal(self.next_core)
        if planes_too:
            pl.when(self.has_up)(lambda: signal(self.up))
            pl.when(self.has_down)(lambda: signal(self.down))
            count = count + self.has_up.astype(jnp.int32) + self.has_down.astype(jnp.int32)
        if turned:
            pl.when(self.crosses)(lambda: signal(self.turned))
            count = count + self.crosses.astype(jnp.int32)
        if ctx_too:
            signal({"ctx": 1 - self.ctx})
            count = count + 1
        if flipped:
            flip = dict(self.turned)
            flip["tp"] = 1 - self.tp
            pl.when(self.crosses)(lambda: signal(flip))
            count = count + self.crosses.astype(jnp.int32)
        pl.semaphore_wait(barrier, count)


class Flow:
    def __init__(self, at, own, slot, sems, kinds=tuple(range(9))):
        self.at, self.own, self.slot = at, own, slot
        self.sems = {kind: sems[i] for i, kind in enumerate(kinds)}

    def copy(self, kind, plane, own=False):
        at = self.at
        half = 1 - at.tp if kind == NEXT_SENT else at.tp
        piece = self.slot(2 * plane + at.core, half)
        device, came = {
            UP_SENT: (at.up, Z_CAME),
            DOWN_SENT: (at.down, Z_CAME),
            TP_SENT: (at.next_tp, TP_CAME),
            OWN_SENT: (at.next_core, OWN_CAME),
            NEXT_SENT: (at.next_core, NEXT_CAME),
        }[kind]
        return pltpu.make_async_remote_copy(
            src_ref=self.own if own else piece,
            dst_ref=piece,
            send_sem=self.sems[kind].at[plane],
            recv_sem=self.sems[came].at[plane],
            device_id=device,
            device_id_type=MESH,
        )

    def came(self, kind, plane):
        at = self.at
        shard = 2 * plane + (at.core if kind in (Z_CAME, TP_CAME) else 1 - at.core)
        half = at.tp if kind in (Z_CAME, OWN_CAME) else 1 - at.tp
        piece = self.slot(shard, half)
        return pltpu.make_async_remote_copy(
            src_ref=piece, dst_ref=piece, send_sem=self.sems[kind].at[plane],
            recv_sem=self.sems[kind].at[plane], device_id=at.next_core, device_id_type=MESH,
        )

    def pieces(self, distance):
        at = self.at
        if distance == 0:
            return [(None, at.z, True, True)]
        return [
            (at.z >= distance, at.z - distance, True, False),
            (at.z < at.planes - distance, at.z + distance, False, True),
        ]

    def each(self, distance, act):
        for there, plane, below, above in self.pieces(distance):
            if there is None:
                act(plane, below, above)
            else:
                pl.when(there)(functools.partial(act, plane, below, above))

    def pass_on(self, distance, z=False, tp=False, core=False, fresh=None, wait=False):
        own = (distance == 0) if fresh is None else fresh

        def act(plane, below, above):
            if wait:
                self.came(Z_CAME, plane).wait_recv()
            if z:
                if below:
                    pl.when(self.at.has_up)(lambda: self.copy(UP_SENT, plane, own).start())
                if above:
                    pl.when(self.at.has_down)(lambda: self.copy(DOWN_SENT, plane, own).start())
            if tp:
                self.copy(TP_SENT, plane, own).start()
            if core:
                self.copy(OWN_SENT, plane, own).start()

        self.each(distance, act)

    def sent(self, distance, z=False, tp=False, core=False):
        def act(plane, below, above):
            if z:
                if below:
                    pl.when(self.at.has_up)(lambda: self.copy(UP_SENT, plane).wait_send())
                if above:
                    pl.when(self.at.has_down)(lambda: self.copy(DOWN_SENT, plane).wait_send())
            if tp:
                self.copy(TP_SENT, plane).wait_send()
            if core:
                self.copy(OWN_SENT, plane).wait_send()

        self.each(distance, act)

    def wait(self, kind, distance):
        self.each(distance, lambda plane, below, above: self.came(kind, plane).wait_recv())

    def pass_next(self, distance, wait=True):
        def act(plane, below, above):
            if wait:
                self.came(TP_CAME, plane).wait_recv()
            self.copy(NEXT_SENT, plane).start()

        self.each(distance, act)

    def sent_next(self, distance):
        self.each(distance, lambda plane, below, above: self.copy(NEXT_SENT, plane).wait_send())


ALONG_Z = (UP_SENT, DOWN_SENT, Z_CAME)
TO_TP = (TP_SENT, TP_CAME)
TO_CORE = (OWN_SENT, OWN_CAME)
TO_NEXT = (NEXT_SENT, NEXT_CAME)
EVERY = ALONG_Z + TO_TP + TO_CORE + TO_NEXT


class Rows:
    def __init__(self, sems):
        self.sems, self.used = sems, 0

    def take(self, kinds):
        rows = [self.sems.at[self.used + i] for i in range(len(kinds))]
        self.used += len(kinds)
        return rows


def block_flows(at, own_e, own_r, full_e, full_r, rows, kinds):
    flows = []
    for block, needs in enumerate(kinds):
        span = pl.ds(block * HIDDEN_BLOCK, HIDDEN_BLOCK)
        flows.append(
            [
                Flow(
                    at, None if own_e is None else own_e.at[:, span],
                    lambda s, h, span=span: full_e.at[s, h, :, span], rows.take(needs), needs,
                ),
                Flow(
                    at, None if own_r is None else own_r.at[span, :],
                    lambda s, h, span=span: full_r.at[s, h, span, :], rows.take(needs), needs,
                ),
            ]
        )
    return flows


def count_rows(first, kinds):
    return len(first) + 2 * sum(len(needs) for needs in kinds)


PROJECT_KINDS = (ALONG_Z, ALONG_Z)
ATTEND_KINDS = (EVERY, ALONG_Z + TO_TP + TO_CORE, ALONG_Z + TO_CORE, ALONG_Z)
MIDDLE_KINDS = ((), TO_TP + TO_NEXT, TO_TP + TO_NEXT, EVERY)


def turned_copy(at, source, target, sems):
    return pltpu.make_async_remote_copy(
        src_ref=source, dst_ref=target, send_sem=sems.at[0], recv_sem=sems.at[1],
        device_id=at.turned, device_id_type=MESH,
    )


class Spread:
    def __init__(self, at, split, full, tag, sums, give, take, pass_tp, stack, beyond, sems):
        self.at, self.split, self.full, self.tag, self.sums = at, split, full, tag, sums
        self.give, self.take, self.pass_tp, self.stack, self.beyond, self.sems = (
            give, take, pass_tp, stack, beyond, sems,
        )
        self.ranks = give.shape[0]
        self.width = split.shape[2]
        self.rest = full.shape[1]

    def remote(self, source, target, index, device):
        return pltpu.make_async_remote_copy(
            src_ref=source, dst_ref=target, send_sem=self.sems.at[0, index], recv_sem=self.sems.at[1, index],
            device_id=device, device_id_type=MESH,
        )

    def between_cores(self):
        return self.remote(self.give, self.take, 0, self.at.next_core)

    def to_tp(self):
        return self.remote(self.pass_tp, self.stack.at[self.at.z, 1], 1, self.at.next_tp)

    def to_ctx(self):
        plane = self.stack.at[self.at.z]
        return self.remote(plane.at[pl.ds(0, 2)], plane.at[pl.ds(2, 2)], 2, {"ctx": 1 - self.at.ctx})

    def along(self, up, plane):
        piece = self.stack.at[plane]
        return pltpu.make_async_remote_copy(
            src_ref=piece, dst_ref=piece, send_sem=self.sems.at[2 + up, plane], recv_sem=self.sems.at[4, plane],
            device_id=self.at.up if up else self.at.down, device_id_type=MESH,
        )

    def over(self, plane):
        return pltpu.make_async_remote_copy(
            src_ref=self.stack.at[plane], dst_ref=self.beyond.at[plane],
            send_sem=self.sems.at[5, plane], recv_sem=self.sems.at[6, plane],
            device_id=self.at.next_core, device_id_type=MESH,
        )

    def rows(self, core):
        return pl.ds(pl.multiple_of(core * self.ranks, self.ranks), self.ranks)

    def start(self):
        theirs = self.rows(1 - self.at.core)
        for half in range(2):
            self.give[:, half * self.width : (half + 1) * self.width] = self.split[half, theirs, :].astype(B16)
        self.give[:, 2 * self.width :] = self.full[theirs, :].astype(B16)
        self.between_cores().start()

    def second(self):
        at, width, rest = self.at, self.width, self.rest
        self.between_cores().wait_recv()
        mine = self.rows(at.core)
        for half, target in ((at.tp, self.stack.at[at.z, 0]), (1 - at.tp, self.pass_tp)):
            span = pl.ds(pl.multiple_of(half * width, 128), width)
            target[:, 0:width] = (self.split[half, mine, :] + self.take[:, span].astype(F32)).astype(B16)
            target[:, width : width + rest] = (
                self.full[mine, :] + self.take[:, 2 * width :].astype(F32)
            ).astype(B16)
            target[:, width + rest :] = self.tag
        self.to_tp().start()

    def third(self):
        self.to_tp().wait_recv()
        self.to_ctx().start()

    def both_ways(self, act_up, act_down, distance):
        at = self.at
        if distance == 0:
            pl.when(at.has_up)(functools.partial(act_up, at.z))
            pl.when(at.has_down)(functools.partial(act_down, at.z))
        else:
            pl.when((at.z >= distance) & at.has_up)(functools.partial(act_up, at.z - distance))
            pl.when((at.z < at.planes - distance) & at.has_down)(functools.partial(act_down, at.z + distance))

    def came(self, distance, act):
        at = self.at
        pl.when(at.z >= distance)(functools.partial(act, at.z - distance))
        pl.when(at.z < at.planes - distance)(functools.partial(act, at.z + distance))

    def planes(self, distance):
        if distance == 0:
            self.to_ctx().wait_recv()
        else:
            self.came(distance, lambda plane: self.along(1, plane).wait_recv())
        if distance < self.at.planes - 1:
            self.both_ways(
                lambda plane: self.along(1, plane).start(), lambda plane: self.along(0, plane).start(), distance
            )
        if distance == 0:
            self.over(self.at.z).start()
        else:
            self.came(distance, lambda plane: self.over(plane).start())

    def finish(self):
        at = self.at
        for plane in range(at.planes):
            self.over(plane).wait_recv()
        keep = self.width + self.rest
        adapters, ranks = self.sums.shape[0], self.ranks
        terms = at.planes * 4 * ranks
        lane = lax.broadcasted_iota(jnp.int32, (terms, 128), 1)
        rank_of = lax.broadcasted_iota(jnp.int32, (terms, 128), 0) % ranks
        for source, core in ((self.stack, at.core), (self.beyond, 1 - at.core)):
            tags = source[:, :, :, keep:].reshape(terms, 128).astype(F32)
            picks = (tags == (lane // ranks).astype(F32)) & (lane % ranks == rank_of)
            choose = jnp.where(picks, 1.0, 0.0).astype(B16)
            for begin in range(0, keep, 512):
                span = pl.ds(begin, min(512, keep - begin))
                total = dot(choose, source[:, :, :, span].reshape(terms, -1), 0, 0)
                for adapter in range(adapters):
                    self.sums[adapter, self.rows(core), span] = total[adapter * ranks : (adapter + 1) * ranks]

    def sent(self):
        self.between_cores().wait_send()
        self.to_tp().wait_send()
        self.to_ctx().wait_send()
        for distance in range(self.at.planes - 1):
            self.both_ways(
                lambda plane: self.along(1, plane).wait_send(),
                lambda plane: self.along(0, plane).wait_send(),
                distance,
            )
        for plane in range(self.at.planes):
            self.over(plane).wait_send()

    @staticmethod
    def scratch(planes, ranks, width, rest):
        wide = width + rest + 128
        return [
            pltpu.VMEM((ranks, 2 * width + rest), B16),
            pltpu.VMEM((ranks, 2 * width + rest), B16),
            pltpu.VMEM((ranks, wide), B16),
            pltpu.VMEM((planes, 4, ranks, wide), B16),
            pltpu.VMEM((planes, 4, ranks, wide), B16),
            pltpu.SemaphoreType.DMA((7, max(planes, 4))),
        ]


ROWS = 256


def project_body(
    planes, blocks,
    tokens_ref, spots_ref, factors_ref, factors_next, shared_ref, offsets_ref, w_ref, own_o, own_e, own_r,
    gain_ref, shift_ref, rates_ref,
    x_out, factors_out, shared_out, offsets_out, w_out, full_o, full_e, full_r,
    q_out, k_out, v_out, xn_out, u_out, cos_out, sin_out,
    x_vm, w_vm, acc, stage, spots_all, factors_vm, offsets_vm, jd_vm,
    w_sems, flow_sems, x_sems, spot_sems, factor_sems, shared_sems, offset_sems, local_sems, out_sems, move_sems,
):
    at = Place(planes)
    rows_all, width = x_vm.shape
    depth, half = w_ref.shape[1:]
    at.greet(True, True)
    chunks = rows_all // ROWS
    parts = [
        Flow(
            at, w_ref.at[part], lambda s, h, part=part: w_out.at[s, h, part],
            [w_sems.at[part, kind] for kind in range(9)],
        )
        for part in range(3)
    ]
    taken = Rows(flow_sems)
    flow_o = Flow(at, own_o, lambda s, h: full_o.at[s, h], taken.take(ALONG_Z), ALONG_Z)
    flows = block_flows(at, own_e, own_r, full_e, full_r, taken, PROJECT_KINDS)
    ahead = [flow_o] + flows[0] + flows[1]
    holds = at.core == at.ctx

    def local(source, target, index):
        return pltpu.make_async_copy(source, target, local_sems.at[index])

    for flow in parts:
        flow.pass_on(0, z=True, tp=True)

    def x_chunk(i):
        span = pl.ds(i * ROWS, ROWS)
        return turned_copy(at, tokens_ref.at[at.tp, span], x_vm.at[span], x_sems.at[i])

    spot_copy = turned_copy(at, spots_ref, spots_all.at[0], spot_sems.at[0])
    spot_here = local(spots_ref, spots_all.at[0], 0)

    @pl.when(at.crosses)
    def _():
        spot_copy.start()
        for i in range(chunks):
            x_chunk(i).start()

    @pl.when(holds)
    def _():
        spot_here.start()
        for i in range(chunks):
            span = pl.ds(i * ROWS, ROWS)
            local(tokens_ref.at[at.tp, span], x_vm.at[span], 1 + i).start()

    for flow in parts:
        flow.pass_on(0, core=True)

    def remote(source, target, sems, device):
        return pltpu.make_async_remote_copy(
            src_ref=source, dst_ref=target, send_sem=sems.at[0], recv_sem=sems.at[1],
            device_id=device, device_id_type=MESH,
        )

    offset_copy = remote(offsets_ref, offsets_out.at[at.tp], offset_sems, at.next_tp)
    offset_came = remote(offsets_ref, offsets_out.at[1 - at.tp], offset_sems, at.next_tp)
    offset_copy.start()
    local(offsets_ref, offsets_out.at[at.tp], 1 + chunks).start()
    next_copy = remote(factors_next, factors_out.at[at.tp], factor_sems.at[0], at.next_tp)
    next_came = remote(factors_next, factors_out.at[1 - at.tp], factor_sems.at[0], at.next_tp)
    own_factors = remote(factors_ref, factors_out.at[at.tp], factor_sems.at[1], at.next_core)
    shared_copy = remote(shared_ref, shared_out, shared_sems, at.next_core)
    next_factors = remote(factors_out.at[1 - at.tp], factors_out.at[1 - at.tp], factor_sems.at[2], at.next_core)

    @pl.when(holds)
    def _():
        next_copy.start()
        own_factors.start()
        shared_copy.start()
        local(factors_ref, factors_out.at[at.tp], 2 + chunks).start()
        local(shared_ref, shared_out, 3 + chunks).start()

    local(w_ref, w_out.at[at.shard, at.tp], 4 + chunks).start()
    local(own_o, full_o.at[at.shard, at.tp], 5 + chunks).start()
    local(own_e, full_e.at[at.shard, at.tp], 6 + chunks).start()
    local(own_r, full_r.at[at.shard, at.tp], 7 + chunks).start()

    @pl.when(at.crosses)
    def _():
        spot_copy.wait_recv()

    @pl.when(holds)
    def _():
        spot_here.wait()

    spot_next = remote(spots_all.at[0], spots_all.at[1], spot_sems.at[1], at.next_core)
    spot_next.start()

    lane = lax.broadcasted_iota(jnp.int32, (1, 128), 1) % 64
    turned = lane < 60
    early = lane % 20 < 10

    def tables(part):
        def body(i, carry):
            span = pl.ds(pl.multiple_of(i * ROWS, ROWS), ROWS)
            angle = dot(spots_all[part, :, span], rates_ref[...], 0, 0)
            out = pl.ds(pl.multiple_of(part * rows_all + i * ROWS, ROWS), ROWS)
            cos_out[out, :] = jnp.where(turned, jnp.cos(angle), 1.0)
            sine = jnp.sin(angle)
            sin_out[out, :] = jnp.where(turned, jnp.where(early, -sine, sine), 0.0)
            return carry

        lax.fori_loop(0, chunks, body, 0)

    tables(0)
    for flow in parts:
        flow.pass_on(1, z=True, tp=True, core=True, wait=True)
    spot_next.wait()
    tables(1)

    @pl.when(holds)
    def _():
        next_came.wait_recv()
        next_factors.start()

    for flow in parts:
        flow.pass_on(2, z=True, tp=True, core=True, wait=True)

    @pl.when(holds)
    def _():
        local(factors_ref, factors_out.at[at.tp], 2 + chunks).wait()
        local(shared_ref, shared_out, 3 + chunks).wait()
        own_factors.wait_send()
        shared_copy.wait_send()
        next_copy.wait_send()
        next_factors.wait_send()

    @pl.when(at.crosses)
    def _():
        own_factors.wait_recv()
        shared_copy.wait_recv()
        remote(factors_out.at[1 - at.tp], factors_out.at[1 - at.tp], factor_sems.at[2], at.next_core).wait_recv()

    offset_copy.wait_send()
    offset_came.wait_recv()
    local(offsets_ref, offsets_out.at[at.tp], 1 + chunks).wait()
    loads = [
        pltpu.make_async_copy(factors_out, factors_vm, out_sems.at[0]),
        pltpu.make_async_copy(offsets_out, offsets_vm, out_sems.at[1]),
        pltpu.make_async_copy(shared_out.at[:, pl.ds(0, width)], jd_vm, out_sems.at[2]),
    ]
    for load in loads:
        load.start()
    for load in loads:
        load.wait()

    kept = []

    def x_ready(i):
        span = pl.ds(i * ROWS, ROWS)

        @pl.when(at.crosses)
        def _():
            x_chunk(i).wait()

        @pl.when(holds)
        def _():
            local(tokens_ref.at[at.tp, span], x_vm.at[span], 1 + i).wait()

        keep = pltpu.make_async_copy(x_vm.at[span], x_out.at[span], x_sems.at[i, 2])
        keep.start()
        kept.append(keep)
        scaled, _ = row_norm(x_vm[span, :].astype(F32))
        xn = (scaled * gain_ref[...] + shift_ref[...]).astype(B16)
        xn_out[span, :] = xn
        u_out[span, :] = dot(xn, jd_vm[...], 1, 1).astype(B16)

    outs = (q_out, k_out, v_out)
    sending = []
    orders = ((0, 1, 2, 3), (1, 0, 2, 3), (2, 3, 1, 0), (3, 2, 1, 0))

    def plane_at(turn):
        plane = jnp.int32(orders[0][turn])
        for z in range(1, planes):
            plane = jnp.where(at.z == z, orders[z][turn], plane)
        return plane

    def to_next(turn):
        for flow in parts:
            flow.came(TP_CAME, plane_at(turn)).wait_recv()
            flow.copy(NEXT_SENT, plane_at(turn)).start()

    def w_load(turn):
        shards_of = pl.ds(2 * plane_at(turn), 2)
        return pltpu.make_async_copy(w_out.at[shards_of], w_vm.at[turn], out_sems.at[turn])

    def take_plane(turn):
        for flow in parts:
            flow.came(OWN_CAME, plane_at(turn)).wait_recv()
            flow.came(NEXT_CAME, plane_at(turn)).wait_recv()
        w_load(turn).start()

    def columns_of(turn):
        return pl.ds(pl.multiple_of(plane_at(turn) * 2 * depth, 2 * depth), 2 * depth)

    wide = rows_all // 2

    def product(turns, owner, part, span):
        value = 0.0
        for turn in turns:
            w = w_vm[turn, :, owner, part].reshape(2 * depth, half)
            value += dot(xn_out[span, columns_of(turn)], w)
        return value

    owners = (1 - at.core, at.core)

    def add_first(turns):
        for order, owner in enumerate(owners):
            for part in range(3):
                for begin in range(0, rows_all, wide):
                    span = pl.ds(begin, wide)
                    acc[order, part, span, :] = product(turns, owner, part, span)

    def add_last(turn):
        for order, owner in enumerate(owners):
            for part in range(3):
                bias = offsets_vm[owner, :, part * half : (part + 1) * half]
                up = factors_vm[owner, :, part * half : (part + 1) * half]
                for begin in range(0, rows_all, wide):
                    span = pl.ds(begin, wide)
                    value = acc[order, part, span, :] + bias + product((turn,), owner, part, span)
                    value += dot(u_out[span, :], up)
                    if part == 2:
                        stage[order, part, span, :] = value.astype(B16)
                        continue
                    for col in range(0, half, 128):
                        piece = value[:, col : col + 128]
                        stage[order, part, span, col : col + 128] = (
                            piece * cos_out[span, :] + partner(piece) * sin_out[span, :]
                        ).astype(B16)
                if order == 0:
                    move = remote(
                        stage.at[order, part], outs[part].at[pl.ds(rows_all, rows_all)],
                        move_sems.at[part], at.next_core,
                    )
                else:
                    move = pltpu.make_async_copy(
                        stage.at[order, part], outs[part].at[pl.ds(0, rows_all)], out_sems.at[4 + part]
                    )
                move.start()
                sending.append(move)

    to_next(0)
    to_next(1)
    for i in range(chunks):
        x_ready(i)
    for flow in parts:
        flow.pass_on(3, tp=True, core=True, wait=True)
    for other in ahead:
        other.pass_on(0, z=True)
    local(w_ref, w_out.at[at.shard, at.tp], 4 + chunks).wait()
    take_plane(0)
    take_plane(1)
    to_next(2)
    take_plane(2)
    for turn in range(3):
        w_load(turn).wait()
    add_first((0, 1, 2))
    to_next(3)
    take_plane(3)
    w_load(3).wait()
    add_last(3)

    for keep in kept:
        keep.wait()
    for other in ahead:
        other.wait(Z_CAME, 1)
        other.sent(0, z=True)
    for flow in parts:
        for far in range(planes):
            flow.sent(far, z=far < planes - 1, tp=True, core=True)
            flow.sent_next(far)
    for i in range(3):
        local((own_o, own_e, own_r)[i], (full_o, full_e, full_r)[i].at[at.shard, at.tp], 5 + i + chunks).wait()

    @pl.when(at.crosses)
    def _():
        spot_copy.wait_send()

    for move in sending:
        move.wait()


def project(planes, tokens, spots, factors, factors_next, shared, offsets, weight, own_o, own_e, own_r, gain, shift, rates):
    rows, width = tokens.shape[1:]
    _, depth, half = weight.shape
    rank = factors.shape[0]
    blocks = own_e.shape[1] // HIDDEN_BLOCK
    chunks = rows // ROWS
    shape = jax.ShapeDtypeStruct
    hbm = pl.BlockSpec(memory_space=pl.ANY)
    vmem = pl.BlockSpec(memory_space=pltpu.VMEM)
    dma = pltpu.SemaphoreType.DMA
    return pl.pallas_call(
        functools.partial(project_body, planes, blocks),
        in_specs=[hbm] * 1 + [vmem] * 12,
        out_specs=[hbm] * 11 + [vmem] * 4,
        out_shape=[
            shape((rows, width), B16),
            shape((2,) + factors.shape, B16),
            shape(shared.shape, B16),
            shape((2,) + offsets.shape, F32),
            shape((2 * planes, 2) + weight.shape, B16),
            shape((2 * planes, 2) + own_o.shape, B16),
            shape((2 * planes, 2) + own_e.shape, B16),
            shape((2 * planes, 2) + own_r.shape, B16),
            shape((2 * rows, half), B16),
            shape((2 * rows, half), B16),
            shape((2 * rows, half), B16),
            shape((rows, width), B16),
            shape((rows, rank), B16),
            shape((2 * rows, 128), F32),
            shape((2 * rows, 128), F32),
        ],
        scratch_shapes=[
            pltpu.VMEM((rows, width), B16),
            pltpu.VMEM((planes, 2, 2) + weight.shape, B16),
            pltpu.VMEM((2, 3, rows, half), F32),
            pltpu.VMEM((2, 3, rows, half), B16),
            pltpu.VMEM((2,) + spots.shape, B16),
            pltpu.VMEM((2,) + factors.shape, B16),
            pltpu.VMEM((2,) + offsets.shape, F32),
            pltpu.VMEM((rank, width), B16),
            dma((3, 9, planes)),
            dma((count_rows(ALONG_Z, PROJECT_KINDS), planes)),
            dma((chunks, 3)),
            dma((2, 2)),
            dma((3, 2)),
            dma((2,)),
            dma((2,)),
            dma((8 + chunks,)),
            dma((7,)),
            dma((3, 2)),
        ],
        compiler_params=pltpu.CompilerParams(
            vmem_limit_bytes=VMEM_LIMIT, collective_id=0, has_side_effects=True
        ),
        cost_estimate=pl.CostEstimate(
            flops=2 * rows * width * 6 * half, bytes_accessed=100 * 2**20, transcendentals=0
        ),
    )(tokens, spots, factors, factors_next, shared, offsets, weight, own_o, own_e, own_r, gain, shift, rates)


def attend_body(
    planes, blocks,
    q_ref, k_ref, v_ref, cot_ref, own_o, own_e, own_r, in_o, in_e, in_r,
    o_ref, inv_ref, e_ref, o_next, cot_out, full_o, full_e, full_r,
    vm_ref, stage, cot_vm, flow_sems, stage_sems, cot_sems,
):
    at = Place(planes)
    rows_all, length = q_ref.shape[0], k_ref.shape[0]
    low = low_lanes()
    pair, turn = pl.program_id(0), pl.program_id(1)
    turns = length // rows_all
    now = pair * turns + turn
    pairs = stage.shape[0] // (turns // 2)
    count = pairs * turns
    taken = Rows(flow_sems)
    flow_o = Flow(at, own_o, lambda s, h: full_o.at[s, h], taken.take(EVERY), EVERY)
    flows = block_flows(at, own_e, own_r, full_e, full_r, taken, ATTEND_KINDS)
    zero = [flow_o] + flows[0]
    last = planes - 1
    cot_move = turned_copy(at, cot_ref.at[at.tp], cot_out, cot_sems)
    cot_load = pltpu.make_async_copy(cot_ref.at[at.tp], cot_vm, cot_sems.at[2])
    cot_keep = pltpu.make_async_copy(cot_vm, cot_out, cot_sems.at[3])

    def when(step, act):
        pl.when(now == min(step * count // 16, count - 1))(act)

    @pl.when(now == 0)
    def _():
        at.greet(True, True)
        for flow in zero:
            flow.pass_on(1, z=True, tp=True, core=True)
            flow.pass_on(0, tp=True, core=True)
        for flow in flows[1]:
            flow.pass_on(1, z=True, core=True)
        pl.when(at.crosses)(lambda: cot_move.start())
        pl.when(jnp.logical_not(at.crosses))(lambda: cot_load.start())
        for flow in flows[1] + flows[2]:
            flow.pass_on(0, core=True)

    def at_3():
        @pl.when(jnp.logical_not(at.crosses))
        def _():
            cot_load.wait()
            cot_keep.start()

        for flow in zero:
            flow.pass_on(2, z=True, tp=True, core=True, wait=True)
        for flow in flows[2]:
            flow.pass_on(0, z=True)

    def at_5():
        for flow in flows[1]:
            flow.pass_on(2, z=True, core=True, wait=True)

    def at_7():
        for flow in zero:
            flow.pass_on(3, tp=True, core=True, wait=True)
        for flow in flows[1]:
            flow.pass_on(0, tp=True)
            flow.pass_on(1, tp=True)
        for flow in flows[2]:
            flow.pass_on(1, z=True, core=True, wait=True)
        for flow in zero:
            flow.pass_next(0)
            flow.pass_next(1)

    def at_9():
        for flow in flows[1]:
            flow.pass_on(3, core=True, wait=True)
        for flow in flows[2]:
            flow.pass_on(2, z=True, core=True, wait=True)

    def at_11():
        for flow in zero:
            flow.pass_next(2)
            flow.pass_next(3)
        for flow in flows[3]:
            flow.pass_on(0, z=True)

    def at_14():
        for flow in flows[2]:
            flow.pass_on(3, core=True, wait=True)

    for step, act in ((3, at_3), (5, at_5), (7, at_7), (9, at_9), (11, at_11), (14, at_14)):
        when(step, act)

    @pl.when(turn == 0)
    def _():
        vm_ref[0] = jnp.where(low, v_ref[...], 1).astype(B16)
        vm_ref[1] = jnp.where(low, 1, v_ref[...]).astype(B16)

    step = min(256, rows_all)
    for begin in range(0, rows_all, step):
        rows = pl.ds(begin, step)
        q = q_ref[rows, :]
        sums = []
        for head in range(2):
            mine = low if head == 0 else ~low
            scores = dot(jnp.where(mine, q, 0).astype(B16), k_ref[...], 1, 1)
            top = jnp.max(scores, 1, keepdims=True)
            weights = jnp.exp2((scores - top) * exp_scale).astype(B16)
            e_ref[head, rows, :] = weights
            sums.append(dot(weights, vm_ref[head]))
        total = pltpu.roll(jnp.where(low, sums[1], sums[0]), 64, 1)
        inverse = 1.0 / total
        o_ref[rows, :] = (jnp.where(low, sums[0], sums[1]) * inverse).astype(B16)
        inv_ref[rows, :] = inverse

    def o_move(index):
        per = turns // 2
        rows = pl.ds(pl.multiple_of(index % per * rows_all, rows_all), rows_all)
        columns = pl.ds(pl.multiple_of(index // per * 128, 128), 128)
        return pltpu.make_async_remote_copy(
            src_ref=stage.at[index], dst_ref=o_next.at[rows, columns],
            send_sem=stage_sems.at[0, index], recv_sem=stage_sems.at[1, index],
            device_id=at.next_core, device_id_type=MESH,
        )

    @pl.when(turn >= turns // 2)
    def _():
        index = pair * (turns // 2) + turn - turns // 2
        stage[index] = o_ref[...]
        o_move(index).start()

    @pl.when(now == count - 1)
    def _():
        for flow in flows[3]:
            flow.wait(Z_CAME, 1)
        for flow in zero + flows[1] + flows[2]:
            for far in range(planes):
                flow.wait(OWN_CAME, far)
        for flow in zero:
            for far in range(planes):
                flow.wait(NEXT_CAME, far)
                flow.sent_next(far)
        for flow in flows[1]:
            for far in range(2):
                flow.wait(TP_CAME, far)
        for flow in zero + flows[1]:
            for far in range(planes):
                flow.sent(far, z=0 < far < last, tp=flow in zero or far < 2, core=True)
        for flow in flows[2]:
            for far in range(planes):
                flow.sent(far, z=far < last, core=True)
        for flow in flows[3]:
            flow.sent(0, z=True)

        @pl.when(at.crosses)
        def _():
            cot_move.wait()

        @pl.when(jnp.logical_not(at.crosses))
        def _():
            cot_keep.wait()

        for index in range(count // 2):
            o_move(index).wait()


def attend(planes, query, key, value, cotangent, own_o, own_e, own_r, full_o, full_e, full_r):
    length, width = query.shape
    block = min(512, length // 2)
    blocks = own_e.shape[1] // HIDDEN_BLOCK
    turns = length // block
    pairs = width // 128
    rows = pl.BlockSpec((block, 128), lambda p, i: (i, p))
    full = pl.BlockSpec((length, 128), lambda p, i: (0, p))
    hbm = pl.BlockSpec(memory_space=pl.ANY)
    shape = jax.ShapeDtypeStruct
    like = lambda array: shape(array.shape, array.dtype)
    dma = pltpu.SemaphoreType.DMA
    return pl.pallas_call(
        functools.partial(attend_body, planes, blocks),
        grid=(pairs, turns),
        in_specs=[rows, full, full] + [hbm] * 7,
        out_specs=[rows, rows, pl.BlockSpec((2, block, length), lambda p, i: (p, i, 0))] + [hbm] * 5,
        out_shape=[
            shape((length, width), B16),
            shape((length, width), F32),
            shape((width // 64, length, length), B16),
            shape((length // 2, width), B16),
            shape(cotangent.shape[1:], B16),
            like(full_o), like(full_e), like(full_r),
        ],
        input_output_aliases={7: 5, 8: 6, 9: 7},
        scratch_shapes=[
            pltpu.VMEM((2, length, 128), B16),
            pltpu.VMEM((pairs * turns // 2, block, 128), B16),
            pltpu.VMEM(cotangent.shape[1:], B16),
            dma((count_rows(EVERY, ATTEND_KINDS), planes)),
            dma((2, pairs * turns // 2)),
            dma((4,)),
        ],
        compiler_params=pltpu.CompilerParams(
            vmem_limit_bytes=VMEM_LIMIT, collective_id=1, has_side_effects=True
        ),
        cost_estimate=pl.CostEstimate(
            flops=16 * length * length * width,
            bytes_accessed=width // 64 * length * length * 2,
            transcendentals=width // 64 * length * length,
        ),
    )(query, key, value, cotangent, own_o, own_e, own_r, full_o, full_e, full_r)


def attend_back_body(
    planes,
    q_ref, k_ref, v_ref, o_ref, inv_ref, g_ref, e_ref, cos_ref, sin_ref, cos_all, sin_all,
    split_ref, full_ref, tag_ref, out_ref,
    own_ref, other_ref, sums_ref, home_ref,
    key_sum, value_sum, vm_ref, q_stage, kv_stage, out_vm, move_sems, out_sems, *spread_refs,
):
    at = Place(planes)
    rows_all, length = q_ref.shape[0], k_ref.shape[0]
    low = low_lanes()
    pair, at_step = pl.program_id(0), pl.program_id(1)
    pairs, turns = q_stage.shape[0], q_stage.shape[1]
    now = pair * turns + at_step
    count = pairs * turns
    local_rows = length // 2
    spread = Spread(at, split_ref, full_ref, tag_ref[...], sums_ref, *spread_refs)
    stays = jnp.logical_not(at.crosses)
    out_load = pltpu.make_async_copy(out_ref, out_vm, out_sems.at[0])
    out_keep = pltpu.make_async_copy(out_vm, home_ref.at[at.tp], out_sems.at[1])
    out_turn = pltpu.make_async_remote_copy(
        src_ref=out_ref, dst_ref=home_ref.at[at.tp], send_sem=out_sems.at[2], recv_sem=out_sems.at[3],
        device_id=at.turned, device_id_type=MESH,
    )

    def out_tp(source):
        return pltpu.make_async_remote_copy(
            src_ref=source, dst_ref=home_ref.at[at.tp], send_sem=out_sems.at[4], recv_sem=out_sems.at[5],
            device_id=at.next_tp, device_id_type=MESH,
        )

    def when(step, act):
        pl.when(now == step)(act)

    @pl.when(now == 0)
    def _():
        pl.when(stays)(lambda: out_load.start())
        at.greet(True, True, True)
        spread.start()

    when(1, spread.second)
    when(2, spread.third)

    @pl.when(now == 3)
    def _():
        spread.planes(0)
        pl.when(at.crosses)(lambda: out_turn.start())

        @pl.when(stays)
        def _():
            out_load.wait()
            out_keep.start()
            out_tp(out_vm).start()

    when(6, lambda: spread.planes(1))

    @pl.when(now == 9)
    def _():
        @pl.when(at.crosses)
        def _():
            out_turn.wait_recv()
            out_tp(home_ref.at[at.tp]).start()

        spread.planes(2)

    when(12, lambda: spread.planes(3))

    @pl.when(at_step == 0)
    def _():
        key_sum[...] = jnp.zeros_like(key_sum)
        value_sum[...] = jnp.zeros_like(value_sum)
        vm_ref[0] = jnp.where(low, v_ref[...], -1).astype(B16)
        vm_ref[1] = jnp.where(low, -1, v_ref[...]).astype(B16)

    step = min(256, rows_all)
    for begin in range(0, rows_all, step):
        rows = pl.ds(begin, step)
        grad = g_ref[rows, :].astype(F32) * inv_ref[rows, :]
        grad_low = grad.astype(B16)
        product = pltpu.roll(grad * o_ref[rows, :].astype(F32), 64, 1).astype(B16)
        q_turned = q_ref[rows, :].T
        g_turned = grad_low.T
        parts = []
        for head in range(2):
            mine = low if head == 0 else ~low
            weights = e_ref[head, rows, :]
            grad_probs = dot(jnp.where(mine, grad_low, product), vm_ref[head], 1, 1)
            grad_scores = (weights.astype(F32) * grad_probs).astype(B16)
            parts.append(dot(grad_scores, k_ref[...]))
            span = pl.ds(head * 64, 64)
            key_sum[span, :] += dot(q_turned[head * 64 : head * 64 + 64], grad_scores)
            value_sum[span, :] += dot(g_turned[head * 64 : head * 64 + 64], weights)
        gq = jnp.where(low, parts[0], parts[1]) * score_scale
        q_stage[pair, at_step, rows, :] = (
            gq * cos_ref[rows, :] + partner(gq * sin_ref[rows, :])
        ).astype(B16)

    def columns(index):
        return pl.ds(pl.multiple_of(index * 128, 128), 128)

    def q_here(pair_index, turn_index):
        rows = pl.ds(pl.multiple_of(turn_index * rows_all, rows_all), rows_all)
        return pltpu.make_async_copy(
            q_stage.at[pair_index, turn_index], own_ref.at[0, rows, columns(pair_index)],
            move_sems.at[0, pair_index * turns + turn_index],
        )

    def q_there(pair_index, turn_index):
        rows = pl.ds(pl.multiple_of(turn_index * rows_all - local_rows, rows_all), rows_all)
        index = pair_index * turns + turn_index
        return pltpu.make_async_remote_copy(
            src_ref=q_stage.at[pair_index, turn_index], dst_ref=other_ref.at[0, rows, columns(pair_index)],
            send_sem=move_sems.at[0, index], recv_sem=move_sems.at[1, index],
            device_id=at.next_core, device_id_type=MESH,
        )

    def kv_here(part, pair_index):
        return pltpu.make_async_copy(
            kv_stage.at[part, pair_index, pl.ds(0, local_rows)], own_ref.at[1 + part, :, columns(pair_index)],
            move_sems.at[2, 2 * pair_index + part],
        )

    def kv_there(part, pair_index):
        index = 2 * pair_index + part
        return pltpu.make_async_remote_copy(
            src_ref=kv_stage.at[part, pair_index, pl.ds(local_rows, local_rows)],
            dst_ref=other_ref.at[1 + part, :, columns(pair_index)],
            send_sem=move_sems.at[3, index], recv_sem=move_sems.at[4, index],
            device_id=at.next_core, device_id_type=MESH,
        )

    pl.when(at_step < turns // 2)(lambda: q_here(pair, at_step).start())
    pl.when(at_step >= turns // 2)(lambda: q_there(pair, at_step).start())

    @pl.when(at_step == turns - 1)
    def _():
        gk = key_sum[...].T * score_scale
        kv_stage[0, pair] = (gk * cos_all[...] + partner(gk * sin_all[...])).astype(B16)
        kv_stage[1, pair] = value_sum[...].T.astype(B16)
        for part in range(2):
            kv_here(part, pair).start()
            kv_there(part, pair).start()

    @pl.when(now == count - 2)
    def _():
        spread.finish()

    @pl.when(now == count - 1)
    def _():
        for pair_index in range(pairs):
            for turn_index in range(turns):
                if turn_index < turns // 2:
                    q_here(pair_index, turn_index).wait()
                else:
                    q_there(pair_index, turn_index).wait()
            for part in range(2):
                kv_here(part, pair_index).wait()
                kv_there(part, pair_index).wait()
        spread.sent()

        @pl.when(stays)
        def _():
            out_keep.wait()
            out_tp(out_vm).wait_send()

        @pl.when(at.crosses)
        def _():
            out_turn.wait_send()
            out_tp(home_ref.at[at.tp]).wait_send()

        pltpu.make_async_remote_copy(
            src_ref=home_ref.at[at.tp], dst_ref=home_ref.at[1 - at.tp], send_sem=out_sems.at[4],
            recv_sem=out_sems.at[5], device_id=at.next_tp, device_id_type=MESH,
        ).wait_recv()


def attend_back(planes, query, key, value, attended, inverse, grad, weights, cosine, sine, split, full, tag, out, adapters):
    length, width = query.shape
    block = min(512, length // 2)
    pairs, turns = width // 128, length // block
    rows = pl.BlockSpec((block, 128), lambda p, i: (i, p))
    whole = pl.BlockSpec((length, 128), lambda p, i: (0, p))
    table = pl.BlockSpec((block, 128), lambda p, i: (i, 0))
    one = lambda array: pl.BlockSpec(
        array.shape, lambda p, i: (0,) * len(array.shape), pipeline_mode=pl.Buffered(1)
    )
    hbm = pl.BlockSpec(memory_space=pl.ANY)
    shape = jax.ShapeDtypeStruct
    dma = pltpu.SemaphoreType.DMA
    ranks = full.shape[0] // 2
    keep = split.shape[2] + full.shape[1]
    sums = shape((adapters, 2 * ranks, keep), F32)
    return pl.pallas_call(
        functools.partial(attend_back_body, planes),
        grid=(pairs, turns),
        in_specs=[
            rows, whole, whole, rows, rows, rows,
            pl.BlockSpec((2, block, length), lambda p, i: (p, i, 0)),
            table, table, one(cosine), one(sine), one(split), one(full), one(tag), hbm,
        ],
        out_specs=[hbm, hbm, one(sums), hbm],
        out_shape=[
            shape((3, length // 2, width), B16), shape((3, length // 2, width), B16), sums,
            shape((2,) + out.shape, B16),
        ],
        scratch_shapes=[
            pltpu.VMEM((128, length), F32),
            pltpu.VMEM((128, length), F32),
            pltpu.VMEM((2, length, 128), B16),
            pltpu.VMEM((pairs, turns, block, 128), B16),
            pltpu.VMEM((2, pairs, length, 128), B16),
            pltpu.VMEM(out.shape, B16),
            dma((5, max(pairs * turns, 2 * pairs))),
            dma((6,)),
        ]
        + Spread.scratch(planes, ranks, split.shape[2], full.shape[1]),
        compiler_params=pltpu.CompilerParams(
            vmem_limit_bytes=VMEM_LIMIT, collective_id=3, has_side_effects=True
        ),
        cost_estimate=pl.CostEstimate(
            flops=20 * length * length * width,
            bytes_accessed=width // 64 * length * length * 2,
            transcendentals=0,
        ),
    )(query, key, value, attended, inverse, grad, weights, cosine, sine, cosine, sine, split, full, tag, out)


def gauss_parts(z):
    t = 1.0 / (1.0 + (0.3275911 * math.sqrt(0.5)) * jnp.abs(z))
    poly = t * (0.254829592 + t * (-0.284496736 + t * (1.421413741 + t * (-1.453152027 + t * 1.061405429))))
    bell = jnp.exp2((z * z) * (-0.5 * math.log2(math.e)))
    upper = 0.5 * poly * bell
    cdf = jnp.where(z >= 0, 1.0 - upper, upper)
    return cdf, bell * (1.0 / math.sqrt(2.0 * math.pi))


def middle_body(
    planes, blocks,
    x_ref, cot_ref, own_ref, other_ref, wo_ref, factors_ref, shared_ref, offsets_ref,
    out_off, gain_ref, shift_ref, shrink_off, in_e, in_r,
    output_ref, gh_ref, t_split, t_full, gatt_out, full_e, full_r,
    hidden, xn_ref, total, back, u2_ref, u3_ref, u4_sum, g4_ref, g3_sum,
    e_vm, r_vm, gown_vm, gother_vm, load_sems, flow_sems, grad_sems,
):
    at = Place(planes)
    f = pl.program_id(0)
    last = 2 * blocks - 1
    core = at.core
    rows_all, width = x_ref.shape
    half = own_ref.shape[1]
    hidden_half = blocks * HIDDEN_BLOCK
    step = 256
    flows = block_flows(at, None, None, full_e, full_r, Rows(flow_sems), MIDDLE_KINDS)
    planes_all = range(planes)

    def pass_on(pair, **how):
        for flow in pair:
            for far in planes_all:
                flow.pass_on(far, fresh=False, **how)

    def pass_next(pair, wait):
        for flow in pair:
            for far in planes_all:
                flow.pass_next(far, wait)

    def arrived(pair, kind):
        for flow in pair:
            for far in planes_all:
                flow.wait(kind, far)

    def loads(index, slot):
        tp_half = jnp.where(index < blocks, at.tp, 1 - at.tp)
        span = pl.ds(pl.multiple_of(index % blocks * HIDDEN_BLOCK, HIDDEN_BLOCK), HIDDEN_BLOCK)
        return (
            pltpu.make_async_copy(full_e.at[:, tp_half, :, span], e_vm.at[slot], load_sems.at[0, slot]),
            pltpu.make_async_copy(full_r.at[:, tp_half, span, :], r_vm.at[slot], load_sems.at[1, slot]),
        )

    def wo_half(part):
        w = wo_ref[:, part]
        return jnp.concatenate([w[i] for i in range(w.shape[0])], axis=1)

    jd, ed, ou, ru = (pl.ds(i * width, width) for i in range(4))
    od = pl.ds(3 * half, half)

    @pl.when(f == 0)
    def _():
        for load in loads(0, 0):
            load.start()
        at.greet(True, False)
        for flow in flows[3]:
            flow.pass_on(1, fresh=False, z=True, core=True)
            flow.pass_on(0, fresh=False, core=True)
        for flow in flows[1]:
            flow.pass_on(2, fresh=False, tp=True)
            flow.pass_on(3, fresh=False, tp=True)
            flow.pass_next(0, False)
            flow.pass_next(1, False)
        pass_on(flows[2], tp=True)
        w_own, w_other = wo_half(core), wo_half(1 - core)
        for begin in range(0, rows_all, step):
            rows = pl.ds(begin, step)
            own, other = own_ref[rows, :], other_ref[rows, :]
            u2 = (
                dot(own, factors_ref[core, :, od], 1, 1) + dot(other, factors_ref[1 - core, :, od], 1, 1)
            ).astype(B16)
            u2_ref[rows, :] = u2
            h = (
                x_ref[rows, :].astype(F32) + dot(own, w_own) + dot(other, w_other)
                + out_off[...] + dot(u2, shared_ref[:, ou])
            )
            hidden[rows, :] = h
            scaled, _ = row_norm(h)
            xn = (scaled * gain_ref[...] + shift_ref[...]).astype(B16)
            xn_ref[rows, :] = xn
            u3_ref[rows, :] = dot(xn, shared_ref[:, ed], 1, 1).astype(B16)
            g4_ref[rows, :] = dot(cot_ref[rows, :], shared_ref[:, ru], 1, 1).astype(B16)
            total[rows, :] = h + shrink_off[...]
            back[rows, :] = jnp.zeros_like(h)
            u4_sum[rows, :] = jnp.zeros((step, u4_sum.shape[1]), F32)
            g3_sum[rows, :] = jnp.zeros((step, g3_sum.shape[1]), F32)
        for flow in flows[3]:
            flow.pass_on(2, fresh=False, z=True, core=True, wait=True)

    @pl.when(f == 1)
    def _():
        for flow in flows[3]:
            flow.pass_on(3, fresh=False, core=True, wait=True)

    @pl.when(f == 2)
    def _():
        pass_on(flows[3], tp=True)
        arrived(flows[3], OWN_CAME)

    @pl.when(f == 3)
    def _():
        for flow in flows[1]:
            flow.pass_next(2)
            flow.pass_next(3)

    @pl.when(f == 4)
    def _():
        pass_next(flows[2], True)
        arrived(flows[1], NEXT_CAME)

    @pl.when(f == 5)
    def _():
        arrived(flows[2], NEXT_CAME)

    @pl.when(f == last - 1)
    def _():
        pass_next(flows[3], True)

    slot = f % 2

    @pl.when(f < last - 1)
    def _():
        for load in loads(f + 1, 1 - slot):
            load.start()

    for load in loads(f, slot):
        load.wait()
    tp_half = jnp.where(f < blocks, at.tp, 1 - at.tp)
    begin_block = f % blocks * HIDDEN_BLOCK

    def block_of(first):
        return pl.ds(pl.multiple_of(first + begin_block, 128), HIDDEN_BLOCK)

    w_e = e_vm[slot].reshape(width, HIDDEN_BLOCK)
    w_r = jnp.concatenate([r_vm[slot, i] for i in range(2 * planes)], axis=1)
    eu = factors_ref[tp_half, :, block_of(4 * half)]
    rd = factors_ref[tp_half, :, block_of(4 * half + hidden_half)]
    wide_off = offsets_ref[tp_half, :, block_of(3 * half)]
    sum_eu, sum_rd = 0.0, 0.0
    for begin in range(0, rows_all, step):
        rows = pl.ds(begin, step)
        u3, g4 = u3_ref[rows, :], g4_ref[rows, :]
        z = dot(xn_ref[rows, :], w_e) + wide_off + dot(u3, eu)
        gact = dot(cot_ref[rows, :], w_r, 1, 1) + dot(g4, rd)
        cdf, density = gauss_parts(z)
        act = (z * cdf).astype(B16)
        gz = (gact * (cdf + z * density)).astype(B16)
        total[rows, :] += dot(act, w_r)
        u4_sum[rows, :] += dot(act, rd, 1, 1)
        back[rows, :] += dot(gz, w_e, 1, 1)
        g3_sum[rows, :] += dot(gz, eu, 1, 1)
        sum_rd += dot(g4, act, 0, 0)
        sum_eu += dot(u3, gz, 0, 0)
    t_split[tp_half, :, block_of(half + hidden_half)] = sum_rd
    t_split[tp_half, :, block_of(half)] = sum_eu

    @pl.when(f == last - 1)
    def _():
        arrived(flows[3], NEXT_CAME)
        for load in loads(f + 1, 1 - slot):
            load.start()

    @pl.when(f == last)
    def _():
        w_own, w_other = wo_half(core), wo_half(1 - core)
        s_ru, s_ed, s_ou, s_own, s_other = 0.0, 0.0, 0.0, 0.0, 0.0
        moves = []
        for index, begin in enumerate(range(0, rows_all, step)):
            rows = pl.ds(begin, step)
            cot = cot_ref[rows, :]
            u4 = u4_sum[rows, :].astype(B16)
            output_ref[rows, :] = (total[rows, :] + dot(u4, shared_ref[:, ru])).astype(B16)
            s_ru += dot(u4, cot, 0, 0)
            g3 = g3_sum[rows, :].astype(B16)
            s_ed += dot(g3, xn_ref[rows, :], 0, 0)
            gx = back[rows, :] + dot(g3, shared_ref[:, ed])
            scaled, inverse = row_norm(hidden[rows, :])
            gh = cot.astype(F32) + back_norm(gx * gain_ref[...], scaled, inverse)
            gh_ref[rows, :] = gh
            gb = gh.astype(B16)
            s_ou += dot(u2_ref[rows, :], gb, 0, 0)
            g2 = dot(gb, shared_ref[:, ou], 1, 1).astype(B16)
            s_own += dot(g2, own_ref[rows, :], 0, 0)
            s_other += dot(g2, other_ref[rows, :], 0, 0)
            gother_vm[rows, :] = (
                dot(gb, w_other, 1, 1) + dot(g2, factors_ref[1 - core, :, od])
            ).astype(B16)
            there = pltpu.make_async_remote_copy(
                src_ref=gother_vm.at[rows], dst_ref=gatt_out.at[pl.ds(rows_all + begin, step)],
                send_sem=grad_sems.at[0, index], recv_sem=grad_sems.at[1, index],
                device_id=at.next_core, device_id_type=MESH,
            )
            there.start()
            gown_vm[rows, :] = (dot(gb, w_own, 1, 1) + dot(g2, factors_ref[core, :, od])).astype(B16)
            here = pltpu.make_async_copy(gown_vm.at[rows], gatt_out.at[rows], grad_sems.at[2, index])
            here.start()
            moves += [there, here]
        t_full[:, 0:width] = s_ou
        t_full[:, width : 2 * width] = s_ed
        t_full[:, 2 * width :] = s_ru
        t_split[core, :, 0:half] = s_own
        t_split[1 - core, :, 0:half] = s_other
        for index, pair in enumerate(flows[1:]):
            for flow in pair:
                for far in planes_all:
                    flow.sent(far, z=index == 2 and far in (1, 2), tp=index > 0 or far > 1, core=index == 2)
                    flow.sent_next(far)
        for move in moves:
            move.wait()


def middle(
    planes, x, cot, attended, other, w_o, factors, shared, offsets, out_off, gain, shift, shrink_off, w_e, w_r
):
    rows, width = x.shape
    half = attended.shape[1]
    shards_, _, depth, hidden_half = w_e.shape
    rank = factors.shape[1]
    blocks = hidden_half // HIDDEN_BLOCK
    one = lambda shape: pl.BlockSpec(
        shape, lambda f: (0,) * len(shape), pipeline_mode=pl.Buffered(1)
    )
    hbm = pl.BlockSpec(memory_space=pl.ANY)
    shape = jax.ShapeDtypeStruct
    dma = pltpu.SemaphoreType.DMA
    chunks = rows // 256
    return pl.pallas_call(
        functools.partial(middle_body, planes, blocks),
        grid=(2 * blocks,),
        in_specs=[
            one((rows, width)), one((rows, width)), one((rows, half)), one((rows, half)),
            one(w_o.shape), one(factors.shape), one(shared.shape), one(offsets.shape),
            one((1, width)), one((1, width)), one((1, width)), one((1, width)), hbm, hbm,
        ],
        out_specs=[
            one((rows, width)), one((rows, width)),
            one((2, rank, half + 2 * hidden_half)), one((rank, 3 * width)), hbm, hbm, hbm,
        ],
        out_shape=[
            shape((rows, width), B16), shape((rows, width), F32),
            shape((2, rank, half + 2 * hidden_half), F32), shape((rank, 3 * width), F32),
            shape((2 * rows, half), B16), shape(w_e.shape, B16), shape(w_r.shape, B16),
        ],
        input_output_aliases={12: 5, 13: 6},
        scratch_shapes=[
            pltpu.VMEM((rows, width), F32), pltpu.VMEM((rows, width), B16),
            pltpu.VMEM((rows, width), F32), pltpu.VMEM((rows, width), F32),
            pltpu.VMEM((rows, rank), B16), pltpu.VMEM((rows, rank), B16),
            pltpu.VMEM((rows, rank), F32), pltpu.VMEM((rows, rank), B16),
            pltpu.VMEM((rows, rank), F32),
            pltpu.VMEM((2, shards_, depth, HIDDEN_BLOCK), B16),
            pltpu.VMEM((2, shards_, HIDDEN_BLOCK, w_r.shape[3]), B16),
            pltpu.VMEM((rows, half), B16), pltpu.VMEM((rows, half), B16),
            dma((2, 2)), dma((count_rows((), MIDDLE_KINDS), planes)), dma((3, chunks)),
        ],
        compiler_params=pltpu.CompilerParams(
            vmem_limit_bytes=VMEM_LIMIT, collective_id=2, has_side_effects=True
        ),
        cost_estimate=pl.CostEstimate(
            flops=2 * rows * width * (16 * hidden_half // 2 + 4 * half),
            bytes_accessed=40 * 2**20,
            transcendentals=rows * hidden_half * 2,
        ),
    )(x, cot, attended, other, w_o, factors, shared, offsets, out_off, gain, shift, shrink_off, w_e, w_r)


def unproject_body(
    planes,
    x_ref, gh_ref, xn_ref, u_ref, gain_ref, w_ref, factors_ref, shared_ref, own_ref, other_ref,
    home_ref, sums_ref,
    own_vm, other_vm, w_vm, x_vm, gh_vm, xn_vm, stage, split, full, g1_vm, load_sems, move_sems, *spread_refs,
):
    at = Place(planes)
    rows_all, width = x_vm.shape
    half = own_vm.shape[2]
    core = at.core
    spread = Spread(at, split, full, shared_ref[0:8, 4 * width :], sums_ref, *spread_refs)
    halves = ((own_vm, core), (other_vm, 1 - core))
    chunks = rows_all // ROWS

    def load(index, source, target):
        return pltpu.make_async_copy(source, target, load_sems.at[index])

    loads = [load(0, own_ref, own_vm), load(1, other_ref, other_vm), load(2, xn_ref, xn_vm)]
    late = [load(3, x_ref, x_vm), load(4, gh_ref, gh_vm)]
    late += [load(5 + order, w_ref.at[:, owner], w_vm.at[order]) for order, (_, owner) in enumerate(halves)]
    for item in loads + late:
        item.start()
    at.greet(True, True, True, True)
    for item in loads:
        item.wait()
    u = u_ref[...]
    g1 = 0.0
    for source, owner in halves:
        for part in range(3):
            columns = pl.ds(part * half, half)
            g1 += dot(source[part], factors_ref[owner, :, columns], 1, 1)
            split[owner, :, columns] = dot(u, source[part], 0, 0)
    g1 = g1.astype(B16)
    g1_vm[...] = g1
    full[...] = dot(g1, xn_vm[...], 0, 0)
    spread.start()
    order = [2, 0, 3, 1]
    for item in late:
        item.wait()
    quarter = rows_all // 2

    def moves(i):
        tp_half = i * ROWS // quarter
        rows = pl.ds(i * ROWS % quarter, ROWS)
        source, target = stage.at[i], home_ref.at[at.tp, rows]

        def remote(device, came):
            return pltpu.make_async_remote_copy(
                src_ref=source, dst_ref=target, send_sem=move_sems.at[0, i], recv_sem=move_sems.at[came, i],
                device_id=device, device_id_type=MESH,
            )

        mine = at.tp == tp_half
        both = dict(at.turned)
        both["tp"] = 1 - at.tp
        return (
            (mine & jnp.logical_not(at.crosses), lambda: pltpu.make_async_copy(source, target, move_sems.at[0, i]), True),
            (mine & at.crosses, lambda: remote(at.turned, 1), False),
            (jnp.logical_not(mine) & jnp.logical_not(at.crosses), lambda: remote(at.next_tp, 2), False),
            (jnp.logical_not(mine) & at.crosses, lambda: remote(both, 2), False),
        )

    stages = [spread.second, spread.third, lambda: spread.planes(0), lambda: spread.planes(1)]
    for count, i in enumerate(order):
        span = pl.ds(i * ROWS, ROWS)
        gx = dot(g1_vm[span, :], shared_ref[:, 0:width])
        for index, (source, _) in enumerate(halves):
            for part in range(3):
                gx += dot(source[part, span, :], w_vm[index, :, part].reshape(width, half), 1, 1)
        scaled, inverse = row_norm(x_vm[span, :].astype(F32))
        stage[i] = (gh_vm[span, :] + back_norm(gx * gain_ref[...], scaled, inverse)).astype(B16)
        for there, move, _ in moves(i):
            pl.when(there)(lambda move=move: move().start())
        stages[count]()
    for distance in range(2, planes):
        spread.planes(distance)
    spread.finish()
    spread.sent()
    for i in range(chunks):
        for there, move, here in moves(i):
            if here:
                pl.when(there)(lambda move=move: move().wait())
            else:
                pl.when(there)(lambda move=move: move().wait_send())
    for i in range(chunks):
        tp_half = i * ROWS // quarter
        rows = pl.ds(i * ROWS % quarter, ROWS)

        def came(slot):
            return pltpu.make_async_remote_copy(
                src_ref=stage.at[i], dst_ref=home_ref.at[slot, rows], send_sem=move_sems.at[0, i],
                recv_sem=move_sems.at[1, i], device_id=at.next_tp, device_id_type=MESH,
            )

        pl.when((at.tp == tp_half) & at.crosses)(lambda came=came: came(at.tp).wait_recv())

    for i in range(chunks):
        tp_half = i * ROWS // quarter
        rows = pl.ds(i * ROWS % quarter, ROWS)

        def came(slot):
            return pltpu.make_async_remote_copy(
                src_ref=stage.at[i], dst_ref=home_ref.at[slot, rows], send_sem=move_sems.at[0, i],
                recv_sem=move_sems.at[2, i], device_id=at.next_tp, device_id_type=MESH,
            )

        pl.when(at.tp == tp_half)(lambda came=came: came(1 - at.tp).wait_recv())


def unproject(planes, x, gh, xn, u, gain, weight, factors, shared, own, other, adapters):
    rows, width = x.shape
    half = own.shape[2]
    rank = factors.shape[1]
    hbm = pl.BlockSpec(memory_space=pl.ANY)
    vmem = pl.BlockSpec(memory_space=pltpu.VMEM)
    shape = jax.ShapeDtypeStruct
    dma = pltpu.SemaphoreType.DMA
    chunks = rows // ROWS
    keep = 3 * half + width
    return pl.pallas_call(
        functools.partial(unproject_body, planes),
        in_specs=[hbm, hbm, hbm, vmem, vmem, hbm, vmem, vmem, hbm, hbm],
        out_specs=[hbm, vmem],
        out_shape=[shape((2, rows // 2, width), B16), shape((adapters, rank, keep), F32)],
        scratch_shapes=[
            pltpu.VMEM(own.shape, B16), pltpu.VMEM(own.shape, B16),
            pltpu.VMEM((2, weight.shape[0]) + weight.shape[2:], B16),
            pltpu.VMEM((rows, width), B16), pltpu.VMEM((rows, width), F32), pltpu.VMEM((rows, width), B16),
            pltpu.VMEM((chunks, ROWS, width), B16),
            pltpu.VMEM((2, rank, 3 * half), F32), pltpu.VMEM((rank, width), F32), pltpu.VMEM((rows, rank), B16),
            dma((7,)), dma((3, chunks)),
        ]
        + Spread.scratch(planes, rank // 2, 3 * half, width),
        compiler_params=pltpu.CompilerParams(
            vmem_limit_bytes=VMEM_LIMIT, collective_id=4, has_side_effects=True
        ),
        cost_estimate=pl.CostEstimate(
            flops=2 * rows * width * 6 * half, bytes_accessed=20 * 2**20, transcendentals=0
        ),
    )(x, gh, xn, u, gain, weight, factors, shared, own, other)


def clip_shards(
    planes,
    tokens,
    cotangent,
    adapter_pick,
    positions,
    first_gain,
    first_shift,
    joined_weight,
    joined_bias,
    output_weight,
    mixing_exit_offset,
    second_gain,
    second_shift,
    expand_weight,
    widening_offset,
    reduce_weight,
    shrinking_offset,
    joined_down,
    joined_up,
    output_down,
    output_up,
    expand_down,
    expand_up,
    reduce_down,
    reduce_up,
):
    tp = lax.axis_index("tp")
    mine_of = lambda array, axis=0: lax.dynamic_index_in_dim(array, tp, axis, keepdims=False)
    half = joined_weight.shape[2]
    hidden_half = expand_weight.shape[1]
    rank = joined_up.shape[1]
    rows = tokens.shape[1]

    pick = lax.dynamic_index_in_dim(adapter_pick, tp, 0, keepdims=False)
    pick_next = lax.dynamic_index_in_dim(adapter_pick, 1 - tp, 0, keepdims=False)

    def row(table, at):
        return lax.dynamic_index_in_dim(table, at, 0, keepdims=False)

    def split_factors(at):
        ju, od, eu, rd = row(joined_up, at), row(output_down, at), row(expand_up, at), row(reduce_down, at)
        return jnp.concatenate([ju.reshape(ju.shape[0], -1), od.T, eu, rd.T], axis=1)

    shared = jnp.concatenate(
        [
            row(joined_down, pick).T, row(expand_down, pick).T, row(output_up, pick), row(reduce_up, pick),
            jnp.full((rank, 128), pick.astype(B16)),
        ],
        axis=1,
    )
    offsets = jnp.concatenate([joined_bias.reshape(-1), widening_offset])[None]

    lane = jnp.arange(128, dtype=jnp.int32) % 64
    rates = jnp.exp((lane % 10).astype(F32) * (-math.log(10000.0) / 10.0))
    rates = jnp.where(lane[None] // 20 == jnp.arange(3)[:, None], rates[None], 0.0)
    high = lax.reduce_precision(rates, 8, 7)
    mid = lax.reduce_precision(rates - high, 8, 7)
    low = lax.reduce_precision(rates - high - mid, 8, 7)
    rates = jnp.concatenate([high, mid, low, jnp.zeros((7, 128), F32)], axis=0).astype(B16)
    spots = mine_of(positions, 1).astype(B16)
    spots = jnp.concatenate([spots, spots, spots, jnp.zeros((7, rows), B16)], axis=0)

    (
        x, factors, shared, offsets, w_j, w_o, w_e, w_r, query, key, value, xn1, u1, cosine, sine,
    ) = project(
        planes, tokens, spots, split_factors(pick), split_factors(pick_next), shared, offsets,
        jnp.transpose(joined_weight, (1, 0, 2)), output_weight, expand_weight, reduce_weight,
        first_gain[None], first_shift[None], rates,
    )
    attended, inverse, weights, other_heads, cot, w_o, w_e, w_r = attend(
        planes, query, key, value, cotangent, output_weight, expand_weight, reduce_weight, w_o, w_e, w_r
    )
    out, gh, split, full, grad_att, w_e, w_r = middle(
        planes, x, cot, attended, other_heads, w_o, factors, shared, offsets,
        mixing_exit_offset[None], second_gain[None], second_shift[None], shrinking_offset[None], w_e, w_r,
    )
    adapters = joined_down.shape[0]
    width = tokens.shape[2]
    tag = shared[: rank // 2, 4 * width :]
    own, other, sums, output = attend_back(
        planes, query, key, value, attended, inverse, grad_att, weights, cosine, sine, split, full, tag, out, adapters
    )
    tokens_grad, late_sums = unproject(
        planes, x, gh, xn1, u1, first_gain[None], w_j, factors, shared, own, other, adapters
    )

    def cut(array, *sizes):
        begin, pieces = 0, []
        for size in sizes:
            pieces.append(array[:, :, begin : begin + size])
            begin += size
        return pieces

    s_od, s_eu, s_rd, s_ou, s_ed, s_ru = cut(sums, half, hidden_half, hidden_half, width, width, width)
    s_fu, s_fd = cut(late_sums, 3 * half, width)
    turn_last = lambda array: jnp.swapaxes(array, 1, 2)
    return (
        output,
        tokens_grad,
        turn_last(s_fd),
        s_fu.reshape(adapters, rank, 3, half),
        turn_last(s_od),
        s_ou,
        turn_last(s_ed),
        s_eu,
        turn_last(s_rd),
        s_ru,
    )


def solution(mesh):
    sizes = dict(mesh.shape)
    if sizes["ctx"] == 2 and sizes["tp"] == 2 and sizes["shard"] == 8:
        body = functools.partial(clip_shards, sizes["shard"] // 2)
    else:
        body = general_shards
    return jax.shard_map(
        body,
        mesh=mesh,
        in_specs=(
            P("shard", "ctx", None),
            P("shard", "ctx", None),
            P("shard"),
            P(None, "shard", "ctx"),
            P(),
            P(),
            P("shard", None, "tp"),
            P(None, "tp"),
            P("tp", "shard"),
            P(),
            P(),
            P(),
            P("shard", "tp"),
            P("tp"),
            P("tp", "shard"),
            P(),
            P(),
            P(None, None, None, "tp"),
            P(None, "tp", None),
            P(),
            P(),
            P(None, None, "tp"),
            P(None, "tp", None),
            P(),
        ),
        out_specs=(
            P("shard", "ctx", None),
            P("shard", ("ctx", "tp"), None),
            P(),
            P(None, None, None, "tp"),
            P(None, "tp", None),
            P(),
            P(),
            P(None, None, "tp"),
            P(None, "tp", None),
            P(),
        ),
        check_vma=False,
    )
```

```python
import functools
import math

import jax
import jax.numpy as jnp
import ml_dtypes
import numpy as np
from jax import lax
from jax.experimental import pallas as pl
from jax.experimental.pallas import tpu as pltpu
from jax.sharding import PartitionSpec as P

eps_norm = 1e-06
score_scale = 0.125


def rope_tables(places):
    band = jnp.arange(10, dtype=jnp.float32)
    rates = jnp.exp(band * (-math.log(10000.0) / 10.0))
    angle = places.astype(jnp.float32)[..., None] * rates
    cos_parts = []
    sin_parts = []
    for band_index in range(3):
        cosine = jnp.cos(angle[band_index])
        sine = jnp.sin(angle[band_index])
        cos_parts = cos_parts + [cosine, cosine]
        sin_parts = sin_parts + [-sine, sine]
    rest_shape = angle.shape[1:-1] + (4,)
    cos_parts.append(jnp.ones(rest_shape, jnp.float32))
    sin_parts.append(jnp.zeros(rest_shape, jnp.float32))
    return (jnp.concatenate(cos_parts, -1), jnp.concatenate(sin_parts, -1))


def swap_pairs(values):
    leading = values.shape[:-1]
    turned = values[..., :60].reshape(leading + (3, 2, 10))[..., ::-1, :].reshape(leading + (60,))
    return jnp.concatenate([turned, values[..., 60:]], -1)


def rotate(values, cosine, sine):
    return values * cosine[..., None, :] + swap_pairs(values) * sine[..., None, :]


def rotate_back(grads, cosine, sine):
    return grads * cosine[..., None, :] + swap_pairs(grads * sine[..., None, :])


def norm_forward(values, gain, shift):
    centred = values - jnp.mean(values, -1, keepdims=True)
    inverse = lax.rsqrt(jnp.mean(centred * centred, -1, keepdims=True) + eps_norm)
    scaled = centred * inverse
    return (scaled * gain + shift, scaled, inverse)


def norm_back(grads, scaled, inverse, gain):
    weighted = grads * gain
    return inverse * (
        weighted
        - jnp.mean(weighted, -1, keepdims=True)
        - scaled * jnp.mean(weighted * scaled, -1, keepdims=True)
    )


def select_factor(choose, table):
    return jnp.einsum("ca,a...->c...", choose, table, preferred_element_type=jnp.float32).astype(
        jnp.bfloat16
    )


def gelu_exact(values):
    return jax.nn.gelu(values, approximate=False)


def matrix_product(form, left, right):
    return jnp.einsum(form, left, right, preferred_element_type=jnp.float32)


def general_shards(
    tokens,
    cotangent,
    adapter_pick,
    positions,
    first_gain,
    first_shift,
    joined_weight,
    joined_bias,
    output_weight,
    mixing_exit_offset,
    second_gain,
    second_shift,
    expand_weight,
    widening_offset,
    reduce_weight,
    shrinking_offset,
    joined_down,
    joined_up,
    output_down,
    output_up,
    expand_down,
    expand_up,
    reduce_down,
    reduce_up,
):
    whole_joined, whole_output, whole_expand, whole_reduce = (
        lax.all_gather(joined_weight, "shard", axis=0, tiled=True),
        lax.all_gather(output_weight, "shard", axis=1, tiled=True),
        lax.all_gather(expand_weight, "shard", axis=0, tiled=True),
        lax.all_gather(reduce_weight, "shard", axis=1, tiled=True),
    )
    clip_count, local_len, width = tokens.shape
    local_width = whole_joined.shape[2]
    head_count = local_width // 64
    choose = (
        adapter_pick[:, None] == jnp.arange(joined_down.shape[0], dtype=jnp.int32)[None, :]
    ).astype(jnp.bfloat16)
    select_joined_down = select_factor(choose, joined_down)
    select_joined_up = select_factor(choose, joined_up)
    select_output_down = select_factor(choose, output_down)
    select_output_up = select_factor(choose, output_up)
    select_expand_down = select_factor(choose, expand_down)
    select_expand_up = select_factor(choose, expand_up)
    select_reduce_down = select_factor(choose, reduce_down)
    select_reduce_up = select_factor(choose, reduce_up)
    cosine, sine = rope_tables(positions)
    block_arguments = tokens.astype(jnp.float32)
    norm_one, scaled_one, inverse_one = norm_forward(block_arguments, first_gain, first_shift)
    initial_standardized = norm_one.astype(jnp.bfloat16)
    initial_slim_derivative = matrix_product(
        "zgh,zhe->zge", initial_standardized, select_joined_down
    ).astype(jnp.bfloat16)
    mapped_vectors = (
        matrix_product("cld,dje->clje", initial_standardized, whole_joined)
        + joined_bias
        + matrix_product("uip,upqg->uiqg", initial_slim_derivative, select_joined_up)
    )
    head_shape = (clip_count, local_len, head_count, 64)
    query = rotate(mapped_vectors[:, :, 0].reshape(head_shape), cosine, sine).astype(jnp.bfloat16)
    keys = rotate(mapped_vectors[:, :, 1].reshape(head_shape), cosine, sine).astype(jnp.bfloat16)
    values = mapped_vectors[:, :, 2].reshape(head_shape).astype(jnp.bfloat16)
    stats_shape = (clip_count, head_count, local_len)
    run_max = jnp.full(stats_shape, -1e30, jnp.float32)
    key_part = lax.all_gather(keys, "ctx", axis=1, tiled=True)
    value_part = lax.all_gather(values, "ctx", axis=1, tiled=True)
    scores = matrix_product("cqhd,ckhd->chqk", query, key_part) * score_scale
    new_max = jnp.maximum(run_max, jnp.max(scores, -1))
    weights = jnp.exp(scores - new_max[..., None])
    run_total = jnp.sum(weights, -1)
    update = matrix_product("chqk,ckhd->cqhd", weights.astype(jnp.bfloat16), value_part)
    accum = update
    run_max, run_total, accum = (new_max, run_total, accum)
    log_total = run_max + jnp.log(run_total)
    attended_full = accum / jnp.transpose(run_total, (0, 2, 1))[..., None]
    mixing_outcome = attended_full.reshape(clip_count, local_len, local_width).astype(jnp.bfloat16)
    out_part = matrix_product("cle,ed->cld", mixing_outcome, whole_output)
    rank_partial = matrix_product("fig,fgt->fit", mixing_outcome, select_output_down)
    output_total, rank_sum = (
        lax.psum(out_part.astype(jnp.bfloat16), "tp").astype(jnp.float32),
        lax.psum(rank_partial.astype(jnp.bfloat16), "tp").astype(jnp.float32),
    )
    middle_slim_derivative = rank_sum.astype(jnp.bfloat16)
    first_hidden = (
        block_arguments
        + output_total
        + mixing_exit_offset
        + matrix_product("wnk,wke->wne", middle_slim_derivative, select_output_up)
    )
    norm_two, scaled_two, inverse_two = norm_forward(first_hidden, second_gain, second_shift)
    latter_standardized = norm_two.astype(jnp.bfloat16)
    penultimate_slim_derivative = matrix_product(
        "zgh,zhe->zge", latter_standardized, select_expand_down
    ).astype(jnp.bfloat16)
    skip_stream_vectors = (
        matrix_product("cld,df->clf", latter_standardized, whole_expand)
        + widening_offset
        + matrix_product("uqz,uze->uqe", penultimate_slim_derivative, select_expand_up)
    )
    activity, gelu_pull = jax.vjp(gelu_exact, skip_stream_vectors)
    gaussian_error_unit = activity.astype(jnp.bfloat16)
    mlp_part = matrix_product("clf,fd->cld", gaussian_error_unit, whole_reduce)
    fourth_rank_partial = matrix_product("xpv,xvy->xpy", gaussian_error_unit, select_reduce_down)
    feedforward_sum, rank_four_sum = (
        lax.psum(mlp_part.astype(jnp.bfloat16), "tp").astype(jnp.float32),
        lax.psum(fourth_rank_partial.astype(jnp.bfloat16), "tp").astype(jnp.float32),
    )
    closing_slim_derivative = rank_four_sum.astype(jnp.bfloat16)
    output = (
        first_hidden
        + feedforward_sum
        + shrinking_offset
        + matrix_product("wnk,wke->wne", closing_slim_derivative, select_reduce_up)
    ).astype(jnp.bfloat16)
    back_joined, back_output, back_expand, back_reduce = (
        lax.all_gather(joined_weight, "shard", axis=0, tiled=True),
        lax.all_gather(output_weight, "shard", axis=1, tiled=True),
        lax.all_gather(expand_weight, "shard", axis=0, tiled=True),
        lax.all_gather(reduce_weight, "shard", axis=1, tiled=True),
    )
    reduce_up_term = matrix_product("vkn,vkm->vnm", closing_slim_derivative, cotangent)
    gradient_fourth = matrix_product("abj,awj->abw", cotangent, select_reduce_up).astype(
        jnp.bfloat16
    )
    reduce_down_term = matrix_product("mpg,mpu->mgu", gaussian_error_unit, gradient_fourth)
    grad_active = matrix_product("cld,fd->clf", cotangent, back_reduce) + matrix_product(
        "gez,guz->geu", gradient_fourth, select_reduce_down
    )
    residual_gradient = gelu_pull(grad_active)[0].astype(jnp.bfloat16)
    expand_up_term = matrix_product("jge,jgn->jen", penultimate_slim_derivative, residual_gradient)
    grad_norm_part = matrix_product("clf,df->cld", residual_gradient, back_expand)
    third_gradient_part = matrix_product("aik,adk->aid", residual_gradient, select_expand_up)
    norm_gradient_sum, grad_three_sum = (
        lax.psum(grad_norm_part.astype(jnp.bfloat16), "tp").astype(jnp.float32),
        lax.psum(third_gradient_part.astype(jnp.bfloat16), "tp").astype(jnp.float32),
    )
    gradient_third = grad_three_sum.astype(jnp.bfloat16)
    expand_down_term = matrix_product("kgt,kgh->kth", latter_standardized, gradient_third)
    second_norm_gradient = norm_gradient_sum + matrix_product(
        "jqt,jit->jqi", gradient_third, select_expand_down
    )
    grad_hidden = cotangent.astype(jnp.float32) + norm_back(
        second_norm_gradient, scaled_two, inverse_two, second_gain
    )
    branch_gradient = grad_hidden.astype(jnp.bfloat16)
    output_up_term = matrix_product("vkn,vkm->vnm", middle_slim_derivative, branch_gradient)
    gradient_second = matrix_product("abj,awj->abw", branch_gradient, select_output_up).astype(
        jnp.bfloat16
    )
    output_down_term = matrix_product("nua,nui->nai", mixing_outcome, gradient_second)
    grad_attended = (
        (
            matrix_product("cld,ed->cle", branch_gradient, back_output)
            + matrix_product("gsq,ghq->gsh", gradient_second, select_output_down)
        )
        .astype(jnp.bfloat16)
        .reshape(head_shape)
    )
    key_whole, value_whole = (
        lax.all_gather(keys, "ctx", axis=1, tiled=True),
        lax.all_gather(values, "ctx", axis=1, tiled=True),
    )
    flat_shape = (clip_count, local_len, local_width)

    def clip_back(items):
        query_clip, key_clip, value_clip, grad_clip, total_clip = items
        scores = matrix_product("qhd,khd->hqk", query_clip, key_clip) * score_scale
        probs = jnp.exp(scores - total_clip[..., None])
        grad_probs = matrix_product("qhd,khd->hqk", grad_clip, value_clip)
        middle = jnp.sum(probs * grad_probs, -1, keepdims=True)
        grad_scores = (probs * (grad_probs - middle)).astype(jnp.bfloat16)
        grad_query = matrix_product("hqk,khd->qhd", grad_scores, key_clip) * score_scale
        grad_key = matrix_product("hqk,qhd->khd", grad_scores, query_clip) * score_scale
        grad_value = matrix_product("hqk,qhd->khd", probs.astype(jnp.bfloat16), grad_clip)
        return (grad_query, grad_key, grad_value)

    grad_query, key_terms, value_terms = lax.map(
        clip_back, (query, key_whole, value_whole, grad_attended, log_total)
    )
    full_len = key_whole.shape[1]
    key_sum, value_sum = (
        lax.psum_scatter(
            key_terms.reshape(clip_count, full_len, local_width).astype(jnp.bfloat16),
            "ctx",
            scatter_dimension=1,
            tiled=True,
        ).astype(jnp.float32),
        lax.psum_scatter(
            value_terms.reshape(clip_count, full_len, local_width).astype(jnp.bfloat16),
            "ctx",
            scatter_dimension=1,
            tiled=True,
        ).astype(jnp.float32),
    )
    query_key_value_gradient = jnp.stack(
        [
            rotate_back(grad_query, cosine, sine).reshape(flat_shape),
            rotate_back(key_sum.reshape(head_shape), cosine, sine).reshape(flat_shape),
            value_sum,
        ],
        axis=2,
    ).astype(jnp.bfloat16)
    joined_up_term = matrix_product(
        "pvh,pvfo->phfo", initial_slim_derivative, query_key_value_gradient
    )
    first_gradient_part = matrix_product(
        "kxsd,ktsd->kxt", query_key_value_gradient, select_joined_up
    )
    grad_norm_one_part = matrix_product("clje,dje->cld", query_key_value_gradient, back_joined)
    gradient_first = lax.psum(first_gradient_part.astype(jnp.bfloat16), "tp")
    grad_norm_share = lax.psum_scatter(
        grad_norm_one_part.astype(jnp.bfloat16), "tp", scatter_dimension=1, tiled=True
    ).astype(jnp.float32)
    joined_down_term = matrix_product("kgt,kgh->kth", initial_standardized, gradient_first)
    half_len = grad_norm_share.shape[1]
    begin = lax.axis_index("tp") * half_len

    def shared_rows(array):
        return lax.dynamic_slice_in_dim(array, begin, half_len, 1)

    grad_norm_one = grad_norm_share + matrix_product(
        "jqt,jit->jqi", shared_rows(gradient_first), select_joined_down
    )
    tokens_grad = (
        shared_rows(grad_hidden)
        + norm_back(grad_norm_one, shared_rows(scaled_one), shared_rows(inverse_one), first_gain)
    ).astype(jnp.bfloat16)
    choose_full = choose.astype(jnp.float32)

    def by_adapter(term):
        return jnp.einsum(
            "ca,c...->a...",
            choose_full,
            term,
            precision=lax.Precision.HIGHEST,
            preferred_element_type=jnp.float32,
        )

    summed = lax.psum(
        (
            by_adapter(joined_down_term),
            by_adapter(joined_up_term),
            by_adapter(output_down_term),
            by_adapter(output_up_term),
            by_adapter(expand_down_term),
            by_adapter(expand_up_term),
            by_adapter(reduce_down_term),
            by_adapter(reduce_up_term),
        ),
        ("shard", "ctx"),
    )
    return (
        output,
        tokens_grad,
        summed[0],
        summed[1],
        summed[2],
        summed[3],
        summed[4],
        summed[5],
        summed[6],
        summed[7],
    )


B16 = jnp.bfloat16
F32 = jnp.float32
VMEM_LIMIT = 60 * 2**20
exp_scale = score_scale * math.log2(math.e)


def dot(left, right, left_dim=1, right_dim=0):
    return lax.dot_general(
        left, right, (((left_dim,), (right_dim,)), ((), ())), preferred_element_type=F32
    )


def params():
    return pltpu.CompilerParams(vmem_limit_bytes=VMEM_LIMIT)


def low_lanes():
    return lax.broadcasted_iota(jnp.int32, (1, 128), 1) < 64


def partner(values):
    lane = lax.broadcasted_iota(jnp.int32, (1, 128), 1) % 64 % 20
    return jnp.where(lane < 10, pltpu.roll(values, 118, 1), pltpu.roll(values, 10, 1))


def row_norm(values):
    centred = values - jnp.mean(values, -1, keepdims=True)
    inverse = lax.rsqrt(jnp.mean(centred * centred, -1, keepdims=True) + eps_norm)
    return centred * inverse, inverse


def back_norm(weighted, scaled, inverse):
    return inverse * (
        weighted
        - jnp.mean(weighted, -1, keepdims=True)
        - scaled * jnp.mean(weighted * scaled, -1, keepdims=True)
    )


MESH = pl.DeviceIdType.MESH
HIDDEN_BLOCK = 512
(UP_SENT, DOWN_SENT, Z_CAME, TP_SENT, TP_CAME, OWN_SENT, OWN_CAME, NEXT_SENT, NEXT_CAME) = range(9)


class Place:
    def __init__(self, planes):
        self.planes = planes
        self.shard = lax.axis_index("shard")
        self.z = self.shard // 2
        self.core = self.shard % 2
        self.ctx = lax.axis_index("ctx")
        self.tp = lax.axis_index("tp")
        self.has_up = self.z < planes - 1
        self.has_down = self.z > 0
        self.crosses = self.core != self.ctx
        self.up = {"shard": self.shard + 2}
        self.down = {"shard": self.shard - 2}
        self.next_tp = {"tp": 1 - self.tp}
        self.next_core = {"shard": 2 * self.z + 1 - self.core}
        self.turned = {"shard": 2 * self.z + self.ctx, "ctx": self.core}

    def greet(self, planes_too, turned, ctx_too=False, flipped=False):
        barrier = pltpu.get_barrier_semaphore()
        count = 2

        def signal(device):
            pl.semaphore_signal(barrier, inc=1, device_id=device, device_id_type=MESH)

        signal(self.next_tp)
        signal(self.next_core)
        if planes_too:
            pl.when(self.has_up)(lambda: signal(self.up))
            pl.when(self.has_down)(lambda: signal(self.down))
            count = count + self.has_up.astype(jnp.int32) + self.has_down.astype(jnp.int32)
        if turned:
            pl.when(self.crosses)(lambda: signal(self.turned))
            count = count + self.crosses.astype(jnp.int32)
        if ctx_too:
            signal({"ctx": 1 - self.ctx})
            count = count + 1
        if flipped:
            flip = dict(self.turned)
            flip["tp"] = 1 - self.tp
            pl.when(self.crosses)(lambda: signal(flip))
            count = count + self.crosses.astype(jnp.int32)
        pl.semaphore_wait(barrier, count)


class Flow:
    def __init__(self, at, own, slot, sems, kinds=tuple(range(9))):
        self.at, self.own, self.slot = at, own, slot
        self.sems = {kind: sems[i] for i, kind in enumerate(kinds)}

    def copy(self, kind, plane, own=False):
        at = self.at
        half = 1 - at.tp if kind == NEXT_SENT else at.tp
        piece = self.slot(2 * plane + at.core, half)
        device, came = {
            UP_SENT: (at.up, Z_CAME),
            DOWN_SENT: (at.down, Z_CAME),
            TP_SENT: (at.next_tp, TP_CAME),
            OWN_SENT: (at.next_core, OWN_CAME),
            NEXT_SENT: (at.next_core, NEXT_CAME),
        }[kind]
        return pltpu.make_async_remote_copy(
            src_ref=self.own if own else piece,
            dst_ref=piece,
            send_sem=self.sems[kind].at[plane],
            recv_sem=self.sems[came].at[plane],
            device_id=device,
            device_id_type=MESH,
        )

    def came(self, kind, plane):
        at = self.at
        shard = 2 * plane + (at.core if kind in (Z_CAME, TP_CAME) else 1 - at.core)
        half = at.tp if kind in (Z_CAME, OWN_CAME) else 1 - at.tp
        piece = self.slot(shard, half)
        return pltpu.make_async_remote_copy(
            src_ref=piece, dst_ref=piece, send_sem=self.sems[kind].at[plane],
            recv_sem=self.sems[kind].at[plane], device_id=at.next_core, device_id_type=MESH,
        )

    def pieces(self, distance):
        at = self.at
        if distance == 0:
            return [(None, at.z, True, True)]
        return [
            (at.z >= distance, at.z - distance, True, False),
            (at.z < at.planes - distance, at.z + distance, False, True),
        ]

    def each(self, distance, act):
        for there, plane, below, above in self.pieces(distance):
            if there is None:
                act(plane, below, above)
            else:
                pl.when(there)(functools.partial(act, plane, below, above))

    def pass_on(self, distance, z=False, tp=False, core=False, fresh=None, wait=False):
        own = (distance == 0) if fresh is None else fresh

        def act(plane, below, above):
            if wait:
                self.came(Z_CAME, plane).wait_recv()
            if z:
                if below:
                    pl.when(self.at.has_up)(lambda: self.copy(UP_SENT, plane, own).start())
                if above:
                    pl.when(self.at.has_down)(lambda: self.copy(DOWN_SENT, plane, own).start())
            if tp:
                self.copy(TP_SENT, plane, own).start()
            if core:
                self.copy(OWN_SENT, plane, own).start()

        self.each(distance, act)

    def sent(self, distance, z=False, tp=False, core=False):
        def act(plane, below, above):
            if z:
                if below:
                    pl.when(self.at.has_up)(lambda: self.copy(UP_SENT, plane).wait_send())
                if above:
                    pl.when(self.at.has_down)(lambda: self.copy(DOWN_SENT, plane).wait_send())
            if tp:
                self.copy(TP_SENT, plane).wait_send()
            if core:
                self.copy(OWN_SENT, plane).wait_send()

        self.each(distance, act)

    def wait(self, kind, distance):
        self.each(distance, lambda plane, below, above: self.came(kind, plane).wait_recv())

    def pass_next(self, distance, wait=True):
        def act(plane, below, above):
            if wait:
                self.came(TP_CAME, plane).wait_recv()
            self.copy(NEXT_SENT, plane).start()

        self.each(distance, act)

    def sent_next(self, distance):
        self.each(distance, lambda plane, below, above: self.copy(NEXT_SENT, plane).wait_send())


ALONG_Z = (UP_SENT, DOWN_SENT, Z_CAME)
TO_TP = (TP_SENT, TP_CAME)
TO_CORE = (OWN_SENT, OWN_CAME)
TO_NEXT = (NEXT_SENT, NEXT_CAME)
EVERY = ALONG_Z + TO_TP + TO_CORE + TO_NEXT


class Rows:
    def __init__(self, sems):
        self.sems, self.used = sems, 0

    def take(self, kinds):
        rows = [self.sems.at[self.used + i] for i in range(len(kinds))]
        self.used += len(kinds)
        return rows


def block_flows(at, own_e, own_r, full_e, full_r, rows, kinds):
    flows = []
    for block, needs in enumerate(kinds):
        span = pl.ds(block * HIDDEN_BLOCK, HIDDEN_BLOCK)
        flows.append(
            [
                Flow(
                    at, None if own_e is None else own_e.at[:, span],
                    lambda s, h, span=span: full_e.at[s, h, :, span], rows.take(needs), needs,
                ),
                Flow(
                    at, None if own_r is None else own_r.at[span, :],
                    lambda s, h, span=span: full_r.at[s, h, span, :], rows.take(needs), needs,
                ),
            ]
        )
    return flows


def count_rows(first, kinds):
    return len(first) + 2 * sum(len(needs) for needs in kinds)


PROJECT_KINDS = (ALONG_Z, ALONG_Z)
ATTEND_KINDS = (EVERY, ALONG_Z + TO_TP + TO_CORE, ALONG_Z + TO_CORE, ALONG_Z)
MIDDLE_KINDS = ((), TO_TP + TO_NEXT, TO_TP + TO_NEXT, EVERY)


def turned_copy(at, source, target, sems):
    return pltpu.make_async_remote_copy(
        src_ref=source, dst_ref=target, send_sem=sems.at[0], recv_sem=sems.at[1],
        device_id=at.turned, device_id_type=MESH,
    )


class Spread:
    def __init__(self, at, split, full, tag, sums, give, take, pass_tp, stack, beyond, sems):
        self.at, self.split, self.full, self.tag, self.sums = at, split, full, tag, sums
        self.give, self.take, self.pass_tp, self.stack, self.beyond, self.sems = (
            give, take, pass_tp, stack, beyond, sems,
        )
        self.ranks = give.shape[0]
        self.width = split.shape[2]
        self.rest = full.shape[1]

    def remote(self, source, target, index, device):
        return pltpu.make_async_remote_copy(
            src_ref=source, dst_ref=target, send_sem=self.sems.at[0, index], recv_sem=self.sems.at[1, index],
            device_id=device, device_id_type=MESH,
        )

    def between_cores(self):
        return self.remote(self.give, self.take, 0, self.at.next_core)

    def to_tp(self):
        return self.remote(self.pass_tp, self.stack.at[self.at.z, 1], 1, self.at.next_tp)

    def to_ctx(self):
        plane = self.stack.at[self.at.z]
        return self.remote(plane.at[pl.ds(0, 2)], plane.at[pl.ds(2, 2)], 2, {"ctx": 1 - self.at.ctx})

    def along(self, up, plane):
        piece = self.stack.at[plane]
        return pltpu.make_async_remote_copy(
            src_ref=piece, dst_ref=piece, send_sem=self.sems.at[2 + up, plane], recv_sem=self.sems.at[4, plane],
            device_id=self.at.up if up else self.at.down, device_id_type=MESH,
        )

    def over(self, plane):
        return pltpu.make_async_remote_copy(
            src_ref=self.stack.at[plane], dst_ref=self.beyond.at[plane],
            send_sem=self.sems.at[5, plane], recv_sem=self.sems.at[6, plane],
            device_id=self.at.next_core, device_id_type=MESH,
        )

    def rows(self, core):
        return pl.ds(pl.multiple_of(core * self.ranks, self.ranks), self.ranks)

    def start(self):
        theirs = self.rows(1 - self.at.core)
        for half in range(2):
            self.give[:, half * self.width : (half + 1) * self.width] = self.split[half, theirs, :].astype(B16)
        self.give[:, 2 * self.width :] = self.full[theirs, :].astype(B16)
        self.between_cores().start()

    def second(self):
        at, width, rest = self.at, self.width, self.rest
        self.between_cores().wait_recv()
        mine = self.rows(at.core)
        for half, target in ((at.tp, self.stack.at[at.z, 0]), (1 - at.tp, self.pass_tp)):
            span = pl.ds(pl.multiple_of(half * width, 128), width)
            target[:, 0:width] = (self.split[half, mine, :] + self.take[:, span].astype(F32)).astype(B16)
            target[:, width : width + rest] = (
                self.full[mine, :] + self.take[:, 2 * width :].astype(F32)
            ).astype(B16)
            target[:, width + rest :] = self.tag
        self.to_tp().start()

    def third(self):
        self.to_tp().wait_recv()
        self.to_ctx().start()

    def both_ways(self, act_up, act_down, distance):
        at = self.at
        if distance == 0:
            pl.when(at.has_up)(functools.partial(act_up, at.z))
            pl.when(at.has_down)(functools.partial(act_down, at.z))
        else:
            pl.when((at.z >= distance) & at.has_up)(functools.partial(act_up, at.z - distance))
            pl.when((at.z < at.planes - distance) & at.has_down)(functools.partial(act_down, at.z + distance))

    def came(self, distance, act):
        at = self.at
        pl.when(at.z >= distance)(functools.partial(act, at.z - distance))
        pl.when(at.z < at.planes - distance)(functools.partial(act, at.z + distance))

    def planes(self, distance):
        if distance == 0:
            self.to_ctx().wait_recv()
        else:
            self.came(distance, lambda plane: self.along(1, plane).wait_recv())
        if distance < self.at.planes - 1:
            self.both_ways(
                lambda plane: self.along(1, plane).start(), lambda plane: self.along(0, plane).start(), distance
            )
        if distance == 0:
            self.over(self.at.z).start()
        else:
            self.came(distance, lambda plane: self.over(plane).start())

    def finish(self):
        at = self.at
        for plane in range(at.planes):
            self.over(plane).wait_recv()
        keep = self.width + self.rest
        adapters, ranks = self.sums.shape[0], self.ranks
        terms = at.planes * 4 * ranks
        lane = lax.broadcasted_iota(jnp.int32, (terms, 128), 1)
        rank_of = lax.broadcasted_iota(jnp.int32, (terms, 128), 0) % ranks
        for source, core in ((self.stack, at.core), (self.beyond, 1 - at.core)):
            tags = source[:, :, :, keep:].reshape(terms, 128).astype(F32)
            picks = (tags == (lane // ranks).astype(F32)) & (lane % ranks == rank_of)
            choose = jnp.where(picks, 1.0, 0.0).astype(B16)
            for begin in range(0, keep, 512):
                span = pl.ds(begin, min(512, keep - begin))
                total = dot(choose, source[:, :, :, span].reshape(terms, -1), 0, 0)
                for adapter in range(adapters):
                    self.sums[adapter, self.rows(core), span] = total[adapter * ranks : (adapter + 1) * ranks]

    def sent(self):
        self.between_cores().wait_send()
        self.to_tp().wait_send()
        self.to_ctx().wait_send()
        for distance in range(self.at.planes - 1):
            self.both_ways(
                lambda plane: self.along(1, plane).wait_send(),
                lambda plane: self.along(0, plane).wait_send(),
                distance,
            )
        for plane in range(self.at.planes):
            self.over(plane).wait_send()

    @staticmethod
    def scratch(planes, ranks, width, rest):
        wide = width + rest + 128
        return [
            pltpu.VMEM((ranks, 2 * width + rest), B16),
            pltpu.VMEM((ranks, 2 * width + rest), B16),
            pltpu.VMEM((ranks, wide), B16),
            pltpu.VMEM((planes, 4, ranks, wide), B16),
            pltpu.VMEM((planes, 4, ranks, wide), B16),
            pltpu.SemaphoreType.DMA((7, max(planes, 4))),
        ]


ROWS = 256


def project_body(
    planes, blocks,
    tokens_ref, pick_ref, places_ref, bias_ref, wide_ref,
    tab_jd, tab_ed, tab_ou, tab_ru, tab_ju, tab_od, tab_eu, tab_rd,
    w_ref, own_o, own_e, own_r, gain_ref, shift_ref, rates_ref,
    x_out, factors_out, shared_out, offsets_out, w_out, full_o, full_e, full_r,
    q_out, k_out, v_out, xn_out, u_out, cos_out, sin_out,
    spots_ref, offsets_ref, factors_ref, factors_next, shared_ref,
    vm_jd, vm_ed, vm_ou, vm_ru, vm_ju, vm_od, vm_eu, vm_rd,
    x_vm, w_vm, acc, stage, spots_all, factors_vm, offsets_vm, jd_vm,
    w_sems, flow_sems, x_sems, spot_sems, factor_sems, shared_sems, offset_sems, local_sems, out_sems, move_sems, table_sems,
):
    at = Place(planes)
    rows_all, width = x_vm.shape
    depth, half = w_ref.shape[1:]
    at.greet(True, True)
    chunks = rows_all // ROWS
    parts = [
        Flow(
            at, w_ref.at[part], lambda s, h, part=part: w_out.at[s, h, part],
            [w_sems.at[part, kind] for kind in range(9)],
        )
        for part in range(3)
    ]
    taken = Rows(flow_sems)
    flow_o = Flow(at, own_o, lambda s, h: full_o.at[s, h], taken.take(ALONG_Z), ALONG_Z)
    flows = block_flows(at, own_e, own_r, full_e, full_r, taken, PROJECT_KINDS)
    ahead = [flow_o] + flows[0] + flows[1]
    holds = at.core == at.ctx

    def local(source, target, index):
        return pltpu.make_async_copy(source, target, local_sems.at[index])

    for flow in parts:
        flow.pass_on(0, z=True, tp=True)
    tables_in = [
        pltpu.make_async_copy(source, target, table_sems.at[i])
        for i, (source, target) in enumerate(
            (
                (tab_jd, vm_jd), (tab_ed, vm_ed), (tab_ou, vm_ou), (tab_ru, vm_ru),
                (tab_ju, vm_ju), (tab_od, vm_od), (tab_eu, vm_eu), (tab_rd, vm_rd),
            )
        )
    ]
    for table in tables_in:
        table.start()
    place_rows = [places_ref[band, pl.ds(at.tp, 1), :].astype(F32) for band in range(3)]
    spots_ref[...] = jnp.concatenate(
        place_rows * 3 + [jnp.zeros((spots_ref.shape[0] - 9, rows_all), F32)], axis=0
    ).astype(B16)
    for part in range(3):
        offsets_ref[:, part * half : (part + 1) * half] = bias_ref[part : part + 1, :]
    offsets_ref[:, 3 * half :] = wide_ref[...]

    def x_chunk(i):
        span = pl.ds(i * ROWS, ROWS)
        return turned_copy(at, tokens_ref.at[at.tp, span], x_vm.at[span], x_sems.at[i])

    spot_copy = turned_copy(at, spots_ref, spots_all.at[0], spot_sems.at[0])

    @pl.when(at.crosses)
    def _():
        spot_copy.start()
        for i in range(chunks):
            x_chunk(i).start()

    @pl.when(holds)
    def _():
        spots_all[0] = spots_ref[...]
        for i in range(chunks):
            span = pl.ds(i * ROWS, ROWS)
            local(tokens_ref.at[at.tp, span], x_vm.at[span], 1 + i).start()

    for flow in parts:
        flow.pass_on(0, core=True)

    def remote(source, target, sems, device):
        return pltpu.make_async_remote_copy(
            src_ref=source, dst_ref=target, send_sem=sems.at[0], recv_sem=sems.at[1],
            device_id=device, device_id_type=MESH,
        )

    offset_copy = remote(offsets_ref, offsets_out.at[at.tp], offset_sems, at.next_tp)
    offset_came = remote(offsets_ref, offsets_out.at[1 - at.tp], offset_sems, at.next_tp)
    offset_copy.start()
    local(offsets_ref, offsets_out.at[at.tp], 1 + chunks).start()
    next_copy = remote(factors_next, factors_out.at[at.tp], factor_sems.at[0], at.next_tp)
    next_came = remote(factors_next, factors_out.at[1 - at.tp], factor_sems.at[0], at.next_tp)
    own_factors = remote(factors_ref, factors_out.at[at.tp], factor_sems.at[1], at.next_core)
    shared_copy = remote(shared_ref, shared_out, shared_sems, at.next_core)
    next_factors = remote(factors_out.at[1 - at.tp], factors_out.at[1 - at.tp], factor_sems.at[2], at.next_core)

    local(w_ref, w_out.at[at.shard, at.tp], 4 + chunks).start()
    local(own_o, full_o.at[at.shard, at.tp], 5 + chunks).start()
    local(own_e, full_e.at[at.shard, at.tp], 6 + chunks).start()
    local(own_r, full_r.at[at.shard, at.tp], 7 + chunks).start()

    @pl.when(at.crosses)
    def _():
        spot_copy.wait_recv()

    spot_next = remote(spots_all.at[0], spots_all.at[1], spot_sems.at[1], at.next_core)
    spot_next.start()

    lane = lax.broadcasted_iota(jnp.int32, (1, 128), 1) % 64
    turned = lane < 60
    early = lane % 20 < 10

    def tables(part):
        def body(i, carry):
            span = pl.ds(pl.multiple_of(i * ROWS, ROWS), ROWS)
            angle = dot(spots_all[part, :, span], rates_ref[...], 0, 0)
            out = pl.ds(pl.multiple_of(part * rows_all + i * ROWS, ROWS), ROWS)
            cos_out[out, :] = jnp.where(turned, jnp.cos(angle), 1.0)
            sine = jnp.sin(angle)
            sin_out[out, :] = jnp.where(turned, jnp.where(early, -sine, sine), 0.0)
            return carry

        lax.fori_loop(0, chunks, body, 0)

    tables(0)

    for table in tables_in:
        table.wait()

    def chosen(table, pick):
        return sum(
            table[i].astype(F32) * jnp.where(pick == i, 1.0, 0.0) for i in range(table.shape[0])
        ).astype(B16)

    picks = (pick_ref[0], pick_ref[1])
    pick = jnp.where(at.tp == 0, picks[0], picks[1])
    for target, which in ((factors_ref, pick), (factors_next, picks[0] + picks[1] - pick)):
        ju = chosen(vm_ju, which)
        for part in range(3):
            target[:, part * half : (part + 1) * half] = ju[part]
        begin = 3 * half
        for table in (vm_od, vm_eu, vm_rd):
            target[:, begin : begin + table.shape[2]] = chosen(table, which)
            begin += table.shape[2]
    for i, table in enumerate((vm_jd, vm_ed, vm_ou, vm_ru)):
        shared_ref[:, i * width : (i + 1) * width] = chosen(table, pick)
    shared_ref[:, 4 * width :] = jnp.full((shared_ref.shape[0], 128), pick.astype(F32)).astype(B16)

    @pl.when(holds)
    def _():
        next_copy.start()
        own_factors.start()
        shared_copy.start()
        local(factors_ref, factors_out.at[at.tp], 2 + chunks).start()
        local(shared_ref, shared_out, 3 + chunks).start()

    for flow in parts:
        flow.pass_on(1, z=True, tp=True, core=True, wait=True)
    spot_next.wait()
    tables(1)

    @pl.when(holds)
    def _():
        next_came.wait_recv()
        next_factors.start()

    for flow in parts:
        flow.pass_on(2, z=True, tp=True, core=True, wait=True)

    @pl.when(holds)
    def _():
        local(factors_ref, factors_out.at[at.tp], 2 + chunks).wait()
        local(shared_ref, shared_out, 3 + chunks).wait()
        own_factors.wait_send()
        shared_copy.wait_send()
        next_copy.wait_send()
        next_factors.wait_send()

    @pl.when(at.crosses)
    def _():
        own_factors.wait_recv()
        shared_copy.wait_recv()
        remote(factors_out.at[1 - at.tp], factors_out.at[1 - at.tp], factor_sems.at[2], at.next_core).wait_recv()

    offset_copy.wait_send()
    offset_came.wait_recv()
    local(offsets_ref, offsets_out.at[at.tp], 1 + chunks).wait()
    loads = [
        pltpu.make_async_copy(factors_out, factors_vm, out_sems.at[0]),
        pltpu.make_async_copy(offsets_out, offsets_vm, out_sems.at[1]),
        pltpu.make_async_copy(shared_out.at[:, pl.ds(0, width)], jd_vm, out_sems.at[2]),
    ]
    for load in loads:
        load.start()
    for load in loads:
        load.wait()

    kept = []

    def x_ready(i):
        span = pl.ds(i * ROWS, ROWS)

        @pl.when(at.crosses)
        def _():
            x_chunk(i).wait()

        @pl.when(holds)
        def _():
            local(tokens_ref.at[at.tp, span], x_vm.at[span], 1 + i).wait()

        keep = pltpu.make_async_copy(x_vm.at[span], x_out.at[span], x_sems.at[i, 2])
        keep.start()
        kept.append(keep)
        scaled, _ = row_norm(x_vm[span, :].astype(F32))
        xn = (scaled * gain_ref[...] + shift_ref[...]).astype(B16)
        xn_out[span, :] = xn
        u_out[span, :] = dot(xn, jd_vm[...], 1, 1).astype(B16)

    outs = (q_out, k_out, v_out)
    sending = []
    orders = ((0, 1, 2, 3), (1, 0, 2, 3), (2, 3, 1, 0), (3, 2, 1, 0))

    def plane_at(turn):
        plane = jnp.int32(orders[0][turn])
        for z in range(1, planes):
            plane = jnp.where(at.z == z, orders[z][turn], plane)
        return plane

    def to_next(turn):
        for flow in parts:
            flow.came(TP_CAME, plane_at(turn)).wait_recv()
            flow.copy(NEXT_SENT, plane_at(turn)).start()

    def w_load(turn):
        shards_of = pl.ds(2 * plane_at(turn), 2)
        return pltpu.make_async_copy(w_out.at[shards_of], w_vm.at[turn], out_sems.at[turn])

    def take_plane(turn):
        for flow in parts:
            flow.came(OWN_CAME, plane_at(turn)).wait_recv()
            flow.came(NEXT_CAME, plane_at(turn)).wait_recv()
        w_load(turn).start()

    def columns_of(turn):
        return pl.ds(pl.multiple_of(plane_at(turn) * 2 * depth, 2 * depth), 2 * depth)

    wide = rows_all // 2

    def product(turns, owner, part, span):
        value = 0.0
        for turn in turns:
            w = w_vm[turn, :, owner, part].reshape(2 * depth, half)
            value += dot(xn_out[span, columns_of(turn)], w)
        return value

    owners = (1 - at.core, at.core)

    def add_first(turns):
        for order, owner in enumerate(owners):
            for part in range(3):
                for begin in range(0, rows_all, wide):
                    span = pl.ds(begin, wide)
                    acc[order, part, span, :] = product(turns, owner, part, span)

    def add_last(turn):
        for order, owner in enumerate(owners):
            for part in range(3):
                bias = offsets_vm[owner, :, part * half : (part + 1) * half]
                up = factors_vm[owner, :, part * half : (part + 1) * half]
                for begin in range(0, rows_all, wide):
                    span = pl.ds(begin, wide)
                    value = acc[order, part, span, :] + bias + product((turn,), owner, part, span)
                    value += dot(u_out[span, :], up)
                    if part == 2:
                        stage[order, part, span, :] = value.astype(B16)
                        continue
                    for col in range(0, half, 128):
                        piece = value[:, col : col + 128]
                        stage[order, part, span, col : col + 128] = (
                            piece * cos_out[span, :] + partner(piece) * sin_out[span, :]
                        ).astype(B16)
                if order == 0:
                    move = remote(
                        stage.at[order, part], outs[part].at[pl.ds(rows_all, rows_all)],
                        move_sems.at[part], at.next_core,
                    )
                else:
                    move = pltpu.make_async_copy(
                        stage.at[order, part], outs[part].at[pl.ds(0, rows_all)], out_sems.at[4 + part]
                    )
                move.start()
                sending.append(move)

    to_next(0)
    to_next(1)
    for i in range(chunks):
        x_ready(i)
    for flow in parts:
        flow.pass_on(3, tp=True, core=True, wait=True)
    for other in ahead:
        other.pass_on(0, z=True)
    local(w_ref, w_out.at[at.shard, at.tp], 4 + chunks).wait()
    take_plane(0)
    take_plane(1)
    to_next(2)
    take_plane(2)
    for turn in range(3):
        w_load(turn).wait()
    add_first((0, 1, 2))
    to_next(3)
    take_plane(3)
    w_load(3).wait()
    add_last(3)

    for keep in kept:
        keep.wait()
    for other in ahead:
        other.wait(Z_CAME, 1)
        other.sent(0, z=True)
    for flow in parts:
        for far in range(planes):
            flow.sent(far, z=far < planes - 1, tp=True, core=True)
            flow.sent_next(far)
    for i in range(3):
        local((own_o, own_e, own_r)[i], (full_o, full_e, full_r)[i].at[at.shard, at.tp], 5 + i + chunks).wait()

    @pl.when(at.crosses)
    def _():
        spot_copy.wait_send()

    for move in sending:
        move.wait()


def project(planes, tokens, picks, places, bias, wide, tables, weight, own_o, own_e, own_r, gain, shift, rates):
    rows, width = tokens.shape[1:]
    _, depth, half = weight.shape
    rank = tables[0].shape[1]
    blocks = own_e.shape[1] // HIDDEN_BLOCK
    chunks = rows // ROWS
    shape = jax.ShapeDtypeStruct
    hbm = pl.BlockSpec(memory_space=pl.ANY)
    vmem = pl.BlockSpec(memory_space=pltpu.VMEM)
    smem = pl.BlockSpec(memory_space=pltpu.SMEM)
    dma = pltpu.SemaphoreType.DMA
    factors = shape((rank, 3 * half + sum(table.shape[2] for table in tables[5:])), B16)
    shared = shape((rank, 4 * width + 128), B16)
    offsets = shape((1, 3 * half + wide.shape[1]), F32)
    spots = shape(rates.shape[:1] + (rows,), B16)
    return pl.pallas_call(
        functools.partial(project_body, planes, blocks),
        in_specs=[hbm, smem] + [vmem] * 3 + [hbm] * 8 + [vmem] * 7,
        out_specs=[hbm] * 11 + [vmem] * 4,
        out_shape=[
            shape((rows, width), B16),
            shape((2,) + factors.shape, B16),
            shape(shared.shape, B16),
            shape((2,) + offsets.shape, F32),
            shape((2 * planes, 2) + weight.shape, B16),
            shape((2 * planes, 2) + own_o.shape, B16),
            shape((2 * planes, 2) + own_e.shape, B16),
            shape((2 * planes, 2) + own_r.shape, B16),
            shape((2 * rows, half), B16),
            shape((2 * rows, half), B16),
            shape((2 * rows, half), B16),
            shape((rows, width), B16),
            shape((rows, rank), B16),
            shape((2 * rows, 128), F32),
            shape((2 * rows, 128), F32),
        ],
        scratch_shapes=[
            pltpu.VMEM(spots.shape, B16),
            pltpu.VMEM(offsets.shape, F32),
            pltpu.VMEM(factors.shape, B16),
            pltpu.VMEM(factors.shape, B16),
            pltpu.VMEM(shared.shape, B16),
        ]
        + [pltpu.VMEM(table.shape, B16) for table in tables]
        + [
            pltpu.VMEM((rows, width), B16),
            pltpu.VMEM((planes, 2, 2) + weight.shape, B16),
            pltpu.VMEM((2, 3, rows, half), F32),
            pltpu.VMEM((2, 3, rows, half), B16),
            pltpu.VMEM((2,) + spots.shape, B16),
            pltpu.VMEM((2,) + factors.shape, B16),
            pltpu.VMEM((2,) + offsets.shape, F32),
            pltpu.VMEM((rank, width), B16),
            dma((3, 9, planes)),
            dma((count_rows(ALONG_Z, PROJECT_KINDS), planes)),
            dma((chunks, 3)),
            dma((2, 2)),
            dma((3, 2)),
            dma((2,)),
            dma((2,)),
            dma((8 + chunks,)),
            dma((7,)),
            dma((3, 2)),
            dma((8,)),
        ],
        compiler_params=pltpu.CompilerParams(
            vmem_limit_bytes=VMEM_LIMIT, collective_id=0, has_side_effects=True
        ),
        cost_estimate=pl.CostEstimate(
            flops=2 * rows * width * 6 * half, bytes_accessed=100 * 2**20, transcendentals=0
        ),
    )(tokens, picks, places, bias, wide, *tables, weight, own_o, own_e, own_r, gain, shift, rates)


def attend_body(
    planes, blocks,
    q_ref, k_ref, v_ref, cot_ref, own_o, own_e, own_r, in_o, in_e, in_r,
    o_ref, inv_ref, e_ref, o_next, cot_out, full_o, full_e, full_r,
    vm_ref, stage, cot_vm, flow_sems, stage_sems, cot_sems,
):
    at = Place(planes)
    rows_all, length = q_ref.shape[0], k_ref.shape[0]
    low = low_lanes()
    pair, turn = pl.program_id(0), pl.program_id(1)
    turns = length // rows_all
    now = pair * turns + turn
    pairs = stage.shape[0] // (turns // 2)
    count = pairs * turns
    taken = Rows(flow_sems)
    flow_o = Flow(at, own_o, lambda s, h: full_o.at[s, h], taken.take(EVERY), EVERY)
    flows = block_flows(at, own_e, own_r, full_e, full_r, taken, ATTEND_KINDS)
    zero = [flow_o] + flows[0]
    last = planes - 1
    cot_move = turned_copy(at, cot_ref.at[at.tp], cot_out, cot_sems)
    cot_load = pltpu.make_async_copy(cot_ref.at[at.tp], cot_vm, cot_sems.at[2])
    cot_keep = pltpu.make_async_copy(cot_vm, cot_out, cot_sems.at[3])

    def when(step, act):
        pl.when(now == min(step * count // 16, count - 1))(act)

    @pl.when(now == 0)
    def _():
        at.greet(True, True)
        for flow in zero:
            flow.pass_on(1, z=True)
            flow.pass_on(0, tp=True)
        pl.when(at.crosses)(lambda: cot_move.start())
        pl.when(jnp.logical_not(at.crosses))(lambda: cot_load.start())
        for flow in zero:
            flow.pass_on(0, core=True)
            flow.pass_on(1, core=True)
        for flow in flows[1] + flows[2]:
            flow.pass_on(0, core=True)

    def at_2():
        for flow in flows[1]:
            flow.pass_on(1, z=True, core=True)
        for flow in zero:
            flow.pass_on(1, tp=True)

    def at_3():
        @pl.when(jnp.logical_not(at.crosses))
        def _():
            cot_load.wait()
            cot_keep.start()

    def at_4():
        for flow in zero:
            flow.pass_on(2, z=True, tp=True, core=True, wait=True)

    def at_5():
        for flow in zero:
            flow.pass_next(0)

    def at_6():
        for flow in flows[1]:
            flow.pass_on(2, z=True, core=True, wait=True)
        for flow in flows[2]:
            flow.pass_on(0, z=True)

    def at_8():
        for flow in zero:
            flow.pass_on(3, tp=True, core=True, wait=True)

    def at_9():
        for flow in zero:
            flow.pass_next(1)
        for flow in flows[1]:
            flow.pass_on(0, tp=True)
            flow.pass_on(1, tp=True)

    def at_10():
        for flow in flows[2]:
            flow.pass_on(1, z=True, core=True, wait=True)
        for flow in flows[1]:
            flow.pass_on(3, core=True, wait=True)

    def at_12():
        for flow in flows[2]:
            flow.pass_on(2, z=True, core=True, wait=True)
        for flow in flows[3]:
            flow.pass_on(0, z=True)
        for flow in zero:
            flow.pass_next(2)
            flow.pass_next(3)

    def at_15():
        for flow in flows[2]:
            flow.pass_on(3, core=True, wait=True)

    for step, act in (
        (2, at_2), (3, at_3), (4, at_4), (5, at_5), (6, at_6), (8, at_8), (9, at_9), (10, at_10),
        (12, at_12), (15, at_15),
    ):
        when(step, act)

    @pl.when(turn == 0)
    def _():
        vm_ref[0] = jnp.where(low, v_ref[...], 1).astype(B16)
        vm_ref[1] = jnp.where(low, 1, v_ref[...]).astype(B16)

    step = min(256, rows_all)
    for begin in range(0, rows_all, step):
        rows = pl.ds(begin, step)
        q = q_ref[rows, :]
        sums = []
        for head in range(2):
            mine = low if head == 0 else ~low
            scores = dot(jnp.where(mine, q, 0).astype(B16), k_ref[...], 1, 1)
            top = jnp.max(scores, 1, keepdims=True)
            weights = jnp.exp2((scores - top) * exp_scale).astype(B16)
            e_ref[head, rows, :] = weights
            sums.append(dot(weights, vm_ref[head]))
        total = pltpu.roll(jnp.where(low, sums[1], sums[0]), 64, 1)
        inverse = 1.0 / total
        o_ref[rows, :] = (jnp.where(low, sums[0], sums[1]) * inverse).astype(B16)
        inv_ref[rows, :] = inverse

    def o_move(index):
        per = turns // 2
        rows = pl.ds(pl.multiple_of(index % per * rows_all, rows_all), rows_all)
        columns = pl.ds(pl.multiple_of(index // per * 128, 128), 128)
        return pltpu.make_async_remote_copy(
            src_ref=stage.at[index], dst_ref=o_next.at[rows, columns],
            send_sem=stage_sems.at[0, index], recv_sem=stage_sems.at[1, index],
            device_id=at.next_core, device_id_type=MESH,
        )

    @pl.when(turn >= turns // 2)
    def _():
        index = pair * (turns // 2) + turn - turns // 2
        stage[index] = o_ref[...]
        o_move(index).start()

    @pl.when(now == count - 1)
    def _():
        for flow in flows[3]:
            flow.wait(Z_CAME, 1)
        for flow in zero + flows[1] + flows[2]:
            for far in range(planes):
                flow.wait(OWN_CAME, far)
        for flow in zero:
            for far in range(planes):
                flow.wait(NEXT_CAME, far)
                flow.sent_next(far)
        for flow in flows[1]:
            for far in range(2):
                flow.wait(TP_CAME, far)
        for flow in zero + flows[1]:
            for far in range(planes):
                flow.sent(far, z=0 < far < last, tp=flow in zero or far < 2, core=True)
        for flow in flows[2]:
            for far in range(planes):
                flow.sent(far, z=far < last, core=True)
        for flow in flows[3]:
            flow.sent(0, z=True)

        @pl.when(at.crosses)
        def _():
            cot_move.wait()

        @pl.when(jnp.logical_not(at.crosses))
        def _():
            cot_keep.wait()

        for index in range(count // 2):
            o_move(index).wait()


def attend(planes, query, key, value, cotangent, own_o, own_e, own_r, full_o, full_e, full_r):
    length, width = query.shape
    block = min(512, length // 2)
    blocks = own_e.shape[1] // HIDDEN_BLOCK
    turns = length // block
    pairs = width // 128
    rows = pl.BlockSpec((block, 128), lambda p, i: (i, p))
    full = pl.BlockSpec((length, 128), lambda p, i: (0, p))
    hbm = pl.BlockSpec(memory_space=pl.ANY)
    shape = jax.ShapeDtypeStruct
    like = lambda array: shape(array.shape, array.dtype)
    dma = pltpu.SemaphoreType.DMA
    return pl.pallas_call(
        functools.partial(attend_body, planes, blocks),
        grid=(pairs, turns),
        in_specs=[rows, full, full] + [hbm] * 7,
        out_specs=[rows, rows, pl.BlockSpec((2, block, length), lambda p, i: (p, i, 0))] + [hbm] * 5,
        out_shape=[
            shape((length, width), B16),
            shape((length, width), F32),
            shape((width // 64, length, length), B16),
            shape((length // 2, width), B16),
            shape(cotangent.shape[1:], B16),
            like(full_o), like(full_e), like(full_r),
        ],
        input_output_aliases={7: 5, 8: 6, 9: 7},
        scratch_shapes=[
            pltpu.VMEM((2, length, 128), B16),
            pltpu.VMEM((pairs * turns // 2, block, 128), B16),
            pltpu.VMEM(cotangent.shape[1:], B16),
            dma((count_rows(EVERY, ATTEND_KINDS), planes)),
            dma((2, pairs * turns // 2)),
            dma((4,)),
        ],
        compiler_params=pltpu.CompilerParams(
            vmem_limit_bytes=VMEM_LIMIT, collective_id=1, has_side_effects=True
        ),
        cost_estimate=pl.CostEstimate(
            flops=16 * length * length * width,
            bytes_accessed=width // 64 * length * length * 2,
            transcendentals=width // 64 * length * length,
        ),
    )(query, key, value, cotangent, own_o, own_e, own_r, full_o, full_e, full_r)


def attend_back_body(
    planes,
    q_ref, k_ref, v_ref, o_ref, inv_ref, g_ref, e_ref, cos_ref, sin_ref, cos_all, sin_all,
    split_ref, full_ref, tag_ref, out_ref,
    own_ref, other_ref, sums_ref, home_ref,
    key_sum, value_sum, vm_ref, q_stage, kv_stage, out_vm, move_sems, out_sems, *spread_refs,
):
    at = Place(planes)
    rows_all, length = q_ref.shape[0], k_ref.shape[0]
    low = low_lanes()
    pair, at_step = pl.program_id(0), pl.program_id(1)
    pairs, turns = q_stage.shape[0], q_stage.shape[1]
    now = pair * turns + at_step
    count = pairs * turns
    local_rows = length // 2
    spread = Spread(at, split_ref, full_ref, tag_ref[...], sums_ref, *spread_refs)
    stays = jnp.logical_not(at.crosses)
    out_load = pltpu.make_async_copy(out_ref, out_vm, out_sems.at[0])
    out_keep = pltpu.make_async_copy(out_vm, home_ref.at[at.tp], out_sems.at[1])
    out_turn = pltpu.make_async_remote_copy(
        src_ref=out_ref, dst_ref=home_ref.at[at.tp], send_sem=out_sems.at[2], recv_sem=out_sems.at[3],
        device_id=at.turned, device_id_type=MESH,
    )

    def out_tp(source):
        return pltpu.make_async_remote_copy(
            src_ref=source, dst_ref=home_ref.at[at.tp], send_sem=out_sems.at[4], recv_sem=out_sems.at[5],
            device_id=at.next_tp, device_id_type=MESH,
        )

    def when(step, act):
        pl.when(now == step)(act)

    @pl.when(now == 0)
    def _():
        pl.when(stays)(lambda: out_load.start())
        at.greet(True, True, True)
        spread.start()
        pl.when(at.crosses)(lambda: out_turn.start())

    when(2, spread.second)

    @pl.when(now == 3)
    def _():
        @pl.when(stays)
        def _():
            out_load.wait()
            out_keep.start()
            out_tp(out_vm).start()

    when(4, spread.third)
    when(6, lambda: spread.planes(0))

    @pl.when(now == 7)
    def _():
        @pl.when(at.crosses)
        def _():
            out_turn.wait_recv()
            out_tp(home_ref.at[at.tp]).start()

    when(9, lambda: spread.planes(1))
    when(12, lambda: spread.planes(2))
    when(15, lambda: spread.planes(3))

    @pl.when(at_step == 0)
    def _():
        key_sum[...] = jnp.zeros_like(key_sum)
        value_sum[...] = jnp.zeros_like(value_sum)
        vm_ref[0] = jnp.where(low, v_ref[...], -1).astype(B16)
        vm_ref[1] = jnp.where(low, -1, v_ref[...]).astype(B16)

    step = min(256, rows_all)
    for begin in range(0, rows_all, step):
        rows = pl.ds(begin, step)
        grad = g_ref[rows, :].astype(F32) * inv_ref[rows, :]
        grad_low = grad.astype(B16)
        product = pltpu.roll(grad * o_ref[rows, :].astype(F32), 64, 1).astype(B16)
        q_turned = q_ref[rows, :].T
        g_turned = grad_low.T
        parts = []
        for head in range(2):
            mine = low if head == 0 else ~low
            weights = e_ref[head, rows, :]
            grad_probs = dot(jnp.where(mine, grad_low, product), vm_ref[head], 1, 1)
            grad_scores = (weights.astype(F32) * grad_probs).astype(B16)
            parts.append(dot(grad_scores, k_ref[...]))
            span = pl.ds(head * 64, 64)
            key_sum[span, :] += dot(q_turned[head * 64 : head * 64 + 64], grad_scores)
            value_sum[span, :] += dot(g_turned[head * 64 : head * 64 + 64], weights)
        gq = jnp.where(low, parts[0], parts[1]) * score_scale
        q_stage[pair, at_step, rows, :] = (
            gq * cos_ref[rows, :] + partner(gq * sin_ref[rows, :])
        ).astype(B16)

    def columns(index):
        return pl.ds(pl.multiple_of(index * 128, 128), 128)

    def q_here(pair_index, turn_index):
        rows = pl.ds(pl.multiple_of(turn_index * rows_all, rows_all), rows_all)
        return pltpu.make_async_copy(
            q_stage.at[pair_index, turn_index], own_ref.at[0, rows, columns(pair_index)],
            move_sems.at[0, pair_index * turns + turn_index],
        )

    def q_there(pair_index, turn_index):
        rows = pl.ds(pl.multiple_of(turn_index * rows_all - local_rows, rows_all), rows_all)
        index = pair_index * turns + turn_index
        return pltpu.make_async_remote_copy(
            src_ref=q_stage.at[pair_index, turn_index], dst_ref=other_ref.at[0, rows, columns(pair_index)],
            send_sem=move_sems.at[0, index], recv_sem=move_sems.at[1, index],
            device_id=at.next_core, device_id_type=MESH,
        )

    def kv_here(part, pair_index):
        return pltpu.make_async_copy(
            kv_stage.at[part, pair_index, pl.ds(0, local_rows)], own_ref.at[1 + part, :, columns(pair_index)],
            move_sems.at[2, 2 * pair_index + part],
        )

    def kv_there(part, pair_index):
        index = 2 * pair_index + part
        return pltpu.make_async_remote_copy(
            src_ref=kv_stage.at[part, pair_index, pl.ds(local_rows, local_rows)],
            dst_ref=other_ref.at[1 + part, :, columns(pair_index)],
            send_sem=move_sems.at[3, index], recv_sem=move_sems.at[4, index],
            device_id=at.next_core, device_id_type=MESH,
        )

    pl.when(at_step < turns // 2)(lambda: q_here(pair, at_step).start())
    pl.when(at_step >= turns // 2)(lambda: q_there(pair, at_step).start())

    @pl.when(at_step == turns - 1)
    def _():
        gk = key_sum[...].T * score_scale
        kv_stage[0, pair] = (gk * cos_all[...] + partner(gk * sin_all[...])).astype(B16)
        kv_stage[1, pair] = value_sum[...].T.astype(B16)
        for part in range(2):
            kv_here(part, pair).start()
            kv_there(part, pair).start()

    @pl.when(now == count - 1)
    def _():
        for pair_index in range(pairs):
            for turn_index in range(turns):
                if turn_index < turns // 2:
                    q_here(pair_index, turn_index).wait()
                else:
                    q_there(pair_index, turn_index).wait()
            for part in range(2):
                kv_here(part, pair_index).wait()
                kv_there(part, pair_index).wait()
        spread.finish()
        spread.sent()

        @pl.when(stays)
        def _():
            out_keep.wait()
            out_tp(out_vm).wait_send()

        @pl.when(at.crosses)
        def _():
            out_turn.wait_send()
            out_tp(home_ref.at[at.tp]).wait_send()

        pltpu.make_async_remote_copy(
            src_ref=home_ref.at[at.tp], dst_ref=home_ref.at[1 - at.tp], send_sem=out_sems.at[4],
            recv_sem=out_sems.at[5], device_id=at.next_tp, device_id_type=MESH,
        ).wait_recv()


def attend_back(planes, query, key, value, attended, inverse, grad, weights, cosine, sine, split, full, tag, out, adapters):
    length, width = query.shape
    block = min(512, length // 2)
    pairs, turns = width // 128, length // block
    rows = pl.BlockSpec((block, 128), lambda p, i: (i, p))
    whole = pl.BlockSpec((length, 128), lambda p, i: (0, p))
    table = pl.BlockSpec((block, 128), lambda p, i: (i, 0))
    one = lambda array: pl.BlockSpec(
        array.shape, lambda p, i: (0,) * len(array.shape), pipeline_mode=pl.Buffered(1)
    )
    hbm = pl.BlockSpec(memory_space=pl.ANY)
    shape = jax.ShapeDtypeStruct
    dma = pltpu.SemaphoreType.DMA
    ranks = full.shape[0] // 2
    keep = split.shape[2] + full.shape[1]
    sums = shape((adapters, 2 * ranks, keep), F32)
    return pl.pallas_call(
        functools.partial(attend_back_body, planes),
        grid=(pairs, turns),
        in_specs=[
            rows, whole, whole, rows, rows, rows,
            pl.BlockSpec((2, block, length), lambda p, i: (p, i, 0)),
            table, table, one(cosine), one(sine), one(split), one(full), one(tag), hbm,
        ],
        out_specs=[hbm, hbm, one(sums), hbm],
        out_shape=[
            shape((3, length // 2, width), B16), shape((3, length // 2, width), B16), sums,
            shape((2,) + out.shape, B16),
        ],
        scratch_shapes=[
            pltpu.VMEM((128, length), F32),
            pltpu.VMEM((128, length), F32),
            pltpu.VMEM((2, length, 128), B16),
            pltpu.VMEM((pairs, turns, block, 128), B16),
            pltpu.VMEM((2, pairs, length, 128), B16),
            pltpu.VMEM(out.shape, B16),
            dma((5, max(pairs * turns, 2 * pairs))),
            dma((6,)),
        ]
        + Spread.scratch(planes, ranks, split.shape[2], full.shape[1]),
        compiler_params=pltpu.CompilerParams(
            vmem_limit_bytes=VMEM_LIMIT, collective_id=3, has_side_effects=True
        ),
        cost_estimate=pl.CostEstimate(
            flops=20 * length * length * width,
            bytes_accessed=width // 64 * length * length * 2,
            transcendentals=0,
        ),
    )(query, key, value, attended, inverse, grad, weights, cosine, sine, cosine, sine, split, full, tag, out)


def gauss_parts(z):
    t = 1.0 / (1.0 + (0.3275911 * math.sqrt(0.5)) * jnp.abs(z))
    poly = t * (0.254829592 + t * (-0.284496736 + t * (1.421413741 + t * (-1.453152027 + t * 1.061405429))))
    bell = jnp.exp2((z * z) * (-0.5 * math.log2(math.e)))
    upper = 0.5 * poly * bell
    cdf = jnp.where(z >= 0, 1.0 - upper, upper)
    return cdf, bell * (1.0 / math.sqrt(2.0 * math.pi))


def middle_body(
    planes, blocks,
    x_ref, cot_ref, own_ref, other_ref, wo_ref, factors_ref, shared_ref, offsets_ref,
    out_off, gain_ref, shift_ref, shrink_off, in_e, in_r,
    output_ref, gh_ref, t_split, t_full, gatt_out, full_e, full_r,
    hidden, xn_ref, total, back, u2_ref, u3_ref, u4_sum, g4_ref, g3_sum,
    e_vm, r_vm, gown_vm, gother_vm, load_sems, flow_sems, grad_sems,
):
    at = Place(planes)
    f = pl.program_id(0)
    last = 2 * blocks - 1
    core = at.core
    rows_all, width = x_ref.shape
    half = own_ref.shape[1]
    hidden_half = blocks * HIDDEN_BLOCK
    step = 256
    flows = block_flows(at, None, None, full_e, full_r, Rows(flow_sems), MIDDLE_KINDS)
    planes_all = range(planes)

    def pass_on(pair, **how):
        for flow in pair:
            for far in planes_all:
                flow.pass_on(far, fresh=False, **how)

    def pass_next(pair, wait):
        for flow in pair:
            for far in planes_all:
                flow.pass_next(far, wait)

    def arrived(pair, kind):
        for flow in pair:
            for far in planes_all:
                flow.wait(kind, far)

    def loads(index, slot):
        tp_half = jnp.where(index < blocks, at.tp, 1 - at.tp)
        span = pl.ds(pl.multiple_of(index % blocks * HIDDEN_BLOCK, HIDDEN_BLOCK), HIDDEN_BLOCK)
        return (
            pltpu.make_async_copy(full_e.at[:, tp_half, :, span], e_vm.at[slot], load_sems.at[0, slot]),
            pltpu.make_async_copy(full_r.at[:, tp_half, span, :], r_vm.at[slot], load_sems.at[1, slot]),
        )

    def wo_half(part):
        w = wo_ref[:, part]
        return jnp.concatenate([w[i] for i in range(w.shape[0])], axis=1)

    jd, ed, ou, ru = (pl.ds(i * width, width) for i in range(4))
    od = pl.ds(3 * half, half)

    @pl.when(f == 0)
    def _():
        for load in loads(0, 0):
            load.start()
        at.greet(True, False)
        for flow in flows[3]:
            flow.pass_on(1, fresh=False, z=True, core=True)
            flow.pass_on(0, fresh=False, core=True)
        for flow in flows[1]:
            flow.pass_on(2, fresh=False, tp=True)
            flow.pass_on(3, fresh=False, tp=True)
            flow.pass_next(0, False)
            flow.pass_next(1, False)
        pass_on(flows[2], tp=True)
        w_own, w_other = wo_half(core), wo_half(1 - core)
        for begin in range(0, rows_all, step):
            rows = pl.ds(begin, step)
            own, other = own_ref[rows, :], other_ref[rows, :]
            u2 = (
                dot(own, factors_ref[core, :, od], 1, 1) + dot(other, factors_ref[1 - core, :, od], 1, 1)
            ).astype(B16)
            u2_ref[rows, :] = u2
            h = (
                x_ref[rows, :].astype(F32) + dot(own, w_own) + dot(other, w_other)
                + out_off[...] + dot(u2, shared_ref[:, ou])
            )
            hidden[rows, :] = h
            scaled, _ = row_norm(h)
            xn = (scaled * gain_ref[...] + shift_ref[...]).astype(B16)
            xn_ref[rows, :] = xn
            u3_ref[rows, :] = dot(xn, shared_ref[:, ed], 1, 1).astype(B16)
            g4_ref[rows, :] = dot(cot_ref[rows, :], shared_ref[:, ru], 1, 1).astype(B16)
            total[rows, :] = h + shrink_off[...]
            back[rows, :] = jnp.zeros_like(h)
            u4_sum[rows, :] = jnp.zeros((step, u4_sum.shape[1]), F32)
            g3_sum[rows, :] = jnp.zeros((step, g3_sum.shape[1]), F32)
        for flow in flows[3]:
            flow.pass_on(2, fresh=False, z=True, core=True, wait=True)

    @pl.when(f == 1)
    def _():
        for flow in flows[3]:
            flow.pass_on(3, fresh=False, core=True, wait=True)

    @pl.when(f == 2)
    def _():
        pass_on(flows[3], tp=True)
        arrived(flows[3], OWN_CAME)

    @pl.when(f == 3)
    def _():
        for flow in flows[1]:
            flow.pass_next(2)
            flow.pass_next(3)

    @pl.when(f == 4)
    def _():
        arrived(flows[1], NEXT_CAME)

    @pl.when(f == last - 2)
    def _():
        pass_next(flows[2], True)

    slot = f % 2

    @pl.when(f < last - 2)
    def _():
        for load in loads(f + 1, 1 - slot):
            load.start()

    for load in loads(f, slot):
        load.wait()
    tp_half = jnp.where(f < blocks, at.tp, 1 - at.tp)
    begin_block = f % blocks * HIDDEN_BLOCK

    def block_of(first):
        return pl.ds(pl.multiple_of(first + begin_block, 128), HIDDEN_BLOCK)

    w_e = e_vm[slot].reshape(width, HIDDEN_BLOCK)
    w_r = jnp.concatenate([r_vm[slot, i] for i in range(2 * planes)], axis=1)
    eu = factors_ref[tp_half, :, block_of(4 * half)]
    rd = factors_ref[tp_half, :, block_of(4 * half + hidden_half)]
    wide_off = offsets_ref[tp_half, :, block_of(3 * half)]
    u3, g4 = u3_ref[...], g4_ref[...]
    z = dot(xn_ref[...], w_e) + wide_off + dot(u3, eu)
    gact = dot(cot_ref[...], w_r, 1, 1) + dot(g4, rd)
    cdf, density = gauss_parts(z)
    act = (z * cdf).astype(B16)
    gz = (gact * (cdf + z * density)).astype(B16)
    total[...] += dot(act, w_r)
    u4_sum[...] += dot(act, rd, 1, 1)
    back[...] += dot(gz, w_e, 1, 1)
    g3_sum[...] += dot(gz, eu, 1, 1)
    sum_rd = dot(g4, act, 0, 0)
    sum_eu = dot(u3, gz, 0, 0)
    t_split[tp_half, :, block_of(half + hidden_half)] = sum_rd
    t_split[tp_half, :, block_of(half)] = sum_eu

    @pl.when(f == last - 2)
    def _():
        arrived(flows[2], NEXT_CAME)

    @pl.when(f == last - 1)
    def _():
        pass_next(flows[3], True)
        arrived(flows[3], NEXT_CAME)

    @pl.when((f == last - 2) | (f == last - 1))
    def _():
        for load in loads(f + 1, 1 - slot):
            load.start()

    @pl.when(f == last)
    def _():
        w_own, w_other = wo_half(core), wo_half(1 - core)
        s_ru, s_ed, s_ou, s_own, s_other = 0.0, 0.0, 0.0, 0.0, 0.0
        moves = []
        for index, begin in enumerate(range(0, rows_all, step)):
            rows = pl.ds(begin, step)
            cot = cot_ref[rows, :]
            u4 = u4_sum[rows, :].astype(B16)
            output_ref[rows, :] = (total[rows, :] + dot(u4, shared_ref[:, ru])).astype(B16)
            s_ru += dot(u4, cot, 0, 0)
            g3 = g3_sum[rows, :].astype(B16)
            s_ed += dot(g3, xn_ref[rows, :], 0, 0)
            gx = back[rows, :] + dot(g3, shared_ref[:, ed])
            scaled, inverse = row_norm(hidden[rows, :])
            gh = cot.astype(F32) + back_norm(gx * gain_ref[...], scaled, inverse)
            gh_ref[rows, :] = gh
            gb = gh.astype(B16)
            s_ou += dot(u2_ref[rows, :], gb, 0, 0)
            g2 = dot(gb, shared_ref[:, ou], 1, 1).astype(B16)
            s_own += dot(g2, own_ref[rows, :], 0, 0)
            s_other += dot(g2, other_ref[rows, :], 0, 0)
            gother_vm[rows, :] = (
                dot(gb, w_other, 1, 1) + dot(g2, factors_ref[1 - core, :, od])
            ).astype(B16)
            there = pltpu.make_async_remote_copy(
                src_ref=gother_vm.at[rows], dst_ref=gatt_out.at[pl.ds(rows_all + begin, step)],
                send_sem=grad_sems.at[0, index], recv_sem=grad_sems.at[1, index],
                device_id=at.next_core, device_id_type=MESH,
            )
            there.start()
            gown_vm[rows, :] = (dot(gb, w_own, 1, 1) + dot(g2, factors_ref[core, :, od])).astype(B16)
            here = pltpu.make_async_copy(gown_vm.at[rows], gatt_out.at[rows], grad_sems.at[2, index])
            here.start()
            moves += [there, here]
        t_full[:, 0:width] = s_ou
        t_full[:, width : 2 * width] = s_ed
        t_full[:, 2 * width :] = s_ru
        t_split[core, :, 0:half] = s_own
        t_split[1 - core, :, 0:half] = s_other
        for index, pair in enumerate(flows[1:]):
            for flow in pair:
                for far in planes_all:
                    flow.sent(far, z=index == 2 and far in (1, 2), tp=index > 0 or far > 1, core=index == 2)
                    flow.sent_next(far)
        for move in moves:
            move.wait()


def middle(
    planes, x, cot, attended, other, w_o, factors, shared, offsets, out_off, gain, shift, shrink_off, w_e, w_r
):
    rows, width = x.shape
    half = attended.shape[1]
    shards_, _, depth, hidden_half = w_e.shape
    rank = factors.shape[1]
    blocks = hidden_half // HIDDEN_BLOCK
    one = lambda shape: pl.BlockSpec(
        shape, lambda f: (0,) * len(shape), pipeline_mode=pl.Buffered(1)
    )
    hbm = pl.BlockSpec(memory_space=pl.ANY)
    shape = jax.ShapeDtypeStruct
    dma = pltpu.SemaphoreType.DMA
    chunks = rows // 256
    return pl.pallas_call(
        functools.partial(middle_body, planes, blocks),
        grid=(2 * blocks,),
        in_specs=[
            one((rows, width)), one((rows, width)), one((rows, half)), one((rows, half)),
            one(w_o.shape), one(factors.shape), one(shared.shape), one(offsets.shape),
            one((1, width)), one((1, width)), one((1, width)), one((1, width)), hbm, hbm,
        ],
        out_specs=[
            one((rows, width)), one((rows, width)),
            one((2, rank, half + 2 * hidden_half)), one((rank, 3 * width)), hbm, hbm, hbm,
        ],
        out_shape=[
            shape((rows, width), B16), shape((rows, width), F32),
            shape((2, rank, half + 2 * hidden_half), F32), shape((rank, 3 * width), F32),
            shape((2 * rows, half), B16), shape(w_e.shape, B16), shape(w_r.shape, B16),
        ],
        input_output_aliases={12: 5, 13: 6},
        scratch_shapes=[
            pltpu.VMEM((rows, width), F32), pltpu.VMEM((rows, width), B16),
            pltpu.VMEM((rows, width), F32), pltpu.VMEM((rows, width), F32),
            pltpu.VMEM((rows, rank), B16), pltpu.VMEM((rows, rank), B16),
            pltpu.VMEM((rows, rank), F32), pltpu.VMEM((rows, rank), B16),
            pltpu.VMEM((rows, rank), F32),
            pltpu.VMEM((2, shards_, depth, HIDDEN_BLOCK), B16),
            pltpu.VMEM((2, shards_, HIDDEN_BLOCK, w_r.shape[3]), B16),
            pltpu.VMEM((rows, half), B16), pltpu.VMEM((rows, half), B16),
            dma((2, 2)), dma((count_rows((), MIDDLE_KINDS), planes)), dma((3, chunks)),
        ],
        compiler_params=pltpu.CompilerParams(
            vmem_limit_bytes=VMEM_LIMIT, collective_id=2, has_side_effects=True
        ),
        cost_estimate=pl.CostEstimate(
            flops=2 * rows * width * (16 * hidden_half // 2 + 4 * half),
            bytes_accessed=40 * 2**20,
            transcendentals=rows * hidden_half * 2,
        ),
    )(x, cot, attended, other, w_o, factors, shared, offsets, out_off, gain, shift, shrink_off, w_e, w_r)


def unproject_body(
    planes,
    x_ref, gh_ref, xn_ref, u_ref, gain_ref, w_ref, factors_ref, shared_ref, own_ref, other_ref,
    home_ref, sums_ref,
    own_vm, other_vm, w_vm, x_vm, gh_vm, xn_vm, stage, split, full, g1_vm, load_sems, move_sems, *spread_refs,
):
    at = Place(planes)
    rows_all, width = x_vm.shape
    half = own_vm.shape[2]
    core = at.core
    spread = Spread(at, split, full, shared_ref[0:8, 4 * width :], sums_ref, *spread_refs)
    halves = ((own_vm, core), (other_vm, 1 - core))
    chunks = rows_all // ROWS

    def load(index, source, target):
        return pltpu.make_async_copy(source, target, load_sems.at[index])

    loads = [load(0, own_ref, own_vm), load(1, other_ref, other_vm), load(2, xn_ref, xn_vm)]
    late = [load(3, x_ref, x_vm), load(4, gh_ref, gh_vm)]
    late += [load(5 + order, w_ref.at[:, owner], w_vm.at[order]) for order, (_, owner) in enumerate(halves)]
    for item in loads + late:
        item.start()
    at.greet(True, True, True, True)
    for item in loads:
        item.wait()
    u = u_ref[...]
    g1 = 0.0
    for source, owner in halves:
        for part in range(3):
            columns = pl.ds(part * half, half)
            g1 += dot(source[part], factors_ref[owner, :, columns], 1, 1)
            split[owner, :, columns] = dot(u, source[part], 0, 0)
    g1 = g1.astype(B16)
    g1_vm[...] = g1
    full[...] = dot(g1, xn_vm[...], 0, 0)
    spread.start()
    order = [2, 0, 3, 1]
    for item in late:
        item.wait()
    quarter = rows_all // 2

    def moves(i):
        tp_half = i * ROWS // quarter
        rows = pl.ds(i * ROWS % quarter, ROWS)
        source, target = stage.at[i], home_ref.at[at.tp, rows]

        def remote(device, came):
            return pltpu.make_async_remote_copy(
                src_ref=source, dst_ref=target, send_sem=move_sems.at[0, i], recv_sem=move_sems.at[came, i],
                device_id=device, device_id_type=MESH,
            )

        mine = at.tp == tp_half
        both = dict(at.turned)
        both["tp"] = 1 - at.tp
        return (
            (mine & jnp.logical_not(at.crosses), lambda: pltpu.make_async_copy(source, target, move_sems.at[0, i]), True),
            (mine & at.crosses, lambda: remote(at.turned, 1), False),
            (jnp.logical_not(mine) & jnp.logical_not(at.crosses), lambda: remote(at.next_tp, 2), False),
            (jnp.logical_not(mine) & at.crosses, lambda: remote(both, 2), False),
        )

    stages = [spread.second, spread.third, lambda: spread.planes(0), lambda: spread.planes(1)]
    for count, i in enumerate(order):
        span = pl.ds(i * ROWS, ROWS)
        gx = dot(g1_vm[span, :], shared_ref[:, 0:width])
        for index, (source, _) in enumerate(halves):
            for part in range(3):
                gx += dot(source[part, span, :], w_vm[index, :, part].reshape(width, half), 1, 1)
        scaled, inverse = row_norm(x_vm[span, :].astype(F32))
        stage[i] = (gh_vm[span, :] + back_norm(gx * gain_ref[...], scaled, inverse)).astype(B16)
        for there, move, _ in moves(i):
            pl.when(there)(lambda move=move: move().start())
        stages[count]()
    for distance in range(2, planes):
        spread.planes(distance)
    spread.finish()
    spread.sent()
    for i in range(chunks):
        for there, move, here in moves(i):
            if here:
                pl.when(there)(lambda move=move: move().wait())
            else:
                pl.when(there)(lambda move=move: move().wait_send())
    for i in range(chunks):
        tp_half = i * ROWS // quarter
        rows = pl.ds(i * ROWS % quarter, ROWS)

        def came(slot):
            return pltpu.make_async_remote_copy(
                src_ref=stage.at[i], dst_ref=home_ref.at[slot, rows], send_sem=move_sems.at[0, i],
                recv_sem=move_sems.at[1, i], device_id=at.next_tp, device_id_type=MESH,
            )

        pl.when((at.tp == tp_half) & at.crosses)(lambda came=came: came(at.tp).wait_recv())

    for i in range(chunks):
        tp_half = i * ROWS // quarter
        rows = pl.ds(i * ROWS % quarter, ROWS)

        def came(slot):
            return pltpu.make_async_remote_copy(
                src_ref=stage.at[i], dst_ref=home_ref.at[slot, rows], send_sem=move_sems.at[0, i],
                recv_sem=move_sems.at[2, i], device_id=at.next_tp, device_id_type=MESH,
            )

        pl.when(at.tp == tp_half)(lambda came=came: came(1 - at.tp).wait_recv())


def unproject(planes, x, gh, xn, u, gain, weight, factors, shared, own, other, adapters):
    rows, width = x.shape
    half = own.shape[2]
    rank = factors.shape[1]
    hbm = pl.BlockSpec(memory_space=pl.ANY)
    vmem = pl.BlockSpec(memory_space=pltpu.VMEM)
    shape = jax.ShapeDtypeStruct
    dma = pltpu.SemaphoreType.DMA
    chunks = rows // ROWS
    keep = 3 * half + width
    return pl.pallas_call(
        functools.partial(unproject_body, planes),
        in_specs=[hbm, hbm, hbm, vmem, vmem, hbm, vmem, vmem, hbm, hbm],
        out_specs=[hbm, vmem],
        out_shape=[shape((2, rows // 2, width), B16), shape((adapters, rank, keep), F32)],
        scratch_shapes=[
            pltpu.VMEM(own.shape, B16), pltpu.VMEM(own.shape, B16),
            pltpu.VMEM((2, weight.shape[0]) + weight.shape[2:], B16),
            pltpu.VMEM((rows, width), B16), pltpu.VMEM((rows, width), F32), pltpu.VMEM((rows, width), B16),
            pltpu.VMEM((chunks, ROWS, width), B16),
            pltpu.VMEM((2, rank, 3 * half), F32), pltpu.VMEM((rank, width), F32), pltpu.VMEM((rows, rank), B16),
            dma((7,)), dma((3, chunks)),
        ]
        + Spread.scratch(planes, rank // 2, 3 * half, width),
        compiler_params=pltpu.CompilerParams(
            vmem_limit_bytes=VMEM_LIMIT, collective_id=4, has_side_effects=True
        ),
        cost_estimate=pl.CostEstimate(
            flops=2 * rows * width * 6 * half, bytes_accessed=20 * 2**20, transcendentals=0
        ),
    )(x, gh, xn, u, gain, weight, factors, shared, own, other)


def rate_parts():
    lane = np.arange(128) % 64
    rates = np.exp((lane % 10).astype(np.float32) * np.float32(-math.log(10000.0) / 10.0)).astype(np.float32)
    rates = np.where(lane[None] // 20 == np.arange(3)[:, None], rates[None], np.float32(0.0)).astype(np.float32)
    parts = []
    for _ in range(3):
        part = rates.astype(ml_dtypes.bfloat16)
        parts.append(part)
        rates = rates - part.astype(np.float32)
    parts.append(np.zeros((7, 128), ml_dtypes.bfloat16))
    return jnp.asarray(np.concatenate(parts, axis=0))


def clip_shards(
    planes,
    tokens,
    cotangent,
    adapter_pick,
    positions,
    first_gain,
    first_shift,
    joined_weight,
    joined_bias,
    output_weight,
    mixing_exit_offset,
    second_gain,
    second_shift,
    expand_weight,
    widening_offset,
    reduce_weight,
    shrinking_offset,
    joined_down,
    joined_up,
    output_down,
    output_up,
    expand_down,
    expand_up,
    reduce_down,
    reduce_up,
):
    half = joined_weight.shape[2]
    hidden_half = expand_weight.shape[1]
    rank = joined_up.shape[1]
    turn_last = lambda array: jnp.swapaxes(array, 1, 2)
    tables = (
        turn_last(joined_down), turn_last(expand_down), output_up, reduce_up,
        turn_last(joined_up), turn_last(output_down), expand_up, turn_last(reduce_down),
    )
    (
        x, factors, shared, offsets, w_j, w_o, w_e, w_r, query, key, value, xn1, u1, cosine, sine,
    ) = project(
        planes, tokens, adapter_pick, positions, joined_bias, widening_offset[None], tables,
        jnp.transpose(joined_weight, (1, 0, 2)), output_weight, expand_weight, reduce_weight,
        first_gain[None], first_shift[None], rate_parts(),
    )
    attended, inverse, weights, other_heads, cot, w_o, w_e, w_r = attend(
        planes, query, key, value, cotangent, output_weight, expand_weight, reduce_weight, w_o, w_e, w_r
    )
    out, gh, split, full, grad_att, w_e, w_r = middle(
        planes, x, cot, attended, other_heads, w_o, factors, shared, offsets,
        mixing_exit_offset[None], second_gain[None], second_shift[None], shrinking_offset[None], w_e, w_r,
    )
    adapters = joined_down.shape[0]
    width = tokens.shape[2]
    tag = shared[: rank // 2, 4 * width :]
    own, other, sums, output = attend_back(
        planes, query, key, value, attended, inverse, grad_att, weights, cosine, sine, split, full, tag, out, adapters
    )
    tokens_grad, late_sums = unproject(
        planes, x, gh, xn1, u1, first_gain[None], w_j, factors, shared, own, other, adapters
    )

    def cut(array, *sizes):
        begin, pieces = 0, []
        for size in sizes:
            pieces.append(array[:, :, begin : begin + size])
            begin += size
        return pieces

    s_od, s_eu, s_rd, s_ou, s_ed, s_ru = cut(sums, half, hidden_half, hidden_half, width, width, width)
    s_fu, s_fd = cut(late_sums, 3 * half, width)
    return (
        output,
        tokens_grad,
        turn_last(s_fd),
        s_fu.reshape(adapters, rank, 3, half),
        turn_last(s_od),
        s_ou,
        turn_last(s_ed),
        s_eu,
        turn_last(s_rd),
        s_ru,
    )


def solution(mesh):
    sizes = dict(mesh.shape)
    if sizes["ctx"] == 2 and sizes["tp"] == 2 and sizes["shard"] == 8:
        body = functools.partial(clip_shards, sizes["shard"] // 2)
    else:
        body = general_shards
    return jax.shard_map(
        body,
        mesh=mesh,
        in_specs=(
            P("shard", "ctx", None),
            P("shard", "ctx", None),
            P("shard"),
            P(None, "shard", "ctx"),
            P(),
            P(),
            P("shard", None, "tp"),
            P(None, "tp"),
            P("tp", "shard"),
            P(),
            P(),
            P(),
            P("shard", "tp"),
            P("tp"),
            P("tp", "shard"),
            P(),
            P(),
            P(None, None, None, "tp"),
            P(None, "tp", None),
            P(),
            P(),
            P(None, None, "tp"),
            P(None, "tp", None),
            P(),
        ),
        out_specs=(
            P("shard", "ctx", None),
            P("shard", ("ctx", "tp"), None),
            P(),
            P(None, None, None, "tp"),
            P(None, "tp", None),
            P(),
            P(),
            P(None, None, "tp"),
            P(None, "tp", None),
            P(),
        ),
        check_vma=False,
    )
```

```python
import functools
import math

import jax
import jax.numpy as jnp
import ml_dtypes
import numpy as np
from jax import lax
from jax.experimental import pallas as pl
from jax.experimental.pallas import tpu as pltpu
from jax.sharding import PartitionSpec as P

eps_norm = 1e-06
score_scale = 0.125


def rope_tables(places):
    band = jnp.arange(10, dtype=jnp.float32)
    rates = jnp.exp(band * (-math.log(10000.0) / 10.0))
    angle = places.astype(jnp.float32)[..., None] * rates
    cos_parts = []
    sin_parts = []
    for band_index in range(3):
        cosine = jnp.cos(angle[band_index])
        sine = jnp.sin(angle[band_index])
        cos_parts = cos_parts + [cosine, cosine]
        sin_parts = sin_parts + [-sine, sine]
    rest_shape = angle.shape[1:-1] + (4,)
    cos_parts.append(jnp.ones(rest_shape, jnp.float32))
    sin_parts.append(jnp.zeros(rest_shape, jnp.float32))
    return (jnp.concatenate(cos_parts, -1), jnp.concatenate(sin_parts, -1))


def swap_pairs(values):
    leading = values.shape[:-1]
    turned = values[..., :60].reshape(leading + (3, 2, 10))[..., ::-1, :].reshape(leading + (60,))
    return jnp.concatenate([turned, values[..., 60:]], -1)


def rotate(values, cosine, sine):
    return values * cosine[..., None, :] + swap_pairs(values) * sine[..., None, :]


def rotate_back(grads, cosine, sine):
    return grads * cosine[..., None, :] + swap_pairs(grads * sine[..., None, :])


def norm_forward(values, gain, shift):
    centred = values - jnp.mean(values, -1, keepdims=True)
    inverse = lax.rsqrt(jnp.mean(centred * centred, -1, keepdims=True) + eps_norm)
    scaled = centred * inverse
    return (scaled * gain + shift, scaled, inverse)


def norm_back(grads, scaled, inverse, gain):
    weighted = grads * gain
    return inverse * (
        weighted
        - jnp.mean(weighted, -1, keepdims=True)
        - scaled * jnp.mean(weighted * scaled, -1, keepdims=True)
    )


def select_factor(choose, table):
    return jnp.einsum("ca,a...->c...", choose, table, preferred_element_type=jnp.float32).astype(
        jnp.bfloat16
    )


def gelu_exact(values):
    return jax.nn.gelu(values, approximate=False)


def matrix_product(form, left, right):
    return jnp.einsum(form, left, right, preferred_element_type=jnp.float32)


def general_shards(
    tokens,
    cotangent,
    adapter_pick,
    positions,
    first_gain,
    first_shift,
    joined_weight,
    joined_bias,
    output_weight,
    mixing_exit_offset,
    second_gain,
    second_shift,
    expand_weight,
    widening_offset,
    reduce_weight,
    shrinking_offset,
    joined_down,
    joined_up,
    output_down,
    output_up,
    expand_down,
    expand_up,
    reduce_down,
    reduce_up,
):
    whole_joined, whole_output, whole_expand, whole_reduce = (
        lax.all_gather(joined_weight, "shard", axis=0, tiled=True),
        lax.all_gather(output_weight, "shard", axis=1, tiled=True),
        lax.all_gather(expand_weight, "shard", axis=0, tiled=True),
        lax.all_gather(reduce_weight, "shard", axis=1, tiled=True),
    )
    clip_count, local_len, width = tokens.shape
    local_width = whole_joined.shape[2]
    head_count = local_width // 64
    choose = (
        adapter_pick[:, None] == jnp.arange(joined_down.shape[0], dtype=jnp.int32)[None, :]
    ).astype(jnp.bfloat16)
    select_joined_down = select_factor(choose, joined_down)
    select_joined_up = select_factor(choose, joined_up)
    select_output_down = select_factor(choose, output_down)
    select_output_up = select_factor(choose, output_up)
    select_expand_down = select_factor(choose, expand_down)
    select_expand_up = select_factor(choose, expand_up)
    select_reduce_down = select_factor(choose, reduce_down)
    select_reduce_up = select_factor(choose, reduce_up)
    cosine, sine = rope_tables(positions)
    block_arguments = tokens.astype(jnp.float32)
    norm_one, scaled_one, inverse_one = norm_forward(block_arguments, first_gain, first_shift)
    initial_standardized = norm_one.astype(jnp.bfloat16)
    initial_slim_derivative = matrix_product(
        "zgh,zhe->zge", initial_standardized, select_joined_down
    ).astype(jnp.bfloat16)
    mapped_vectors = (
        matrix_product("cld,dje->clje", initial_standardized, whole_joined)
        + joined_bias
        + matrix_product("uip,upqg->uiqg", initial_slim_derivative, select_joined_up)
    )
    head_shape = (clip_count, local_len, head_count, 64)
    query = rotate(mapped_vectors[:, :, 0].reshape(head_shape), cosine, sine).astype(jnp.bfloat16)
    keys = rotate(mapped_vectors[:, :, 1].reshape(head_shape), cosine, sine).astype(jnp.bfloat16)
    values = mapped_vectors[:, :, 2].reshape(head_shape).astype(jnp.bfloat16)
    stats_shape = (clip_count, head_count, local_len)
    run_max = jnp.full(stats_shape, -1e30, jnp.float32)
    key_part = lax.all_gather(keys, "ctx", axis=1, tiled=True)
    value_part = lax.all_gather(values, "ctx", axis=1, tiled=True)
    scores = matrix_product("cqhd,ckhd->chqk", query, key_part) * score_scale
    new_max = jnp.maximum(run_max, jnp.max(scores, -1))
    weights = jnp.exp(scores - new_max[..., None])
    run_total = jnp.sum(weights, -1)
    update = matrix_product("chqk,ckhd->cqhd", weights.astype(jnp.bfloat16), value_part)
    accum = update
    run_max, run_total, accum = (new_max, run_total, accum)
    log_total = run_max + jnp.log(run_total)
    attended_full = accum / jnp.transpose(run_total, (0, 2, 1))[..., None]
    mixing_outcome = attended_full.reshape(clip_count, local_len, local_width).astype(jnp.bfloat16)
    out_part = matrix_product("cle,ed->cld", mixing_outcome, whole_output)
    rank_partial = matrix_product("fig,fgt->fit", mixing_outcome, select_output_down)
    output_total, rank_sum = (
        lax.psum(out_part.astype(jnp.bfloat16), "tp").astype(jnp.float32),
        lax.psum(rank_partial.astype(jnp.bfloat16), "tp").astype(jnp.float32),
    )
    middle_slim_derivative = rank_sum.astype(jnp.bfloat16)
    first_hidden = (
        block_arguments
        + output_total
        + mixing_exit_offset
        + matrix_product("wnk,wke->wne", middle_slim_derivative, select_output_up)
    )
    norm_two, scaled_two, inverse_two = norm_forward(first_hidden, second_gain, second_shift)
    latter_standardized = norm_two.astype(jnp.bfloat16)
    penultimate_slim_derivative = matrix_product(
        "zgh,zhe->zge", latter_standardized, select_expand_down
    ).astype(jnp.bfloat16)
    skip_stream_vectors = (
        matrix_product("cld,df->clf", latter_standardized, whole_expand)
        + widening_offset
        + matrix_product("uqz,uze->uqe", penultimate_slim_derivative, select_expand_up)
    )
    activity, gelu_pull = jax.vjp(gelu_exact, skip_stream_vectors)
    gaussian_error_unit = activity.astype(jnp.bfloat16)
    mlp_part = matrix_product("clf,fd->cld", gaussian_error_unit, whole_reduce)
    fourth_rank_partial = matrix_product("xpv,xvy->xpy", gaussian_error_unit, select_reduce_down)
    feedforward_sum, rank_four_sum = (
        lax.psum(mlp_part.astype(jnp.bfloat16), "tp").astype(jnp.float32),
        lax.psum(fourth_rank_partial.astype(jnp.bfloat16), "tp").astype(jnp.float32),
    )
    closing_slim_derivative = rank_four_sum.astype(jnp.bfloat16)
    output = (
        first_hidden
        + feedforward_sum
        + shrinking_offset
        + matrix_product("wnk,wke->wne", closing_slim_derivative, select_reduce_up)
    ).astype(jnp.bfloat16)
    back_joined, back_output, back_expand, back_reduce = (
        lax.all_gather(joined_weight, "shard", axis=0, tiled=True),
        lax.all_gather(output_weight, "shard", axis=1, tiled=True),
        lax.all_gather(expand_weight, "shard", axis=0, tiled=True),
        lax.all_gather(reduce_weight, "shard", axis=1, tiled=True),
    )
    reduce_up_term = matrix_product("vkn,vkm->vnm", closing_slim_derivative, cotangent)
    gradient_fourth = matrix_product("abj,awj->abw", cotangent, select_reduce_up).astype(
        jnp.bfloat16
    )
    reduce_down_term = matrix_product("mpg,mpu->mgu", gaussian_error_unit, gradient_fourth)
    grad_active = matrix_product("cld,fd->clf", cotangent, back_reduce) + matrix_product(
        "gez,guz->geu", gradient_fourth, select_reduce_down
    )
    residual_gradient = gelu_pull(grad_active)[0].astype(jnp.bfloat16)
    expand_up_term = matrix_product("jge,jgn->jen", penultimate_slim_derivative, residual_gradient)
    grad_norm_part = matrix_product("clf,df->cld", residual_gradient, back_expand)
    third_gradient_part = matrix_product("aik,adk->aid", residual_gradient, select_expand_up)
    norm_gradient_sum, grad_three_sum = (
        lax.psum(grad_norm_part.astype(jnp.bfloat16), "tp").astype(jnp.float32),
        lax.psum(third_gradient_part.astype(jnp.bfloat16), "tp").astype(jnp.float32),
    )
    gradient_third = grad_three_sum.astype(jnp.bfloat16)
    expand_down_term = matrix_product("kgt,kgh->kth", latter_standardized, gradient_third)
    second_norm_gradient = norm_gradient_sum + matrix_product(
        "jqt,jit->jqi", gradient_third, select_expand_down
    )
    grad_hidden = cotangent.astype(jnp.float32) + norm_back(
        second_norm_gradient, scaled_two, inverse_two, second_gain
    )
    branch_gradient = grad_hidden.astype(jnp.bfloat16)
    output_up_term = matrix_product("vkn,vkm->vnm", middle_slim_derivative, branch_gradient)
    gradient_second = matrix_product("abj,awj->abw", branch_gradient, select_output_up).astype(
        jnp.bfloat16
    )
    output_down_term = matrix_product("nua,nui->nai", mixing_outcome, gradient_second)
    grad_attended = (
        (
            matrix_product("cld,ed->cle", branch_gradient, back_output)
            + matrix_product("gsq,ghq->gsh", gradient_second, select_output_down)
        )
        .astype(jnp.bfloat16)
        .reshape(head_shape)
    )
    key_whole, value_whole = (
        lax.all_gather(keys, "ctx", axis=1, tiled=True),
        lax.all_gather(values, "ctx", axis=1, tiled=True),
    )
    flat_shape = (clip_count, local_len, local_width)

    def clip_back(items):
        query_clip, key_clip, value_clip, grad_clip, total_clip = items
        scores = matrix_product("qhd,khd->hqk", query_clip, key_clip) * score_scale
        probs = jnp.exp(scores - total_clip[..., None])
        grad_probs = matrix_product("qhd,khd->hqk", grad_clip, value_clip)
        middle = jnp.sum(probs * grad_probs, -1, keepdims=True)
        grad_scores = (probs * (grad_probs - middle)).astype(jnp.bfloat16)
        grad_query = matrix_product("hqk,khd->qhd", grad_scores, key_clip) * score_scale
        grad_key = matrix_product("hqk,qhd->khd", grad_scores, query_clip) * score_scale
        grad_value = matrix_product("hqk,qhd->khd", probs.astype(jnp.bfloat16), grad_clip)
        return (grad_query, grad_key, grad_value)

    grad_query, key_terms, value_terms = lax.map(
        clip_back, (query, key_whole, value_whole, grad_attended, log_total)
    )
    full_len = key_whole.shape[1]
    key_sum, value_sum = (
        lax.psum_scatter(
            key_terms.reshape(clip_count, full_len, local_width).astype(jnp.bfloat16),
            "ctx",
            scatter_dimension=1,
            tiled=True,
        ).astype(jnp.float32),
        lax.psum_scatter(
            value_terms.reshape(clip_count, full_len, local_width).astype(jnp.bfloat16),
            "ctx",
            scatter_dimension=1,
            tiled=True,
        ).astype(jnp.float32),
    )
    query_key_value_gradient = jnp.stack(
        [
            rotate_back(grad_query, cosine, sine).reshape(flat_shape),
            rotate_back(key_sum.reshape(head_shape), cosine, sine).reshape(flat_shape),
            value_sum,
        ],
        axis=2,
    ).astype(jnp.bfloat16)
    joined_up_term = matrix_product(
        "pvh,pvfo->phfo", initial_slim_derivative, query_key_value_gradient
    )
    first_gradient_part = matrix_product(
        "kxsd,ktsd->kxt", query_key_value_gradient, select_joined_up
    )
    grad_norm_one_part = matrix_product("clje,dje->cld", query_key_value_gradient, back_joined)
    gradient_first = lax.psum(first_gradient_part.astype(jnp.bfloat16), "tp")
    grad_norm_share = lax.psum_scatter(
        grad_norm_one_part.astype(jnp.bfloat16), "tp", scatter_dimension=1, tiled=True
    ).astype(jnp.float32)
    joined_down_term = matrix_product("kgt,kgh->kth", initial_standardized, gradient_first)
    half_len = grad_norm_share.shape[1]
    begin = lax.axis_index("tp") * half_len

    def shared_rows(array):
        return lax.dynamic_slice_in_dim(array, begin, half_len, 1)

    grad_norm_one = grad_norm_share + matrix_product(
        "jqt,jit->jqi", shared_rows(gradient_first), select_joined_down
    )
    tokens_grad = (
        shared_rows(grad_hidden)
        + norm_back(grad_norm_one, shared_rows(scaled_one), shared_rows(inverse_one), first_gain)
    ).astype(jnp.bfloat16)
    choose_full = choose.astype(jnp.float32)

    def by_adapter(term):
        return jnp.einsum(
            "ca,c...->a...",
            choose_full,
            term,
            precision=lax.Precision.HIGHEST,
            preferred_element_type=jnp.float32,
        )

    summed = lax.psum(
        (
            by_adapter(joined_down_term),
            by_adapter(joined_up_term),
            by_adapter(output_down_term),
            by_adapter(output_up_term),
            by_adapter(expand_down_term),
            by_adapter(expand_up_term),
            by_adapter(reduce_down_term),
            by_adapter(reduce_up_term),
        ),
        ("shard", "ctx"),
    )
    return (
        output,
        tokens_grad,
        summed[0],
        summed[1],
        summed[2],
        summed[3],
        summed[4],
        summed[5],
        summed[6],
        summed[7],
    )


B16 = jnp.bfloat16
F32 = jnp.float32
VMEM_LIMIT = 60 * 2**20
exp_scale = score_scale * math.log2(math.e)


def dot(left, right, left_dim=1, right_dim=0):
    return lax.dot_general(
        left, right, (((left_dim,), (right_dim,)), ((), ())), preferred_element_type=F32
    )


def params():
    return pltpu.CompilerParams(vmem_limit_bytes=VMEM_LIMIT)


def low_lanes():
    return lax.broadcasted_iota(jnp.int32, (1, 128), 1) < 64


def partner(values):
    lane = lax.broadcasted_iota(jnp.int32, (1, 128), 1) % 64 % 20
    return jnp.where(lane < 10, pltpu.roll(values, 118, 1), pltpu.roll(values, 10, 1))


def row_norm(values):
    centred = values - jnp.mean(values, -1, keepdims=True)
    inverse = lax.rsqrt(jnp.mean(centred * centred, -1, keepdims=True) + eps_norm)
    return centred * inverse, inverse


def back_norm(weighted, scaled, inverse):
    return inverse * (
        weighted
        - jnp.mean(weighted, -1, keepdims=True)
        - scaled * jnp.mean(weighted * scaled, -1, keepdims=True)
    )


MESH = pl.DeviceIdType.MESH
HIDDEN_BLOCK = 512
(UP_SENT, DOWN_SENT, Z_CAME, TP_SENT, TP_CAME, OWN_SENT, OWN_CAME, NEXT_SENT, NEXT_CAME) = range(9)


class Place:
    def __init__(self, planes):
        self.planes = planes
        self.shard = lax.axis_index("shard")
        self.z = self.shard // 2
        self.core = self.shard % 2
        self.ctx = lax.axis_index("ctx")
        self.tp = lax.axis_index("tp")
        self.has_up = self.z < planes - 1
        self.has_down = self.z > 0
        self.crosses = self.core != self.ctx
        self.up = {"shard": self.shard + 2}
        self.down = {"shard": self.shard - 2}
        self.next_tp = {"tp": 1 - self.tp}
        self.next_core = {"shard": 2 * self.z + 1 - self.core}
        self.turned = {"shard": 2 * self.z + self.ctx, "ctx": self.core}

    def greet(self, planes_too, turned, ctx_too=False, flipped=False):
        barrier = pltpu.get_barrier_semaphore()
        count = 2

        def signal(device):
            pl.semaphore_signal(barrier, inc=1, device_id=device, device_id_type=MESH)

        signal(self.next_tp)
        signal(self.next_core)
        if planes_too:
            pl.when(self.has_up)(lambda: signal(self.up))
            pl.when(self.has_down)(lambda: signal(self.down))
            count = count + self.has_up.astype(jnp.int32) + self.has_down.astype(jnp.int32)
        if turned:
            pl.when(self.crosses)(lambda: signal(self.turned))
            count = count + self.crosses.astype(jnp.int32)
        if ctx_too:
            signal({"ctx": 1 - self.ctx})
            count = count + 1
        if flipped:
            flip = dict(self.turned)
            flip["tp"] = 1 - self.tp
            pl.when(self.crosses)(lambda: signal(flip))
            count = count + self.crosses.astype(jnp.int32)
        pl.semaphore_wait(barrier, count)


class Flow:
    def __init__(self, at, own, slot, sems, kinds=tuple(range(9))):
        self.at, self.own, self.slot = at, own, slot
        self.sems = {kind: sems[i] for i, kind in enumerate(kinds)}

    def copy(self, kind, plane, own=False):
        at = self.at
        half = 1 - at.tp if kind == NEXT_SENT else at.tp
        piece = self.slot(2 * plane + at.core, half)
        device, came = {
            UP_SENT: (at.up, Z_CAME),
            DOWN_SENT: (at.down, Z_CAME),
            TP_SENT: (at.next_tp, TP_CAME),
            OWN_SENT: (at.next_core, OWN_CAME),
            NEXT_SENT: (at.next_core, NEXT_CAME),
        }[kind]
        return pltpu.make_async_remote_copy(
            src_ref=self.own if own else piece,
            dst_ref=piece,
            send_sem=self.sems[kind].at[plane],
            recv_sem=self.sems[came].at[plane],
            device_id=device,
            device_id_type=MESH,
        )

    def came(self, kind, plane):
        at = self.at
        shard = 2 * plane + (at.core if kind in (Z_CAME, TP_CAME) else 1 - at.core)
        half = at.tp if kind in (Z_CAME, OWN_CAME) else 1 - at.tp
        piece = self.slot(shard, half)
        return pltpu.make_async_remote_copy(
            src_ref=piece, dst_ref=piece, send_sem=self.sems[kind].at[plane],
            recv_sem=self.sems[kind].at[plane], device_id=at.next_core, device_id_type=MESH,
        )

    def pieces(self, distance):
        at = self.at
        if distance == 0:
            return [(None, at.z, True, True)]
        return [
            (at.z >= distance, at.z - distance, True, False),
            (at.z < at.planes - distance, at.z + distance, False, True),
        ]

    def each(self, distance, act):
        for there, plane, below, above in self.pieces(distance):
            if there is None:
                act(plane, below, above)
            else:
                pl.when(there)(functools.partial(act, plane, below, above))

    def pass_on(self, distance, z=False, tp=False, core=False, fresh=None, wait=False):
        own = (distance == 0) if fresh is None else fresh

        def act(plane, below, above):
            if wait:
                self.came(Z_CAME, plane).wait_recv()
            if z:
                if below:
                    pl.when(self.at.has_up)(lambda: self.copy(UP_SENT, plane, own).start())
                if above:
                    pl.when(self.at.has_down)(lambda: self.copy(DOWN_SENT, plane, own).start())
            if tp:
                self.copy(TP_SENT, plane, own).start()
            if core:
                self.copy(OWN_SENT, plane, own).start()

        self.each(distance, act)

    def sent(self, distance, z=False, tp=False, core=False):
        def act(plane, below, above):
            if z:
                if below:
                    pl.when(self.at.has_up)(lambda: self.copy(UP_SENT, plane).wait_send())
                if above:
                    pl.when(self.at.has_down)(lambda: self.copy(DOWN_SENT, plane).wait_send())
            if tp:
                self.copy(TP_SENT, plane).wait_send()
            if core:
                self.copy(OWN_SENT, plane).wait_send()

        self.each(distance, act)

    def wait(self, kind, distance):
        self.each(distance, lambda plane, below, above: self.came(kind, plane).wait_recv())

    def pass_next(self, distance, wait=True):
        def act(plane, below, above):
            if wait:
                self.came(TP_CAME, plane).wait_recv()
            self.copy(NEXT_SENT, plane).start()

        self.each(distance, act)

    def sent_next(self, distance):
        self.each(distance, lambda plane, below, above: self.copy(NEXT_SENT, plane).wait_send())


ALONG_Z = (UP_SENT, DOWN_SENT, Z_CAME)
TO_TP = (TP_SENT, TP_CAME)
TO_CORE = (OWN_SENT, OWN_CAME)
TO_NEXT = (NEXT_SENT, NEXT_CAME)
EVERY = ALONG_Z + TO_TP + TO_CORE + TO_NEXT


class Rows:
    def __init__(self, sems):
        self.sems, self.used = sems, 0

    def take(self, kinds):
        rows = [self.sems.at[self.used + i] for i in range(len(kinds))]
        self.used += len(kinds)
        return rows


def block_flows(at, own_e, own_r, full_e, full_r, rows, kinds):
    flows = []
    for block, needs in enumerate(kinds):
        span = pl.ds(block * HIDDEN_BLOCK, HIDDEN_BLOCK)
        flows.append(
            [
                Flow(
                    at, None if own_e is None else own_e.at[:, span],
                    lambda s, h, span=span: full_e.at[s, h, :, span], rows.take(needs), needs,
                ),
                Flow(
                    at, None if own_r is None else own_r.at[span, :],
                    lambda s, h, span=span: full_r.at[s, h, span, :], rows.take(needs), needs,
                ),
            ]
        )
    return flows


def count_rows(first, kinds):
    return len(first) + 2 * sum(len(needs) for needs in kinds)


PROJECT_KINDS = (ALONG_Z, ALONG_Z)
ATTEND_KINDS = (EVERY, ALONG_Z + TO_TP + TO_CORE, ALONG_Z + TO_CORE, ALONG_Z)
MIDDLE_KINDS = ((), TO_NEXT, TO_TP + TO_NEXT, EVERY)


def turned_copy(at, source, target, sems):
    return pltpu.make_async_remote_copy(
        src_ref=source, dst_ref=target, send_sem=sems.at[0], recv_sem=sems.at[1],
        device_id=at.turned, device_id_type=MESH,
    )


class Spread:
    def __init__(self, at, split, full, tag, sums, give, take, pass_tp, stack, beyond, sems):
        self.at, self.split, self.full, self.tag, self.sums = at, split, full, tag, sums
        self.give, self.take, self.pass_tp, self.stack, self.beyond, self.sems = (
            give, take, pass_tp, stack, beyond, sems,
        )
        self.ranks = give.shape[0]
        self.width = split.shape[2]
        self.rest = full.shape[1]

    def remote(self, source, target, index, device):
        return pltpu.make_async_remote_copy(
            src_ref=source, dst_ref=target, send_sem=self.sems.at[0, index], recv_sem=self.sems.at[1, index],
            device_id=device, device_id_type=MESH,
        )

    def between_cores(self):
        return self.remote(self.give, self.take, 0, self.at.next_core)

    def to_tp(self):
        return self.remote(self.pass_tp, self.stack.at[self.at.z, 1], 1, self.at.next_tp)

    def to_ctx(self):
        plane = self.stack.at[self.at.z]
        return self.remote(plane.at[pl.ds(0, 2)], plane.at[pl.ds(2, 2)], 2, {"ctx": 1 - self.at.ctx})

    def along(self, up, plane):
        piece = self.stack.at[plane]
        return pltpu.make_async_remote_copy(
            src_ref=piece, dst_ref=piece, send_sem=self.sems.at[2 + up, plane], recv_sem=self.sems.at[4, plane],
            device_id=self.at.up if up else self.at.down, device_id_type=MESH,
        )

    def over(self, plane):
        return pltpu.make_async_remote_copy(
            src_ref=self.stack.at[plane], dst_ref=self.beyond.at[plane],
            send_sem=self.sems.at[5, plane], recv_sem=self.sems.at[6, plane],
            device_id=self.at.next_core, device_id_type=MESH,
        )

    def rows(self, core):
        return pl.ds(pl.multiple_of(core * self.ranks, self.ranks), self.ranks)

    def start(self):
        theirs = self.rows(1 - self.at.core)
        for half in range(2):
            self.give[:, half * self.width : (half + 1) * self.width] = self.split[half, theirs, :].astype(B16)
        self.give[:, 2 * self.width :] = self.full[theirs, :].astype(B16)
        self.between_cores().start()

    def second(self):
        at, width, rest = self.at, self.width, self.rest
        self.between_cores().wait_recv()
        mine = self.rows(at.core)
        for half, target in ((at.tp, self.stack.at[at.z, 0]), (1 - at.tp, self.pass_tp)):
            span = pl.ds(pl.multiple_of(half * width, 128), width)
            target[:, 0:width] = (self.split[half, mine, :] + self.take[:, span].astype(F32)).astype(B16)
            target[:, width : width + rest] = (
                self.full[mine, :] + self.take[:, 2 * width :].astype(F32)
            ).astype(B16)
            target[:, width + rest :] = self.tag
        self.to_tp().start()

    def third(self):
        self.to_tp().wait_recv()
        self.to_ctx().start()

    def both_ways(self, act_up, act_down, distance):
        at = self.at
        if distance == 0:
            pl.when(at.has_up)(functools.partial(act_up, at.z))
            pl.when(at.has_down)(functools.partial(act_down, at.z))
        else:
            pl.when((at.z >= distance) & at.has_up)(functools.partial(act_up, at.z - distance))
            pl.when((at.z < at.planes - distance) & at.has_down)(functools.partial(act_down, at.z + distance))

    def came(self, distance, act):
        at = self.at
        pl.when(at.z >= distance)(functools.partial(act, at.z - distance))
        pl.when(at.z < at.planes - distance)(functools.partial(act, at.z + distance))

    def planes(self, distance):
        if distance == 0:
            self.to_ctx().wait_recv()
        else:
            self.came(distance, lambda plane: self.along(1, plane).wait_recv())
        if distance < self.at.planes - 1:
            self.both_ways(
                lambda plane: self.along(1, plane).start(), lambda plane: self.along(0, plane).start(), distance
            )
        if distance == 0:
            self.over(self.at.z).start()
        else:
            self.came(distance, lambda plane: self.over(plane).start())

    def finish(self):
        at = self.at
        for plane in range(at.planes):
            self.over(plane).wait_recv()
        keep = self.width + self.rest
        adapters, ranks = self.sums.shape[0], self.ranks
        terms = at.planes * 4 * ranks
        lane = lax.broadcasted_iota(jnp.int32, (terms, 128), 1)
        rank_of = lax.broadcasted_iota(jnp.int32, (terms, 128), 0) % ranks
        for source, core in ((self.stack, at.core), (self.beyond, 1 - at.core)):
            tags = source[:, :, :, keep:].reshape(terms, 128).astype(F32)
            picks = (tags == (lane // ranks).astype(F32)) & (lane % ranks == rank_of)
            choose = jnp.where(picks, 1.0, 0.0).astype(B16)
            for begin in range(0, keep, 512):
                span = pl.ds(begin, min(512, keep - begin))
                total = dot(choose, source[:, :, :, span].reshape(terms, -1), 0, 0)
                for adapter in range(adapters):
                    self.sums[adapter, self.rows(core), span] = total[adapter * ranks : (adapter + 1) * ranks]

    def sent(self):
        self.between_cores().wait_send()
        self.to_tp().wait_send()
        self.to_ctx().wait_send()
        for distance in range(self.at.planes - 1):
            self.both_ways(
                lambda plane: self.along(1, plane).wait_send(),
                lambda plane: self.along(0, plane).wait_send(),
                distance,
            )
        for plane in range(self.at.planes):
            self.over(plane).wait_send()

    @staticmethod
    def scratch(planes, ranks, width, rest):
        wide = width + rest + 128
        return [
            pltpu.VMEM((ranks, 2 * width + rest), B16),
            pltpu.VMEM((ranks, 2 * width + rest), B16),
            pltpu.VMEM((ranks, wide), B16),
            pltpu.VMEM((planes, 4, ranks, wide), B16),
            pltpu.VMEM((planes, 4, ranks, wide), B16),
            pltpu.SemaphoreType.DMA((7, max(planes, 4))),
        ]


ROWS = 256


def project_body(
    planes, blocks,
    tokens_ref, pick_ref, places_ref, bias_ref, wide_ref,
    tab_jd, tab_ed, tab_ou, tab_ru, tab_ju, tab_od, tab_eu, tab_rd,
    w_ref, own_o, own_e, own_r, gain_ref, shift_ref, rates_ref,
    x_out, factors_out, shared_out, offsets_out, w_out, full_o, full_e, full_r,
    q_out, k_out, v_out, xn_out, u_out, cos_out, sin_out,
    spots_ref, offsets_ref, factors_ref, factors_next, shared_ref,
    vm_jd, vm_ed, vm_ou, vm_ru, vm_ju, vm_od, vm_eu, vm_rd,
    x_vm, w_vm, acc, stage, spots_all, factors_vm, offsets_vm, jd_vm,
    w_sems, flow_sems, x_sems, spot_sems, factor_sems, shared_sems, offset_sems, local_sems, out_sems, move_sems, table_sems,
):
    at = Place(planes)
    rows_all, width = x_vm.shape
    depth, half = w_ref.shape[1:]
    at.greet(True, True)
    chunks = rows_all // ROWS
    parts = [
        Flow(
            at, w_ref.at[part], lambda s, h, part=part: w_out.at[s, h, part],
            [w_sems.at[part, kind] for kind in range(9)],
        )
        for part in range(3)
    ]
    taken = Rows(flow_sems)
    flow_o = Flow(at, own_o, lambda s, h: full_o.at[s, h], taken.take(ALONG_Z), ALONG_Z)
    flows = block_flows(at, own_e, own_r, full_e, full_r, taken, PROJECT_KINDS)
    ahead = [flow_o] + flows[0] + flows[1]
    holds = at.core == at.ctx

    def local(source, target, index):
        return pltpu.make_async_copy(source, target, local_sems.at[index])

    for flow in parts:
        flow.pass_on(0, z=True, tp=True)
    tables_in = [
        pltpu.make_async_copy(source, target, table_sems.at[i])
        for i, (source, target) in enumerate(
            (
                (tab_jd, vm_jd), (tab_ed, vm_ed), (tab_ou, vm_ou), (tab_ru, vm_ru),
                (tab_ju, vm_ju), (tab_od, vm_od), (tab_eu, vm_eu), (tab_rd, vm_rd),
            )
        )
    ]
    for table in tables_in:
        table.start()
    place_rows = [places_ref[band, pl.ds(at.tp, 1), :].astype(F32) for band in range(3)]
    spots_ref[...] = jnp.concatenate(
        place_rows * 3 + [jnp.zeros((spots_ref.shape[0] - 9, rows_all), F32)], axis=0
    ).astype(B16)
    for part in range(3):
        offsets_ref[:, part * half : (part + 1) * half] = bias_ref[part : part + 1, :]
    offsets_ref[:, 3 * half :] = wide_ref[...]

    def x_chunk(i):
        span = pl.ds(i * ROWS, ROWS)
        return turned_copy(at, tokens_ref.at[at.tp, span], x_vm.at[span], x_sems.at[i])

    spot_copy = turned_copy(at, spots_ref, spots_all.at[0], spot_sems.at[0])

    @pl.when(at.crosses)
    def _():
        spot_copy.start()
        for i in range(chunks):
            x_chunk(i).start()

    @pl.when(holds)
    def _():
        spots_all[0] = spots_ref[...]
        for i in range(chunks):
            span = pl.ds(i * ROWS, ROWS)
            local(tokens_ref.at[at.tp, span], x_vm.at[span], 1 + i).start()

    for flow in parts:
        flow.pass_on(0, core=True)

    def remote(source, target, sems, device):
        return pltpu.make_async_remote_copy(
            src_ref=source, dst_ref=target, send_sem=sems.at[0], recv_sem=sems.at[1],
            device_id=device, device_id_type=MESH,
        )

    offset_copy = remote(offsets_ref, offsets_out.at[at.tp], offset_sems, at.next_tp)
    offset_came = remote(offsets_ref, offsets_out.at[1 - at.tp], offset_sems, at.next_tp)
    offset_copy.start()
    local(offsets_ref, offsets_out.at[at.tp], 1 + chunks).start()
    next_copy = remote(factors_next, factors_out.at[at.tp], factor_sems.at[0], at.next_tp)
    next_came = remote(factors_next, factors_out.at[1 - at.tp], factor_sems.at[0], at.next_tp)
    own_factors = remote(factors_ref, factors_out.at[at.tp], factor_sems.at[1], at.next_core)
    shared_copy = remote(shared_ref, shared_out, shared_sems, at.next_core)
    next_factors = remote(factors_out.at[1 - at.tp], factors_out.at[1 - at.tp], factor_sems.at[2], at.next_core)

    local(w_ref, w_out.at[at.shard, at.tp], 4 + chunks).start()
    local(own_o, full_o.at[at.shard, at.tp], 5 + chunks).start()
    local(own_e, full_e.at[at.shard, at.tp], 6 + chunks).start()
    local(own_r, full_r.at[at.shard, at.tp], 7 + chunks).start()

    @pl.when(at.crosses)
    def _():
        spot_copy.wait_recv()

    spot_next = remote(spots_all.at[0], spots_all.at[1], spot_sems.at[1], at.next_core)
    spot_next.start()

    lane = lax.broadcasted_iota(jnp.int32, (1, 128), 1) % 64
    turned = lane < 60
    early = lane % 20 < 10

    def tables(part):
        def body(i, carry):
            span = pl.ds(pl.multiple_of(i * ROWS, ROWS), ROWS)
            angle = dot(spots_all[part, :, span], rates_ref[...], 0, 0)
            out = pl.ds(pl.multiple_of(part * rows_all + i * ROWS, ROWS), ROWS)
            cos_out[out, :] = jnp.where(turned, jnp.cos(angle), 1.0)
            sine = jnp.sin(angle)
            sin_out[out, :] = jnp.where(turned, jnp.where(early, -sine, sine), 0.0)
            return carry

        lax.fori_loop(0, chunks, body, 0)

    tables(0)

    for table in tables_in:
        table.wait()

    def chosen(table, pick):
        return sum(
            table[i].astype(F32) * jnp.where(pick == i, 1.0, 0.0) for i in range(table.shape[0])
        ).astype(B16)

    picks = (pick_ref[0], pick_ref[1])
    pick = jnp.where(at.tp == 0, picks[0], picks[1])
    for target, which in ((factors_ref, pick), (factors_next, picks[0] + picks[1] - pick)):
        ju = chosen(vm_ju, which)
        for part in range(3):
            target[:, part * half : (part + 1) * half] = ju[part]
        begin = 3 * half
        for table in (vm_od, vm_eu, vm_rd):
            target[:, begin : begin + table.shape[2]] = chosen(table, which)
            begin += table.shape[2]
    for i, table in enumerate((vm_jd, vm_ed, vm_ou, vm_ru)):
        shared_ref[:, i * width : (i + 1) * width] = chosen(table, pick)
    shared_ref[:, 4 * width :] = jnp.full((shared_ref.shape[0], 128), pick.astype(F32)).astype(B16)

    @pl.when(holds)
    def _():
        next_copy.start()
        own_factors.start()
        shared_copy.start()
        local(factors_ref, factors_out.at[at.tp], 2 + chunks).start()
        local(shared_ref, shared_out, 3 + chunks).start()

    for flow in parts:
        flow.pass_on(1, z=True, tp=True, core=True, wait=True)
    spot_next.wait()
    tables(1)

    @pl.when(holds)
    def _():
        next_came.wait_recv()
        next_factors.start()

    for flow in parts:
        flow.pass_on(2, z=True, tp=True, core=True, wait=True)

    @pl.when(holds)
    def _():
        local(factors_ref, factors_out.at[at.tp], 2 + chunks).wait()
        local(shared_ref, shared_out, 3 + chunks).wait()
        own_factors.wait_send()
        shared_copy.wait_send()
        next_copy.wait_send()
        next_factors.wait_send()

    @pl.when(at.crosses)
    def _():
        own_factors.wait_recv()
        shared_copy.wait_recv()
        remote(factors_out.at[1 - at.tp], factors_out.at[1 - at.tp], factor_sems.at[2], at.next_core).wait_recv()

    offset_copy.wait_send()
    offset_came.wait_recv()
    local(offsets_ref, offsets_out.at[at.tp], 1 + chunks).wait()
    loads = [
        pltpu.make_async_copy(factors_out, factors_vm, out_sems.at[0]),
        pltpu.make_async_copy(offsets_out, offsets_vm, out_sems.at[1]),
        pltpu.make_async_copy(shared_out.at[:, pl.ds(0, width)], jd_vm, out_sems.at[2]),
    ]
    for load in loads:
        load.start()
    for load in loads:
        load.wait()

    kept = []

    def x_ready(i):
        span = pl.ds(i * ROWS, ROWS)

        @pl.when(at.crosses)
        def _():
            x_chunk(i).wait()

        @pl.when(holds)
        def _():
            local(tokens_ref.at[at.tp, span], x_vm.at[span], 1 + i).wait()

        keep = pltpu.make_async_copy(x_vm.at[span], x_out.at[span], x_sems.at[i, 2])
        keep.start()
        kept.append(keep)
        scaled, _ = row_norm(x_vm[span, :].astype(F32))
        xn = (scaled * gain_ref[...] + shift_ref[...]).astype(B16)
        xn_out[span, :] = xn
        u_out[span, :] = dot(xn, jd_vm[...], 1, 1).astype(B16)

    outs = (q_out, k_out, v_out)
    sending = []
    orders = ((0, 1, 2, 3), (1, 0, 2, 3), (2, 3, 1, 0), (3, 2, 1, 0))

    def plane_at(turn):
        plane = jnp.int32(orders[0][turn])
        for z in range(1, planes):
            plane = jnp.where(at.z == z, orders[z][turn], plane)
        return plane

    def to_next(turn):
        for flow in parts:
            flow.came(TP_CAME, plane_at(turn)).wait_recv()
            flow.copy(NEXT_SENT, plane_at(turn)).start()

    def w_load(turn):
        shards_of = pl.ds(2 * plane_at(turn), 2)
        return pltpu.make_async_copy(w_out.at[shards_of], w_vm.at[turn], out_sems.at[turn])

    def take_plane(turn):
        for flow in parts:
            flow.came(OWN_CAME, plane_at(turn)).wait_recv()
            flow.came(NEXT_CAME, plane_at(turn)).wait_recv()
        w_load(turn).start()

    def columns_of(turn):
        return pl.ds(pl.multiple_of(plane_at(turn) * 2 * depth, 2 * depth), 2 * depth)

    wide = rows_all // 2

    def product(turns, owner, part, span):
        value = 0.0
        for turn in turns:
            w = w_vm[turn, :, owner, part].reshape(2 * depth, half)
            value += dot(xn_out[span, columns_of(turn)], w)
        return value

    owners = (1 - at.core, at.core)

    def add_first(turns):
        for order, owner in enumerate(owners):
            for part in range(3):
                for begin in range(0, rows_all, wide):
                    span = pl.ds(begin, wide)
                    acc[order, part, span, :] = product(turns, owner, part, span)

    def add_last(turn):
        for order, owner in enumerate(owners):
            for part in range(3):
                bias = offsets_vm[owner, :, part * half : (part + 1) * half]
                up = factors_vm[owner, :, part * half : (part + 1) * half]
                for begin in range(0, rows_all, wide):
                    span = pl.ds(begin, wide)
                    value = acc[order, part, span, :] + bias + product((turn,), owner, part, span)
                    value += dot(u_out[span, :], up)
                    if part == 2:
                        stage[order, part, span, :] = value.astype(B16)
                        continue
                    for col in range(0, half, 128):
                        piece = value[:, col : col + 128]
                        stage[order, part, span, col : col + 128] = (
                            piece * cos_out[span, :] + partner(piece) * sin_out[span, :]
                        ).astype(B16)
                if order == 0:
                    move = remote(
                        stage.at[order, part], outs[part].at[pl.ds(rows_all, rows_all)],
                        move_sems.at[part], at.next_core,
                    )
                else:
                    move = pltpu.make_async_copy(
                        stage.at[order, part], outs[part].at[pl.ds(0, rows_all)], out_sems.at[4 + part]
                    )
                move.start()
                sending.append(move)

    to_next(0)
    to_next(1)
    for i in range(chunks):
        x_ready(i)
    for flow in parts:
        flow.pass_on(3, tp=True, core=True, wait=True)
    for other in ahead:
        other.pass_on(0, z=True)
    local(w_ref, w_out.at[at.shard, at.tp], 4 + chunks).wait()
    take_plane(0)
    take_plane(1)
    to_next(2)
    take_plane(2)
    for turn in range(3):
        w_load(turn).wait()
    add_first((0, 1, 2))
    to_next(3)
    take_plane(3)
    w_load(3).wait()
    add_last(3)

    for keep in kept:
        keep.wait()
    for other in ahead:
        other.wait(Z_CAME, 1)
        other.sent(0, z=True)
    for flow in parts:
        for far in range(planes):
            flow.sent(far, z=far < planes - 1, tp=True, core=True)
            flow.sent_next(far)
    for i in range(3):
        local((own_o, own_e, own_r)[i], (full_o, full_e, full_r)[i].at[at.shard, at.tp], 5 + i + chunks).wait()

    @pl.when(at.crosses)
    def _():
        spot_copy.wait_send()

    for move in sending:
        move.wait()


def project(planes, tokens, picks, places, bias, wide, tables, weight, own_o, own_e, own_r, gain, shift, rates):
    rows, width = tokens.shape[1:]
    _, depth, half = weight.shape
    rank = tables[0].shape[1]
    blocks = own_e.shape[1] // HIDDEN_BLOCK
    chunks = rows // ROWS
    shape = jax.ShapeDtypeStruct
    hbm = pl.BlockSpec(memory_space=pl.ANY)
    vmem = pl.BlockSpec(memory_space=pltpu.VMEM)
    smem = pl.BlockSpec(memory_space=pltpu.SMEM)
    dma = pltpu.SemaphoreType.DMA
    factors = shape((rank, 3 * half + sum(table.shape[2] for table in tables[5:])), B16)
    shared = shape((rank, 4 * width + 128), B16)
    offsets = shape((1, 3 * half + wide.shape[1]), F32)
    spots = shape(rates.shape[:1] + (rows,), B16)
    return pl.pallas_call(
        functools.partial(project_body, planes, blocks),
        in_specs=[hbm, smem] + [vmem] * 3 + [hbm] * 8 + [vmem] * 7,
        out_specs=[hbm] * 11 + [vmem] * 4,
        out_shape=[
            shape((rows, width), B16),
            shape((2,) + factors.shape, B16),
            shape(shared.shape, B16),
            shape((2,) + offsets.shape, F32),
            shape((2 * planes, 2) + weight.shape, B16),
            shape((2 * planes, 2) + own_o.shape, B16),
            shape((2 * planes, 2) + own_e.shape, B16),
            shape((2 * planes, 2) + own_r.shape, B16),
            shape((2 * rows, half), B16),
            shape((2 * rows, half), B16),
            shape((2 * rows, half), B16),
            shape((rows, width), B16),
            shape((rows, rank), B16),
            shape((2 * rows, 128), F32),
            shape((2 * rows, 128), F32),
        ],
        scratch_shapes=[
            pltpu.VMEM(spots.shape, B16),
            pltpu.VMEM(offsets.shape, F32),
            pltpu.VMEM(factors.shape, B16),
            pltpu.VMEM(factors.shape, B16),
            pltpu.VMEM(shared.shape, B16),
        ]
        + [pltpu.VMEM(table.shape, B16) for table in tables]
        + [
            pltpu.VMEM((rows, width), B16),
            pltpu.VMEM((planes, 2, 2) + weight.shape, B16),
            pltpu.VMEM((2, 3, rows, half), F32),
            pltpu.VMEM((2, 3, rows, half), B16),
            pltpu.VMEM((2,) + spots.shape, B16),
            pltpu.VMEM((2,) + factors.shape, B16),
            pltpu.VMEM((2,) + offsets.shape, F32),
            pltpu.VMEM((rank, width), B16),
            dma((3, 9, planes)),
            dma((count_rows(ALONG_Z, PROJECT_KINDS), planes)),
            dma((chunks, 3)),
            dma((2, 2)),
            dma((3, 2)),
            dma((2,)),
            dma((2,)),
            dma((8 + chunks,)),
            dma((7,)),
            dma((3, 2)),
            dma((8,)),
        ],
        compiler_params=pltpu.CompilerParams(
            vmem_limit_bytes=VMEM_LIMIT, collective_id=0, has_side_effects=True
        ),
        cost_estimate=pl.CostEstimate(
            flops=2 * rows * width * 6 * half, bytes_accessed=100 * 2**20, transcendentals=0
        ),
    )(tokens, picks, places, bias, wide, *tables, weight, own_o, own_e, own_r, gain, shift, rates)


def attend_body(
    planes, blocks,
    q_ref, k_ref, v_ref, cot_ref, own_o, own_e, own_r, in_o, in_e, in_r,
    o_ref, inv_ref, e_ref, o_next, cot_out, full_o, full_e, full_r,
    vm_ref, stage, cot_vm, flow_sems, stage_sems, cot_sems,
):
    at = Place(planes)
    rows_all, length = q_ref.shape[0], k_ref.shape[0]
    low = low_lanes()
    pair, turn = pl.program_id(0), pl.program_id(1)
    turns = length // rows_all
    now = pair * turns + turn
    pairs = stage.shape[0] // (turns // 2)
    count = pairs * turns
    taken = Rows(flow_sems)
    flow_o = Flow(at, own_o, lambda s, h: full_o.at[s, h], taken.take(EVERY), EVERY)
    flows = block_flows(at, own_e, own_r, full_e, full_r, taken, ATTEND_KINDS)
    zero = [flow_o] + flows[0]
    last = planes - 1
    cot_move = turned_copy(at, cot_ref.at[at.tp], cot_out, cot_sems)
    cot_load = pltpu.make_async_copy(cot_ref.at[at.tp], cot_vm, cot_sems.at[2])
    cot_keep = pltpu.make_async_copy(cot_vm, cot_out, cot_sems.at[3])

    def when(step, act):
        pl.when(now == min(step * count // 16, count - 1))(act)

    @pl.when(now == 0)
    def _():
        at.greet(True, True)
        for flow in zero:
            flow.pass_on(1, z=True)
            flow.pass_on(0, tp=True)
        pl.when(at.crosses)(lambda: cot_move.start())
        pl.when(jnp.logical_not(at.crosses))(lambda: cot_load.start())
        for flow in zero:
            flow.pass_on(0, core=True)
            flow.pass_on(1, core=True)
        for flow in flows[1] + flows[2]:
            flow.pass_on(0, core=True)

    def at_2():
        for flow in flows[1]:
            flow.pass_on(1, z=True, core=True)
        for flow in zero:
            flow.pass_on(1, tp=True)

    def at_3():
        @pl.when(jnp.logical_not(at.crosses))
        def _():
            cot_load.wait()
            cot_keep.start()

    def at_4():
        for flow in zero:
            flow.pass_on(2, z=True, tp=True, core=True, wait=True)

    def at_5():
        for flow in zero:
            flow.pass_next(0)

    def at_6():
        for flow in flows[1]:
            flow.pass_on(2, z=True, core=True, wait=True)
        for flow in flows[2]:
            flow.pass_on(0, z=True)

    def at_8():
        for flow in zero:
            flow.pass_on(3, tp=True, core=True, wait=True)

    def at_9():
        for flow in zero:
            flow.pass_next(1)
        for flow in flows[1]:
            flow.pass_on(0, tp=True)
            flow.pass_on(1, tp=True)

    def at_10():
        for flow in flows[2]:
            flow.pass_on(1, z=True, core=True, wait=True)
        for flow in flows[1]:
            flow.pass_on(3, core=True, wait=True)

    def at_12():
        for flow in flows[2]:
            flow.pass_on(2, z=True, core=True, wait=True)
        for flow in flows[3]:
            flow.pass_on(0, z=True)
        for flow in flows[1]:
            flow.pass_on(2, tp=True)
            flow.pass_on(3, tp=True)
        for flow in zero:
            flow.pass_next(2)
            flow.pass_next(3)

    def at_15():
        for flow in flows[2]:
            flow.pass_on(3, core=True, wait=True)

    for step, act in (
        (2, at_2), (3, at_3), (4, at_4), (5, at_5), (6, at_6), (8, at_8), (9, at_9), (10, at_10),
        (12, at_12), (15, at_15),
    ):
        when(step, act)

    @pl.when(turn == 0)
    def _():
        vm_ref[0] = jnp.where(low, v_ref[...], 1).astype(B16)
        vm_ref[1] = jnp.where(low, 1, v_ref[...]).astype(B16)

    step = min(256, rows_all)
    for begin in range(0, rows_all, step):
        rows = pl.ds(begin, step)
        q = q_ref[rows, :]
        sums = []
        for head in range(2):
            mine = low if head == 0 else ~low
            scores = dot(jnp.where(mine, q, 0).astype(B16), k_ref[...], 1, 1)
            top = jnp.max(scores, 1, keepdims=True)
            weights = jnp.exp2((scores - top) * exp_scale).astype(B16)
            e_ref[head, rows, :] = weights
            sums.append(dot(weights, vm_ref[head]))
        total = pltpu.roll(jnp.where(low, sums[1], sums[0]), 64, 1)
        inverse = 1.0 / total
        o_ref[rows, :] = (jnp.where(low, sums[0], sums[1]) * inverse).astype(B16)
        inv_ref[rows, :] = inverse

    def o_move(index):
        per = turns // 2
        rows = pl.ds(pl.multiple_of(index % per * rows_all, rows_all), rows_all)
        columns = pl.ds(pl.multiple_of(index // per * 128, 128), 128)
        return pltpu.make_async_remote_copy(
            src_ref=stage.at[index], dst_ref=o_next.at[rows, columns],
            send_sem=stage_sems.at[0, index], recv_sem=stage_sems.at[1, index],
            device_id=at.next_core, device_id_type=MESH,
        )

    @pl.when(turn >= turns // 2)
    def _():
        index = pair * (turns // 2) + turn - turns // 2
        stage[index] = o_ref[...]
        o_move(index).start()

    @pl.when(now == count - 1)
    def _():
        for flow in flows[3]:
            flow.wait(Z_CAME, 1)
        for flow in zero + flows[1] + flows[2]:
            for far in range(planes):
                flow.wait(OWN_CAME, far)
        for flow in zero:
            for far in range(planes):
                flow.wait(NEXT_CAME, far)
                flow.sent_next(far)
        for flow in flows[1]:
            for far in range(planes):
                flow.wait(TP_CAME, far)
        for flow in zero + flows[1]:
            for far in range(planes):
                flow.sent(far, z=0 < far < last, tp=True, core=True)
        for flow in flows[2]:
            for far in range(planes):
                flow.sent(far, z=far < last, core=True)
        for flow in flows[3]:
            flow.sent(0, z=True)

        @pl.when(at.crosses)
        def _():
            cot_move.wait()

        @pl.when(jnp.logical_not(at.crosses))
        def _():
            cot_keep.wait()

        for index in range(count // 2):
            o_move(index).wait()


def attend(planes, query, key, value, cotangent, own_o, own_e, own_r, full_o, full_e, full_r):
    length, width = query.shape
    block = min(512, length // 2)
    blocks = own_e.shape[1] // HIDDEN_BLOCK
    turns = length // block
    pairs = width // 128
    rows = pl.BlockSpec((block, 128), lambda p, i: (i, p))
    full = pl.BlockSpec((length, 128), lambda p, i: (0, p))
    hbm = pl.BlockSpec(memory_space=pl.ANY)
    shape = jax.ShapeDtypeStruct
    like = lambda array: shape(array.shape, array.dtype)
    dma = pltpu.SemaphoreType.DMA
    return pl.pallas_call(
        functools.partial(attend_body, planes, blocks),
        grid=(pairs, turns),
        in_specs=[rows, full, full] + [hbm] * 7,
        out_specs=[rows, rows, pl.BlockSpec((2, block, length), lambda p, i: (p, i, 0))] + [hbm] * 5,
        out_shape=[
            shape((length, width), B16),
            shape((length, width), F32),
            shape((width // 64, length, length), B16),
            shape((length // 2, width), B16),
            shape(cotangent.shape[1:], B16),
            like(full_o), like(full_e), like(full_r),
        ],
        input_output_aliases={7: 5, 8: 6, 9: 7},
        scratch_shapes=[
            pltpu.VMEM((2, length, 128), B16),
            pltpu.VMEM((pairs * turns // 2, block, 128), B16),
            pltpu.VMEM(cotangent.shape[1:], B16),
            dma((count_rows(EVERY, ATTEND_KINDS), planes)),
            dma((2, pairs * turns // 2)),
            dma((4,)),
        ],
        compiler_params=pltpu.CompilerParams(
            vmem_limit_bytes=VMEM_LIMIT, collective_id=1, has_side_effects=True
        ),
        cost_estimate=pl.CostEstimate(
            flops=16 * length * length * width,
            bytes_accessed=width // 64 * length * length * 2,
            transcendentals=width // 64 * length * length,
        ),
    )(query, key, value, cotangent, own_o, own_e, own_r, full_o, full_e, full_r)


def attend_back_body(
    planes,
    q_ref, k_ref, v_ref, o_ref, inv_ref, g_ref, e_ref, cos_ref, sin_ref, cos_all, sin_all,
    split_ref, full_ref, tag_ref, out_ref,
    own_ref, other_ref, sums_ref, home_ref,
    key_sum, value_sum, vm_ref, q_stage, kv_stage, out_vm, move_sems, out_sems, *spread_refs,
):
    at = Place(planes)
    rows_all, length = q_ref.shape[0], k_ref.shape[0]
    low = low_lanes()
    pair, at_step = pl.program_id(0), pl.program_id(1)
    pairs, turns = q_stage.shape[0], q_stage.shape[1]
    now = pair * turns + at_step
    count = pairs * turns
    local_rows = length // 2
    spread = Spread(at, split_ref, full_ref, tag_ref[...], sums_ref, *spread_refs)
    stays = jnp.logical_not(at.crosses)
    out_load = pltpu.make_async_copy(out_ref, out_vm, out_sems.at[0])
    out_keep = pltpu.make_async_copy(out_vm, home_ref.at[at.tp], out_sems.at[1])
    out_turn = pltpu.make_async_remote_copy(
        src_ref=out_ref, dst_ref=home_ref.at[at.tp], send_sem=out_sems.at[2], recv_sem=out_sems.at[3],
        device_id=at.turned, device_id_type=MESH,
    )

    def out_tp(source):
        return pltpu.make_async_remote_copy(
            src_ref=source, dst_ref=home_ref.at[at.tp], send_sem=out_sems.at[4], recv_sem=out_sems.at[5],
            device_id=at.next_tp, device_id_type=MESH,
        )

    def when(step, act):
        pl.when(now == step)(act)

    @pl.when(now == 0)
    def _():
        pl.when(stays)(lambda: out_load.start())
        at.greet(True, True, True)
        spread.start()
        pl.when(at.crosses)(lambda: out_turn.start())

    when(2, spread.second)

    @pl.when(now == 3)
    def _():
        @pl.when(stays)
        def _():
            out_load.wait()
            out_keep.start()
            out_tp(out_vm).start()

    when(4, spread.third)
    when(6, lambda: spread.planes(0))

    @pl.when(now == 7)
    def _():
        @pl.when(at.crosses)
        def _():
            out_turn.wait_recv()
            out_tp(home_ref.at[at.tp]).start()

    when(9, lambda: spread.planes(1))
    when(12, lambda: spread.planes(2))
    when(15, lambda: spread.planes(3))

    @pl.when(at_step == 0)
    def _():
        key_sum[...] = jnp.zeros_like(key_sum)
        value_sum[...] = jnp.zeros_like(value_sum)
        vm_ref[0] = jnp.where(low, v_ref[...], -1).astype(B16)
        vm_ref[1] = jnp.where(low, -1, v_ref[...]).astype(B16)

    step = min(256, rows_all)
    for begin in range(0, rows_all, step):
        rows = pl.ds(begin, step)
        grad = g_ref[rows, :].astype(F32) * inv_ref[rows, :]
        grad_low = grad.astype(B16)
        product = pltpu.roll(grad * o_ref[rows, :].astype(F32), 64, 1).astype(B16)
        q_turned = q_ref[rows, :].T
        g_turned = grad_low.T
        parts = []
        for head in range(2):
            mine = low if head == 0 else ~low
            weights = e_ref[head, rows, :]
            grad_probs = dot(jnp.where(mine, grad_low, product), vm_ref[head], 1, 1)
            grad_scores = (weights.astype(F32) * grad_probs).astype(B16)
            parts.append(dot(grad_scores, k_ref[...]))
            span = pl.ds(head * 64, 64)
            key_sum[span, :] += dot(q_turned[head * 64 : head * 64 + 64], grad_scores)
            value_sum[span, :] += dot(g_turned[head * 64 : head * 64 + 64], weights)
        gq = jnp.where(low, parts[0], parts[1]) * score_scale
        q_stage[pair, at_step, rows, :] = (
            gq * cos_ref[rows, :] + partner(gq * sin_ref[rows, :])
        ).astype(B16)

    def columns(index):
        return pl.ds(pl.multiple_of(index * 128, 128), 128)

    def q_here(pair_index, turn_index):
        rows = pl.ds(pl.multiple_of(turn_index * rows_all, rows_all), rows_all)
        return pltpu.make_async_copy(
            q_stage.at[pair_index, turn_index], own_ref.at[0, rows, columns(pair_index)],
            move_sems.at[0, pair_index * turns + turn_index],
        )

    def q_there(pair_index, turn_index):
        rows = pl.ds(pl.multiple_of(turn_index * rows_all - local_rows, rows_all), rows_all)
        index = pair_index * turns + turn_index
        return pltpu.make_async_remote_copy(
            src_ref=q_stage.at[pair_index, turn_index], dst_ref=other_ref.at[0, rows, columns(pair_index)],
            send_sem=move_sems.at[0, index], recv_sem=move_sems.at[1, index],
            device_id=at.next_core, device_id_type=MESH,
        )

    def kv_here(part, pair_index):
        return pltpu.make_async_copy(
            kv_stage.at[part, pair_index, pl.ds(0, local_rows)], own_ref.at[1 + part, :, columns(pair_index)],
            move_sems.at[2, 2 * pair_index + part],
        )

    def kv_there(part, pair_index):
        index = 2 * pair_index + part
        return pltpu.make_async_remote_copy(
            src_ref=kv_stage.at[part, pair_index, pl.ds(local_rows, local_rows)],
            dst_ref=other_ref.at[1 + part, :, columns(pair_index)],
            send_sem=move_sems.at[3, index], recv_sem=move_sems.at[4, index],
            device_id=at.next_core, device_id_type=MESH,
        )

    pl.when(at_step < turns // 2)(lambda: q_here(pair, at_step).start())
    pl.when(at_step >= turns // 2)(lambda: q_there(pair, at_step).start())

    @pl.when(at_step == turns - 1)
    def _():
        gk = key_sum[...].T * score_scale
        kv_stage[0, pair] = (gk * cos_all[...] + partner(gk * sin_all[...])).astype(B16)
        kv_stage[1, pair] = value_sum[...].T.astype(B16)
        for part in range(2):
            kv_here(part, pair).start()
            kv_there(part, pair).start()

    @pl.when(now == count - 1)
    def _():
        for pair_index in range(pairs):
            for turn_index in range(turns):
                if turn_index < turns // 2:
                    q_here(pair_index, turn_index).wait()
                else:
                    q_there(pair_index, turn_index).wait()
            for part in range(2):
                kv_here(part, pair_index).wait()
                kv_there(part, pair_index).wait()
        spread.finish()
        spread.sent()

        @pl.when(stays)
        def _():
            out_keep.wait()
            out_tp(out_vm).wait_send()

        @pl.when(at.crosses)
        def _():
            out_turn.wait_send()
            out_tp(home_ref.at[at.tp]).wait_send()

        pltpu.make_async_remote_copy(
            src_ref=home_ref.at[at.tp], dst_ref=home_ref.at[1 - at.tp], send_sem=out_sems.at[4],
            recv_sem=out_sems.at[5], device_id=at.next_tp, device_id_type=MESH,
        ).wait_recv()


def attend_back(planes, query, key, value, attended, inverse, grad, weights, cosine, sine, split, full, tag, out, adapters):
    length, width = query.shape
    block = min(512, length // 2)
    pairs, turns = width // 128, length // block
    rows = pl.BlockSpec((block, 128), lambda p, i: (i, p))
    whole = pl.BlockSpec((length, 128), lambda p, i: (0, p))
    table = pl.BlockSpec((block, 128), lambda p, i: (i, 0))
    one = lambda array: pl.BlockSpec(
        array.shape, lambda p, i: (0,) * len(array.shape), pipeline_mode=pl.Buffered(1)
    )
    hbm = pl.BlockSpec(memory_space=pl.ANY)
    shape = jax.ShapeDtypeStruct
    dma = pltpu.SemaphoreType.DMA
    ranks = full.shape[0] // 2
    keep = split.shape[2] + full.shape[1]
    sums = shape((adapters, 2 * ranks, keep), F32)
    return pl.pallas_call(
        functools.partial(attend_back_body, planes),
        grid=(pairs, turns),
        in_specs=[
            rows, whole, whole, rows, rows, rows,
            pl.BlockSpec((2, block, length), lambda p, i: (p, i, 0)),
            table, table, one(cosine), one(sine), one(split), one(full), one(tag), hbm,
        ],
        out_specs=[hbm, hbm, one(sums), hbm],
        out_shape=[
            shape((3, length // 2, width), B16), shape((3, length // 2, width), B16), sums,
            shape((2,) + out.shape, B16),
        ],
        scratch_shapes=[
            pltpu.VMEM((128, length), F32),
            pltpu.VMEM((128, length), F32),
            pltpu.VMEM((2, length, 128), B16),
            pltpu.VMEM((pairs, turns, block, 128), B16),
            pltpu.VMEM((2, pairs, length, 128), B16),
            pltpu.VMEM(out.shape, B16),
            dma((5, max(pairs * turns, 2 * pairs))),
            dma((6,)),
        ]
        + Spread.scratch(planes, ranks, split.shape[2], full.shape[1]),
        compiler_params=pltpu.CompilerParams(
            vmem_limit_bytes=VMEM_LIMIT, collective_id=3, has_side_effects=True
        ),
        cost_estimate=pl.CostEstimate(
            flops=20 * length * length * width,
            bytes_accessed=width // 64 * length * length * 2,
            transcendentals=0,
        ),
    )(query, key, value, attended, inverse, grad, weights, cosine, sine, cosine, sine, split, full, tag, out)


def gauss_parts(z):
    t = 1.0 / (1.0 + (0.3275911 * math.sqrt(0.5)) * jnp.abs(z))
    poly = t * (0.254829592 + t * (-0.284496736 + t * (1.421413741 + t * (-1.453152027 + t * 1.061405429))))
    bell = jnp.exp2((z * z) * (-0.5 * math.log2(math.e)))
    upper = 0.5 * poly * bell
    cdf = jnp.where(z >= 0, 1.0 - upper, upper)
    return cdf, bell * (1.0 / math.sqrt(2.0 * math.pi))


def middle_body(
    planes, blocks,
    x_ref, cot_ref, own_ref, other_ref, wo_ref, factors_ref, shared_ref, offsets_ref,
    out_off, gain_ref, shift_ref, shrink_off, in_e, in_r,
    output_ref, gh_ref, t_split, t_full, gatt_out, full_e, full_r,
    hidden, xn_ref, total, back, u2_ref, u3_ref, u4_sum, g4_ref, g3_sum,
    e_vm, r_vm, gown_vm, gother_vm, load_sems, flow_sems, grad_sems,
):
    at = Place(planes)
    f = pl.program_id(0)
    last = 2 * blocks - 1
    core = at.core
    rows_all, width = x_ref.shape
    half = own_ref.shape[1]
    hidden_half = blocks * HIDDEN_BLOCK
    step = 256
    flows = block_flows(at, None, None, full_e, full_r, Rows(flow_sems), MIDDLE_KINDS)
    planes_all = range(planes)

    def pass_on(pair, **how):
        for flow in pair:
            for far in planes_all:
                flow.pass_on(far, fresh=False, **how)

    def pass_next(pair, wait):
        for flow in pair:
            for far in planes_all:
                flow.pass_next(far, wait)

    def arrived(pair, kind):
        for flow in pair:
            for far in planes_all:
                flow.wait(kind, far)

    def loads(index, slot):
        tp_half = jnp.where(index < blocks, at.tp, 1 - at.tp)
        span = pl.ds(pl.multiple_of(index % blocks * HIDDEN_BLOCK, HIDDEN_BLOCK), HIDDEN_BLOCK)
        return (
            pltpu.make_async_copy(full_e.at[:, tp_half, :, span], e_vm.at[slot], load_sems.at[0, slot]),
            pltpu.make_async_copy(full_r.at[:, tp_half, span, :], r_vm.at[slot], load_sems.at[1, slot]),
        )

    def wo_half(part):
        w = wo_ref[:, part]
        return jnp.concatenate([w[i] for i in range(w.shape[0])], axis=1)

    jd, ed, ou, ru = (pl.ds(i * width, width) for i in range(4))
    od = pl.ds(3 * half, half)

    @pl.when(f == 0)
    def _():
        for load in loads(0, 0):
            load.start()
        at.greet(True, False)
        for flow in flows[3]:
            flow.pass_on(1, fresh=False, z=True, core=True)
            flow.pass_on(0, fresh=False, core=True)
        for flow in flows[1]:
            for far in planes_all:
                flow.pass_next(far, False)
        pass_on(flows[2], tp=True)
        w_own, w_other = wo_half(core), wo_half(1 - core)
        for begin in range(0, rows_all, step):
            rows = pl.ds(begin, step)
            own, other = own_ref[rows, :], other_ref[rows, :]
            u2 = (
                dot(own, factors_ref[core, :, od], 1, 1) + dot(other, factors_ref[1 - core, :, od], 1, 1)
            ).astype(B16)
            u2_ref[rows, :] = u2
            h = (
                x_ref[rows, :].astype(F32) + dot(own, w_own) + dot(other, w_other)
                + out_off[...] + dot(u2, shared_ref[:, ou])
            )
            hidden[rows, :] = h
            scaled, _ = row_norm(h)
            xn = (scaled * gain_ref[...] + shift_ref[...]).astype(B16)
            xn_ref[rows, :] = xn
            u3_ref[rows, :] = dot(xn, shared_ref[:, ed], 1, 1).astype(B16)
            g4_ref[rows, :] = dot(cot_ref[rows, :], shared_ref[:, ru], 1, 1).astype(B16)
            total[rows, :] = h + shrink_off[...]
            back[rows, :] = jnp.zeros_like(h)
            u4_sum[rows, :] = jnp.zeros((step, u4_sum.shape[1]), F32)
            g3_sum[rows, :] = jnp.zeros((step, g3_sum.shape[1]), F32)
        for flow in flows[3]:
            flow.pass_on(2, fresh=False, z=True, core=True, wait=True)

    @pl.when(f == 1)
    def _():
        for flow in flows[3]:
            flow.pass_on(3, fresh=False, core=True, wait=True)

    @pl.when(f == 2)
    def _():
        pass_on(flows[3], tp=True)
        arrived(flows[3], OWN_CAME)

    @pl.when(f == 4)
    def _():
        pass_next(flows[2], True)
        arrived(flows[1], NEXT_CAME)

    @pl.when(f == last - 2)
    def _():
        arrived(flows[2], NEXT_CAME)

    @pl.when(f == last - 1)
    def _():
        pass_next(flows[3], True)

    slot = f % 2

    @pl.when(f < last - 1)
    def _():
        for load in loads(f + 1, 1 - slot):
            load.start()

    for load in loads(f, slot):
        load.wait()
    tp_half = jnp.where(f < blocks, at.tp, 1 - at.tp)
    begin_block = f % blocks * HIDDEN_BLOCK

    def block_of(first):
        return pl.ds(pl.multiple_of(first + begin_block, 128), HIDDEN_BLOCK)

    w_e = e_vm[slot].reshape(width, HIDDEN_BLOCK)
    w_r = jnp.concatenate([r_vm[slot, i] for i in range(2 * planes)], axis=1)
    eu = factors_ref[tp_half, :, block_of(4 * half)]
    rd = factors_ref[tp_half, :, block_of(4 * half + hidden_half)]
    wide_off = offsets_ref[tp_half, :, block_of(3 * half)]
    u3, g4 = u3_ref[...], g4_ref[...]
    z = dot(xn_ref[...], w_e) + wide_off + dot(u3, eu)
    gact = dot(cot_ref[...], w_r, 1, 1) + dot(g4, rd)
    cdf, density = gauss_parts(z)
    act = (z * cdf).astype(B16)
    gz = (gact * (cdf + z * density)).astype(B16)
    total[...] += dot(act, w_r)
    u4_sum[...] += dot(act, rd, 1, 1)
    back[...] += dot(gz, w_e, 1, 1)
    g3_sum[...] += dot(gz, eu, 1, 1)
    sum_rd = dot(g4, act, 0, 0)
    sum_eu = dot(u3, gz, 0, 0)
    t_split[tp_half, :, block_of(half + hidden_half)] = sum_rd
    t_split[tp_half, :, block_of(half)] = sum_eu

    @pl.when(f == last - 1)
    def _():
        arrived(flows[3], NEXT_CAME)
        for load in loads(f + 1, 1 - slot):
            load.start()

    @pl.when(f == last)
    def _():
        w_own, w_other = wo_half(core), wo_half(1 - core)
        s_ru, s_ed, s_ou, s_own, s_other = 0.0, 0.0, 0.0, 0.0, 0.0
        moves = []
        for index, begin in enumerate(range(0, rows_all, step)):
            rows = pl.ds(begin, step)
            cot = cot_ref[rows, :]
            u4 = u4_sum[rows, :].astype(B16)
            output_ref[rows, :] = (total[rows, :] + dot(u4, shared_ref[:, ru])).astype(B16)
            s_ru += dot(u4, cot, 0, 0)
            g3 = g3_sum[rows, :].astype(B16)
            s_ed += dot(g3, xn_ref[rows, :], 0, 0)
            gx = back[rows, :] + dot(g3, shared_ref[:, ed])
            scaled, inverse = row_norm(hidden[rows, :])
            gh = cot.astype(F32) + back_norm(gx * gain_ref[...], scaled, inverse)
            gh_ref[rows, :] = gh
            gb = gh.astype(B16)
            s_ou += dot(u2_ref[rows, :], gb, 0, 0)
            g2 = dot(gb, shared_ref[:, ou], 1, 1).astype(B16)
            s_own += dot(g2, own_ref[rows, :], 0, 0)
            s_other += dot(g2, other_ref[rows, :], 0, 0)
            gother_vm[rows, :] = (
                dot(gb, w_other, 1, 1) + dot(g2, factors_ref[1 - core, :, od])
            ).astype(B16)
            there = pltpu.make_async_remote_copy(
                src_ref=gother_vm.at[rows], dst_ref=gatt_out.at[pl.ds(rows_all + begin, step)],
                send_sem=grad_sems.at[0, index], recv_sem=grad_sems.at[1, index],
                device_id=at.next_core, device_id_type=MESH,
            )
            there.start()
            gown_vm[rows, :] = (dot(gb, w_own, 1, 1) + dot(g2, factors_ref[core, :, od])).astype(B16)
            here = pltpu.make_async_copy(gown_vm.at[rows], gatt_out.at[rows], grad_sems.at[2, index])
            here.start()
            moves += [there, here]
        t_full[:, 0:width] = s_ou
        t_full[:, width : 2 * width] = s_ed
        t_full[:, 2 * width :] = s_ru
        t_split[core, :, 0:half] = s_own
        t_split[1 - core, :, 0:half] = s_other
        for index, pair in enumerate(flows[1:]):
            for flow in pair:
                for far in planes_all:
                    flow.sent(far, z=index == 2 and far in (1, 2), tp=index > 0, core=index == 2)
                    flow.sent_next(far)
        for move in moves:
            move.wait()


def middle(
    planes, x, cot, attended, other, w_o, factors, shared, offsets, out_off, gain, shift, shrink_off, w_e, w_r
):
    rows, width = x.shape
    half = attended.shape[1]
    shards_, _, depth, hidden_half = w_e.shape
    rank = factors.shape[1]
    blocks = hidden_half // HIDDEN_BLOCK
    one = lambda shape: pl.BlockSpec(
        shape, lambda f: (0,) * len(shape), pipeline_mode=pl.Buffered(1)
    )
    hbm = pl.BlockSpec(memory_space=pl.ANY)
    shape = jax.ShapeDtypeStruct
    dma = pltpu.SemaphoreType.DMA
    chunks = rows // 256
    return pl.pallas_call(
        functools.partial(middle_body, planes, blocks),
        grid=(2 * blocks,),
        in_specs=[
            one((rows, width)), one((rows, width)), one((rows, half)), one((rows, half)),
            one(w_o.shape), one(factors.shape), one(shared.shape), one(offsets.shape),
            one((1, width)), one((1, width)), one((1, width)), one((1, width)), hbm, hbm,
        ],
        out_specs=[
            one((rows, width)), one((rows, width)),
            one((2, rank, half + 2 * hidden_half)), one((rank, 3 * width)), hbm, hbm, hbm,
        ],
        out_shape=[
            shape((rows, width), B16), shape((rows, width), F32),
            shape((2, rank, half + 2 * hidden_half), F32), shape((rank, 3 * width), F32),
            shape((2 * rows, half), B16), shape(w_e.shape, B16), shape(w_r.shape, B16),
        ],
        input_output_aliases={12: 5, 13: 6},
        scratch_shapes=[
            pltpu.VMEM((rows, width), F32), pltpu.VMEM((rows, width), B16),
            pltpu.VMEM((rows, width), F32), pltpu.VMEM((rows, width), F32),
            pltpu.VMEM((rows, rank), B16), pltpu.VMEM((rows, rank), B16),
            pltpu.VMEM((rows, rank), F32), pltpu.VMEM((rows, rank), B16),
            pltpu.VMEM((rows, rank), F32),
            pltpu.VMEM((2, shards_, depth, HIDDEN_BLOCK), B16),
            pltpu.VMEM((2, shards_, HIDDEN_BLOCK, w_r.shape[3]), B16),
            pltpu.VMEM((rows, half), B16), pltpu.VMEM((rows, half), B16),
            dma((2, 2)), dma((count_rows((), MIDDLE_KINDS), planes)), dma((3, chunks)),
        ],
        compiler_params=pltpu.CompilerParams(
            vmem_limit_bytes=VMEM_LIMIT, collective_id=2, has_side_effects=True
        ),
        cost_estimate=pl.CostEstimate(
            flops=2 * rows * width * (16 * hidden_half // 2 + 4 * half),
            bytes_accessed=40 * 2**20,
            transcendentals=rows * hidden_half * 2,
        ),
    )(x, cot, attended, other, w_o, factors, shared, offsets, out_off, gain, shift, shrink_off, w_e, w_r)


def unproject_body(
    planes,
    x_ref, gh_ref, xn_ref, u_ref, gain_ref, w_ref, factors_ref, shared_ref, own_ref, other_ref,
    home_ref, sums_ref,
    own_vm, other_vm, w_vm, x_vm, gh_vm, xn_vm, stage, split, full, g1_vm, load_sems, move_sems, *spread_refs,
):
    at = Place(planes)
    rows_all, width = x_vm.shape
    half = own_vm.shape[2]
    core = at.core
    spread = Spread(at, split, full, shared_ref[0:8, 4 * width :], sums_ref, *spread_refs)
    halves = ((own_vm, core), (other_vm, 1 - core))
    chunks = rows_all // ROWS

    def load(index, source, target):
        return pltpu.make_async_copy(source, target, load_sems.at[index])

    loads = [load(0, own_ref, own_vm), load(1, other_ref, other_vm), load(2, xn_ref, xn_vm)]
    late = [load(3, x_ref, x_vm), load(4, gh_ref, gh_vm)]
    late += [load(5 + order, w_ref.at[:, owner], w_vm.at[order]) for order, (_, owner) in enumerate(halves)]
    for item in loads + late:
        item.start()
    at.greet(True, True, True, True)
    for item in loads:
        item.wait()
    u = u_ref[...]
    g1 = 0.0
    for source, owner in halves:
        for part in range(3):
            columns = pl.ds(part * half, half)
            g1 += dot(source[part], factors_ref[owner, :, columns], 1, 1)
            split[owner, :, columns] = dot(u, source[part], 0, 0)
    g1 = g1.astype(B16)
    g1_vm[...] = g1
    full[...] = dot(g1, xn_vm[...], 0, 0)
    spread.start()
    order = [2, 0, 3, 1]
    for item in late:
        item.wait()
    quarter = rows_all // 2

    def moves(i):
        tp_half = i * ROWS // quarter
        rows = pl.ds(i * ROWS % quarter, ROWS)
        source, target = stage.at[i], home_ref.at[at.tp, rows]

        def remote(device, came):
            return pltpu.make_async_remote_copy(
                src_ref=source, dst_ref=target, send_sem=move_sems.at[0, i], recv_sem=move_sems.at[came, i],
                device_id=device, device_id_type=MESH,
            )

        mine = at.tp == tp_half
        both = dict(at.turned)
        both["tp"] = 1 - at.tp
        return (
            (mine & jnp.logical_not(at.crosses), lambda: pltpu.make_async_copy(source, target, move_sems.at[0, i]), True),
            (mine & at.crosses, lambda: remote(at.turned, 1), False),
            (jnp.logical_not(mine) & jnp.logical_not(at.crosses), lambda: remote(at.next_tp, 2), False),
            (jnp.logical_not(mine) & at.crosses, lambda: remote(both, 2), False),
        )

    spread.second()
    stages = [spread.third, lambda: spread.planes(0), lambda: spread.planes(1), lambda: spread.planes(2)]
    for count, i in enumerate(order):
        span = pl.ds(i * ROWS, ROWS)
        gx = dot(g1_vm[span, :], shared_ref[:, 0:width])
        for index, (source, _) in enumerate(halves):
            for part in range(3):
                gx += dot(source[part, span, :], w_vm[index, :, part].reshape(width, half), 1, 1)
        scaled, inverse = row_norm(x_vm[span, :].astype(F32))
        stage[i] = (gh_vm[span, :] + back_norm(gx * gain_ref[...], scaled, inverse)).astype(B16)
        for there, move, _ in moves(i):
            pl.when(there)(lambda move=move: move().start())
        stages[count]()
    for distance in range(3, planes):
        spread.planes(distance)
    spread.finish()
    spread.sent()
    for i in range(chunks):
        for there, move, here in moves(i):
            if here:
                pl.when(there)(lambda move=move: move().wait())
            else:
                pl.when(there)(lambda move=move: move().wait_send())
    for i in range(chunks):
        tp_half = i * ROWS // quarter
        rows = pl.ds(i * ROWS % quarter, ROWS)

        def came(slot):
            return pltpu.make_async_remote_copy(
                src_ref=stage.at[i], dst_ref=home_ref.at[slot, rows], send_sem=move_sems.at[0, i],
                recv_sem=move_sems.at[1, i], device_id=at.next_tp, device_id_type=MESH,
            )

        pl.when((at.tp == tp_half) & at.crosses)(lambda came=came: came(at.tp).wait_recv())

    for i in range(chunks):
        tp_half = i * ROWS // quarter
        rows = pl.ds(i * ROWS % quarter, ROWS)

        def came(slot):
            return pltpu.make_async_remote_copy(
                src_ref=stage.at[i], dst_ref=home_ref.at[slot, rows], send_sem=move_sems.at[0, i],
                recv_sem=move_sems.at[2, i], device_id=at.next_tp, device_id_type=MESH,
            )

        pl.when(at.tp == tp_half)(lambda came=came: came(1 - at.tp).wait_recv())


def unproject(planes, x, gh, xn, u, gain, weight, factors, shared, own, other, adapters):
    rows, width = x.shape
    half = own.shape[2]
    rank = factors.shape[1]
    hbm = pl.BlockSpec(memory_space=pl.ANY)
    vmem = pl.BlockSpec(memory_space=pltpu.VMEM)
    shape = jax.ShapeDtypeStruct
    dma = pltpu.SemaphoreType.DMA
    chunks = rows // ROWS
    keep = 3 * half + width
    return pl.pallas_call(
        functools.partial(unproject_body, planes),
        in_specs=[hbm, hbm, hbm, vmem, vmem, hbm, vmem, vmem, hbm, hbm],
        out_specs=[hbm, vmem],
        out_shape=[shape((2, rows // 2, width), B16), shape((adapters, rank, keep), F32)],
        scratch_shapes=[
            pltpu.VMEM(own.shape, B16), pltpu.VMEM(own.shape, B16),
            pltpu.VMEM((2, weight.shape[0]) + weight.shape[2:], B16),
            pltpu.VMEM((rows, width), B16), pltpu.VMEM((rows, width), F32), pltpu.VMEM((rows, width), B16),
            pltpu.VMEM((chunks, ROWS, width), B16),
            pltpu.VMEM((2, rank, 3 * half), F32), pltpu.VMEM((rank, width), F32), pltpu.VMEM((rows, rank), B16),
            dma((7,)), dma((3, chunks)),
        ]
        + Spread.scratch(planes, rank // 2, 3 * half, width),
        compiler_params=pltpu.CompilerParams(
            vmem_limit_bytes=VMEM_LIMIT, collective_id=4, has_side_effects=True
        ),
        cost_estimate=pl.CostEstimate(
            flops=2 * rows * width * 6 * half, bytes_accessed=20 * 2**20, transcendentals=0
        ),
    )(x, gh, xn, u, gain, weight, factors, shared, own, other)


def rate_parts():
    lane = np.arange(128) % 64
    rates = np.exp((lane % 10).astype(np.float32) * np.float32(-math.log(10000.0) / 10.0)).astype(np.float32)
    rates = np.where(lane[None] // 20 == np.arange(3)[:, None], rates[None], np.float32(0.0)).astype(np.float32)
    parts = []
    for _ in range(3):
        part = rates.astype(ml_dtypes.bfloat16)
        parts.append(part)
        rates = rates - part.astype(np.float32)
    parts.append(np.zeros((7, 128), ml_dtypes.bfloat16))
    return jnp.asarray(np.concatenate(parts, axis=0))


def clip_shards(
    planes,
    tokens,
    cotangent,
    adapter_pick,
    positions,
    first_gain,
    first_shift,
    joined_weight,
    joined_bias,
    output_weight,
    mixing_exit_offset,
    second_gain,
    second_shift,
    expand_weight,
    widening_offset,
    reduce_weight,
    shrinking_offset,
    joined_down,
    joined_up,
    output_down,
    output_up,
    expand_down,
    expand_up,
    reduce_down,
    reduce_up,
):
    half = joined_weight.shape[2]
    hidden_half = expand_weight.shape[1]
    rank = joined_up.shape[1]
    turn_last = lambda array: jnp.swapaxes(array, 1, 2)
    tables = (
        turn_last(joined_down), turn_last(expand_down), output_up, reduce_up,
        turn_last(joined_up), turn_last(output_down), expand_up, turn_last(reduce_down),
    )
    (
        x, factors, shared, offsets, w_j, w_o, w_e, w_r, query, key, value, xn1, u1, cosine, sine,
    ) = project(
        planes, tokens, adapter_pick, positions, joined_bias, widening_offset[None], tables,
        jnp.transpose(joined_weight, (1, 0, 2)), output_weight, expand_weight, reduce_weight,
        first_gain[None], first_shift[None], rate_parts(),
    )
    attended, inverse, weights, other_heads, cot, w_o, w_e, w_r = attend(
        planes, query, key, value, cotangent, output_weight, expand_weight, reduce_weight, w_o, w_e, w_r
    )
    out, gh, split, full, grad_att, w_e, w_r = middle(
        planes, x, cot, attended, other_heads, w_o, factors, shared, offsets,
        mixing_exit_offset[None], second_gain[None], second_shift[None], shrinking_offset[None], w_e, w_r,
    )
    adapters = joined_down.shape[0]
    width = tokens.shape[2]
    tag = shared[: rank // 2, 4 * width :]
    own, other, sums, output = attend_back(
        planes, query, key, value, attended, inverse, grad_att, weights, cosine, sine, split, full, tag, out, adapters
    )
    tokens_grad, late_sums = unproject(
        planes, x, gh, xn1, u1, first_gain[None], w_j, factors, shared, own, other, adapters
    )

    def cut(array, *sizes):
        begin, pieces = 0, []
        for size in sizes:
            pieces.append(array[:, :, begin : begin + size])
            begin += size
        return pieces

    s_od, s_eu, s_rd, s_ou, s_ed, s_ru = cut(sums, half, hidden_half, hidden_half, width, width, width)
    s_fu, s_fd = cut(late_sums, 3 * half, width)
    return (
        output,
        tokens_grad,
        turn_last(s_fd),
        s_fu.reshape(adapters, rank, 3, half),
        turn_last(s_od),
        s_ou,
        turn_last(s_ed),
        s_eu,
        turn_last(s_rd),
        s_ru,
    )


def solution(mesh):
    sizes = dict(mesh.shape)
    if sizes["ctx"] == 2 and sizes["tp"] == 2 and sizes["shard"] == 8:
        body = functools.partial(clip_shards, sizes["shard"] // 2)
    else:
        body = general_shards
    return jax.shard_map(
        body,
        mesh=mesh,
        in_specs=(
            P("shard", "ctx", None),
            P("shard", "ctx", None),
            P("shard"),
            P(None, "shard", "ctx"),
            P(),
            P(),
            P("shard", None, "tp"),
            P(None, "tp"),
            P("tp", "shard"),
            P(),
            P(),
            P(),
            P("shard", "tp"),
            P("tp"),
            P("tp", "shard"),
            P(),
            P(),
            P(None, None, None, "tp"),
            P(None, "tp", None),
            P(),
            P(),
            P(None, None, "tp"),
            P(None, "tp", None),
            P(),
        ),
        out_specs=(
            P("shard", "ctx", None),
            P("shard", ("ctx", "tp"), None),
            P(),
            P(None, None, None, "tp"),
            P(None, "tp", None),
            P(),
            P(),
            P(None, None, "tp"),
            P(None, "tp", None),
            P(),
        ),
        check_vma=False,
    )
```

```python
import functools
import math

import jax
import jax.numpy as jnp
import ml_dtypes
import numpy as np
from jax import lax
from jax.experimental import pallas as pl
from jax.experimental.pallas import tpu as pltpu
from jax.sharding import PartitionSpec as P

eps_norm = 1e-06
score_scale = 0.125


def rope_tables(places):
    band = jnp.arange(10, dtype=jnp.float32)
    rates = jnp.exp(band * (-math.log(10000.0) / 10.0))
    angle = places.astype(jnp.float32)[..., None] * rates
    cos_parts = []
    sin_parts = []
    for band_index in range(3):
        cosine = jnp.cos(angle[band_index])
        sine = jnp.sin(angle[band_index])
        cos_parts = cos_parts + [cosine, cosine]
        sin_parts = sin_parts + [-sine, sine]
    rest_shape = angle.shape[1:-1] + (4,)
    cos_parts.append(jnp.ones(rest_shape, jnp.float32))
    sin_parts.append(jnp.zeros(rest_shape, jnp.float32))
    return (jnp.concatenate(cos_parts, -1), jnp.concatenate(sin_parts, -1))


def swap_pairs(values):
    leading = values.shape[:-1]
    turned = values[..., :60].reshape(leading + (3, 2, 10))[..., ::-1, :].reshape(leading + (60,))
    return jnp.concatenate([turned, values[..., 60:]], -1)


def rotate(values, cosine, sine):
    return values * cosine[..., None, :] + swap_pairs(values) * sine[..., None, :]


def rotate_back(grads, cosine, sine):
    return grads * cosine[..., None, :] + swap_pairs(grads * sine[..., None, :])


def norm_forward(values, gain, shift):
    centred = values - jnp.mean(values, -1, keepdims=True)
    inverse = lax.rsqrt(jnp.mean(centred * centred, -1, keepdims=True) + eps_norm)
    scaled = centred * inverse
    return (scaled * gain + shift, scaled, inverse)


def norm_back(grads, scaled, inverse, gain):
    weighted = grads * gain
    return inverse * (
        weighted
        - jnp.mean(weighted, -1, keepdims=True)
        - scaled * jnp.mean(weighted * scaled, -1, keepdims=True)
    )


def select_factor(choose, table):
    return jnp.einsum("ca,a...->c...", choose, table, preferred_element_type=jnp.float32).astype(
        jnp.bfloat16
    )


def gelu_exact(values):
    return jax.nn.gelu(values, approximate=False)


def matrix_product(form, left, right):
    return jnp.einsum(form, left, right, preferred_element_type=jnp.float32)


def general_shards(
    tokens,
    cotangent,
    adapter_pick,
    positions,
    first_gain,
    first_shift,
    joined_weight,
    joined_bias,
    output_weight,
    mixing_exit_offset,
    second_gain,
    second_shift,
    expand_weight,
    widening_offset,
    reduce_weight,
    shrinking_offset,
    joined_down,
    joined_up,
    output_down,
    output_up,
    expand_down,
    expand_up,
    reduce_down,
    reduce_up,
):
    whole_joined, whole_output, whole_expand, whole_reduce = (
        lax.all_gather(joined_weight, "shard", axis=0, tiled=True),
        lax.all_gather(output_weight, "shard", axis=1, tiled=True),
        lax.all_gather(expand_weight, "shard", axis=0, tiled=True),
        lax.all_gather(reduce_weight, "shard", axis=1, tiled=True),
    )
    clip_count, local_len, width = tokens.shape
    local_width = whole_joined.shape[2]
    head_count = local_width // 64
    choose = (
        adapter_pick[:, None] == jnp.arange(joined_down.shape[0], dtype=jnp.int32)[None, :]
    ).astype(jnp.bfloat16)
    select_joined_down = select_factor(choose, joined_down)
    select_joined_up = select_factor(choose, joined_up)
    select_output_down = select_factor(choose, output_down)
    select_output_up = select_factor(choose, output_up)
    select_expand_down = select_factor(choose, expand_down)
    select_expand_up = select_factor(choose, expand_up)
    select_reduce_down = select_factor(choose, reduce_down)
    select_reduce_up = select_factor(choose, reduce_up)
    cosine, sine = rope_tables(positions)
    block_arguments = tokens.astype(jnp.float32)
    norm_one, scaled_one, inverse_one = norm_forward(block_arguments, first_gain, first_shift)
    initial_standardized = norm_one.astype(jnp.bfloat16)
    initial_slim_derivative = matrix_product(
        "zgh,zhe->zge", initial_standardized, select_joined_down
    ).astype(jnp.bfloat16)
    mapped_vectors = (
        matrix_product("cld,dje->clje", initial_standardized, whole_joined)
        + joined_bias
        + matrix_product("uip,upqg->uiqg", initial_slim_derivative, select_joined_up)
    )
    head_shape = (clip_count, local_len, head_count, 64)
    query = rotate(mapped_vectors[:, :, 0].reshape(head_shape), cosine, sine).astype(jnp.bfloat16)
    keys = rotate(mapped_vectors[:, :, 1].reshape(head_shape), cosine, sine).astype(jnp.bfloat16)
    values = mapped_vectors[:, :, 2].reshape(head_shape).astype(jnp.bfloat16)
    stats_shape = (clip_count, head_count, local_len)
    run_max = jnp.full(stats_shape, -1e30, jnp.float32)
    key_part = lax.all_gather(keys, "ctx", axis=1, tiled=True)
    value_part = lax.all_gather(values, "ctx", axis=1, tiled=True)
    scores = matrix_product("cqhd,ckhd->chqk", query, key_part) * score_scale
    new_max = jnp.maximum(run_max, jnp.max(scores, -1))
    weights = jnp.exp(scores - new_max[..., None])
    run_total = jnp.sum(weights, -1)
    update = matrix_product("chqk,ckhd->cqhd", weights.astype(jnp.bfloat16), value_part)
    accum = update
    run_max, run_total, accum = (new_max, run_total, accum)
    log_total = run_max + jnp.log(run_total)
    attended_full = accum / jnp.transpose(run_total, (0, 2, 1))[..., None]
    mixing_outcome = attended_full.reshape(clip_count, local_len, local_width).astype(jnp.bfloat16)
    out_part = matrix_product("cle,ed->cld", mixing_outcome, whole_output)
    rank_partial = matrix_product("fig,fgt->fit", mixing_outcome, select_output_down)
    output_total, rank_sum = (
        lax.psum(out_part.astype(jnp.bfloat16), "tp").astype(jnp.float32),
        lax.psum(rank_partial.astype(jnp.bfloat16), "tp").astype(jnp.float32),
    )
    middle_slim_derivative = rank_sum.astype(jnp.bfloat16)
    first_hidden = (
        block_arguments
        + output_total
        + mixing_exit_offset
        + matrix_product("wnk,wke->wne", middle_slim_derivative, select_output_up)
    )
    norm_two, scaled_two, inverse_two = norm_forward(first_hidden, second_gain, second_shift)
    latter_standardized = norm_two.astype(jnp.bfloat16)
    penultimate_slim_derivative = matrix_product(
        "zgh,zhe->zge", latter_standardized, select_expand_down
    ).astype(jnp.bfloat16)
    skip_stream_vectors = (
        matrix_product("cld,df->clf", latter_standardized, whole_expand)
        + widening_offset
        + matrix_product("uqz,uze->uqe", penultimate_slim_derivative, select_expand_up)
    )
    activity, gelu_pull = jax.vjp(gelu_exact, skip_stream_vectors)
    gaussian_error_unit = activity.astype(jnp.bfloat16)
    mlp_part = matrix_product("clf,fd->cld", gaussian_error_unit, whole_reduce)
    fourth_rank_partial = matrix_product("xpv,xvy->xpy", gaussian_error_unit, select_reduce_down)
    feedforward_sum, rank_four_sum = (
        lax.psum(mlp_part.astype(jnp.bfloat16), "tp").astype(jnp.float32),
        lax.psum(fourth_rank_partial.astype(jnp.bfloat16), "tp").astype(jnp.float32),
    )
    closing_slim_derivative = rank_four_sum.astype(jnp.bfloat16)
    output = (
        first_hidden
        + feedforward_sum
        + shrinking_offset
        + matrix_product("wnk,wke->wne", closing_slim_derivative, select_reduce_up)
    ).astype(jnp.bfloat16)
    back_joined, back_output, back_expand, back_reduce = (
        lax.all_gather(joined_weight, "shard", axis=0, tiled=True),
        lax.all_gather(output_weight, "shard", axis=1, tiled=True),
        lax.all_gather(expand_weight, "shard", axis=0, tiled=True),
        lax.all_gather(reduce_weight, "shard", axis=1, tiled=True),
    )
    reduce_up_term = matrix_product("vkn,vkm->vnm", closing_slim_derivative, cotangent)
    gradient_fourth = matrix_product("abj,awj->abw", cotangent, select_reduce_up).astype(
        jnp.bfloat16
    )
    reduce_down_term = matrix_product("mpg,mpu->mgu", gaussian_error_unit, gradient_fourth)
    grad_active = matrix_product("cld,fd->clf", cotangent, back_reduce) + matrix_product(
        "gez,guz->geu", gradient_fourth, select_reduce_down
    )
    residual_gradient = gelu_pull(grad_active)[0].astype(jnp.bfloat16)
    expand_up_term = matrix_product("jge,jgn->jen", penultimate_slim_derivative, residual_gradient)
    grad_norm_part = matrix_product("clf,df->cld", residual_gradient, back_expand)
    third_gradient_part = matrix_product("aik,adk->aid", residual_gradient, select_expand_up)
    norm_gradient_sum, grad_three_sum = (
        lax.psum(grad_norm_part.astype(jnp.bfloat16), "tp").astype(jnp.float32),
        lax.psum(third_gradient_part.astype(jnp.bfloat16), "tp").astype(jnp.float32),
    )
    gradient_third = grad_three_sum.astype(jnp.bfloat16)
    expand_down_term = matrix_product("kgt,kgh->kth", latter_standardized, gradient_third)
    second_norm_gradient = norm_gradient_sum + matrix_product(
        "jqt,jit->jqi", gradient_third, select_expand_down
    )
    grad_hidden = cotangent.astype(jnp.float32) + norm_back(
        second_norm_gradient, scaled_two, inverse_two, second_gain
    )
    branch_gradient = grad_hidden.astype(jnp.bfloat16)
    output_up_term = matrix_product("vkn,vkm->vnm", middle_slim_derivative, branch_gradient)
    gradient_second = matrix_product("abj,awj->abw", branch_gradient, select_output_up).astype(
        jnp.bfloat16
    )
    output_down_term = matrix_product("nua,nui->nai", mixing_outcome, gradient_second)
    grad_attended = (
        (
            matrix_product("cld,ed->cle", branch_gradient, back_output)
            + matrix_product("gsq,ghq->gsh", gradient_second, select_output_down)
        )
        .astype(jnp.bfloat16)
        .reshape(head_shape)
    )
    key_whole, value_whole = (
        lax.all_gather(keys, "ctx", axis=1, tiled=True),
        lax.all_gather(values, "ctx", axis=1, tiled=True),
    )
    flat_shape = (clip_count, local_len, local_width)

    def clip_back(items):
        query_clip, key_clip, value_clip, grad_clip, total_clip = items
        scores = matrix_product("qhd,khd->hqk", query_clip, key_clip) * score_scale
        probs = jnp.exp(scores - total_clip[..., None])
        grad_probs = matrix_product("qhd,khd->hqk", grad_clip, value_clip)
        middle = jnp.sum(probs * grad_probs, -1, keepdims=True)
        grad_scores = (probs * (grad_probs - middle)).astype(jnp.bfloat16)
        grad_query = matrix_product("hqk,khd->qhd", grad_scores, key_clip) * score_scale
        grad_key = matrix_product("hqk,qhd->khd", grad_scores, query_clip) * score_scale
        grad_value = matrix_product("hqk,qhd->khd", probs.astype(jnp.bfloat16), grad_clip)
        return (grad_query, grad_key, grad_value)

    grad_query, key_terms, value_terms = lax.map(
        clip_back, (query, key_whole, value_whole, grad_attended, log_total)
    )
    full_len = key_whole.shape[1]
    key_sum, value_sum = (
        lax.psum_scatter(
            key_terms.reshape(clip_count, full_len, local_width).astype(jnp.bfloat16),
            "ctx",
            scatter_dimension=1,
            tiled=True,
        ).astype(jnp.float32),
        lax.psum_scatter(
            value_terms.reshape(clip_count, full_len, local_width).astype(jnp.bfloat16),
            "ctx",
            scatter_dimension=1,
            tiled=True,
        ).astype(jnp.float32),
    )
    query_key_value_gradient = jnp.stack(
        [
            rotate_back(grad_query, cosine, sine).reshape(flat_shape),
            rotate_back(key_sum.reshape(head_shape), cosine, sine).reshape(flat_shape),
            value_sum,
        ],
        axis=2,
    ).astype(jnp.bfloat16)
    joined_up_term = matrix_product(
        "pvh,pvfo->phfo", initial_slim_derivative, query_key_value_gradient
    )
    first_gradient_part = matrix_product(
        "kxsd,ktsd->kxt", query_key_value_gradient, select_joined_up
    )
    grad_norm_one_part = matrix_product("clje,dje->cld", query_key_value_gradient, back_joined)
    gradient_first = lax.psum(first_gradient_part.astype(jnp.bfloat16), "tp")
    grad_norm_share = lax.psum_scatter(
        grad_norm_one_part.astype(jnp.bfloat16), "tp", scatter_dimension=1, tiled=True
    ).astype(jnp.float32)
    joined_down_term = matrix_product("kgt,kgh->kth", initial_standardized, gradient_first)
    half_len = grad_norm_share.shape[1]
    begin = lax.axis_index("tp") * half_len

    def shared_rows(array):
        return lax.dynamic_slice_in_dim(array, begin, half_len, 1)

    grad_norm_one = grad_norm_share + matrix_product(
        "jqt,jit->jqi", shared_rows(gradient_first), select_joined_down
    )
    tokens_grad = (
        shared_rows(grad_hidden)
        + norm_back(grad_norm_one, shared_rows(scaled_one), shared_rows(inverse_one), first_gain)
    ).astype(jnp.bfloat16)
    choose_full = choose.astype(jnp.float32)

    def by_adapter(term):
        return jnp.einsum(
            "ca,c...->a...",
            choose_full,
            term,
            precision=lax.Precision.HIGHEST,
            preferred_element_type=jnp.float32,
        )

    summed = lax.psum(
        (
            by_adapter(joined_down_term),
            by_adapter(joined_up_term),
            by_adapter(output_down_term),
            by_adapter(output_up_term),
            by_adapter(expand_down_term),
            by_adapter(expand_up_term),
            by_adapter(reduce_down_term),
            by_adapter(reduce_up_term),
        ),
        ("shard", "ctx"),
    )
    return (
        output,
        tokens_grad,
        summed[0],
        summed[1],
        summed[2],
        summed[3],
        summed[4],
        summed[5],
        summed[6],
        summed[7],
    )


B16 = jnp.bfloat16
F32 = jnp.float32
VMEM_LIMIT = 60 * 2**20
exp_scale = score_scale * math.log2(math.e)


def dot(left, right, left_dim=1, right_dim=0):
    return lax.dot_general(
        left, right, (((left_dim,), (right_dim,)), ((), ())), preferred_element_type=F32
    )


def params():
    return pltpu.CompilerParams(vmem_limit_bytes=VMEM_LIMIT)


def low_lanes():
    return lax.broadcasted_iota(jnp.int32, (1, 128), 1) < 64


def partner(values):
    lane = lax.broadcasted_iota(jnp.int32, (1, 128), 1) % 64 % 20
    return jnp.where(lane < 10, pltpu.roll(values, 118, 1), pltpu.roll(values, 10, 1))


def row_norm(values):
    centred = values - jnp.mean(values, -1, keepdims=True)
    inverse = lax.rsqrt(jnp.mean(centred * centred, -1, keepdims=True) + eps_norm)
    return centred * inverse, inverse


def back_norm(weighted, scaled, inverse):
    return inverse * (
        weighted
        - jnp.mean(weighted, -1, keepdims=True)
        - scaled * jnp.mean(weighted * scaled, -1, keepdims=True)
    )


MESH = pl.DeviceIdType.MESH
HIDDEN_BLOCK = 512
(UP_SENT, DOWN_SENT, Z_CAME, TP_SENT, TP_CAME, OWN_SENT, OWN_CAME, NEXT_SENT, NEXT_CAME) = range(9)


class Place:
    def __init__(self, planes):
        self.planes = planes
        self.shard = lax.axis_index("shard")
        self.z = self.shard // 2
        self.core = self.shard % 2
        self.ctx = lax.axis_index("ctx")
        self.tp = lax.axis_index("tp")
        self.has_up = self.z < planes - 1
        self.has_down = self.z > 0
        self.crosses = self.core != self.ctx
        self.up = {"shard": self.shard + 2}
        self.down = {"shard": self.shard - 2}
        self.next_tp = {"tp": 1 - self.tp}
        self.next_core = {"shard": 2 * self.z + 1 - self.core}
        self.turned = {"shard": 2 * self.z + self.ctx, "ctx": self.core}

    def greet(self, planes_too, turned, ctx_too=False, flipped=False):
        barrier = pltpu.get_barrier_semaphore()
        count = 2

        def signal(device):
            pl.semaphore_signal(barrier, inc=1, device_id=device, device_id_type=MESH)

        signal(self.next_tp)
        signal(self.next_core)
        if planes_too:
            pl.when(self.has_up)(lambda: signal(self.up))
            pl.when(self.has_down)(lambda: signal(self.down))
            count = count + self.has_up.astype(jnp.int32) + self.has_down.astype(jnp.int32)
        if turned:
            pl.when(self.crosses)(lambda: signal(self.turned))
            count = count + self.crosses.astype(jnp.int32)
        if ctx_too:
            signal({"ctx": 1 - self.ctx})
            count = count + 1
        if flipped:
            flip = dict(self.turned)
            flip["tp"] = 1 - self.tp
            pl.when(self.crosses)(lambda: signal(flip))
            count = count + self.crosses.astype(jnp.int32)
        pl.semaphore_wait(barrier, count)


class Flow:
    def __init__(self, at, own, slot, sems, kinds=tuple(range(9))):
        self.at, self.own, self.slot = at, own, slot
        self.sems = {kind: sems[i] for i, kind in enumerate(kinds)}

    def copy(self, kind, plane, own=False):
        at = self.at
        half = 1 - at.tp if kind == NEXT_SENT else at.tp
        piece = self.slot(2 * plane + at.core, half)
        device, came = {
            UP_SENT: (at.up, Z_CAME),
            DOWN_SENT: (at.down, Z_CAME),
            TP_SENT: (at.next_tp, TP_CAME),
            OWN_SENT: (at.next_core, OWN_CAME),
            NEXT_SENT: (at.next_core, NEXT_CAME),
        }[kind]
        return pltpu.make_async_remote_copy(
            src_ref=self.own if own else piece,
            dst_ref=piece,
            send_sem=self.sems[kind].at[plane],
            recv_sem=self.sems[came].at[plane],
            device_id=device,
            device_id_type=MESH,
        )

    def came(self, kind, plane):
        at = self.at
        shard = 2 * plane + (at.core if kind in (Z_CAME, TP_CAME) else 1 - at.core)
        half = at.tp if kind in (Z_CAME, OWN_CAME) else 1 - at.tp
        piece = self.slot(shard, half)
        return pltpu.make_async_remote_copy(
            src_ref=piece, dst_ref=piece, send_sem=self.sems[kind].at[plane],
            recv_sem=self.sems[kind].at[plane], device_id=at.next_core, device_id_type=MESH,
        )

    def pieces(self, distance):
        at = self.at
        if distance == 0:
            return [(None, at.z, True, True)]
        return [
            (at.z >= distance, at.z - distance, True, False),
            (at.z < at.planes - distance, at.z + distance, False, True),
        ]

    def each(self, distance, act):
        for there, plane, below, above in self.pieces(distance):
            if there is None:
                act(plane, below, above)
            else:
                pl.when(there)(functools.partial(act, plane, below, above))

    def pass_on(self, distance, z=False, tp=False, core=False, fresh=None, wait=False):
        own = (distance == 0) if fresh is None else fresh

        def act(plane, below, above):
            if wait:
                self.came(Z_CAME, plane).wait_recv()
            if z:
                if below:
                    pl.when(self.at.has_up)(lambda: self.copy(UP_SENT, plane, own).start())
                if above:
                    pl.when(self.at.has_down)(lambda: self.copy(DOWN_SENT, plane, own).start())
            if tp:
                self.copy(TP_SENT, plane, own).start()
            if core:
                self.copy(OWN_SENT, plane, own).start()

        self.each(distance, act)

    def sent(self, distance, z=False, tp=False, core=False):
        def act(plane, below, above):
            if z:
                if below:
                    pl.when(self.at.has_up)(lambda: self.copy(UP_SENT, plane).wait_send())
                if above:
                    pl.when(self.at.has_down)(lambda: self.copy(DOWN_SENT, plane).wait_send())
            if tp:
                self.copy(TP_SENT, plane).wait_send()
            if core:
                self.copy(OWN_SENT, plane).wait_send()

        self.each(distance, act)

    def wait(self, kind, distance):
        self.each(distance, lambda plane, below, above: self.came(kind, plane).wait_recv())

    def pass_next(self, distance, wait=True):
        def act(plane, below, above):
            if wait:
                self.came(TP_CAME, plane).wait_recv()
            self.copy(NEXT_SENT, plane).start()

        self.each(distance, act)

    def sent_next(self, distance):
        self.each(distance, lambda plane, below, above: self.copy(NEXT_SENT, plane).wait_send())


ALONG_Z = (UP_SENT, DOWN_SENT, Z_CAME)
TO_TP = (TP_SENT, TP_CAME)
TO_CORE = (OWN_SENT, OWN_CAME)
TO_NEXT = (NEXT_SENT, NEXT_CAME)
EVERY = ALONG_Z + TO_TP + TO_CORE + TO_NEXT


class Rows:
    def __init__(self, sems):
        self.sems, self.used = sems, 0

    def take(self, kinds):
        rows = [self.sems.at[self.used + i] for i in range(len(kinds))]
        self.used += len(kinds)
        return rows


def block_flows(at, own_e, own_r, full_e, full_r, rows, kinds):
    flows = []
    for block, needs in enumerate(kinds):
        span = pl.ds(block * HIDDEN_BLOCK, HIDDEN_BLOCK)
        flows.append(
            [
                Flow(
                    at, None if own_e is None else own_e.at[:, span],
                    lambda s, h, span=span: full_e.at[s, h, :, span], rows.take(needs), needs,
                ),
                Flow(
                    at, None if own_r is None else own_r.at[span, :],
                    lambda s, h, span=span: full_r.at[s, h, span, :], rows.take(needs), needs,
                ),
            ]
        )
    return flows


def count_rows(first, kinds):
    return len(first) + 2 * sum(len(needs) for needs in kinds)


PROJECT_KINDS = (ALONG_Z, ALONG_Z)
ATTEND_KINDS = (EVERY, ALONG_Z + TO_TP + TO_CORE, ALONG_Z + TO_CORE, ALONG_Z)
MIDDLE_KINDS = ((), TO_NEXT, TO_TP + TO_NEXT, EVERY)


def turned_copy(at, source, target, sems):
    return pltpu.make_async_remote_copy(
        src_ref=source, dst_ref=target, send_sem=sems.at[0], recv_sem=sems.at[1],
        device_id=at.turned, device_id_type=MESH,
    )


class Spread:
    def __init__(self, at, split, full, tag, sums, give, take, pass_tp, stack, beyond, sems):
        self.at, self.split, self.full, self.tag, self.sums = at, split, full, tag, sums
        self.give, self.take, self.pass_tp, self.stack, self.beyond, self.sems = (
            give, take, pass_tp, stack, beyond, sems,
        )
        self.ranks = give.shape[0]
        self.width = split.shape[2]
        self.rest = full.shape[1]

    def remote(self, source, target, index, device):
        return pltpu.make_async_remote_copy(
            src_ref=source, dst_ref=target, send_sem=self.sems.at[0, index], recv_sem=self.sems.at[1, index],
            device_id=device, device_id_type=MESH,
        )

    def between_cores(self):
        return self.remote(self.give, self.take, 0, self.at.next_core)

    def to_tp(self):
        return self.remote(self.pass_tp, self.stack.at[self.at.z, 1], 1, self.at.next_tp)

    def to_ctx(self):
        plane = self.stack.at[self.at.z]
        return self.remote(plane.at[pl.ds(0, 2)], plane.at[pl.ds(2, 2)], 2, {"ctx": 1 - self.at.ctx})

    def along(self, up, plane):
        piece = self.stack.at[plane]
        return pltpu.make_async_remote_copy(
            src_ref=piece, dst_ref=piece, send_sem=self.sems.at[2 + up, plane], recv_sem=self.sems.at[4, plane],
            device_id=self.at.up if up else self.at.down, device_id_type=MESH,
        )

    def over(self, plane):
        return pltpu.make_async_remote_copy(
            src_ref=self.stack.at[plane], dst_ref=self.beyond.at[plane],
            send_sem=self.sems.at[5, plane], recv_sem=self.sems.at[6, plane],
            device_id=self.at.next_core, device_id_type=MESH,
        )

    def rows(self, core):
        return pl.ds(pl.multiple_of(core * self.ranks, self.ranks), self.ranks)

    def start(self):
        theirs = self.rows(1 - self.at.core)
        for half in range(2):
            self.give[:, half * self.width : (half + 1) * self.width] = self.split[half, theirs, :].astype(B16)
        self.give[:, 2 * self.width :] = self.full[theirs, :].astype(B16)
        self.between_cores().start()

    def second(self):
        at, width, rest = self.at, self.width, self.rest
        self.between_cores().wait_recv()
        mine = self.rows(at.core)
        for half, target in ((at.tp, self.stack.at[at.z, 0]), (1 - at.tp, self.pass_tp)):
            span = pl.ds(pl.multiple_of(half * width, 128), width)
            target[:, 0:width] = (self.split[half, mine, :] + self.take[:, span].astype(F32)).astype(B16)
            target[:, width : width + rest] = (
                self.full[mine, :] + self.take[:, 2 * width :].astype(F32)
            ).astype(B16)
            target[:, width + rest :] = self.tag
        self.to_tp().start()

    def third(self):
        self.to_tp().wait_recv()
        self.to_ctx().start()

    def both_ways(self, act_up, act_down, distance):
        at = self.at
        if distance == 0:
            pl.when(at.has_up)(functools.partial(act_up, at.z))
            pl.when(at.has_down)(functools.partial(act_down, at.z))
        else:
            pl.when((at.z >= distance) & at.has_up)(functools.partial(act_up, at.z - distance))
            pl.when((at.z < at.planes - distance) & at.has_down)(functools.partial(act_down, at.z + distance))

    def came(self, distance, act):
        at = self.at
        pl.when(at.z >= distance)(functools.partial(act, at.z - distance))
        pl.when(at.z < at.planes - distance)(functools.partial(act, at.z + distance))

    def planes(self, distance):
        if distance == 0:
            self.to_ctx().wait_recv()
        else:
            self.came(distance, lambda plane: self.along(1, plane).wait_recv())
        if distance < self.at.planes - 1:
            self.both_ways(
                lambda plane: self.along(1, plane).start(), lambda plane: self.along(0, plane).start(), distance
            )
        if distance == 0:
            self.over(self.at.z).start()
        else:
            self.came(distance, lambda plane: self.over(plane).start())

    def finish(self):
        at = self.at
        for plane in range(at.planes):
            self.over(plane).wait_recv()
        keep = self.width + self.rest
        adapters, ranks = self.sums.shape[0], self.ranks
        terms = at.planes * 4 * ranks
        lane = lax.broadcasted_iota(jnp.int32, (terms, 128), 1)
        rank_of = lax.broadcasted_iota(jnp.int32, (terms, 128), 0) % ranks
        for source, core in ((self.stack, at.core), (self.beyond, 1 - at.core)):
            tags = source[:, :, :, keep:].reshape(terms, 128).astype(F32)
            picks = (tags == (lane // ranks).astype(F32)) & (lane % ranks == rank_of)
            choose = jnp.where(picks, 1.0, 0.0).astype(B16)
            for begin in range(0, keep, 512):
                span = pl.ds(begin, min(512, keep - begin))
                total = dot(choose, source[:, :, :, span].reshape(terms, -1), 0, 0)
                for adapter in range(adapters):
                    self.sums[adapter, self.rows(core), span] = total[adapter * ranks : (adapter + 1) * ranks]

    def sent(self):
        self.between_cores().wait_send()
        self.to_tp().wait_send()
        self.to_ctx().wait_send()
        for distance in range(self.at.planes - 1):
            self.both_ways(
                lambda plane: self.along(1, plane).wait_send(),
                lambda plane: self.along(0, plane).wait_send(),
                distance,
            )
        for plane in range(self.at.planes):
            self.over(plane).wait_send()

    @staticmethod
    def scratch(planes, ranks, width, rest):
        wide = width + rest + 128
        return [
            pltpu.VMEM((ranks, 2 * width + rest), B16),
            pltpu.VMEM((ranks, 2 * width + rest), B16),
            pltpu.VMEM((ranks, wide), B16),
            pltpu.VMEM((planes, 4, ranks, wide), B16),
            pltpu.VMEM((planes, 4, ranks, wide), B16),
            pltpu.SemaphoreType.DMA((7, max(planes, 4))),
        ]


ROWS = 256


def project_body(
    planes, blocks,
    tokens_ref, pick_ref, places_ref, bias_ref, wide_ref,
    tab_jd, tab_ed, tab_ou, tab_ru, tab_ju, tab_od, tab_eu, tab_rd,
    w_ref, own_o, own_e, own_r, gain_ref, shift_ref, rates_ref,
    x_out, factors_out, shared_out, offsets_out, w_out, full_o, full_e, full_r,
    q_out, k_out, v_out, xn_out, u_out, cos_out, sin_out,
    spots_ref, offsets_ref, factors_ref, factors_next, shared_ref,
    vm_jd, vm_ed, vm_ou, vm_ru, vm_ju, vm_od, vm_eu, vm_rd,
    x_vm, w_vm, acc, stage, spots_all, factors_vm, offsets_vm, jd_vm,
    w_sems, flow_sems, x_sems, spot_sems, factor_sems, shared_sems, offset_sems, local_sems, out_sems, move_sems, table_sems,
):
    at = Place(planes)
    rows_all, width = x_vm.shape
    depth, half = w_ref.shape[1:]
    at.greet(True, True)
    chunks = rows_all // ROWS
    parts = [
        Flow(
            at, w_ref.at[part], lambda s, h, part=part: w_out.at[s, h, part],
            [w_sems.at[part, kind] for kind in range(9)],
        )
        for part in range(3)
    ]
    taken = Rows(flow_sems)
    flow_o = Flow(at, own_o, lambda s, h: full_o.at[s, h], taken.take(ALONG_Z), ALONG_Z)
    flows = block_flows(at, own_e, own_r, full_e, full_r, taken, PROJECT_KINDS)
    ahead = [flow_o] + flows[0] + flows[1]
    holds = at.core == at.ctx

    def local(source, target, index):
        return pltpu.make_async_copy(source, target, local_sems.at[index])

    for flow in parts:
        flow.pass_on(0, z=True, tp=True)
    tables_in = [
        pltpu.make_async_copy(source, target, table_sems.at[i])
        for i, (source, target) in enumerate(
            (
                (tab_jd, vm_jd), (tab_ed, vm_ed), (tab_ou, vm_ou), (tab_ru, vm_ru),
                (tab_ju, vm_ju), (tab_od, vm_od), (tab_eu, vm_eu), (tab_rd, vm_rd),
            )
        )
    ]
    for table in tables_in:
        table.start()
    place_rows = [places_ref[band, pl.ds(at.tp, 1), :].astype(F32) for band in range(3)]
    spots_ref[...] = jnp.concatenate(
        place_rows * 3 + [jnp.zeros((spots_ref.shape[0] - 9, rows_all), F32)], axis=0
    ).astype(B16)
    for part in range(3):
        offsets_ref[:, part * half : (part + 1) * half] = bias_ref[part : part + 1, :]
    offsets_ref[:, 3 * half :] = wide_ref[...]

    def x_chunk(i):
        span = pl.ds(i * ROWS, ROWS)
        return turned_copy(at, tokens_ref.at[at.tp, span], x_vm.at[span], x_sems.at[i])

    spot_copy = turned_copy(at, spots_ref, spots_all.at[0], spot_sems.at[0])

    @pl.when(at.crosses)
    def _():
        spot_copy.start()
        for i in range(chunks):
            x_chunk(i).start()

    @pl.when(holds)
    def _():
        spots_all[0] = spots_ref[...]
        for i in range(chunks):
            span = pl.ds(i * ROWS, ROWS)
            local(tokens_ref.at[at.tp, span], x_vm.at[span], 1 + i).start()

    for flow in parts:
        flow.pass_on(0, core=True)

    def remote(source, target, sems, device):
        return pltpu.make_async_remote_copy(
            src_ref=source, dst_ref=target, send_sem=sems.at[0], recv_sem=sems.at[1],
            device_id=device, device_id_type=MESH,
        )

    offset_copy = remote(offsets_ref, offsets_out.at[at.tp], offset_sems, at.next_tp)
    offset_came = remote(offsets_ref, offsets_out.at[1 - at.tp], offset_sems, at.next_tp)
    offset_copy.start()
    local(offsets_ref, offsets_out.at[at.tp], 1 + chunks).start()
    next_copy = remote(factors_next, factors_out.at[at.tp], factor_sems.at[0], at.next_tp)
    next_came = remote(factors_next, factors_out.at[1 - at.tp], factor_sems.at[0], at.next_tp)
    own_factors = remote(factors_ref, factors_out.at[at.tp], factor_sems.at[1], at.next_core)
    shared_copy = remote(shared_ref, shared_out, shared_sems, at.next_core)
    next_factors = remote(factors_out.at[1 - at.tp], factors_out.at[1 - at.tp], factor_sems.at[2], at.next_core)

    local(w_ref, w_out.at[at.shard, at.tp], 4 + chunks).start()
    local(own_o, full_o.at[at.shard, at.tp], 5 + chunks).start()
    local(own_e, full_e.at[at.shard, at.tp], 6 + chunks).start()
    local(own_r, full_r.at[at.shard, at.tp], 7 + chunks).start()

    @pl.when(at.crosses)
    def _():
        spot_copy.wait_recv()

    spot_next = remote(spots_all.at[0], spots_all.at[1], spot_sems.at[1], at.next_core)
    spot_next.start()

    lane = lax.broadcasted_iota(jnp.int32, (1, 128), 1) % 64
    turned = lane < 60
    early = lane % 20 < 10

    def tables(part):
        def body(i, carry):
            span = pl.ds(pl.multiple_of(i * ROWS, ROWS), ROWS)
            angle = dot(spots_all[part, :, span], rates_ref[...], 0, 0)
            out = pl.ds(pl.multiple_of(part * rows_all + i * ROWS, ROWS), ROWS)
            cos_out[out, :] = jnp.where(turned, jnp.cos(angle), 1.0)
            sine = jnp.sin(angle)
            sin_out[out, :] = jnp.where(turned, jnp.where(early, -sine, sine), 0.0)
            return carry

        lax.fori_loop(0, chunks, body, 0)

    tables(0)

    for table in tables_in:
        table.wait()

    def chosen(table, pick):
        return sum(
            table[i].astype(F32) * jnp.where(pick == i, 1.0, 0.0) for i in range(table.shape[0])
        ).astype(B16)

    picks = (pick_ref[0], pick_ref[1])
    pick = jnp.where(at.tp == 0, picks[0], picks[1])
    for target, which in ((factors_ref, pick), (factors_next, picks[0] + picks[1] - pick)):
        ju = chosen(vm_ju, which)
        for part in range(3):
            target[:, part * half : (part + 1) * half] = ju[part]
        begin = 3 * half
        for table in (vm_od, vm_eu, vm_rd):
            target[:, begin : begin + table.shape[2]] = chosen(table, which)
            begin += table.shape[2]
    for i, table in enumerate((vm_jd, vm_ed, vm_ou, vm_ru)):
        shared_ref[:, i * width : (i + 1) * width] = chosen(table, pick)
    shared_ref[:, 4 * width :] = jnp.full((shared_ref.shape[0], 128), pick.astype(F32)).astype(B16)

    @pl.when(holds)
    def _():
        next_copy.start()
        own_factors.start()
        shared_copy.start()
        local(factors_ref, factors_out.at[at.tp], 2 + chunks).start()
        local(shared_ref, shared_out, 3 + chunks).start()

    for flow in parts:
        flow.pass_on(1, z=True, tp=True, core=True, wait=True)
    spot_next.wait()
    tables(1)

    @pl.when(holds)
    def _():
        next_came.wait_recv()
        next_factors.start()

    for flow in parts:
        flow.pass_on(2, z=True, tp=True, core=True, wait=True)

    @pl.when(holds)
    def _():
        local(factors_ref, factors_out.at[at.tp], 2 + chunks).wait()
        local(shared_ref, shared_out, 3 + chunks).wait()
        own_factors.wait_send()
        shared_copy.wait_send()
        next_copy.wait_send()
        next_factors.wait_send()

    @pl.when(at.crosses)
    def _():
        own_factors.wait_recv()
        shared_copy.wait_recv()
        remote(factors_out.at[1 - at.tp], factors_out.at[1 - at.tp], factor_sems.at[2], at.next_core).wait_recv()

    offset_copy.wait_send()
    offset_came.wait_recv()
    local(offsets_ref, offsets_out.at[at.tp], 1 + chunks).wait()
    loads = [
        pltpu.make_async_copy(factors_out, factors_vm, out_sems.at[0]),
        pltpu.make_async_copy(offsets_out, offsets_vm, out_sems.at[1]),
        pltpu.make_async_copy(shared_out.at[:, pl.ds(0, width)], jd_vm, out_sems.at[2]),
    ]
    for load in loads:
        load.start()
    for load in loads:
        load.wait()

    kept = []

    def x_ready(i):
        span = pl.ds(i * ROWS, ROWS)

        @pl.when(at.crosses)
        def _():
            x_chunk(i).wait()

        @pl.when(holds)
        def _():
            local(tokens_ref.at[at.tp, span], x_vm.at[span], 1 + i).wait()

        keep = pltpu.make_async_copy(x_vm.at[span], x_out.at[span], x_sems.at[i, 2])
        keep.start()
        kept.append(keep)
        scaled, _ = row_norm(x_vm[span, :].astype(F32))
        xn = (scaled * gain_ref[...] + shift_ref[...]).astype(B16)
        xn_out[span, :] = xn
        u_out[span, :] = dot(xn, jd_vm[...], 1, 1).astype(B16)

    outs = (q_out, k_out, v_out)
    sending = []
    orders = ((0, 1, 2, 3), (1, 0, 2, 3), (2, 3, 1, 0), (3, 2, 1, 0))

    def plane_at(turn):
        plane = jnp.int32(orders[0][turn])
        for z in range(1, planes):
            plane = jnp.where(at.z == z, orders[z][turn], plane)
        return plane

    def to_next(turn):
        for flow in parts:
            flow.came(TP_CAME, plane_at(turn)).wait_recv()
            flow.copy(NEXT_SENT, plane_at(turn)).start()

    def w_load(turn):
        shards_of = pl.ds(2 * plane_at(turn), 2)
        return pltpu.make_async_copy(w_out.at[shards_of], w_vm.at[turn], out_sems.at[turn])

    def take_plane(turn):
        for flow in parts:
            flow.came(OWN_CAME, plane_at(turn)).wait_recv()
            flow.came(NEXT_CAME, plane_at(turn)).wait_recv()
        w_load(turn).start()

    def columns_of(turn):
        return pl.ds(pl.multiple_of(plane_at(turn) * 2 * depth, 2 * depth), 2 * depth)

    wide = rows_all // 2

    def product(turns, owner, part, span):
        value = 0.0
        for turn in turns:
            w = w_vm[turn, :, owner, part].reshape(2 * depth, half)
            value += dot(xn_out[span, columns_of(turn)], w)
        return value

    owners = (1 - at.core, at.core)

    def add_first(turns):
        for order, owner in enumerate(owners):
            for part in range(3):
                for begin in range(0, rows_all, wide):
                    span = pl.ds(begin, wide)
                    acc[order, part, span, :] = product(turns, owner, part, span)

    def add_last(turn):
        for order, owner in enumerate(owners):
            for part in range(3):
                bias = offsets_vm[owner, :, part * half : (part + 1) * half]
                up = factors_vm[owner, :, part * half : (part + 1) * half]
                for begin in range(0, rows_all, wide):
                    span = pl.ds(begin, wide)
                    value = acc[order, part, span, :] + bias + product((turn,), owner, part, span)
                    value += dot(u_out[span, :], up)
                    if part == 2:
                        stage[order, part, span, :] = value.astype(B16)
                        continue
                    for col in range(0, half, 128):
                        piece = value[:, col : col + 128]
                        stage[order, part, span, col : col + 128] = (
                            piece * cos_out[span, :] + partner(piece) * sin_out[span, :]
                        ).astype(B16)
                if order == 0:
                    move = remote(
                        stage.at[order, part], outs[part].at[pl.ds(rows_all, rows_all)],
                        move_sems.at[part], at.next_core,
                    )
                else:
                    move = pltpu.make_async_copy(
                        stage.at[order, part], outs[part].at[pl.ds(0, rows_all)], out_sems.at[4 + part]
                    )
                move.start()
                sending.append(move)

    to_next(0)
    to_next(1)
    for i in range(chunks):
        x_ready(i)
    for flow in parts:
        flow.pass_on(3, tp=True, core=True, wait=True)
    for other in ahead:
        other.pass_on(0, z=True)
    local(w_ref, w_out.at[at.shard, at.tp], 4 + chunks).wait()
    take_plane(0)
    take_plane(1)
    to_next(2)
    take_plane(2)
    for turn in range(3):
        w_load(turn).wait()
    add_first((0, 1, 2))
    to_next(3)
    take_plane(3)
    w_load(3).wait()
    add_last(3)

    for keep in kept:
        keep.wait()
    for other in ahead:
        other.wait(Z_CAME, 1)
        other.sent(0, z=True)
    for flow in parts:
        for far in range(planes):
            flow.sent(far, z=far < planes - 1, tp=True, core=True)
            flow.sent_next(far)
    for i in range(3):
        local((own_o, own_e, own_r)[i], (full_o, full_e, full_r)[i].at[at.shard, at.tp], 5 + i + chunks).wait()

    @pl.when(at.crosses)
    def _():
        spot_copy.wait_send()

    for move in sending:
        move.wait()


def project(planes, tokens, picks, places, bias, wide, tables, weight, own_o, own_e, own_r, gain, shift, rates):
    rows, width = tokens.shape[1:]
    _, depth, half = weight.shape
    rank = tables[0].shape[1]
    blocks = own_e.shape[1] // HIDDEN_BLOCK
    chunks = rows // ROWS
    shape = jax.ShapeDtypeStruct
    hbm = pl.BlockSpec(memory_space=pl.ANY)
    vmem = pl.BlockSpec(memory_space=pltpu.VMEM)
    smem = pl.BlockSpec(memory_space=pltpu.SMEM)
    dma = pltpu.SemaphoreType.DMA
    factors = shape((rank, 3 * half + sum(table.shape[2] for table in tables[5:])), B16)
    shared = shape((rank, 4 * width + 128), B16)
    offsets = shape((1, 3 * half + wide.shape[1]), F32)
    spots = shape(rates.shape[:1] + (rows,), B16)
    return pl.pallas_call(
        functools.partial(project_body, planes, blocks),
        in_specs=[hbm, smem] + [vmem] * 3 + [hbm] * 8 + [vmem] * 7,
        out_specs=[hbm] * 11 + [vmem] * 4,
        out_shape=[
            shape((rows, width), B16),
            shape((2,) + factors.shape, B16),
            shape(shared.shape, B16),
            shape((2,) + offsets.shape, F32),
            shape((2 * planes, 2) + weight.shape, B16),
            shape((2 * planes, 2) + own_o.shape, B16),
            shape((2 * planes, 2) + own_e.shape, B16),
            shape((2 * planes, 2) + own_r.shape, B16),
            shape((2 * rows, half), B16),
            shape((2 * rows, half), B16),
            shape((2 * rows, half), B16),
            shape((rows, width), B16),
            shape((rows, rank), B16),
            shape((2 * rows, 128), F32),
            shape((2 * rows, 128), F32),
        ],
        scratch_shapes=[
            pltpu.VMEM(spots.shape, B16),
            pltpu.VMEM(offsets.shape, F32),
            pltpu.VMEM(factors.shape, B16),
            pltpu.VMEM(factors.shape, B16),
            pltpu.VMEM(shared.shape, B16),
        ]
        + [pltpu.VMEM(table.shape, B16) for table in tables]
        + [
            pltpu.VMEM((rows, width), B16),
            pltpu.VMEM((planes, 2, 2) + weight.shape, B16),
            pltpu.VMEM((2, 3, rows, half), F32),
            pltpu.VMEM((2, 3, rows, half), B16),
            pltpu.VMEM((2,) + spots.shape, B16),
            pltpu.VMEM((2,) + factors.shape, B16),
            pltpu.VMEM((2,) + offsets.shape, F32),
            pltpu.VMEM((rank, width), B16),
            dma((3, 9, planes)),
            dma((count_rows(ALONG_Z, PROJECT_KINDS), planes)),
            dma((chunks, 3)),
            dma((2, 2)),
            dma((3, 2)),
            dma((2,)),
            dma((2,)),
            dma((8 + chunks,)),
            dma((7,)),
            dma((3, 2)),
            dma((8,)),
        ],
        compiler_params=pltpu.CompilerParams(
            vmem_limit_bytes=VMEM_LIMIT, collective_id=0, has_side_effects=True
        ),
        cost_estimate=pl.CostEstimate(
            flops=2 * rows * width * 6 * half, bytes_accessed=100 * 2**20, transcendentals=0
        ),
    )(tokens, picks, places, bias, wide, *tables, weight, own_o, own_e, own_r, gain, shift, rates)


def attend_body(
    planes, blocks,
    q_ref, k_ref, v_ref, cot_ref, own_o, own_e, own_r, in_o, in_e, in_r,
    o_ref, inv_ref, e_ref, o_next, cot_out, full_o, full_e, full_r,
    vm_ref, stage, cot_vm, flow_sems, stage_sems, cot_sems,
):
    at = Place(planes)
    rows_all, length = q_ref.shape[0], k_ref.shape[0]
    low = low_lanes()
    pair, turn = pl.program_id(0), pl.program_id(1)
    turns = length // rows_all
    now = pair * turns + turn
    pairs = stage.shape[0] // (turns // 2)
    count = pairs * turns
    taken = Rows(flow_sems)
    flow_o = Flow(at, own_o, lambda s, h: full_o.at[s, h], taken.take(EVERY), EVERY)
    flows = block_flows(at, own_e, own_r, full_e, full_r, taken, ATTEND_KINDS)
    zero = [flow_o] + flows[0]
    last = planes - 1
    cot_move = turned_copy(at, cot_ref.at[at.tp], cot_out, cot_sems)
    cot_load = pltpu.make_async_copy(cot_ref.at[at.tp], cot_vm, cot_sems.at[2])
    cot_keep = pltpu.make_async_copy(cot_vm, cot_out, cot_sems.at[3])

    def when(step, act):
        pl.when(now == min(step * count // 16, count - 1))(act)

    @pl.when(now == 0)
    def _():
        at.greet(True, True)
        for flow in zero:
            flow.pass_on(1, z=True)
            flow.pass_on(0, tp=True)
        pl.when(at.crosses)(lambda: cot_move.start())
        pl.when(jnp.logical_not(at.crosses))(lambda: cot_load.start())
        for flow in zero:
            flow.pass_on(0, core=True)
            flow.pass_on(1, core=True)
        for flow in flows[1] + flows[2]:
            flow.pass_on(0, core=True)

    def at_2():
        for flow in flows[1]:
            flow.pass_on(1, z=True, core=True)
        for flow in zero:
            flow.pass_on(1, tp=True)

    def at_3():
        @pl.when(jnp.logical_not(at.crosses))
        def _():
            cot_load.wait()
            cot_keep.start()

    def at_4():
        for flow in zero:
            flow.pass_on(2, z=True, tp=True, core=True, wait=True)

    def at_5():
        for flow in zero:
            flow.pass_next(0)

    def at_6():
        for flow in flows[1]:
            flow.pass_on(2, z=True, core=True, wait=True)
        for flow in flows[2]:
            flow.pass_on(0, z=True)

    def at_8():
        for flow in zero:
            flow.pass_on(3, tp=True, core=True, wait=True)

    def at_9():
        for flow in zero:
            flow.pass_next(1)
        for flow in flows[1]:
            flow.pass_on(0, tp=True)
            flow.pass_on(1, tp=True)

    def at_10():
        for flow in flows[2]:
            flow.pass_on(1, z=True, core=True, wait=True)
        for flow in flows[1]:
            flow.pass_on(3, core=True, wait=True)

    def at_12():
        for flow in flows[2]:
            flow.pass_on(2, z=True, core=True, wait=True)
        for flow in flows[3]:
            flow.pass_on(0, z=True)
        for flow in flows[1]:
            flow.pass_on(2, tp=True)
            flow.pass_on(3, tp=True)
        for flow in zero:
            flow.pass_next(2)
            flow.pass_next(3)

    def at_15():
        for flow in flows[2]:
            flow.pass_on(3, core=True, wait=True)

    for step, act in (
        (2, at_2), (3, at_3), (4, at_4), (5, at_5), (6, at_6), (8, at_8), (9, at_9), (10, at_10),
        (12, at_12), (15, at_15),
    ):
        when(step, act)

    @pl.when(turn == 0)
    def _():
        vm_ref[0] = jnp.where(low, v_ref[...], 1).astype(B16)
        vm_ref[1] = jnp.where(low, 1, v_ref[...]).astype(B16)

    step = min(256, rows_all)
    for begin in range(0, rows_all, step):
        rows = pl.ds(begin, step)
        q = q_ref[rows, :]
        sums = []
        for head in range(2):
            mine = low if head == 0 else ~low
            scores = dot(jnp.where(mine, q, 0).astype(B16), k_ref[...], 1, 1)
            top = jnp.max(scores, 1, keepdims=True)
            weights = jnp.exp2((scores - top) * exp_scale).astype(B16)
            e_ref[head, rows, :] = weights
            sums.append(dot(weights, vm_ref[head]))
        total = pltpu.roll(jnp.where(low, sums[1], sums[0]), 64, 1)
        inverse = 1.0 / total
        o_ref[rows, :] = (jnp.where(low, sums[0], sums[1]) * inverse).astype(B16)
        inv_ref[rows, :] = inverse

    def o_move(index):
        per = turns // 2
        rows = pl.ds(pl.multiple_of(index % per * rows_all, rows_all), rows_all)
        columns = pl.ds(pl.multiple_of(index // per * 128, 128), 128)
        return pltpu.make_async_remote_copy(
            src_ref=stage.at[index], dst_ref=o_next.at[rows, columns],
            send_sem=stage_sems.at[0, index], recv_sem=stage_sems.at[1, index],
            device_id=at.next_core, device_id_type=MESH,
        )

    @pl.when(turn >= turns // 2)
    def _():
        index = pair * (turns // 2) + turn - turns // 2
        stage[index] = o_ref[...]
        o_move(index).start()

    @pl.when(now == count - 1)
    def _():
        for flow in flows[3]:
            flow.wait(Z_CAME, 1)
        for flow in zero + flows[1] + flows[2]:
            for far in range(planes):
                flow.wait(OWN_CAME, far)
        for flow in zero:
            for far in range(planes):
                flow.wait(NEXT_CAME, far)
                flow.sent_next(far)
        for flow in flows[1]:
            for far in range(planes):
                flow.wait(TP_CAME, far)
        for flow in zero + flows[1]:
            for far in range(planes):
                flow.sent(far, z=0 < far < last, tp=True, core=True)
        for flow in flows[2]:
            for far in range(planes):
                flow.sent(far, z=far < last, core=True)
        for flow in flows[3]:
            flow.sent(0, z=True)

        @pl.when(at.crosses)
        def _():
            cot_move.wait()

        @pl.when(jnp.logical_not(at.crosses))
        def _():
            cot_keep.wait()

        for index in range(count // 2):
            o_move(index).wait()


def attend(planes, query, key, value, cotangent, own_o, own_e, own_r, full_o, full_e, full_r):
    length, width = query.shape
    block = min(512, length // 2)
    blocks = own_e.shape[1] // HIDDEN_BLOCK
    turns = length // block
    pairs = width // 128
    rows = pl.BlockSpec((block, 128), lambda p, i: (i, p))
    full = pl.BlockSpec((length, 128), lambda p, i: (0, p))
    hbm = pl.BlockSpec(memory_space=pl.ANY)
    shape = jax.ShapeDtypeStruct
    like = lambda array: shape(array.shape, array.dtype)
    dma = pltpu.SemaphoreType.DMA
    return pl.pallas_call(
        functools.partial(attend_body, planes, blocks),
        grid=(pairs, turns),
        in_specs=[rows, full, full] + [hbm] * 7,
        out_specs=[rows, rows, pl.BlockSpec((2, block, length), lambda p, i: (p, i, 0))] + [hbm] * 5,
        out_shape=[
            shape((length, width), B16),
            shape((length, width), F32),
            shape((width // 64, length, length), B16),
            shape((length // 2, width), B16),
            shape(cotangent.shape[1:], B16),
            like(full_o), like(full_e), like(full_r),
        ],
        input_output_aliases={7: 5, 8: 6, 9: 7},
        scratch_shapes=[
            pltpu.VMEM((2, length, 128), B16),
            pltpu.VMEM((pairs * turns // 2, block, 128), B16),
            pltpu.VMEM(cotangent.shape[1:], B16),
            dma((count_rows(EVERY, ATTEND_KINDS), planes)),
            dma((2, pairs * turns // 2)),
            dma((4,)),
        ],
        compiler_params=pltpu.CompilerParams(
            vmem_limit_bytes=VMEM_LIMIT, collective_id=1, has_side_effects=True
        ),
        cost_estimate=pl.CostEstimate(
            flops=16 * length * length * width,
            bytes_accessed=width // 64 * length * length * 2,
            transcendentals=width // 64 * length * length,
        ),
    )(query, key, value, cotangent, own_o, own_e, own_r, full_o, full_e, full_r)


def attend_back_body(
    planes,
    q_ref, k_ref, v_ref, o_ref, inv_ref, g_ref, e_ref, cos_ref, sin_ref, cos_all, sin_all,
    split_ref, full_ref, tag_ref, out_ref,
    own_ref, other_ref, sums_ref, home_ref,
    key_sum, value_sum, vm_ref, q_stage, kv_stage, out_vm, move_sems, out_sems, *spread_refs,
):
    at = Place(planes)
    rows_all, length = q_ref.shape[0], k_ref.shape[0]
    low = low_lanes()
    pair, at_step = pl.program_id(0), pl.program_id(1)
    pairs, turns = q_stage.shape[0], q_stage.shape[1]
    now = pair * turns + at_step
    count = pairs * turns
    local_rows = length // 2
    spread = Spread(at, split_ref, full_ref, tag_ref[...], sums_ref, *spread_refs)
    stays = jnp.logical_not(at.crosses)
    out_load = pltpu.make_async_copy(out_ref, out_vm, out_sems.at[0])
    out_keep = pltpu.make_async_copy(out_vm, home_ref.at[at.tp], out_sems.at[1])
    out_turn = pltpu.make_async_remote_copy(
        src_ref=out_ref, dst_ref=home_ref.at[at.tp], send_sem=out_sems.at[2], recv_sem=out_sems.at[3],
        device_id=at.turned, device_id_type=MESH,
    )

    def out_tp(source):
        return pltpu.make_async_remote_copy(
            src_ref=source, dst_ref=home_ref.at[at.tp], send_sem=out_sems.at[4], recv_sem=out_sems.at[5],
            device_id=at.next_tp, device_id_type=MESH,
        )

    def when(step, act):
        pl.when(now == step)(act)

    @pl.when(now == 0)
    def _():
        pl.when(stays)(lambda: out_load.start())
        at.greet(True, True, True)
        spread.start()

    when(2, spread.second)

    @pl.when(now == 3)
    def _():
        @pl.when(stays)
        def _():
            out_load.wait()
            out_keep.start()
            out_tp(out_vm).start()

    when(4, spread.third)

    @pl.when(now == 5)
    def _():
        pl.when(at.crosses)(lambda: out_turn.start())

    when(6, lambda: spread.planes(0))

    @pl.when(now == 11)
    def _():
        @pl.when(at.crosses)
        def _():
            out_turn.wait_recv()
            out_tp(home_ref.at[at.tp]).start()

    when(9, lambda: spread.planes(1))
    when(12, lambda: spread.planes(2))
    when(15, lambda: spread.planes(3))

    @pl.when(at_step == 0)
    def _():
        key_sum[...] = jnp.zeros_like(key_sum)
        value_sum[...] = jnp.zeros_like(value_sum)
        vm_ref[0] = jnp.where(low, v_ref[...], -1).astype(B16)
        vm_ref[1] = jnp.where(low, -1, v_ref[...]).astype(B16)

    step = min(256, rows_all)
    for begin in range(0, rows_all, step):
        rows = pl.ds(begin, step)
        grad = g_ref[rows, :].astype(F32) * inv_ref[rows, :]
        grad_low = grad.astype(B16)
        product = pltpu.roll(grad * o_ref[rows, :].astype(F32), 64, 1).astype(B16)
        q_turned = q_ref[rows, :].T
        g_turned = grad_low.T
        parts = []
        for head in range(2):
            mine = low if head == 0 else ~low
            weights = e_ref[head, rows, :]
            grad_probs = dot(jnp.where(mine, grad_low, product), vm_ref[head], 1, 1)
            grad_scores = (weights.astype(F32) * grad_probs).astype(B16)
            parts.append(dot(grad_scores, k_ref[...]))
            span = pl.ds(head * 64, 64)
            key_sum[span, :] += dot(q_turned[head * 64 : head * 64 + 64], grad_scores)
            value_sum[span, :] += dot(g_turned[head * 64 : head * 64 + 64], weights)
        gq = jnp.where(low, parts[0], parts[1]) * score_scale
        q_stage[pair, at_step, rows, :] = (
            gq * cos_ref[rows, :] + partner(gq * sin_ref[rows, :])
        ).astype(B16)

    def columns(index):
        return pl.ds(pl.multiple_of(index * 128, 128), 128)

    def q_here(pair_index, turn_index):
        rows = pl.ds(pl.multiple_of(turn_index * rows_all, rows_all), rows_all)
        return pltpu.make_async_copy(
            q_stage.at[pair_index, turn_index], own_ref.at[0, rows, columns(pair_index)],
            move_sems.at[0, pair_index * turns + turn_index],
        )

    def q_there(pair_index, turn_index):
        rows = pl.ds(pl.multiple_of(turn_index * rows_all - local_rows, rows_all), rows_all)
        index = pair_index * turns + turn_index
        return pltpu.make_async_remote_copy(
            src_ref=q_stage.at[pair_index, turn_index], dst_ref=other_ref.at[0, rows, columns(pair_index)],
            send_sem=move_sems.at[0, index], recv_sem=move_sems.at[1, index],
            device_id=at.next_core, device_id_type=MESH,
        )

    def kv_here(part, pair_index):
        return pltpu.make_async_copy(
            kv_stage.at[part, pair_index, pl.ds(0, local_rows)], own_ref.at[1 + part, :, columns(pair_index)],
            move_sems.at[2, 2 * pair_index + part],
        )

    def kv_there(part, pair_index):
        index = 2 * pair_index + part
        return pltpu.make_async_remote_copy(
            src_ref=kv_stage.at[part, pair_index, pl.ds(local_rows, local_rows)],
            dst_ref=other_ref.at[1 + part, :, columns(pair_index)],
            send_sem=move_sems.at[3, index], recv_sem=move_sems.at[4, index],
            device_id=at.next_core, device_id_type=MESH,
        )

    pl.when(at_step < turns // 2)(lambda: q_here(pair, at_step).start())
    pl.when(at_step >= turns // 2)(lambda: q_there(pair, at_step).start())

    @pl.when(at_step == turns - 1)
    def _():
        gk = key_sum[...].T * score_scale
        kv_stage[0, pair] = (gk * cos_all[...] + partner(gk * sin_all[...])).astype(B16)
        kv_stage[1, pair] = value_sum[...].T.astype(B16)
        for part in range(2):
            kv_here(part, pair).start()
            kv_there(part, pair).start()

    @pl.when(now == count - 1)
    def _():
        for pair_index in range(pairs):
            for turn_index in range(turns):
                if turn_index < turns // 2:
                    q_here(pair_index, turn_index).wait()
                else:
                    q_there(pair_index, turn_index).wait()
            for part in range(2):
                kv_here(part, pair_index).wait()
                kv_there(part, pair_index).wait()
        spread.finish()
        spread.sent()

        @pl.when(stays)
        def _():
            out_keep.wait()
            out_tp(out_vm).wait_send()

        @pl.when(at.crosses)
        def _():
            out_turn.wait_send()
            out_tp(home_ref.at[at.tp]).wait_send()

        pltpu.make_async_remote_copy(
            src_ref=home_ref.at[at.tp], dst_ref=home_ref.at[1 - at.tp], send_sem=out_sems.at[4],
            recv_sem=out_sems.at[5], device_id=at.next_tp, device_id_type=MESH,
        ).wait_recv()


def attend_back(planes, query, key, value, attended, inverse, grad, weights, cosine, sine, split, full, tag, out, adapters):
    length, width = query.shape
    block = min(512, length // 2)
    pairs, turns = width // 128, length // block
    rows = pl.BlockSpec((block, 128), lambda p, i: (i, p))
    whole = pl.BlockSpec((length, 128), lambda p, i: (0, p))
    table = pl.BlockSpec((block, 128), lambda p, i: (i, 0))
    one = lambda array: pl.BlockSpec(
        array.shape, lambda p, i: (0,) * len(array.shape), pipeline_mode=pl.Buffered(1)
    )
    hbm = pl.BlockSpec(memory_space=pl.ANY)
    shape = jax.ShapeDtypeStruct
    dma = pltpu.SemaphoreType.DMA
    ranks = full.shape[0] // 2
    keep = split.shape[2] + full.shape[1]
    sums = shape((adapters, 2 * ranks, keep), F32)
    return pl.pallas_call(
        functools.partial(attend_back_body, planes),
        grid=(pairs, turns),
        in_specs=[
            rows, whole, whole, rows, rows, rows,
            pl.BlockSpec((2, block, length), lambda p, i: (p, i, 0)),
            table, table, one(cosine), one(sine), one(split), one(full), one(tag), hbm,
        ],
        out_specs=[hbm, hbm, one(sums), hbm],
        out_shape=[
            shape((3, length // 2, width), B16), shape((3, length // 2, width), B16), sums,
            shape((2,) + out.shape, B16),
        ],
        scratch_shapes=[
            pltpu.VMEM((128, length), F32),
            pltpu.VMEM((128, length), F32),
            pltpu.VMEM((2, length, 128), B16),
            pltpu.VMEM((pairs, turns, block, 128), B16),
            pltpu.VMEM((2, pairs, length, 128), B16),
            pltpu.VMEM(out.shape, B16),
            dma((5, max(pairs * turns, 2 * pairs))),
            dma((6,)),
        ]
        + Spread.scratch(planes, ranks, split.shape[2], full.shape[1]),
        compiler_params=pltpu.CompilerParams(
            vmem_limit_bytes=VMEM_LIMIT, collective_id=3, has_side_effects=True
        ),
        cost_estimate=pl.CostEstimate(
            flops=20 * length * length * width,
            bytes_accessed=width // 64 * length * length * 2,
            transcendentals=0,
        ),
    )(query, key, value, attended, inverse, grad, weights, cosine, sine, cosine, sine, split, full, tag, out)


def gauss_parts(z):
    t = 1.0 / (1.0 + (0.3275911 * math.sqrt(0.5)) * jnp.abs(z))
    poly = t * (0.254829592 + t * (-0.284496736 + t * (1.421413741 + t * (-1.453152027 + t * 1.061405429))))
    bell = jnp.exp2((z * z) * (-0.5 * math.log2(math.e)))
    upper = 0.5 * poly * bell
    cdf = jnp.where(z >= 0, 1.0 - upper, upper)
    return cdf, bell * (1.0 / math.sqrt(2.0 * math.pi))


def middle_body(
    planes, blocks,
    x_ref, cot_ref, own_ref, other_ref, wo_ref, factors_ref, shared_ref, offsets_ref,
    out_off, gain_ref, shift_ref, shrink_off, in_e, in_r,
    output_ref, gh_ref, t_split, t_full, gatt_out, full_e, full_r,
    hidden, xn_ref, total, back, u2_ref, u3_ref, u4_sum, g4_ref, g3_sum,
    e_vm, r_vm, gown_vm, gother_vm, load_sems, flow_sems, grad_sems,
):
    at = Place(planes)
    f = pl.program_id(0)
    last = 2 * blocks - 1
    core = at.core
    rows_all, width = x_ref.shape
    half = own_ref.shape[1]
    hidden_half = blocks * HIDDEN_BLOCK
    step = 256
    flows = block_flows(at, None, None, full_e, full_r, Rows(flow_sems), MIDDLE_KINDS)
    planes_all = range(planes)

    def pass_on(pair, **how):
        for flow in pair:
            for far in planes_all:
                flow.pass_on(far, fresh=False, **how)

    def pass_next(pair, wait):
        for flow in pair:
            for far in planes_all:
                flow.pass_next(far, wait)

    def arrived(pair, kind):
        for flow in pair:
            for far in planes_all:
                flow.wait(kind, far)

    def loads(index, slot):
        tp_half = jnp.where(index < blocks, at.tp, 1 - at.tp)
        span = pl.ds(pl.multiple_of(index % blocks * HIDDEN_BLOCK, HIDDEN_BLOCK), HIDDEN_BLOCK)
        return (
            pltpu.make_async_copy(full_e.at[:, tp_half, :, span], e_vm.at[slot], load_sems.at[0, slot]),
            pltpu.make_async_copy(full_r.at[:, tp_half, span, :], r_vm.at[slot], load_sems.at[1, slot]),
        )

    def wo_half(part):
        w = wo_ref[:, part]
        return jnp.concatenate([w[i] for i in range(w.shape[0])], axis=1)

    jd, ed, ou, ru = (pl.ds(i * width, width) for i in range(4))
    od = pl.ds(3 * half, half)

    @pl.when(f == 0)
    def _():
        for load in loads(0, 0):
            load.start()
        at.greet(True, False)
        for flow in flows[3]:
            flow.pass_on(1, fresh=False, z=True, core=True)
            flow.pass_on(0, fresh=False, core=True)
        for flow in flows[1]:
            for far in planes_all:
                flow.pass_next(far, False)
        pass_on(flows[2], tp=True)
        w_own, w_other = wo_half(core), wo_half(1 - core)
        for begin in range(0, rows_all, step):
            rows = pl.ds(begin, step)
            own, other = own_ref[rows, :], other_ref[rows, :]
            u2 = (
                dot(own, factors_ref[core, :, od], 1, 1) + dot(other, factors_ref[1 - core, :, od], 1, 1)
            ).astype(B16)
            u2_ref[rows, :] = u2
            h = (
                x_ref[rows, :].astype(F32) + dot(own, w_own) + dot(other, w_other)
                + out_off[...] + dot(u2, shared_ref[:, ou])
            )
            hidden[rows, :] = h
            scaled, _ = row_norm(h)
            xn = (scaled * gain_ref[...] + shift_ref[...]).astype(B16)
            xn_ref[rows, :] = xn
            u3_ref[rows, :] = dot(xn, shared_ref[:, ed], 1, 1).astype(B16)
            g4_ref[rows, :] = dot(cot_ref[rows, :], shared_ref[:, ru], 1, 1).astype(B16)
            total[rows, :] = h + shrink_off[...]
            back[rows, :] = jnp.zeros_like(h)
            u4_sum[rows, :] = jnp.zeros((step, u4_sum.shape[1]), F32)
            g3_sum[rows, :] = jnp.zeros((step, g3_sum.shape[1]), F32)
        for flow in flows[3]:
            flow.pass_on(2, fresh=False, z=True, core=True, wait=True)

    @pl.when(f == 1)
    def _():
        for flow in flows[3]:
            flow.pass_on(3, fresh=False, core=True, wait=True)

    @pl.when(f == 2)
    def _():
        pass_on(flows[3], tp=True)
        arrived(flows[3], OWN_CAME)

    @pl.when(f == 4)
    def _():
        pass_next(flows[2], True)
        arrived(flows[1], NEXT_CAME)

    @pl.when(f == last - 2)
    def _():
        arrived(flows[2], NEXT_CAME)

    @pl.when(f == last - 1)
    def _():
        pass_next(flows[3], True)

    slot = f % 2

    @pl.when(f < last - 1)
    def _():
        for load in loads(f + 1, 1 - slot):
            load.start()

    for load in loads(f, slot):
        load.wait()
    tp_half = jnp.where(f < blocks, at.tp, 1 - at.tp)
    begin_block = f % blocks * HIDDEN_BLOCK

    def block_of(first):
        return pl.ds(pl.multiple_of(first + begin_block, 128), HIDDEN_BLOCK)

    w_e = e_vm[slot].reshape(width, HIDDEN_BLOCK)
    w_r = jnp.concatenate([r_vm[slot, i] for i in range(2 * planes)], axis=1)
    eu = factors_ref[tp_half, :, block_of(4 * half)]
    rd = factors_ref[tp_half, :, block_of(4 * half + hidden_half)]
    wide_off = offsets_ref[tp_half, :, block_of(3 * half)]
    u3, g4 = u3_ref[...], g4_ref[...]
    z = dot(xn_ref[...], w_e) + wide_off + dot(u3, eu)
    gact = dot(cot_ref[...], w_r, 1, 1) + dot(g4, rd)
    cdf, density = gauss_parts(z)
    act = (z * cdf).astype(B16)
    gz = (gact * (cdf + z * density)).astype(B16)
    total[...] += dot(act, w_r)
    u4_sum[...] += dot(act, rd, 1, 1)
    back[...] += dot(gz, w_e, 1, 1)
    g3_sum[...] += dot(gz, eu, 1, 1)
    sum_rd = dot(g4, act, 0, 0)
    sum_eu = dot(u3, gz, 0, 0)
    t_split[tp_half, :, block_of(half + hidden_half)] = sum_rd
    t_split[tp_half, :, block_of(half)] = sum_eu

    @pl.when(f == last - 1)
    def _():
        arrived(flows[3], NEXT_CAME)
        for load in loads(f + 1, 1 - slot):
            load.start()

    @pl.when(f == last)
    def _():
        w_own, w_other = wo_half(core), wo_half(1 - core)
        s_ru, s_ed, s_ou, s_own, s_other = 0.0, 0.0, 0.0, 0.0, 0.0
        moves = []
        for index, begin in enumerate(range(0, rows_all, step)):
            rows = pl.ds(begin, step)
            cot = cot_ref[rows, :]
            u4 = u4_sum[rows, :].astype(B16)
            output_ref[rows, :] = (total[rows, :] + dot(u4, shared_ref[:, ru])).astype(B16)
            s_ru += dot(u4, cot, 0, 0)
            g3 = g3_sum[rows, :].astype(B16)
            s_ed += dot(g3, xn_ref[rows, :], 0, 0)
            gx = back[rows, :] + dot(g3, shared_ref[:, ed])
            scaled, inverse = row_norm(hidden[rows, :])
            gh = cot.astype(F32) + back_norm(gx * gain_ref[...], scaled, inverse)
            gh_ref[rows, :] = gh
            gb = gh.astype(B16)
            s_ou += dot(u2_ref[rows, :], gb, 0, 0)
            g2 = dot(gb, shared_ref[:, ou], 1, 1).astype(B16)
            s_own += dot(g2, own_ref[rows, :], 0, 0)
            s_other += dot(g2, other_ref[rows, :], 0, 0)
            gother_vm[rows, :] = (
                dot(gb, w_other, 1, 1) + dot(g2, factors_ref[1 - core, :, od])
            ).astype(B16)
            there = pltpu.make_async_remote_copy(
                src_ref=gother_vm.at[rows], dst_ref=gatt_out.at[pl.ds(rows_all + begin, step)],
                send_sem=grad_sems.at[0, index], recv_sem=grad_sems.at[1, index],
                device_id=at.next_core, device_id_type=MESH,
            )
            there.start()
            gown_vm[rows, :] = (dot(gb, w_own, 1, 1) + dot(g2, factors_ref[core, :, od])).astype(B16)
            here = pltpu.make_async_copy(gown_vm.at[rows], gatt_out.at[rows], grad_sems.at[2, index])
            here.start()
            moves += [there, here]
        t_full[:, 0:width] = s_ou
        t_full[:, width : 2 * width] = s_ed
        t_full[:, 2 * width :] = s_ru
        t_split[core, :, 0:half] = s_own
        t_split[1 - core, :, 0:half] = s_other
        for index, pair in enumerate(flows[1:]):
            for flow in pair:
                for far in planes_all:
                    flow.sent(far, z=index == 2 and far in (1, 2), tp=index > 0, core=index == 2)
                    flow.sent_next(far)
        for move in moves:
            move.wait()


def middle(
    planes, x, cot, attended, other, w_o, factors, shared, offsets, out_off, gain, shift, shrink_off, w_e, w_r
):
    rows, width = x.shape
    half = attended.shape[1]
    shards_, _, depth, hidden_half = w_e.shape
    rank = factors.shape[1]
    blocks = hidden_half // HIDDEN_BLOCK
    one = lambda shape: pl.BlockSpec(
        shape, lambda f: (0,) * len(shape), pipeline_mode=pl.Buffered(1)
    )
    hbm = pl.BlockSpec(memory_space=pl.ANY)
    shape = jax.ShapeDtypeStruct
    dma = pltpu.SemaphoreType.DMA
    chunks = rows // 256
    return pl.pallas_call(
        functools.partial(middle_body, planes, blocks),
        grid=(2 * blocks,),
        in_specs=[
            one((rows, width)), one((rows, width)), one((rows, half)), one((rows, half)),
            one(w_o.shape), one(factors.shape), one(shared.shape), one(offsets.shape),
            one((1, width)), one((1, width)), one((1, width)), one((1, width)), hbm, hbm,
        ],
        out_specs=[
            one((rows, width)), one((rows, width)),
            one((2, rank, half + 2 * hidden_half)), one((rank, 3 * width)), hbm, hbm, hbm,
        ],
        out_shape=[
            shape((rows, width), B16), shape((rows, width), F32),
            shape((2, rank, half + 2 * hidden_half), F32), shape((rank, 3 * width), F32),
            shape((2 * rows, half), B16), shape(w_e.shape, B16), shape(w_r.shape, B16),
        ],
        input_output_aliases={12: 5, 13: 6},
        scratch_shapes=[
            pltpu.VMEM((rows, width), F32), pltpu.VMEM((rows, width), B16),
            pltpu.VMEM((rows, width), F32), pltpu.VMEM((rows, width), F32),
            pltpu.VMEM((rows, rank), B16), pltpu.VMEM((rows, rank), B16),
            pltpu.VMEM((rows, rank), F32), pltpu.VMEM((rows, rank), B16),
            pltpu.VMEM((rows, rank), F32),
            pltpu.VMEM((2, shards_, depth, HIDDEN_BLOCK), B16),
            pltpu.VMEM((2, shards_, HIDDEN_BLOCK, w_r.shape[3]), B16),
            pltpu.VMEM((rows, half), B16), pltpu.VMEM((rows, half), B16),
            dma((2, 2)), dma((count_rows((), MIDDLE_KINDS), planes)), dma((3, chunks)),
        ],
        compiler_params=pltpu.CompilerParams(
            vmem_limit_bytes=VMEM_LIMIT, collective_id=2, has_side_effects=True
        ),
        cost_estimate=pl.CostEstimate(
            flops=2 * rows * width * (16 * hidden_half // 2 + 4 * half),
            bytes_accessed=40 * 2**20,
            transcendentals=rows * hidden_half * 2,
        ),
    )(x, cot, attended, other, w_o, factors, shared, offsets, out_off, gain, shift, shrink_off, w_e, w_r)


def unproject_body(
    planes,
    x_ref, gh_ref, xn_ref, u_ref, gain_ref, w_ref, factors_ref, shared_ref, own_ref, other_ref,
    home_ref, sums_ref,
    own_vm, other_vm, w_vm, x_vm, gh_vm, xn_vm, stage, split, full, g1_vm, load_sems, move_sems, *spread_refs,
):
    at = Place(planes)
    rows_all, width = x_vm.shape
    half = own_vm.shape[2]
    core = at.core
    spread = Spread(at, split, full, shared_ref[0:8, 4 * width :], sums_ref, *spread_refs)
    halves = ((own_vm, core), (other_vm, 1 - core))
    chunks = rows_all // ROWS

    def load(index, source, target):
        return pltpu.make_async_copy(source, target, load_sems.at[index])

    loads = [load(0, own_ref, own_vm), load(1, other_ref, other_vm), load(2, xn_ref, xn_vm)]
    late = [load(3, x_ref, x_vm), load(4, gh_ref, gh_vm)]
    late += [load(5 + order, w_ref.at[:, owner], w_vm.at[order]) for order, (_, owner) in enumerate(halves)]
    for item in loads + late:
        item.start()
    at.greet(True, True, True, True)
    for item in loads:
        item.wait()
    u = u_ref[...]
    g1 = 0.0
    for source, owner in halves:
        for part in range(3):
            columns = pl.ds(part * half, half)
            g1 += dot(source[part], factors_ref[owner, :, columns], 1, 1)
            split[owner, :, columns] = dot(u, source[part], 0, 0)
    g1 = g1.astype(B16)
    g1_vm[...] = g1
    full[...] = dot(g1, xn_vm[...], 0, 0)
    spread.start()
    order = [2, 0, 3, 1]
    for item in late:
        item.wait()
    quarter = rows_all // 2

    def moves(i):
        tp_half = i * ROWS // quarter
        rows = pl.ds(i * ROWS % quarter, ROWS)
        source, target = stage.at[i], home_ref.at[at.tp, rows]

        def remote(device, came):
            return pltpu.make_async_remote_copy(
                src_ref=source, dst_ref=target, send_sem=move_sems.at[0, i], recv_sem=move_sems.at[came, i],
                device_id=device, device_id_type=MESH,
            )

        mine = at.tp == tp_half
        both = dict(at.turned)
        both["tp"] = 1 - at.tp
        return (
            (mine & jnp.logical_not(at.crosses), lambda: pltpu.make_async_copy(source, target, move_sems.at[0, i]), True),
            (mine & at.crosses, lambda: remote(at.turned, 1), False),
            (jnp.logical_not(mine) & jnp.logical_not(at.crosses), lambda: remote(at.next_tp, 2), False),
            (jnp.logical_not(mine) & at.crosses, lambda: remote(both, 2), False),
        )

    spread.second()
    stages = [spread.third, lambda: spread.planes(0), lambda: spread.planes(1), lambda: spread.planes(2)]
    for count, i in enumerate(order):
        span = pl.ds(i * ROWS, ROWS)
        gx = dot(g1_vm[span, :], shared_ref[:, 0:width])
        for index, (source, _) in enumerate(halves):
            for part in range(3):
                gx += dot(source[part, span, :], w_vm[index, :, part].reshape(width, half), 1, 1)
        scaled, inverse = row_norm(x_vm[span, :].astype(F32))
        stage[i] = (gh_vm[span, :] + back_norm(gx * gain_ref[...], scaled, inverse)).astype(B16)
        for there, move, _ in moves(i):
            pl.when(there)(lambda move=move: move().start())
        stages[count]()
    for distance in range(3, planes):
        spread.planes(distance)
    spread.finish()
    spread.sent()
    for i in range(chunks):
        for there, move, here in moves(i):
            if here:
                pl.when(there)(lambda move=move: move().wait())
            else:
                pl.when(there)(lambda move=move: move().wait_send())
    for i in range(chunks):
        tp_half = i * ROWS // quarter
        rows = pl.ds(i * ROWS % quarter, ROWS)

        def came(slot):
            return pltpu.make_async_remote_copy(
                src_ref=stage.at[i], dst_ref=home_ref.at[slot, rows], send_sem=move_sems.at[0, i],
                recv_sem=move_sems.at[1, i], device_id=at.next_tp, device_id_type=MESH,
            )

        pl.when((at.tp == tp_half) & at.crosses)(lambda came=came: came(at.tp).wait_recv())

    for i in range(chunks):
        tp_half = i * ROWS // quarter
        rows = pl.ds(i * ROWS % quarter, ROWS)

        def came(slot):
            return pltpu.make_async_remote_copy(
                src_ref=stage.at[i], dst_ref=home_ref.at[slot, rows], send_sem=move_sems.at[0, i],
                recv_sem=move_sems.at[2, i], device_id=at.next_tp, device_id_type=MESH,
            )

        pl.when(at.tp == tp_half)(lambda came=came: came(1 - at.tp).wait_recv())


def unproject(planes, x, gh, xn, u, gain, weight, factors, shared, own, other, adapters):
    rows, width = x.shape
    half = own.shape[2]
    rank = factors.shape[1]
    hbm = pl.BlockSpec(memory_space=pl.ANY)
    vmem = pl.BlockSpec(memory_space=pltpu.VMEM)
    shape = jax.ShapeDtypeStruct
    dma = pltpu.SemaphoreType.DMA
    chunks = rows // ROWS
    keep = 3 * half + width
    return pl.pallas_call(
        functools.partial(unproject_body, planes),
        in_specs=[hbm, hbm, hbm, vmem, vmem, hbm, vmem, vmem, hbm, hbm],
        out_specs=[hbm, vmem],
        out_shape=[shape((2, rows // 2, width), B16), shape((adapters, rank, keep), F32)],
        scratch_shapes=[
            pltpu.VMEM(own.shape, B16), pltpu.VMEM(own.shape, B16),
            pltpu.VMEM((2, weight.shape[0]) + weight.shape[2:], B16),
            pltpu.VMEM((rows, width), B16), pltpu.VMEM((rows, width), F32), pltpu.VMEM((rows, width), B16),
            pltpu.VMEM((chunks, ROWS, width), B16),
            pltpu.VMEM((2, rank, 3 * half), F32), pltpu.VMEM((rank, width), F32), pltpu.VMEM((rows, rank), B16),
            dma((7,)), dma((3, chunks)),
        ]
        + Spread.scratch(planes, rank // 2, 3 * half, width),
        compiler_params=pltpu.CompilerParams(
            vmem_limit_bytes=VMEM_LIMIT, collective_id=4, has_side_effects=True
        ),
        cost_estimate=pl.CostEstimate(
            flops=2 * rows * width * 6 * half, bytes_accessed=20 * 2**20, transcendentals=0
        ),
    )(x, gh, xn, u, gain, weight, factors, shared, own, other)


def rate_parts():
    lane = np.arange(128) % 64
    rates = np.exp((lane % 10).astype(np.float32) * np.float32(-math.log(10000.0) / 10.0)).astype(np.float32)
    rates = np.where(lane[None] // 20 == np.arange(3)[:, None], rates[None], np.float32(0.0)).astype(np.float32)
    parts = []
    for _ in range(3):
        part = rates.astype(ml_dtypes.bfloat16)
        parts.append(part)
        rates = rates - part.astype(np.float32)
    parts.append(np.zeros((7, 128), ml_dtypes.bfloat16))
    return jnp.asarray(np.concatenate(parts, axis=0))


def clip_shards(
    planes,
    tokens,
    cotangent,
    adapter_pick,
    positions,
    first_gain,
    first_shift,
    joined_weight,
    joined_bias,
    output_weight,
    mixing_exit_offset,
    second_gain,
    second_shift,
    expand_weight,
    widening_offset,
    reduce_weight,
    shrinking_offset,
    joined_down,
    joined_up,
    output_down,
    output_up,
    expand_down,
    expand_up,
    reduce_down,
    reduce_up,
):
    half = joined_weight.shape[2]
    hidden_half = expand_weight.shape[1]
    rank = joined_up.shape[1]
    turn_last = lambda array: jnp.swapaxes(array, 1, 2)
    tables = (
        turn_last(joined_down), turn_last(expand_down), output_up, reduce_up,
        turn_last(joined_up), turn_last(output_down), expand_up, turn_last(reduce_down),
    )
    (
        x, factors, shared, offsets, w_j, w_o, w_e, w_r, query, key, value, xn1, u1, cosine, sine,
    ) = project(
        planes, tokens, adapter_pick, positions, joined_bias, widening_offset[None], tables,
        jnp.transpose(joined_weight, (1, 0, 2)), output_weight, expand_weight, reduce_weight,
        first_gain[None], first_shift[None], rate_parts(),
    )
    attended, inverse, weights, other_heads, cot, w_o, w_e, w_r = attend(
        planes, query, key, value, cotangent, output_weight, expand_weight, reduce_weight, w_o, w_e, w_r
    )
    out, gh, split, full, grad_att, w_e, w_r = middle(
        planes, x, cot, attended, other_heads, w_o, factors, shared, offsets,
        mixing_exit_offset[None], second_gain[None], second_shift[None], shrinking_offset[None], w_e, w_r,
    )
    adapters = joined_down.shape[0]
    width = tokens.shape[2]
    tag = shared[: rank // 2, 4 * width :]
    own, other, sums, output = attend_back(
        planes, query, key, value, attended, inverse, grad_att, weights, cosine, sine, split, full, tag, out, adapters
    )
    tokens_grad, late_sums = unproject(
        planes, x, gh, xn1, u1, first_gain[None], w_j, factors, shared, own, other, adapters
    )

    def cut(array, *sizes):
        begin, pieces = 0, []
        for size in sizes:
            pieces.append(array[:, :, begin : begin + size])
            begin += size
        return pieces

    s_od, s_eu, s_rd, s_ou, s_ed, s_ru = cut(sums, half, hidden_half, hidden_half, width, width, width)
    s_fu, s_fd = cut(late_sums, 3 * half, width)
    return (
        output,
        tokens_grad,
        turn_last(s_fd),
        s_fu.reshape(adapters, rank, 3, half),
        turn_last(s_od),
        s_ou,
        turn_last(s_ed),
        s_eu,
        turn_last(s_rd),
        s_ru,
    )


def solution(mesh):
    sizes = dict(mesh.shape)
    if sizes["ctx"] == 2 and sizes["tp"] == 2 and sizes["shard"] == 8:
        body = functools.partial(clip_shards, sizes["shard"] // 2)
    else:
        body = general_shards
    return jax.shard_map(
        body,
        mesh=mesh,
        in_specs=(
            P("shard", "ctx", None),
            P("shard", "ctx", None),
            P("shard"),
            P(None, "shard", "ctx"),
            P(),
            P(),
            P("shard", None, "tp"),
            P(None, "tp"),
            P("tp", "shard"),
            P(),
            P(),
            P(),
            P("shard", "tp"),
            P("tp"),
            P("tp", "shard"),
            P(),
            P(),
            P(None, None, None, "tp"),
            P(None, "tp", None),
            P(),
            P(),
            P(None, None, "tp"),
            P(None, "tp", None),
            P(),
        ),
        out_specs=(
            P("shard", "ctx", None),
            P("shard", ("ctx", "tp"), None),
            P(),
            P(None, None, None, "tp"),
            P(None, "tp", None),
            P(),
            P(),
            P(None, None, "tp"),
            P(None, "tp", None),
            P(),
        ),
        check_vma=False,
    )
```
